32 devices in a mesh: section: 2 (over y), row: 4 (over x, core), col: 4 (over z).
Axes of the slice: x: 2, y: 2, z: 4, core: 2. Of those that a mesh axis runs over, the one named last changes fastest.
Arguments:
- inputs: bfloat16 [2, 4096, 2048], P(None, 'row', 'col'), may hold values from -6 to 6
- cotangent: bfloat16 [2, 4096, 2048], P(None, 'row', 'col'), may hold values from -6 to 6
- block_ids: int32 [2, 4096], replicated, may hold values from 0 to 31, never falling along the last dimension, each value on 1 to 256 neighbouring positions
- norm_gains: float32 [2, 2, 2048], P('section', None, 'col'), may hold values from 0.5 to 1.5
- norm_shifts: float32 [2, 2, 2048], P('section', None, 'col'), may hold values from -1 to 1
- qkv_weight: bfloat16 [2, 2048, 3, 2048], P('section', 'row', None, 'col'), may hold values from -0.125 to 0.125
- qkv_bias: float32 [2, 3, 2048], P('section', None, 'col'), may hold values from -3 to 3
- out_weight: bfloat16 [2, 2048, 2048], P('section', 'row', 'col'), may hold values from -0.375 to 0.375
- gate_up_weight: bfloat16 [2, 2048, 2, 5632], P('section', 'row', None, 'col'), may hold values from -0.125 to 0.125
- down_weight: bfloat16 [2, 2048, 5632], P('section', 'row', 'col'), may hold values from -0.109375 to 0.109375
Outputs:
- hidden_states: bfloat16 [2, 2, 4096, 2048], P('section', None, 'row', 'col')
- input_grads: float32 [2, 2, 4096, 2048], P('section', None, 'row', 'col')
- norm_gain_grads: float32 [2, 2, 2048], P('section', None, 'col')
- norm_shift_grads: float32 [2, 2, 2048], P('section', None, 'col')
- qkv_weight_grad: float32 [2, 2048, 3, 2048], P('section', 'row', None, 'col')
- qkv_bias_grad: float32 [2, 3, 2048], P('section', None, 'col')
- out_weight_grad: float32 [2, 2048, 2048], P('section', 'row', 'col')
- gate_up_grad: float32 [2, 2048, 2, 5632], P('section', 'row', None, 'col')
- down_grad: float32 [2, 2048, 5632], P('section', 'row', 'col')
The draws below stay inside these ranges and needn't reach their ends.
Inputs may be any that keep to these rules, and one draw needn't show every extreme that they name: `block_ids`: along each sequence the block ids never fall; a block holds 1 to 256 tokens, and some block exactly 256.
All inputs are finite; a program needn't handle non-finite values.
Results may differ from the reference program's by a relative error of at most 0.013.
Values may be sent and summed in bfloat16 or wider, within the bound.
A program may use at most 576 MiB of HBM per device.

```python
import math
import jax
import jax.numpy as jnp
import numpy as np
from jax import lax

D = 2048
HEADS = 32
HEAD_DIM = 64
ROT = 16
FF = 5632
MB = 2
SEQ = 4096
BLOCK = 256
BLOCKS = 32


def steps_of(stream_key, shape, shards, smallest, largest):
    gain = 1.0
    for axis_at, blocks in shards:
        steps = jax.random.uniform(jax.random.fold_in(jax.random.fold_in(stream_key, 6), axis_at), (blocks,), jnp.float32, smallest / len(shards), largest / len(shards))
        gain = gain * jnp.repeat(jnp.exp(steps), shape[axis_at] // blocks).reshape((-1,) + (1,) * (len(shape) - 1 - axis_at))
    return gain


def length_profile(number_of, total, reach, lean):
    weights = [(1 << 20) // math.isqrt(grade ** lean) + 1 for grade in range(2, number_of + 1)]
    rest, given = total - reach - (number_of - 1), [1] * (number_of - 1)
    while rest > 0:
        candidates = [i for i in range(number_of - 1) if given[i] < reach]
        mass, remaining = sum([weights[i] for i in candidates]), rest
        for i in candidates:
            more = min(reach - given[i], max(1, remaining * weights[i] // mass), rest)
            given[i] = given[i] + more
            rest = rest - more
    return np.array([reach] + given)


def ragged_sizes(key, amount, total, reach, skew):
    if amount == 2:
        one = jax.random.randint(key, (), max(1, total - reach), min(reach, total - 1) + 1)
        return jnp.stack([one, total - one])
    sizes = jnp.asarray(length_profile(amount, total, reach, skew), jnp.int32)
    pairs = (amount - 1) // 2
    giver, sink = sizes[1:1 + 2 * pairs:2], sizes[2:2 + 2 * pairs:2]
    margin = jnp.minimum(giver - 1, reach - sink)
    passed = jax.random.randint(jax.random.fold_in(key, 1), (pairs,), 0, 1 << 20) % (margin + 1)
    sizes = sizes.at[1:1 + 2 * pairs:2].set(giver - passed).at[2:2 + 2 * pairs:2].set(sink + passed)
    return sizes[jax.random.permutation(jax.random.fold_in(key, 2), amount)]


def scatter_about(stream_key, shape, spread, reach, split=(), kind=jnp.bfloat16):
    loudness = steps_of(stream_key, shape, split, -0.22, 0.18) if split else 1.0
    values = jax.random.normal(stream_key, shape, jnp.float32) * spread * loudness
    return jnp.minimum(jnp.maximum(values, -reach), reach).astype(kind)


def setup_inputs(seed: int = 0) -> dict:
    key_of = jax.random.split(jax.random.key(seed), 11)
    inputs = scatter_about(key_of[0], (MB, SEQ, D), 1.0, 6.0, ((1, 4), (2, 4)))
    cotangent = scatter_about(key_of[1], (MB, SEQ, D), 1.0, 6.0, ((1, 4), (2, 4)))
    block_ids = jax.vmap(lambda own: jnp.searchsorted(jnp.cumsum(ragged_sizes(own, BLOCKS, SEQ, BLOCK, 1)), jnp.arange(SEQ), side="right"))(jax.random.split(key_of[2], MB)).reshape((MB, SEQ)).astype(jnp.int32)
    norm_gains = jnp.clip(1.0 + 0.1 * jax.random.normal(key_of[3], (2, 2, D), jnp.float32), 0.5, 1.5)
    norm_shifts = scatter_about(key_of[4], (2, 2, D), 0.2, 1.0, ((0, 2), (2, 4)), jnp.float32)
    qkv_weight = scatter_about(key_of[5], (2, D, 3, D), D ** -0.5, 0.125, ((0, 2), (1, 4), (3, 4)))
    qkv_bias = scatter_about(key_of[6], (2, 3, D), 0.5, 3.0, ((0, 2), (2, 4)), jnp.float32)
    out_weight = scatter_about(key_of[7], (2, D, D), (D // 8) ** -0.5, 0.375, ((0, 2), (1, 4), (2, 4)))
    gate_up_weight = scatter_about(key_of[8], (2, D, 2, FF), D ** -0.5, 0.125, ((0, 2), (1, 4), (3, 4)))
    down_weight = scatter_about(key_of[9], (2, D, FF), (FF // 2) ** -0.5, 0.109375, ((0, 2), (1, 4), (2, 4)))
    return {"inputs": inputs, "cotangent": cotangent, "block_ids": block_ids, "norm_gains": norm_gains, "norm_shifts": norm_shifts, "qkv_weight": qkv_weight, "qkv_bias": qkv_bias, "out_weight": out_weight, "gate_up_weight": gate_up_weight, "down_weight": down_weight}


@jax.custom_vjp
def low(v):
    return lax.optimization_barrier(v.astype(jnp.bfloat16)).astype(jnp.float32)

@jax.custom_vjp
def low_back(v):
    return v

def low_keep(v):
    return (low(v), None)

def low_pass(kept, grad):
    return (grad,)

def back_keep(v):
    return (v, None)

def back_low(kept, grad):
    return (low(grad),)
low.defvjp(low_keep, low_pass)
low_back.defvjp(back_keep, back_low)
epsilon = 1e-05
highest = lax.Precision.HIGHEST

def rotary_tables(positions):
    half_dims = ROT // 2
    inverse_freq = 1.0 / 10000.0 ** (jnp.arange(half_dims, dtype=jnp.float32) * 2.0 / ROT)
    angles = positions.astype(jnp.float32)[:, None] * inverse_freq[None, :]
    return (jnp.cos(angles)[:, None, :], jnp.sin(angles)[:, None, :])

def rotate(values, cosine_table, sine_table):
    half_dims = ROT // 2
    first_half = values[..., :half_dims]
    second_half = values[..., half_dims:ROT]
    return jnp.concatenate([first_half * cosine_table - second_half * sine_table, second_half * cosine_table + first_half * sine_table, values[..., ROT:]], axis=-1)

def layer_norm(values, norm_gain, offset):
    mean_value = lax.optimization_barrier(jnp.mean(values, axis=-1, keepdims=True))
    variance = lax.optimization_barrier(jnp.mean(values * values, axis=-1, keepdims=True)) - mean_value * mean_value
    return (values - mean_value) * lax.rsqrt(variance + epsilon) * norm_gain + offset

def attention(queries, keys_all, values_all, block_all):
    row_count = min(512, SEQ)
    block_count = SEQ // row_count
    score_scale = HEAD_DIM ** (-0.5)

    def one_block(pieces):
        query_block, block_rows = pieces
        scores = low_back(jnp.einsum('qhd,khd->hqk', query_block, keys_all, precision=highest) * score_scale)
        visible = block_all[None, None, :] <= block_rows[None, :, None]
        scores = jnp.where(visible, scores, -1e+30)
        row_max = lax.optimization_barrier(jnp.max(scores, axis=-1, keepdims=True))
        weights = jnp.exp(scores - row_max)
        chances = low(weights / lax.optimization_barrier(jnp.sum(weights, axis=-1, keepdims=True)))
        return jnp.einsum('hqk,khd->qhd', chances, values_all, precision=highest)
    outcome = lax.map(jax.checkpoint(one_block), (queries.reshape(block_count, row_count, HEADS, HEAD_DIM), block_all.reshape(block_count, row_count)))
    return outcome.reshape(SEQ, HEADS, HEAD_DIM)

def run_layer(stream, params, block_all, cosine_table, sine_table):
    gains, shifts, qkv_w, qkv_b, out_w, gate_up_w, down_w = params
    normed = low(layer_norm(stream, gains[0], shifts[0]))
    qkv_rows = low_back(jnp.einsum('td,dsk->tsk', normed, qkv_w, precision=highest) + qkv_b)
    queries = low(rotate(qkv_rows[:, 0].reshape(SEQ, HEADS, HEAD_DIM), cosine_table, sine_table))
    keys_rot = low(rotate(qkv_rows[:, 1].reshape(SEQ, HEADS, HEAD_DIM), cosine_table, sine_table))
    values = low(qkv_rows[:, 2].reshape(SEQ, HEADS, HEAD_DIM))
    attn_mix = attention(queries, keys_rot, values, block_all).reshape(SEQ, D)
    attn_mix = low(low_back(attn_mix))
    after_attn = stream + low_back(jnp.dot(attn_mix, out_w.T, precision=highest))
    normed_two = low(layer_norm(low(after_attn), gains[1], shifts[1]))
    gate_up = low_back(jnp.einsum('td,dsf->tsf', normed_two, gate_up_w, precision=highest))
    hidden = low(jax.nn.silu(gate_up[:, 0]) * gate_up[:, 1])
    return low(after_attn + low_back(jnp.dot(hidden, down_w.T, precision=highest)))

def reference(inputs, cotangent, block_ids, norm_gains, norm_shifts, qkv_weight, qkv_bias, out_weight, gate_up_weight, down_weight):
    positions = jnp.arange(SEQ, dtype=jnp.int32)
    cosine_table, sine_table = rotary_tables(positions)
    stacked = tuple((array.astype(jnp.float32) for array in (norm_gains, norm_shifts, qkv_weight, qkv_bias, out_weight, gate_up_weight, down_weight)))
    params_first = tuple((array[0] for array in stacked))
    params_second = tuple((array[1] for array in stacked))

    def one_batch(totals, pieces):
        stream, cot_rows, block_all = pieces

        def apply_layer(values, params):
            return run_layer(values, params, block_all, cosine_table, sine_table)
        middle, pull_first = jax.vjp(apply_layer, stream.astype(jnp.float32), params_first)
        final, pull_second = jax.vjp(apply_layer, middle, params_second)
        d_middle, grads_second = pull_second(cot_rows.astype(jnp.float32))
        d_stream, grads_first = pull_first(d_middle)
        totals = tuple((total + jnp.stack([first_grad, second_grad]) for total, first_grad, second_grad in zip(totals, grads_first, grads_second)))
        return (totals, (middle.astype(jnp.bfloat16), final.astype(jnp.bfloat16), d_stream, d_middle))
    zeros = tuple((jnp.zeros(array.shape, jnp.float32) for array in stacked))
    totals, (middles, finals, d_streams, d_middles) = lax.scan(one_batch, zeros, (inputs, cotangent, block_ids))
    hidden_states = jnp.stack([middles, finals])
    input_grads = jnp.stack([d_streams, d_middles])
    return (hidden_states, input_grads, totals[0], totals[1], totals[2], totals[3], totals[4], totals[5], totals[6])
```

```python
import functools

import jax
import jax.numpy as jnp
from jax import lax
from jax.experimental import pallas as pl
from jax.experimental.pallas import tpu as pltpu
from jax.sharding import PartitionSpec as P

D = 2048
HEADS = 32
HEAD_DIM = 64
ROT = 16
LANES = 128
REACH = 256


epsilon = 1e-05

def dot_last(a,b):
    return lax.dot_general(a,b,(((1,),(1,)),((),())),preferred_element_type=jnp.float32)
def dot_first(a,b):
    return lax.dot_general(a,b,(((0,),(0,)),((),())),preferred_element_type=jnp.float32)

def lanes_of(rows, head):
    lane = lax.broadcasted_iota(jnp.int32, (rows,128), 1)
    return (lane//HEAD_DIM)==head

def attend_kernel(heads, bq, bk, bid_q, bid_k, q_ref, k_ref, v_ref, o_ref, lse_ref, vone, scores):
    i = pl.program_id(0)
    seq = k_ref.shape[0]
    @pl.when(i==0)
    def _():
        for h in range(heads):
            vone[h] = jnp.where(lanes_of(seq,h), v_ref[...], jnp.ones((),jnp.bfloat16))
    q = q_ref[...]
    free = i*(bq//bk)
    last = jnp.minimum(((i+1)*bq+REACH+bk-1)//bk, seq//bk)
    qs = [jnp.where(lanes_of(bq,h), q, jnp.zeros((),jnp.bfloat16)) for h in range(heads)]
    def fold(s, m):
        for c in range(bk//128):
            m = jnp.maximum(m, s[:, c*128:(c+1)*128])
        return m
    def plain(t, ms):
        keys = k_ref[pl.ds(t*bk,bk),:]
        out=[]
        for h in range(heads):
            s=dot_last(qs[h], keys)
            scores[h,:,pl.ds(t*bk,bk)] = s
            out.append(fold(s, ms[h]))
        return tuple(out)
    def masked(t, ms):
        keys = k_ref[pl.ds(t*bk,bk),:]
        vis = bid_k[:, pl.ds(t*bk,bk)] <= bid_q[...]
        out=[]
        for h in range(heads):
            s=jnp.where(vis, dot_last(qs[h], keys), -1e30)
            scores[h,:,pl.ds(t*bk,bk)] = s
            out.append(fold(s, ms[h]))
        return tuple(out)
    ms = tuple(jnp.full((bq,128),-1e30,jnp.float32) for _ in range(heads))
    ms = lax.fori_loop(0, free, plain, ms)
    ms = lax.fori_loop(free, last, masked, ms)
    ms = [jnp.max(m,axis=1,keepdims=True) for m in ms]
    def mix(t, accs):
        out=[]
        for h in range(heads):
            p=jnp.exp(scores[h,:,pl.ds(t*bk,bk)]-ms[h]).astype(jnp.bfloat16)
            out.append(accs[h]+jnp.dot(p, vone[h,pl.ds(t*bk,bk),:], preferred_element_type=jnp.float32))
        return tuple(out)
    accs = lax.fori_loop(0, last, mix, tuple(jnp.zeros((bq,128),jnp.float32) for _ in range(heads)))
    total=None
    lse=None
    for h in range(heads):
        sums = pltpu.roll(accs[h], HEAD_DIM, 1)
        o = accs[h]/sums
        l = ms[h] + jnp.log(sums)
        mine = lanes_of(bq,h)
        total = jnp.where(mine, o, 0.0 if total is None else total)
        lse = jnp.where(mine, l, 0.0 if lse is None else lse)
    o_ref[...] = total.astype(jnp.bfloat16)
    lse_ref[...] = lse.T

def attend(q,k,v,block_all,heads,bq=512,bk=512):
    seq=q.shape[0]
    vm=pl.BlockSpec(memory_space=pltpu.VMEM)
    return pl.pallas_call(
        functools.partial(attend_kernel, heads,bq,bk),
        grid=(seq//bq,),
        in_specs=[pl.BlockSpec((bq,1),lambda i:(i,0)), pl.BlockSpec((1,seq),lambda i:(0,0)),
                  pl.BlockSpec((bq,128),lambda i:(i,0)), pl.BlockSpec((seq,128),lambda i:(0,0)), pl.BlockSpec((seq,128),lambda i:(0,0))],
        out_specs=[pl.BlockSpec((bq,128),lambda i:(i,0)), pl.BlockSpec((128,bq),lambda i:(0,i))],
        out_shape=[jax.ShapeDtypeStruct((seq,128),jnp.bfloat16), jax.ShapeDtypeStruct((128,seq),jnp.float32)],
        scratch_shapes=[pltpu.VMEM((heads,seq,128),jnp.bfloat16), pltpu.VMEM((heads,bq,seq),jnp.float32)],
        compiler_params=pltpu.CompilerParams(vmem_limit_bytes=56*2**20),
        cost_estimate=pl.CostEstimate(flops=heads*seq*seq*256,bytes_accessed=seq*128*12,transcendentals=heads*seq*seq//2),
    )(block_all.reshape(seq,1), block_all.reshape(1,seq), q,k,v)

def spin(x, cosines, sines):
    lane = lax.broadcasted_iota(jnp.int32, x.shape, 1)
    other = jnp.where(lane % ROT < ROT//2, pltpu.roll(x, 128-ROT//2, 1), pltpu.roll(x, ROT//2, 1))
    return x*cosines + other*sines

def attend_back_kernel(heads, bq, bk, bid_q, bid_k, q_ref, k_ref, v_ref, g_ref, o_ref, lse_ref, cos_ref, sin_ref,
                       dq_ref, dk_ref, dv_ref, kone, dk_acc, dv_acc):
    i = pl.program_id(0)
    seq = k_ref.shape[0]
    zero = jnp.zeros((),jnp.bfloat16)
    @pl.when(i==0)
    def _():
        for h in range(heads):
            kone[h] = jnp.where(lanes_of(seq,h), k_ref[...], zero)
        dk_acc[...] = jnp.zeros_like(dk_acc)
        dv_acc[...] = jnp.zeros_like(dv_acc)
    q = q_ref[...]; g = g_ref[...]
    prod = (g.astype(jnp.float32)*o_ref[...].astype(jnp.float32)).T
    deltas = [jnp.sum(prod[h*HEAD_DIM:(h+1)*HEAD_DIM],axis=0,keepdims=True) for h in range(heads)]
    lses = [lse_ref[h*HEAD_DIM:h*HEAD_DIM+1,:] for h in range(heads)]
    qs = [jnp.where(lanes_of(bq,h), q, zero) for h in range(heads)]
    gs = [jnp.where(lanes_of(bq,h), g, zero) for h in range(heads)]
    free = i*(bq//bk)
    last = jnp.minimum(((i+1)*bq+REACH+bk-1)//bk, seq//bk)
    def tile(t, dq, hide):
        here = pl.ds(t*bk,bk)
        keys = k_ref[here,:]; vals = v_ref[here,:]
        dv = dv_acc[here,:]; dk = dk_acc[here,:]
        if hide: vis = bid_k[here,:] <= bid_q[...]
        for h in range(heads):
            s = dot_last(keys, qs[h])
            if hide: s = jnp.where(vis, s, -1e30)
            p = jnp.exp(s - lses[h])
            dp = dot_last(vals, gs[h])
            ds = (p*(dp-deltas[h])).astype(jnp.bfloat16)
            dv = dv + jnp.dot(p.astype(jnp.bfloat16), gs[h], preferred_element_type=jnp.float32)
            dk = dk + jnp.dot(ds, qs[h], preferred_element_type=jnp.float32)
            dq = dq + dot_first(ds, kone[h,here,:])
        dv_acc[here,:] = dv; dk_acc[here,:] = dk
        return dq
    dq = jnp.zeros((bq,128),jnp.float32)
    dq = lax.fori_loop(0, free, lambda t,c: tile(t,c,False), dq)
    dq = lax.fori_loop(free, last, lambda t,c: tile(t,c,True), dq)
    rows = pl.ds(i*bq,bq)
    dq_ref[...] = spin(dq*(HEAD_DIM**-0.5), cos_ref[rows,:], -sin_ref[rows,:]).astype(jnp.bfloat16)
    @pl.when(i==pl.num_programs(0)-1)
    def _():
        dk_ref[...] = spin(dk_acc[...], cos_ref[...], -sin_ref[...]).astype(jnp.bfloat16)
        dv_ref[...] = dv_acc[...].astype(jnp.bfloat16)

def attend_back(q,k,v,g,o,lse,block_all,cosines,sines,heads,bq=512,bk=512):
    seq=q.shape[0]
    row=pl.BlockSpec((bq,128),lambda i:(i,0)); whole=pl.BlockSpec((seq,128),lambda i:(0,0))
    return pl.pallas_call(
        functools.partial(attend_back_kernel, heads,bq,bk),
        grid=(seq//bq,),
        in_specs=[pl.BlockSpec((1,bq),lambda i:(0,i)), pl.BlockSpec((seq,1),lambda i:(0,0)), row, whole, whole, row, row,
                  pl.BlockSpec((128,bq),lambda i:(0,i)), whole, whole],
        out_specs=[row, whole, whole],
        out_shape=[jax.ShapeDtypeStruct((seq,128),jnp.bfloat16)]*3,
        scratch_shapes=[pltpu.VMEM((heads,seq,128),jnp.bfloat16), pltpu.VMEM((seq,128),jnp.float32), pltpu.VMEM((seq,128),jnp.float32)],
        compiler_params=pltpu.CompilerParams(vmem_limit_bytes=56*2**20),
        cost_estimate=pl.CostEstimate(flops=heads*seq*seq*640,bytes_accessed=seq*128*20,transcendentals=heads*seq*seq//2),
    )(block_all.reshape(1,seq), block_all.reshape(seq,1), q,k,v,g,o,lse,cosines,sines)


def lanes_padded(values):
    width = values.shape[-1]
    if width == LANES:
        return values
    return jnp.pad(values, ((0, 0), (0, LANES - width)))


def rotary_lanes(positions, width):
    half_dims = ROT // 2
    inverse_freq = 1.0 / 10000.0 ** (jnp.arange(half_dims, dtype=jnp.float32) * 2.0 / ROT)
    angles = positions.astype(jnp.float32)[:, None] * inverse_freq[None, :]
    cosine, sine = jnp.cos(angles), jnp.sin(angles)
    rest = jnp.zeros((positions.shape[0], HEAD_DIM - ROT), jnp.float32)
    cosines = jnp.concatenate([cosine, cosine, rest + 1.0], axis=1)
    sines = jnp.concatenate([-sine, sine, rest], axis=1)
    return jnp.tile(cosines, (1, width // HEAD_DIM)), jnp.tile(sines, (1, width // HEAD_DIM))


def rotate(values, cosines, sines):
    lane = lax.broadcasted_iota(jnp.int32, values.shape, 1)
    other = jnp.where(
        lane % ROT < ROT // 2, jnp.roll(values, -(ROT // 2), axis=1), jnp.roll(values, ROT // 2, axis=1)
    )
    return values * cosines + other * sines


def statistics(values):
    mean = jnp.mean(values, axis=-1, keepdims=True)
    spread = jnp.mean(values * values, axis=-1, keepdims=True) - mean * mean
    return mean, lax.rsqrt(spread + epsilon)


def layer_norm(values, gain, shift):
    values = values.astype(jnp.float32)
    mean, inverse = statistics(values)
    return ((values - mean) * inverse * gain + shift).astype(jnp.bfloat16)


def norm_back(grads, values, gain):
    values = values.astype(jnp.float32)
    grads = grads.astype(jnp.float32)
    mean, inverse = statistics(values)
    centred = (values - mean) * inverse
    scaled = grads * gain
    back = inverse * (
        scaled
        - jnp.mean(scaled, axis=-1, keepdims=True)
        - centred * jnp.mean(scaled * centred, axis=-1, keepdims=True)
    )
    return back, jnp.stack([jnp.sum(grads * centred, axis=0), jnp.sum(grads, axis=0)])


def summed_rows(partial):
    return lax.psum_scatter(partial.astype(jnp.bfloat16), "col", scatter_dimension=0, tiled=True)


def gathered_rows(own):
    return lax.all_gather(own, "col", axis=0, tiled=True)


def product(left, right):
    return jnp.dot(left, right, preferred_element_type=jnp.float32)


def per_device(
    inputs,
    cotangent,
    block_ids,
    norm_gains,
    norm_shifts,
    qkv_weight,
    qkv_bias,
    out_weight,
    gate_up_weight,
    down_weight,
):
    section = lax.axis_index("section")
    row = lax.axis_index("row")
    col = lax.axis_index("col")
    rows_axis = lax.axis_size("row")
    cols_axis = lax.axis_size("col")
    tokens, width = inputs.shape[1:]
    owned = tokens // cols_axis
    units = down_weight.shape[2]
    seq = tokens * rows_axis
    copies = max(1, rows_axis * HEAD_DIM // width)
    head_width = width * copies // rows_axis
    heads = head_width // HEAD_DIM
    both = ("section", "row")

    def weights_of(block):
        block = block[0].reshape(block.shape[1], -1)
        return lax.all_gather(block, both, axis=0, tiled=True).reshape(2, D, -1)

    qkv_w = weights_of(qkv_weight)
    out_w = weights_of(out_weight)
    gate_up_w = weights_of(gate_up_weight)
    down_w = weights_of(down_weight)
    small = lax.all_gather(
        jnp.concatenate([norm_gains, norm_shifts], axis=1), "section", axis=0, tiled=True
    )
    small = lax.all_gather(small, "col", axis=2, tiled=True)
    gains, shifts = small[:, :2], small[:, 2:]
    bias = lax.all_gather(qkv_bias, "section", axis=0, tiled=True).reshape(2, -1)

    ids = lax.dynamic_index_in_dim(block_ids, section, 0, keepdims=False)
    positions = row * tokens + jnp.arange(tokens, dtype=jnp.int32)
    cosines, sines = rotary_lanes(positions, width)
    cos_all, sin_all = rotary_lanes(jnp.arange(seq, dtype=jnp.int32), LANES)

    def mine(values):
        return lax.dynamic_slice_in_dim(values, col * owned, owned, 0)

    def my_features(values):
        return lax.dynamic_slice_in_dim(values, col * width, width, 1)

    def to_heads(values):
        if copies > 1:
            whole = values.reshape(values.shape[:-1] + (-1, HEAD_DIM))
            values = jnp.repeat(whole, copies, axis=-2).reshape(values.shape[:-1] + (-1,))
        return lax.all_to_all(values, "row", values.ndim - 1, 0, tiled=True)

    def from_heads(values):
        values = lax.all_to_all(values, "row", 0, values.ndim - 1, tiled=True)
        if copies > 1:
            whole = values.reshape(values.shape[:-1] + (-1, copies, HEAD_DIM))
            values = whole[..., 0, :].reshape(values.shape[:-1] + (-1,))
        return values

    def by_features(values):
        return lax.all_to_all(values, "col", 1, 0, tiled=True)

    stream = lax.all_gather(
        lax.dynamic_index_in_dim(inputs, section, 0, keepdims=False), "col", axis=1, tiled=True
    )
    kept = []
    hidden_out = []
    for layer in range(2):
        normed = layer_norm(stream, gains[layer, 0], shifts[layer, 0])
        qkv = product(normed, qkv_w[layer]) + bias[layer]
        query = rotate(qkv[:, :width], cosines, sines).astype(jnp.bfloat16) * (HEAD_DIM**-0.5)
        key = rotate(qkv[:, width : 2 * width], cosines, sines).astype(jnp.bfloat16)
        value = qkv[:, 2 * width :].astype(jnp.bfloat16)
        spread = to_heads(jnp.stack([query.astype(jnp.bfloat16), key, value]).transpose(1, 0, 2))
        query, key, value = (lanes_padded(spread[:, i]) for i in range(3))
        mixed, log_sums = attend(query, key, value, ids, heads)
        attn_mix = from_heads(mixed[:, :head_width])
        after = mine(stream).astype(jnp.float32) + summed_rows(
            product(attn_mix, out_w[layer].T)
        ).astype(jnp.float32)
        after_low = after.astype(jnp.bfloat16)
        normed_two = gathered_rows(layer_norm(after_low, gains[layer, 1], shifts[layer, 1]))
        gate_up = product(normed_two, gate_up_w[layer])
        gate, up = gate_up[:, :units], gate_up[:, units:]
        hidden = (jax.nn.silu(gate) * up).astype(jnp.bfloat16)
        result = (
            after + summed_rows(product(hidden, down_w[layer].T)).astype(jnp.float32)
        ).astype(jnp.bfloat16)
        kept.append(
            (stream, normed, query, key, value, mixed, log_sums, attn_mix, after_low, normed_two, gate_up, hidden)
        )
        if layer == 0:
            stream = gathered_rows(result)
            hidden_out.append(my_features(stream))
        else:
            hidden_out.append(by_features(result))

    branch = lax.all_gather(
        lax.dynamic_index_in_dim(cotangent, section, 0, keepdims=False), "col", axis=1, tiled=True
    )
    grad = mine(branch).astype(jnp.float32)
    weight_grads = [None, None]
    small_grads = [None, None]
    bias_grads = [None, None]
    input_out = [None, None]
    for layer in (1, 0):
        (
            stream, normed, query, key, value, mixed, log_sums, attn_mix, after_low, normed_two, gate_up, hidden
        ) = kept[layer]
        gate, up = gate_up[:, :units], gate_up[:, units:]
        down_term = dot_first(branch, hidden)
        d_hidden = product(branch, down_w[layer])
        sig = jax.nn.sigmoid(gate)
        d_gate = d_hidden * up * sig * (1.0 + gate * (1.0 - sig))
        d_up = d_hidden * gate * sig
        d_gate_up = jnp.concatenate([d_gate, d_up], axis=1).astype(jnp.bfloat16)
        gate_up_term = dot_first(normed_two, d_gate_up)
        d_normed_two = summed_rows(dot_last(d_gate_up, gate_up_w[layer]))
        back, sums_two = norm_back(d_normed_two, after_low, gains[layer, 1])
        d_after = grad + back
        grad_attn = gathered_rows(d_after.astype(jnp.bfloat16))
        d_mix = product(grad_attn, out_w[layer]).astype(jnp.bfloat16)
        out_term = dot_first(grad_attn, attn_mix)
        d_mixed = lanes_padded(to_heads(d_mix))
        d_query, d_key, d_value = attend_back(
            query, key, value, d_mixed, mixed, log_sums, ids, cos_all, sin_all, heads
        )
        d_spread = jnp.stack([d[:, :head_width] for d in (d_query, d_key, d_value)])
        d_qkv = from_heads(d_spread.transpose(1, 0, 2)).reshape(tokens, -1)
        bias_grads[layer] = jnp.sum(d_qkv.astype(jnp.float32), axis=0)
        qkv_term = dot_first(normed, d_qkv)
        d_normed = summed_rows(dot_last(d_qkv, qkv_w[layer]))
        back, sums_one = norm_back(d_normed, mine(stream), gains[layer, 0])
        d_input = (d_after + back)
        small_grads[layer] = jnp.stack([sums_one, sums_two], axis=1)
        weight_grads[layer] = (qkv_term, out_term, gate_up_term, down_term)
        if layer == 1:
            grad = d_input
            branch = gathered_rows(d_input.astype(jnp.bfloat16))
            input_out[1] = my_features(branch)
        else:
            input_out[0] = by_features(d_input.astype(jnp.bfloat16))

    def by_section(first, second):
        keep = jnp.where(section == 0, first, second)
        give = jnp.where(section == 0, second, first)
        got = lax.ppermute(give, "section", [(0, 1), (1, 0)])
        return jnp.stack([jnp.where(section == 0, keep, got), jnp.where(section == 0, got, keep)])

    hidden_states = by_section(*hidden_out)
    input_grads = by_section(*input_out).astype(jnp.float32)

    def summed_weights(first, second):
        terms = jnp.concatenate([first, second], axis=0).astype(jnp.bfloat16)
        return lax.psum_scatter(terms, both, scatter_dimension=0, tiled=True).astype(jnp.float32)

    qkv_grad, out_grad, gate_up_grad, down_grad = (
        summed_weights(first, second) for first, second in zip(*weight_grads)
    )
    bias_sum = lax.psum(jnp.stack(bias_grads), both)
    bias_sum = lax.dynamic_index_in_dim(bias_sum, section, 0, keepdims=True)
    small_sum = lax.psum(jnp.stack(small_grads), ("section", "row", "col"))
    small_sum = lax.dynamic_index_in_dim(small_sum, section, 0, keepdims=False)
    small_sum = lax.dynamic_slice_in_dim(small_sum, col * width, width, 2)
    return (
        hidden_states[None],
        input_grads[None],
        small_sum[0][None],
        small_sum[1][None],
        qkv_grad.reshape(qkv_weight.shape),
        bias_sum.reshape(qkv_bias.shape),
        out_grad[None],
        gate_up_grad.reshape(gate_up_weight.shape),
        down_grad[None],
    )


def solution(mesh):
    in_specs = (
        P(None, "row", "col"),
        P(None, "row", "col"),
        P(),
        P("section", None, "col"),
        P("section", None, "col"),
        P("section", "row", None, "col"),
        P("section", None, "col"),
        P("section", "row", "col"),
        P("section", "row", None, "col"),
        P("section", "row", "col"),
    )
    out_specs = (
        P("section", None, "row", "col"),
        P("section", None, "row", "col"),
        P("section", None, "col"),
        P("section", None, "col"),
        P("section", "row", None, "col"),
        P("section", None, "col"),
        P("section", "row", "col"),
        P("section", "row", None, "col"),
        P("section", "row", "col"),
    )
    return jax.shard_map(
        per_device, mesh=mesh, in_specs=in_specs, out_specs=out_specs, check_vma=False
    )
```

```python
import functools

import jax
import jax.numpy as jnp
from jax import lax
from jax.experimental import pallas as pl
from jax.experimental.pallas import tpu as pltpu
from jax.sharding import PartitionSpec as P

D = 2048
HEADS = 32
HEAD_DIM = 64
ROT = 16
LANES = 128
REACH = 256
RELAY_ROWS = 16


epsilon = 1e-05


def dot_last(a, b):
    return lax.dot_general(a, b, (((1,), (1,)), ((), ())), preferred_element_type=jnp.float32)


def dot_first(a, b):
    return lax.dot_general(a, b, (((0,), (0,)), ((), ())), preferred_element_type=jnp.float32)


def lanes_of(rows, head):
    lane = lax.broadcasted_iota(jnp.int32, (rows, LANES), 1)
    return lane // HEAD_DIM == head


def spin(x, cosines, sines):
    lane = lax.broadcasted_iota(jnp.int32, x.shape, 1)
    ahead, behind = pltpu.roll(x, LANES - ROT // 2, 1), pltpu.roll(x, ROT // 2, 1)
    return x * cosines + jnp.where(lane % ROT < ROT // 2, ahead, behind) * sines


def meet(axis, n):
    me = lax.axis_index(axis)
    barrier = pltpu.get_barrier_semaphore()
    for d in range(1, n):
        pl.semaphore_signal(
            barrier, 1, device_id={axis: lax.rem(me + d, n)}, device_id_type=pl.DeviceIdType.MESH
        )
    pl.semaphore_wait(barrier, n - 1)


def remote(source, target, sent, got, axis, device):
    return pltpu.make_async_remote_copy(
        src_ref=source,
        dst_ref=target,
        send_sem=sent,
        recv_sem=got,
        device_id={axis: device},
        device_id_type=pl.DeviceIdType.MESH,
    )


def columns(which, size=LANES):
    return pl.ds(pl.multiple_of(which * size, size), size)


def attend_kernel(
    heads, n, bq, bk, bid_q, bid_k, qkv, cosines, sines,
    spread, mixed, lse_ref, mix, vone, scores, leaving, qkv_sent, qkv_got, mix_sent, mix_got,
):
    me = lax.axis_index("row")
    tokens = qkv.shape[0]
    seq = n * tokens
    here = pl.ds(pl.multiple_of(me * tokens, tokens), tokens)
    low = jnp.bfloat16
    meet("row", n)

    def parts(t):
        cos, sin = cosines[...], sines[...]
        query = spin(qkv[:, columns(t)], cos, sin).astype(low) * jnp.asarray(HEAD_DIM**-0.5, low)
        key = spin(qkv[:, columns(n + t)], cos, sin).astype(low)
        return query.astype(low), key, qkv[:, columns(2 * n + t)].astype(low)

    def leave(d):
        to = lax.rem(me + d, n)
        return remote(leaving.at[d - 1], spread.at[:, here], qkv_sent.at[d - 1], qkv_got.at[me], "row", to)

    for d in range(1, n):
        for k, part in enumerate(parts(lax.rem(me + d, n))):
            leaving[d - 1, k] = part
        leave(d).start()
    for k, part in enumerate(parts(me)):
        spread[k, here, :] = part

    def come(row):
        @pl.when(row != me)
        def _():
            there = pl.ds(row * tokens, tokens)
            remote(leaving.at[0], spread.at[:, there], qkv_sent.at[0], qkv_got.at[row], "row", me).wait_recv()

        there = pl.ds(row * tokens, tokens)
        for h in range(heads):
            vone[h, there, :] = jnp.where(lanes_of(tokens, h), spread[2, there, :], jnp.ones((), low))

    def mix_copy(i, device):
        rows = pl.ds(lax.rem(i, tokens // bq) * bq, bq)
        return remote(
            mixed.at[pl.ds(i * bq, bq)], mix.at[rows, columns(me)], mix_sent.at[i], mix_got.at[me, lax.rem(i, tokens // bq)], "row", device
        )

    def block(i, carry):
        rows = pl.ds(pl.multiple_of(i * bq, bq), bq)
        q = spread[0, rows, :]
        bid = bid_q[rows, :]
        free = i * (bq // bk)
        last = jnp.minimum(((i + 1) * bq + REACH + bk - 1) // bk, seq // bk)
        qs = [jnp.where(lanes_of(bq, h), q, jnp.zeros((), low)) for h in range(heads)]

        def score(t, tops, hide):
            span = pl.ds(pl.multiple_of(t * bk, bk), bk)
            keys = spread[1, span, :]
            if hide:
                visible = bid_k[:, span] <= bid
            found = []
            for h in range(heads):
                s = dot_last(qs[h], keys)
                if hide:
                    s = jnp.where(visible, s, -1e30)
                scores[h, :, span] = s
                top = tops[h]
                for c in range(bk // LANES):
                    top = jnp.maximum(top, s[:, c * LANES : (c + 1) * LANES])
                found.append(top)
            return tuple(found)

        tops = tuple(jnp.full((bq, LANES), -1e30, jnp.float32) for _ in range(heads))
        tops = lax.fori_loop(0, free, lambda t, c: score(t, c, False), tops)
        tops = lax.fori_loop(free, last, lambda t, c: score(t, c, True), tops)
        tops = [jnp.max(top, axis=1, keepdims=True) for top in tops]

        def gather(t, sums):
            span = pl.ds(pl.multiple_of(t * bk, bk), bk)
            found = []
            for h in range(heads):
                p = jnp.exp(scores[h, :, span] - tops[h]).astype(low)
                found.append(sums[h] + jnp.dot(p, vone[h, span, :], preferred_element_type=jnp.float32))
            return tuple(found)

        sums = tuple(jnp.zeros((bq, LANES), jnp.float32) for _ in range(heads))
        sums = lax.fori_loop(0, last, gather, sums)
        outcome = jnp.zeros((bq, LANES), jnp.float32)
        lse = jnp.zeros((bq, LANES), jnp.float32)
        for h in range(heads):
            totals = pltpu.roll(sums[h], HEAD_DIM, 1)
            outcome = jnp.where(lanes_of(bq, h), sums[h] / totals, outcome)
            lse = jnp.where(lanes_of(bq, h), tops[h] + jnp.log(totals), lse)
        mixed[rows, :] = outcome.astype(low)
        lse_ref[:, rows] = lse.T
        return carry

    per_row = tokens // bq
    for row in range(n):
        if row == 0:
            come(0)
        if row + 1 < n:
            come(row + 1)

        def run(half, carry, row=row):
            i = row * per_row + half
            block(i, 0)

            @pl.when(row == me)
            def _():
                mix[pl.ds(pl.multiple_of(half * bq, bq), bq), columns(me)] = mixed[pl.ds(pl.multiple_of(i * bq, bq), bq), :]

            @pl.when(row != me)
            def _():
                mix_copy(i, row).start()

            return carry

        lax.fori_loop(0, per_row, run, 0)

    for d in range(1, n):
        leave(d).wait_send()
    for i in range(n * per_row):
        @pl.when(i // per_row != me)
        def _(i=i):
            mix_copy(i, me).wait_send()

    for row in range(n):
        @pl.when(row != me)
        def _(row=row):
            for half in range(per_row):
                rows = pl.ds(half * bq, bq)
                remote(
                    mixed.at[pl.ds(0, bq)], mix.at[rows, columns(row)], mix_sent.at[0], mix_got.at[row, half], "row", me
                ).wait_recv()


def attend(number, qkv, block_all, cosines, sines, heads, n, bq=512, bk=512):
    tokens = qkv.shape[0]
    bq, bk = min(bq, tokens), min(bk, tokens)
    seq = n * tokens
    vmem = pl.BlockSpec(memory_space=pltpu.VMEM)
    low = jnp.bfloat16
    return pl.pallas_call(
        functools.partial(attend_kernel, heads, n, bq, bk),
        in_specs=[vmem] * 5,
        out_specs=[vmem] * 4,
        out_shape=[
            jax.ShapeDtypeStruct((3, seq, LANES), low),
            jax.ShapeDtypeStruct((seq, LANES), low),
            jax.ShapeDtypeStruct((LANES, seq), jnp.float32),
            jax.ShapeDtypeStruct((tokens, n * LANES), low),
        ],
        scratch_shapes=[
            pltpu.VMEM((heads, seq, LANES), low),
            pltpu.VMEM((heads, bq, seq), jnp.float32),
            pltpu.VMEM((n - 1, 3, tokens, LANES), low),
            pltpu.SemaphoreType.DMA((n - 1,)),
            pltpu.SemaphoreType.DMA((n,)),
            pltpu.SemaphoreType.DMA((seq // bq,)),
            pltpu.SemaphoreType.DMA((n, tokens // bq)),
        ],
        compiler_params=pltpu.CompilerParams(
            collective_id=number, has_side_effects=True, vmem_limit_bytes=58 * 2**20
        ),
        cost_estimate=pl.CostEstimate(flops=10**10, bytes_accessed=2 * 10**8, transcendentals=0),
    )(block_all.reshape(seq, 1), block_all.reshape(1, seq), qkv, cosines, sines)


def attend_back_kernel(
    heads, n, bq, bk, bid_q, bid_k, d_mix, spread, mixed, lse_ref, cosines, sines,
    d_qkv, grads, kone, dk_acc, dv_acc, leaving, g_sent, g_got, back_sent, back_got,
):
    me = lax.axis_index("row")
    tokens = d_mix.shape[0]
    seq = n * tokens
    per_row = tokens // bq
    blocks = n * per_row
    low = jnp.bfloat16
    zero = jnp.zeros((), low)
    here = pl.ds(pl.multiple_of(me * tokens, tokens), tokens)
    meet("row", n)

    def give(d):
        to = lax.rem(me + d, n)
        return remote(d_mix.at[:, columns(to)], grads.at[here], g_sent.at[d - 1], g_got.at[me], "row", to)

    for d in range(1, n):
        give(d).start()
    grads[here, :] = d_mix[:, columns(me)]
    for h in range(heads):
        kone[h] = jnp.where(lanes_of(seq, h), spread[1], zero)
    dk_acc[...] = jnp.zeros_like(dk_acc)
    dv_acc[...] = jnp.zeros_like(dv_acc)

    def tile(t, dq, hide, stuff):
        qs, gs, lses, deltas, bid = stuff
        span = pl.ds(pl.multiple_of(t * bk, bk), bk)
        keys, values = spread[1, span, :], spread[2, span, :]
        dv, dk = dv_acc[span, :], dk_acc[span, :]
        if hide:
            visible = bid_k[span, :] <= bid
        for h in range(heads):
            s = dot_last(keys, qs[h])
            if hide:
                s = jnp.where(visible, s, -1e30)
            p = jnp.exp(s - lses[h])
            dp = dot_last(values, gs[h])
            ds = (p * (dp - deltas[h])).astype(low)
            dv = dv + jnp.dot(p.astype(low), gs[h], preferred_element_type=jnp.float32)
            dk = dk + jnp.dot(ds, qs[h], preferred_element_type=jnp.float32)
            dq = dq + dot_first(ds, kone[h, span, :])
        dv_acc[span, :] = dv
        dk_acc[span, :] = dk
        return dq

    def block(i):
        rows = pl.ds(pl.multiple_of(i * bq, bq), bq)
        q, g = spread[0, rows, :], grads[rows, :]
        product = (g.astype(jnp.float32) * mixed[rows, :].astype(jnp.float32)).T
        span = lambda h: slice(h * HEAD_DIM, (h + 1) * HEAD_DIM)
        deltas = [jnp.sum(product[span(h)], axis=0, keepdims=True) for h in range(heads)]
        lses = [lse_ref[h * HEAD_DIM : h * HEAD_DIM + 1, rows] for h in range(heads)]
        qs = [jnp.where(lanes_of(bq, h), q, zero) for h in range(heads)]
        gs = [jnp.where(lanes_of(bq, h), g, zero) for h in range(heads)]
        stuff = (qs, gs, lses, deltas, bid_q[:, rows])
        free = i * (bq // bk)
        last = jnp.minimum(((i + 1) * bq + REACH + bk - 1) // bk, seq // bk)
        dq = jnp.zeros((bq, LANES), jnp.float32)
        dq = lax.fori_loop(0, free, lambda t, c: tile(t, c, False, stuff), dq)
        dq = lax.fori_loop(free, last, lambda t, c: tile(t, c, True, stuff), dq)
        return spin(dq * (HEAD_DIM**-0.5), cosines[rows, :], -sines[rows, :]).astype(low)

    def back_copy(k, i, device):
        half = lax.rem(i, per_row)
        rows = pl.ds(pl.multiple_of(half * bq, bq), bq)
        return remote(
            leaving.at[k, pl.ds(pl.multiple_of(i * bq, bq), bq)],
            d_qkv.at[rows, columns(k * n + me)],
            back_sent.at[k, i],
            back_got.at[k, me, half],
            "row",
            device,
        )

    def send(k, i, values):
        row = i // per_row
        half = lax.rem(i, per_row)

        @pl.when(row == me)
        def _():
            d_qkv[pl.ds(pl.multiple_of(half * bq, bq), bq), columns(k * n + me)] = values

        @pl.when(row != me)
        def _():
            leaving[k, pl.ds(pl.multiple_of(i * bq, bq), bq), :] = values
            back_copy(k, i, row).start()

    def keys_done(i):
        rows = pl.ds(pl.multiple_of(i * bq, bq), bq)
        send(1, i, spin(dk_acc[rows, :], cosines[rows, :], -sines[rows, :]).astype(low))
        send(2, i, dv_acc[rows, :].astype(low))

    for row in range(n - 1, -1, -1):
        @pl.when(row != me)
        def _(row=row):
            there = pl.ds(row * tokens, tokens)
            remote(d_mix.at[:, columns(0)], grads.at[there], g_sent.at[0], g_got.at[row], "row", me).wait_recv()

        def run(step, carry, row=row):
            i = row * per_row + per_row - 1 - step
            send(0, i, block(i))

            @pl.when(i + 1 < blocks)
            def _():
                keys_done(i + 1)

            return carry

        lax.fori_loop(0, per_row, run, 0)
    keys_done(0)

    for d in range(1, n):
        give(d).wait_send()

    def settle(i, carry):
        @pl.when(i // per_row != me)
        def _():
            half = lax.rem(i, per_row)
            rows = pl.ds(pl.multiple_of(half * bq, bq), bq)
            for k in range(3):
                back_copy(k, i, me).wait_send()
                remote(
                    leaving.at[k, pl.ds(0, bq)],
                    d_qkv.at[rows, columns(k * n + i // per_row)],
                    back_sent.at[k, 0],
                    back_got.at[k, i // per_row, half],
                    "row",
                    me,
                ).wait_recv()

        return carry

    lax.fori_loop(0, blocks, settle, 0)


def attend_back(number, d_mix, spread, mixed, lse, block_all, cosines, sines, heads, n, bq=512, bk=512):
    tokens = d_mix.shape[0]
    bq, bk = min(bq, tokens), min(bk, tokens)
    seq = n * tokens
    vmem = pl.BlockSpec(memory_space=pltpu.VMEM)
    low = jnp.bfloat16
    return pl.pallas_call(
        functools.partial(attend_back_kernel, heads, n, bq, bk),
        in_specs=[vmem] * 8,
        out_specs=vmem,
        out_shape=jax.ShapeDtypeStruct((tokens, 3 * n * LANES), low),
        scratch_shapes=[
            pltpu.VMEM((seq, LANES), low),
            pltpu.VMEM((heads, seq, LANES), low),
            pltpu.VMEM((seq, LANES), jnp.float32),
            pltpu.VMEM((seq, LANES), jnp.float32),
            pltpu.VMEM((3, seq, LANES), low),
            pltpu.SemaphoreType.DMA((n - 1,)),
            pltpu.SemaphoreType.DMA((n,)),
            pltpu.SemaphoreType.DMA((3, seq // bq)),
            pltpu.SemaphoreType.DMA((3, n, tokens // bq)),
        ],
        compiler_params=pltpu.CompilerParams(
            collective_id=number, has_side_effects=True, vmem_limit_bytes=58 * 2**20
        ),
        cost_estimate=pl.CostEstimate(flops=10**10, bytes_accessed=3 * 10**8, transcendentals=0),
    )(block_all.reshape(1, seq), block_all.reshape(seq, 1), d_mix, spread, mixed, lse, cosines, sines)


def norm_parts(values):
    mean = jnp.mean(values, axis=-1, keepdims=True)
    spread = jnp.mean(values * values, axis=-1, keepdims=True) - mean * mean
    return mean, lax.rsqrt(spread + epsilon)


def after_attention(total, c, ins, outs):
    stream, gain, shift = ins
    (after_ref,) = outs
    after = stream[c].astype(jnp.float32) + total
    after_ref[c] = after
    values = after.astype(jnp.bfloat16).astype(jnp.float32)
    mean, inverse = norm_parts(values)
    return ((values - mean) * inverse * gain[...] + shift[...]).astype(jnp.bfloat16)


def after_hidden(total, c, ins, outs):
    (after,) = ins
    return (after[c] + total).astype(jnp.bfloat16)


def behind_norm(total, c, ins, outs):
    grad, values_ref, gain = ins
    grad_ref, sums = outs
    values = values_ref[c].astype(jnp.bfloat16).astype(jnp.float32)
    mean, inverse = norm_parts(values)
    centred = (values - mean) * inverse
    scaled = total * gain[...]
    back = inverse * (
        scaled
        - jnp.mean(scaled, axis=-1, keepdims=True)
        - centred * jnp.mean(scaled * centred, axis=-1, keepdims=True)
    )
    given = grad[c] + back
    grad_ref[c] = given
    here = [jnp.sum(total * centred, axis=0, keepdims=True), jnp.sum(total, axis=0, keepdims=True)]

    @pl.when(c == 0)
    def _():
        sums[...] = jnp.zeros_like(sums)

    sums[...] += jnp.concatenate(here, axis=0)
    return given.astype(jnp.bfloat16)


def relay_kernel(middle, n_ins, n_outs, n, chunks, lag, spread, partial, *refs):
    ins, refs = refs[:n_ins], refs[n_ins:]
    whole, outs, refs = refs[0], refs[1 : 1 + n_outs], refs[1 + n_outs :]
    arrived, outgoing, total, sum_sent, sum_got, block_sent, block_got = refs
    i = lax.axis_index("col")
    width = whole.shape[-1]
    first, last = i == 0, i == n - 1

    barrier = pltpu.get_barrier_semaphore()
    if spread:
        for d in range(1, n):
            pl.semaphore_signal(barrier, 1, device_id={"col": lax.rem(i + d, n)}, device_id_type=pl.DeviceIdType.MESH)
        pl.semaphore_wait(barrier, n - 1)
    else:
        @pl.when(i > 0)
        def _():
            pl.semaphore_signal(barrier, 1, device_id={"col": i - 1}, device_id_type=pl.DeviceIdType.MESH)

        @pl.when(i < n - 1)
        def _():
            pl.semaphore_signal(barrier, 1, device_id={"col": i + 1}, device_id_type=pl.DeviceIdType.MESH)

        @pl.when(first | last)
        def _():
            pl.semaphore_wait(barrier, 1)

        @pl.when((i > 0) & (i < n - 1))
        def _():
            pl.semaphore_wait(barrier, 2)

    def remote_col(source, target, sent, got, device):
        return remote(source, target, sent, got, "col", device)

    def sum_copy(c, j, right):
        slot = j + 1 if right else j
        return remote_col(
            outgoing.at[c, j], arrived.at[c, slot], sum_sent.at[c, j], sum_got.at[c, slot], i + 1 if right else i - 1
        )

    def block_copy(c, o, right, own=False):
        sent = n if own and not right else o
        return remote_col(whole.at[c, o], whole.at[c, o], block_sent.at[c, sent], block_got.at[c, o], i + 1 if right else i - 1)

    def slice_copy(c, d):
        to = lax.rem(i + d, n)
        source = outgoing.at[c, i, :, pl.ds(pl.multiple_of(to * width, 128), width)]
        return remote_col(source, whole.at[c, i], block_sent.at[c, d], block_got.at[c, i], to)

    def arrive(c, slot):
        remote_col(outgoing.at[c, 0], arrived.at[c, slot], sum_sent.at[c, 0], sum_got.at[c, slot], i).wait_recv()

    def middle_slot(k):
        return jnp.maximum(lag * k + n - 1 - k, lag * (n - 1 - k) + k)

    def at(now, slot, allowed):
        since = now - slot
        c = jnp.maximum(since, 0) // n
        return c, allowed & (since >= 0) & (lax.rem(jnp.maximum(since, 0), n) == 0) & (since < n * chunks)

    def step(now, carry):
        for j in range(n - 1, 0, -1):
            c, due = at(now, lag * i + n - 1 - j, i < j)

            @pl.when(due & first)
            def _(c=c, j=j):
                outgoing[c, j] = partial[c, j]

            @pl.when(due & (i > 0))
            def _(c=c, j=j):
                arrive(c, j + 1)
                both = arrived[c, j + 1].astype(jnp.float32) + partial[c, j].astype(jnp.float32)
                outgoing[c, j] = both.astype(jnp.bfloat16)

            @pl.when(due)
            def _(c=c, j=j):
                sum_copy(c, j, True).start()

        for j in range(n - 1):
            c, due = at(now, lag * (n - 1 - i) + j, i > j)

            @pl.when(due & last)
            def _(c=c, j=j):
                outgoing[c, j] = partial[c, j]

            @pl.when(due & (i < n - 1))
            def _(c=c, j=j):
                arrive(c, j)
                both = arrived[c, j].astype(jnp.float32) + partial[c, j].astype(jnp.float32)
                outgoing[c, j] = both.astype(jnp.bfloat16)

            @pl.when(due)
            def _(c=c, j=j):
                sum_copy(c, j, False).start()

        c, due = at(now, middle_slot(i), i >= 0)

        @pl.when(due)
        def _():
            total[...] = partial[c, i].astype(jnp.float32)

        @pl.when(due & (i > 0))
        def _():
            arrive(c, i + 1)
            total[...] += arrived[c, i + 1].astype(jnp.float32)

        @pl.when(due & (i < n - 1))
        def _():
            arrive(c, i)
            total[...] += arrived[c, i].astype(jnp.float32)

        @pl.when(due)
        def _():
            block = middle(total[...], c, ins, outs)
            if spread:
                outgoing[c, i] = block
                for d in range(1, n):
                    slice_copy(c, d).start()
                whole[c, i] = outgoing[c, i, :, pl.ds(pl.multiple_of(i * width, 128), width)]
            else:
                whole[c, i] = block

        if spread:
            return carry

        @pl.when(due & (i < n - 1))
        def _():
            block_copy(c, i, True, own=True).start()

        @pl.when(due & (i > 0))
        def _():
            block_copy(c, i, False, own=True).start()

        for o in range(n - 1):
            c, due = at(now, middle_slot(o) + lag * (i - o), i > o)

            @pl.when(due)
            def _(c=c, o=o):
                block_copy(c, o, True).wait_recv()

            @pl.when(due & (i < n - 1))
            def _(c=c, o=o):
                block_copy(c, o, True).start()

        for o in range(1, n):
            c, due = at(now, middle_slot(o) + lag * (o - i), i < o)

            @pl.when(due)
            def _(c=c, o=o):
                block_copy(c, o, False).wait_recv()

            @pl.when(due & (i > 0))
            def _(c=c, o=o):
                block_copy(c, o, False).start()

        return carry

    lax.fori_loop(0, n * (chunks - 1) + 2 * lag * (n - 1) + 1, step, 0)

    def settle(c, carry):
        for j in range(n):
            @pl.when(j != i)
            def _(j=j):
                sum_copy(c, j, True).wait_send()
                if spread:
                    remote_col(outgoing.at[c, j, :, pl.ds(0, width)], whole.at[c, j], block_sent.at[c, 0], block_got.at[c, j], i).wait_recv()

        if spread:
            for d in range(1, n):
                slice_copy(c, d).wait_send()
            return carry
        for o in range(n):
            @pl.when((o <= i) & (i < n - 1))
            def _(o=o):
                block_copy(c, o, True).wait_send()

            @pl.when((o > i) & (i > 0))
            def _(o=o):
                block_copy(c, o, True).wait_send()

        @pl.when(i > 0)
        def _():
            block_copy(c, i, False, own=True).wait_send()

        return carry

    lax.fori_loop(0, chunks, settle, 0)


def relay(middle, number, partial, ins, outs, n, spread=False, lag=3, rows=RELAY_ROWS):
    tokens, features = partial.shape
    owned = tokens // n
    chunks = owned // rows
    blocks = lambda values: values.reshape(chunks, rows, features) if values.shape[0] == owned else values
    ins = [blocks(values) for values in ins]
    out_shapes = [
        jax.ShapeDtypeStruct((chunks, n, rows, features // n if spread else features), jnp.bfloat16)
    ] + [
        jax.ShapeDtypeStruct((chunks, rows, features) if shape[0] == owned else shape, jnp.float32) for shape in outs
    ]
    vmem = pl.BlockSpec(memory_space=pltpu.VMEM)
    whole, *rest = pl.pallas_call(
        functools.partial(relay_kernel, middle, len(ins), len(outs), n, chunks, lag, spread),
        in_specs=[vmem] * (1 + len(ins)),
        out_specs=[vmem] * len(out_shapes),
        out_shape=out_shapes,
        scratch_shapes=[
            pltpu.VMEM((chunks, n + 1, rows, features), jnp.bfloat16),
            pltpu.VMEM((chunks, n, rows, features), jnp.bfloat16),
            pltpu.VMEM((rows, features), jnp.float32),
            pltpu.SemaphoreType.DMA((chunks, n)),
            pltpu.SemaphoreType.DMA((chunks, n + 1)),
            pltpu.SemaphoreType.DMA((chunks, n + 1)),
            pltpu.SemaphoreType.DMA((chunks, n)),
        ],
        compiler_params=pltpu.CompilerParams(
            collective_id=number, has_side_effects=True, vmem_limit_bytes=56 * 2**20
        ),
        cost_estimate=pl.CostEstimate(flops=0, bytes_accessed=35 * 10**7, transcendentals=0),
    )(partial.reshape(chunks, n, rows, features), *ins)
    rest = [values.reshape(owned, features) if values.ndim == 3 else values for values in rest]
    return [whole.reshape(tokens, -1)] + rest


def gather_kernel(n, chunks, lag, own, small, whole, smalls, sent, got, small_sent, small_got):
    section, i = lax.axis_index("section"), lax.axis_index("col")
    rows, width = own.shape[0] // chunks, own.shape[1]
    others = [(s, d) for s in range(2) for d in range(n) if (s, d) != (0, 0)]
    place = lambda s, d: {"section": lax.rem(section + s, 2), "col": lax.rem(i + d, n)}
    barrier = pltpu.get_barrier_semaphore()
    for s, d in others:
        pl.semaphore_signal(barrier, 1, device_id=place(s, d), device_id_type=pl.DeviceIdType.MESH)
    pl.semaphore_wait(barrier, len(others))

    def small_copy(s, d):
        return pltpu.make_async_remote_copy(
            src_ref=small,
            dst_ref=smalls.at[section, i],
            send_sem=small_sent.at[s, d],
            recv_sem=small_got.at[section, i],
            device_id=place(s, d),
            device_id_type=pl.DeviceIdType.MESH,
        )

    for s, d in others:
        small_copy(s, d).start()
    smalls[section, i] = small[...]

    def block(c, o, right, mine=False):
        part = whole.at[pl.ds(pl.multiple_of(c * rows, rows), rows), columns(o, width)]
        return remote(
            part, part, sent.at[c, n if mine and not right else o], got.at[c, o], "col", i + 1 if right else i - 1
        )

    def at(now, slot, allowed):
        since = jnp.maximum(now - slot, 0)
        return since // (n - 1), allowed & (now >= slot) & (lax.rem(since, n - 1) == 0) & (since < (n - 1) * chunks)

    def step(now, carry):
        c, due = at(now, 0, i >= 0)

        @pl.when(due)
        def _():
            here = pl.ds(pl.multiple_of(c * rows, rows), rows)
            whole[here, columns(i, width)] = own[here, :]

        @pl.when(due & (i < n - 1))
        def _():
            block(c, i, True, True).start()

        @pl.when(due & (i > 0))
        def _():
            block(c, i, False, True).start()

        for o in range(n):
            c, due = at(now, lag * jnp.abs(i - o), i != o)

            @pl.when(due)
            def _(c=c, o=o):
                block(c, o, True).wait_recv()

            @pl.when(due & (i > o) & (i < n - 1))
            def _(c=c, o=o):
                block(c, o, True).start()

            @pl.when(due & (i < o) & (i > 0))
            def _(c=c, o=o):
                block(c, o, False).start()

        return carry

    lax.fori_loop(0, (n - 1) * (chunks - 1) + lag * (n - 1) + 1, step, 0)

    def settle(c, carry):
        for o in range(n):
            @pl.when(((o <= i) & (i < n - 1)) | ((o > i) & (i > 0)))
            def _(o=o):
                block(c, o, True).wait_send()

        @pl.when(i > 0)
        def _():
            block(c, i, False, True).wait_send()

        return carry

    lax.fori_loop(0, chunks, settle, 0)
    for s, d in others:
        small_copy(s, d).wait_send()
        from_s, from_d = lax.rem(section + s, 2), lax.rem(i + d, n)
        pltpu.make_async_remote_copy(
            src_ref=small,
            dst_ref=smalls.at[from_s, from_d],
            send_sem=small_sent.at[s, d],
            recv_sem=small_got.at[from_s, from_d],
            device_id=place(s, d),
            device_id_type=pl.DeviceIdType.MESH,
        ).wait_recv()


def gathered(number, own, small, n, lag=3, rows=64):
    tokens, width = own.shape
    chunks = tokens // rows
    vmem = pl.BlockSpec(memory_space=pltpu.VMEM)
    return pl.pallas_call(
        functools.partial(gather_kernel, n, chunks, lag),
        in_specs=[vmem] * 2,
        out_specs=[vmem] * 2,
        out_shape=[
            jax.ShapeDtypeStruct((tokens, n * width), own.dtype),
            jax.ShapeDtypeStruct((2, n) + small.shape, small.dtype),
        ],
        scratch_shapes=[
            pltpu.SemaphoreType.DMA((chunks, n + 1)),
            pltpu.SemaphoreType.DMA((chunks, n)),
            pltpu.SemaphoreType.DMA((2, n)),
            pltpu.SemaphoreType.DMA((2, n)),
        ],
        compiler_params=pltpu.CompilerParams(
            collective_id=number, has_side_effects=True, vmem_limit_bytes=40 * 2**20
        ),
        cost_estimate=pl.CostEstimate(flops=0, bytes_accessed=25 * 10**7, transcendentals=0),
    )(own, small)


def layer_norm(values, gain, shift):
    values = values.astype(jnp.float32)
    mean, inverse = norm_parts(values)
    return ((values - mean) * inverse * gain + shift).astype(jnp.bfloat16)


def rotary_lanes(positions):
    half_dims = ROT // 2
    inverse_freq = 1.0 / 10000.0 ** (jnp.arange(half_dims, dtype=jnp.float32) * 2.0 / ROT)
    angles = positions.astype(jnp.float32)[:, None] * inverse_freq[None, :]
    cosine, sine = jnp.cos(angles), jnp.sin(angles)
    rest = jnp.zeros((positions.shape[0], HEAD_DIM - ROT), jnp.float32)
    cosines = jnp.concatenate([cosine, cosine, rest + 1.0], axis=1)
    sines = jnp.concatenate([-sine, sine, rest], axis=1)
    return jnp.tile(cosines, (1, LANES // HEAD_DIM)), jnp.tile(sines, (1, LANES // HEAD_DIM))


def product(left, right):
    return jnp.dot(left, right, preferred_element_type=jnp.float32)


def per_device(
    inputs,
    cotangent,
    block_ids,
    norm_gains,
    norm_shifts,
    qkv_weight,
    qkv_bias,
    out_weight,
    gate_up_weight,
    down_weight,
):
    section = lax.axis_index("section")
    row = lax.axis_index("row")
    col = lax.axis_index("col")
    rows_axis = lax.axis_size("row")
    cols_axis = lax.axis_size("col")
    tokens, width = inputs.shape[1:]
    owned = tokens // cols_axis
    units = down_weight.shape[2]
    seq = tokens * rows_axis
    both = ("section", "row")
    whole_lanes = width == rows_axis * LANES
    heads = LANES // HEAD_DIM if whole_lanes else 1
    copies = 1 if whole_lanes else rows_axis * HEAD_DIM // width

    def expand(values):
        if whole_lanes:
            return values
        values = values.reshape(tokens, -1, width // HEAD_DIM, HEAD_DIM)
        values = jnp.pad(jnp.repeat(values, copies, axis=2), ((0, 0), (0, 0), (0, 0), (0, LANES - HEAD_DIM)))
        return values.reshape(tokens, -1)

    def contract(values):
        if whole_lanes:
            return values
        values = values.reshape(tokens, -1, rows_axis, LANES)[:, :, ::copies, :HEAD_DIM]
        return values.reshape(tokens, -1)

    def weights_of(block):
        block = block[0].reshape(block.shape[1], -1)
        return lax.all_gather(block, both, axis=0, tiled=True).reshape(2, D, -1)

    def mine(values):
        blocks = values.reshape(owned // RELAY_ROWS, cols_axis, RELAY_ROWS, -1)
        return lax.dynamic_index_in_dim(blocks, col, 1, keepdims=False).reshape(owned, -1)

    def my_features(values):
        return lax.dynamic_slice_in_dim(values, col * width, width, 1)

    own_small = jnp.concatenate([norm_gains[0], norm_shifts[0], qkv_bias[0], jnp.zeros((1, width), jnp.float32)])
    stream, small = gathered(6, lax.dynamic_index_in_dim(inputs, section, 0, keepdims=False), own_small, cols_axis)
    whole_small = small.transpose(0, 2, 1, 3).reshape(2, own_small.shape[0], D)
    gains, shifts = whole_small[:, :2], whole_small[:, 2:4]
    bias = lax.dynamic_index_in_dim(small, col, 1, keepdims=False)[:, 4:7].reshape(2, -1)

    qkv_w = weights_of(qkv_weight)
    out_w = weights_of(out_weight)
    gate_up_w = weights_of(gate_up_weight)
    down_w = weights_of(down_weight)

    ids = lax.dynamic_index_in_dim(block_ids, section, 0, keepdims=False)
    cos_all, sin_all = rotary_lanes(jnp.arange(seq, dtype=jnp.int32))
    cosines, sines = (lax.dynamic_slice_in_dim(table, row * tokens, tokens, 0) for table in (cos_all, sin_all))
    branch = lax.all_gather(
        lax.dynamic_index_in_dim(cotangent, section, 0, keepdims=False), "col", axis=1, tiled=True
    )

    kept = []
    hidden_out = []
    for layer in range(2):
        normed = layer_norm(stream, gains[layer, 0], shifts[layer, 0])
        qkv = product(normed, qkv_w[layer]) + bias[layer]
        spread, mixed, log_sums, attn_mix = attend(7, expand(qkv), ids, cosines, sines, heads, rows_axis)
        attn_mix = contract(attn_mix)
        normed_two, after = relay(
            after_attention,
            0,
            product(attn_mix, out_w[layer].T).astype(jnp.bfloat16),
            [mine(stream), gains[layer, 1:], shifts[layer, 1:]],
            [(owned, D)],
            cols_axis,
        )
        gate_up = product(normed_two, gate_up_w[layer])
        gate, up = gate_up[:, :units], gate_up[:, units:]
        hidden = (jax.nn.silu(gate) * up).astype(jnp.bfloat16)
        kept.append((stream, normed, spread, mixed, log_sums, attn_mix, after, normed_two, gate_up, hidden))
        partial = product(hidden, down_w[layer].T)
        if layer == 0:
            (stream,) = relay(after_hidden, 1, partial.astype(jnp.bfloat16), [after], [], cols_axis)
            hidden_out.append(my_features(stream))
        else:
            blocks = partial.reshape(owned // RELAY_ROWS, cols_axis, RELAY_ROWS, D)
            owner = lax.broadcasted_iota(jnp.int32, blocks.shape, 1) == col
            blocks = blocks + jnp.where(owner, after.reshape(-1, 1, RELAY_ROWS, D), 0.0)
            result = blocks.reshape(tokens, D).astype(jnp.bfloat16)
            hidden_out.append(lax.psum_scatter(result, "col", scatter_dimension=1, tiled=True))

    grad = mine(branch).astype(jnp.float32)
    weight_grads = [[], []]
    small_grads = [None, None]
    bias_grads = [None, None]
    input_out = [None, None]

    def collect(layer, term):
        term = lax.psum_scatter(term, "row", scatter_dimension=0, tiled=True)
        got = lax.ppermute(term, "section", [(1 - layer, layer)])
        weight_grads[layer].append(term.astype(jnp.float32) + got.astype(jnp.float32))

    def together(*values):
        return lax.optimization_barrier(values)

    for layer in (1, 0):
        stream, normed, spread, mixed, log_sums, attn_mix, after, normed_two, gate_up, hidden = kept[layer]
        gate, up = gate_up[:, :units], gate_up[:, units:]
        d_hidden = product(branch, down_w[layer])
        sig = jax.nn.sigmoid(gate)
        d_gate = d_hidden * up * sig * (1.0 + gate * (1.0 - sig))
        d_up = d_hidden * gate * sig
        d_gate_up = jnp.concatenate([d_gate, d_up], axis=1).astype(jnp.bfloat16)
        partial, down_term, gate_up_term = together(
            dot_last(d_gate_up, gate_up_w[layer]).astype(jnp.bfloat16),
            dot_first(branch, hidden).astype(jnp.bfloat16),
            dot_first(normed_two, d_gate_up).astype(jnp.bfloat16),
        )
        collect(layer, down_term)
        collect(layer, gate_up_term)
        grad_attn, d_after, sums_two = relay(
            behind_norm, 3, partial, [grad, after, gains[layer, 1:]], [(owned, D), (2, D)], cols_axis
        )
        d_mix, out_term = together(
            product(grad_attn, out_w[layer]).astype(jnp.bfloat16), dot_first(grad_attn, attn_mix).astype(jnp.bfloat16)
        )
        collect(layer, out_term)
        d_qkv = contract(
            attend_back(8, expand(d_mix), spread, mixed, log_sums, ids, cos_all, sin_all, heads, rows_axis)
        )
        partial, qkv_term, bias_grads[layer] = together(
            dot_last(d_qkv, qkv_w[layer]).astype(jnp.bfloat16),
            dot_first(normed, d_qkv).astype(jnp.bfloat16),
            jnp.sum(d_qkv.astype(jnp.float32), axis=0),
        )
        collect(layer, qkv_term)
        branch, grad, sums_one = relay(
            behind_norm,
            4 + layer,
            partial,
            [d_after, mine(stream), gains[layer, :1]],
            [(owned, D), (2, D)],
            cols_axis,
            spread=layer == 0,
        )
        small_grads[layer] = jnp.stack([sums_one, sums_two], axis=1)
        input_out[layer] = my_features(branch) if layer == 1 else branch

    def by_section(first, second):
        keep = jnp.where(section == 0, first, second)
        give = jnp.where(section == 0, second, first)
        got = lax.ppermute(give, "section", [(0, 1), (1, 0)])
        return jnp.stack([jnp.where(section == 0, keep, got), jnp.where(section == 0, got, keep)])

    hidden_states = by_section(*hidden_out)
    input_grads = by_section(*input_out).astype(jnp.float32)
    down_grad, gate_up_grad, out_grad, qkv_grad = (
        jnp.where(section == 0, first, second) for first, second in zip(*weight_grads)
    )
    bias_sum = lax.psum(jnp.stack(bias_grads), both)
    bias_sum = lax.dynamic_index_in_dim(bias_sum, section, 0, keepdims=True)
    small_sum = lax.psum_scatter(jnp.stack(small_grads), "col", scatter_dimension=3, tiled=True)
    small_sum = lax.psum(small_sum, both)
    small_sum = lax.dynamic_index_in_dim(small_sum, section, 0, keepdims=False)
    return (
        hidden_states[None],
        input_grads[None],
        small_sum[0][None],
        small_sum[1][None],
        qkv_grad.reshape(qkv_weight.shape),
        bias_sum.reshape(qkv_bias.shape),
        out_grad[None],
        gate_up_grad.reshape(gate_up_weight.shape),
        down_grad[None],
    )


def solution(mesh):
    in_specs = (
        P(None, "row", "col"),
        P(None, "row", "col"),
        P(),
        P("section", None, "col"),
        P("section", None, "col"),
        P("section", "row", None, "col"),
        P("section", None, "col"),
        P("section", "row", "col"),
        P("section", "row", None, "col"),
        P("section", "row", "col"),
    )
    out_specs = (
        P("section", None, "row", "col"),
        P("section", None, "row", "col"),
        P("section", None, "col"),
        P("section", None, "col"),
        P("section", "row", None, "col"),
        P("section", None, "col"),
        P("section", "row", "col"),
        P("section", "row", None, "col"),
        P("section", "row", "col"),
    )
    return jax.shard_map(
        per_device, mesh=mesh, in_specs=in_specs, out_specs=out_specs, check_vma=False
    )
```

```python
import functools

import jax
import jax.numpy as jnp
from jax import lax
from jax.experimental import pallas as pl
from jax.experimental.pallas import tpu as pltpu
from jax.sharding import PartitionSpec as P

D = 2048
HEADS = 32
HEAD_DIM = 64
ROT = 16
LANES = 128
REACH = 256
RELAY_ROWS = 16


epsilon = 1e-05


def dot_last(a, b):
    return lax.dot_general(a, b, (((1,), (1,)), ((), ())), preferred_element_type=jnp.float32)


def dot_first(a, b):
    return lax.dot_general(a, b, (((0,), (0,)), ((), ())), preferred_element_type=jnp.float32)


def lanes_of(rows, head):
    lane = lax.broadcasted_iota(jnp.int32, (rows, LANES), 1)
    return lane // HEAD_DIM == head


def spin(x, cosines, sines):
    lane = lax.broadcasted_iota(jnp.int32, x.shape, 1)
    ahead, behind = pltpu.roll(x, LANES - ROT // 2, 1), pltpu.roll(x, ROT // 2, 1)
    return x * cosines + jnp.where(lane % ROT < ROT // 2, ahead, behind) * sines


def meet(axis, n):
    me = lax.axis_index(axis)
    barrier = pltpu.get_barrier_semaphore()
    for d in range(1, n):
        pl.semaphore_signal(
            barrier, 1, device_id={axis: lax.rem(me + d, n)}, device_id_type=pl.DeviceIdType.MESH
        )
    pl.semaphore_wait(barrier, n - 1)


def remote(source, target, sent, got, axis, device):
    return pltpu.make_async_remote_copy(
        src_ref=source,
        dst_ref=target,
        send_sem=sent,
        recv_sem=got,
        device_id={axis: device},
        device_id_type=pl.DeviceIdType.MESH,
    )


def columns(which, size=LANES):
    return pl.ds(pl.multiple_of(which * size, size), size)


def attend_kernel(
    heads, n, bq, bk, bid_q, bid_k, qkv, cosines, sines, *refs
):
    spread, mixed, lse_ref, mix, vone, scores, leaving, qkv_sent, qkv_got, mix_sent, mix_got = refs[-11:]
    me = lax.axis_index("row")
    tokens = qkv.shape[0]
    seq = n * tokens
    here = pl.ds(pl.multiple_of(me * tokens, tokens), tokens)
    low = jnp.bfloat16
    meet("row", n)

    def parts(t):
        cos, sin = cosines[here, :], sines[here, :]
        query = spin(qkv[:, columns(t)], cos, sin).astype(low) * jnp.asarray(HEAD_DIM**-0.5, low)
        key = spin(qkv[:, columns(n + t)], cos, sin).astype(low)
        return query.astype(low), key, qkv[:, columns(2 * n + t)].astype(low)

    def leave(d):
        to = lax.rem(me + d, n)
        return remote(leaving.at[d - 1], spread.at[:, here], qkv_sent.at[d - 1], qkv_got.at[me], "row", to)

    for d in range(1, n):
        for k, part in enumerate(parts(lax.rem(me + d, n))):
            leaving[d - 1, k] = part
        leave(d).start()
    for k, part in enumerate(parts(me)):
        spread[k, here, :] = part

    def come(row):
        @pl.when(row != me)
        def _():
            there = pl.ds(row * tokens, tokens)
            remote(leaving.at[0], spread.at[:, there], qkv_sent.at[0], qkv_got.at[row], "row", me).wait_recv()

        there = pl.ds(row * tokens, tokens)
        for h in range(heads):
            vone[h, there, :] = jnp.where(lanes_of(tokens, h), spread[2, there, :], jnp.ones((), low))

    def mix_copy(i, device):
        rows = pl.ds(lax.rem(i, tokens // bq) * bq, bq)
        return remote(
            mixed.at[pl.ds(i * bq, bq)], mix.at[rows, columns(me)], mix_sent.at[i], mix_got.at[me, lax.rem(i, tokens // bq)], "row", device
        )

    def block(i, carry):
        rows = pl.ds(pl.multiple_of(i * bq, bq), bq)
        q = spread[0, rows, :]
        bid = bid_q[rows, :]
        free = i * (bq // bk)
        last = jnp.minimum(((i + 1) * bq + REACH + bk - 1) // bk, seq // bk)
        qs = [jnp.where(lanes_of(bq, h), q, jnp.zeros((), low)) for h in range(heads)]

        def score(t, tops, hide):
            span = pl.ds(pl.multiple_of(t * bk, bk), bk)
            keys = spread[1, span, :]
            if hide:
                visible = bid_k[:, span] <= bid
            found = []
            for h in range(heads):
                s = dot_last(qs[h], keys)
                if hide:
                    s = jnp.where(visible, s, -1e30)
                scores[h, :, span] = s
                top = tops[h]
                for c in range(bk // LANES):
                    top = jnp.maximum(top, s[:, c * LANES : (c + 1) * LANES])
                found.append(top)
            return tuple(found)

        tops = tuple(jnp.full((bq, LANES), -1e30, jnp.float32) for _ in range(heads))
        tops = lax.fori_loop(0, free, lambda t, c: score(t, c, False), tops)
        tops = lax.fori_loop(free, last, lambda t, c: score(t, c, True), tops)
        tops = [jnp.max(top, axis=1, keepdims=True) for top in tops]

        def gather(t, sums):
            span = pl.ds(pl.multiple_of(t * bk, bk), bk)
            found = []
            for h in range(heads):
                p = jnp.exp(scores[h, :, span] - tops[h]).astype(low)
                found.append(sums[h] + jnp.dot(p, vone[h, span, :], preferred_element_type=jnp.float32))
            return tuple(found)

        sums = tuple(jnp.zeros((bq, LANES), jnp.float32) for _ in range(heads))
        sums = lax.fori_loop(0, last, gather, sums)
        outcome = jnp.zeros((bq, LANES), jnp.float32)
        lse = jnp.zeros((bq, LANES), jnp.float32)
        for h in range(heads):
            totals = pltpu.roll(sums[h], HEAD_DIM, 1)
            outcome = jnp.where(lanes_of(bq, h), sums[h] / totals, outcome)
            lse = jnp.where(lanes_of(bq, h), tops[h] + jnp.log(totals), lse)
        mixed[rows, :] = outcome.astype(low)
        lse_ref[:, rows] = lse.T
        return carry

    per_row = tokens // bq
    for row in range(n):
        if row == 0:
            come(0)
        if row + 1 < n:
            come(row + 1)

        def run(half, carry, row=row):
            i = row * per_row + half
            block(i, 0)

            @pl.when(row == me)
            def _():
                mix[pl.ds(pl.multiple_of(half * bq, bq), bq), columns(me)] = mixed[pl.ds(pl.multiple_of(i * bq, bq), bq), :]

            @pl.when(row != me)
            def _():
                mix_copy(i, row).start()

            return carry

        lax.fori_loop(0, per_row, run, 0)

    for d in range(1, n):
        leave(d).wait_send()
    for i in range(n * per_row):
        @pl.when(i // per_row != me)
        def _(i=i):
            mix_copy(i, me).wait_send()

    for row in range(n):
        @pl.when(row != me)
        def _(row=row):
            for half in range(per_row):
                rows = pl.ds(half * bq, bq)
                remote(
                    mixed.at[pl.ds(0, bq)], mix.at[rows, columns(row)], mix_sent.at[0], mix_got.at[row, half], "row", me
                ).wait_recv()


def attend(number, qkv, block_all, cosines, sines, heads, n, behind=(), bq=512, bk=512):
    tokens = qkv.shape[0]
    bq, bk = min(bq, tokens), min(bk, tokens)
    seq = n * tokens
    vmem = pl.BlockSpec(memory_space=pltpu.VMEM)
    low = jnp.bfloat16
    return pl.pallas_call(
        functools.partial(attend_kernel, heads, n, bq, bk),
        in_specs=[vmem] * 5 + [pl.BlockSpec(memory_space=pl.ANY)] * len(behind),
        out_specs=[vmem] * 4,
        out_shape=[
            jax.ShapeDtypeStruct((3, seq, LANES), low),
            jax.ShapeDtypeStruct((seq, LANES), low),
            jax.ShapeDtypeStruct((LANES, seq), jnp.float32),
            jax.ShapeDtypeStruct((tokens, n * LANES), low),
        ],
        scratch_shapes=[
            pltpu.VMEM((heads, seq, LANES), low),
            pltpu.VMEM((heads, bq, seq), jnp.float32),
            pltpu.VMEM((n - 1, 3, tokens, LANES), low),
            pltpu.SemaphoreType.DMA((n - 1,)),
            pltpu.SemaphoreType.DMA((n,)),
            pltpu.SemaphoreType.DMA((seq // bq,)),
            pltpu.SemaphoreType.DMA((n, tokens // bq)),
        ],
        compiler_params=pltpu.CompilerParams(
            collective_id=number, has_side_effects=True, vmem_limit_bytes=58 * 2**20
        ),
        cost_estimate=pl.CostEstimate(flops=10**10, bytes_accessed=2 * 10**8, transcendentals=0),
    )(block_all.reshape(seq, 1), block_all.reshape(1, seq), qkv, cosines, sines, *behind)


def attend_back_kernel(
    heads, n, bq, bk, bid_q, bid_k, d_mix, spread, mixed, lse_ref, cosines, sines, *refs
):
    d_qkv, grads, kone, dk_acc, dv_acc, leaving, g_sent, g_got, back_sent, back_got = refs[-10:]
    me = lax.axis_index("row")
    tokens = d_mix.shape[0]
    seq = n * tokens
    per_row = tokens // bq
    blocks = n * per_row
    low = jnp.bfloat16
    zero = jnp.zeros((), low)
    here = pl.ds(pl.multiple_of(me * tokens, tokens), tokens)
    meet("row", n)

    def give(d):
        to = lax.rem(me + d, n)
        return remote(d_mix.at[:, columns(to)], grads.at[here], g_sent.at[d - 1], g_got.at[me], "row", to)

    for d in range(1, n):
        give(d).start()
    grads[here, :] = d_mix[:, columns(me)]
    for h in range(heads):
        kone[h] = jnp.where(lanes_of(seq, h), spread[1], zero)
    dk_acc[...] = jnp.zeros_like(dk_acc)
    dv_acc[...] = jnp.zeros_like(dv_acc)

    def tile(t, dq, hide, stuff):
        qs, gs, lses, deltas, bid = stuff
        span = pl.ds(pl.multiple_of(t * bk, bk), bk)
        keys, values = spread[1, span, :], spread[2, span, :]
        dv, dk = dv_acc[span, :], dk_acc[span, :]
        if hide:
            visible = bid_k[span, :] <= bid
        for h in range(heads):
            s = dot_last(keys, qs[h])
            if hide:
                s = jnp.where(visible, s, -1e30)
            p = jnp.exp(s - lses[h])
            dp = dot_last(values, gs[h])
            ds = (p * (dp - deltas[h])).astype(low)
            dv = dv + jnp.dot(p.astype(low), gs[h], preferred_element_type=jnp.float32)
            dk = dk + jnp.dot(ds, qs[h], preferred_element_type=jnp.float32)
            dq = dq + dot_first(ds, kone[h, span, :])
        dv_acc[span, :] = dv
        dk_acc[span, :] = dk
        return dq

    def block(i):
        rows = pl.ds(pl.multiple_of(i * bq, bq), bq)
        q, g = spread[0, rows, :], grads[rows, :]
        product = (g.astype(jnp.float32) * mixed[rows, :].astype(jnp.float32)).T
        span = lambda h: slice(h * HEAD_DIM, (h + 1) * HEAD_DIM)
        deltas = [jnp.sum(product[span(h)], axis=0, keepdims=True) for h in range(heads)]
        lses = [lse_ref[h * HEAD_DIM : h * HEAD_DIM + 1, rows] for h in range(heads)]
        qs = [jnp.where(lanes_of(bq, h), q, zero) for h in range(heads)]
        gs = [jnp.where(lanes_of(bq, h), g, zero) for h in range(heads)]
        stuff = (qs, gs, lses, deltas, bid_q[:, rows])
        free = i * (bq // bk)
        last = jnp.minimum(((i + 1) * bq + REACH + bk - 1) // bk, seq // bk)
        dq = jnp.zeros((bq, LANES), jnp.float32)
        dq = lax.fori_loop(0, free, lambda t, c: tile(t, c, False, stuff), dq)
        dq = lax.fori_loop(free, last, lambda t, c: tile(t, c, True, stuff), dq)
        return spin(dq * (HEAD_DIM**-0.5), cosines[rows, :], -sines[rows, :]).astype(low)

    def back_copy(k, i, device):
        half = lax.rem(i, per_row)
        rows = pl.ds(pl.multiple_of(half * bq, bq), bq)
        return remote(
            leaving.at[k, pl.ds(pl.multiple_of(i * bq, bq), bq)],
            d_qkv.at[rows, columns(k * n + me)],
            back_sent.at[k, i],
            back_got.at[k, me, half],
            "row",
            device,
        )

    def send(k, i, values):
        row = i // per_row
        half = lax.rem(i, per_row)

        @pl.when(row == me)
        def _():
            d_qkv[pl.ds(pl.multiple_of(half * bq, bq), bq), columns(k * n + me)] = values

        @pl.when(row != me)
        def _():
            leaving[k, pl.ds(pl.multiple_of(i * bq, bq), bq), :] = values
            back_copy(k, i, row).start()

    def keys_done(i):
        rows = pl.ds(pl.multiple_of(i * bq, bq), bq)
        send(1, i, spin(dk_acc[rows, :], cosines[rows, :], -sines[rows, :]).astype(low))
        send(2, i, dv_acc[rows, :].astype(low))

    for row in range(n - 1, -1, -1):
        @pl.when(row != me)
        def _(row=row):
            there = pl.ds(row * tokens, tokens)
            remote(d_mix.at[:, columns(0)], grads.at[there], g_sent.at[0], g_got.at[row], "row", me).wait_recv()

        def run(step, carry, row=row):
            i = row * per_row + per_row - 1 - step
            send(0, i, block(i))

            @pl.when(i + 1 < blocks)
            def _():
                keys_done(i + 1)

            return carry

        lax.fori_loop(0, per_row, run, 0)
    keys_done(0)

    for d in range(1, n):
        give(d).wait_send()

    def settle(i, carry):
        @pl.when(i // per_row != me)
        def _():
            half = lax.rem(i, per_row)
            rows = pl.ds(pl.multiple_of(half * bq, bq), bq)
            for k in range(3):
                back_copy(k, i, me).wait_send()
                remote(
                    leaving.at[k, pl.ds(0, bq)],
                    d_qkv.at[rows, columns(k * n + i // per_row)],
                    back_sent.at[k, 0],
                    back_got.at[k, i // per_row, half],
                    "row",
                    me,
                ).wait_recv()

        return carry

    lax.fori_loop(0, blocks, settle, 0)


def attend_back(number, d_mix, spread, mixed, lse, block_all, cosines, sines, heads, n, behind=(), bq=512, bk=512):
    tokens = d_mix.shape[0]
    bq, bk = min(bq, tokens), min(bk, tokens)
    seq = n * tokens
    vmem = pl.BlockSpec(memory_space=pltpu.VMEM)
    low = jnp.bfloat16
    return pl.pallas_call(
        functools.partial(attend_back_kernel, heads, n, bq, bk),
        in_specs=[vmem] * 8 + [pl.BlockSpec(memory_space=pl.ANY)] * len(behind),
        out_specs=vmem,
        out_shape=jax.ShapeDtypeStruct((tokens, 3 * n * LANES), low),
        scratch_shapes=[
            pltpu.VMEM((seq, LANES), low),
            pltpu.VMEM((heads, seq, LANES), low),
            pltpu.VMEM((seq, LANES), jnp.float32),
            pltpu.VMEM((seq, LANES), jnp.float32),
            pltpu.VMEM((3, seq, LANES), low),
            pltpu.SemaphoreType.DMA((n - 1,)),
            pltpu.SemaphoreType.DMA((n,)),
            pltpu.SemaphoreType.DMA((3, seq // bq)),
            pltpu.SemaphoreType.DMA((3, n, tokens // bq)),
        ],
        compiler_params=pltpu.CompilerParams(
            collective_id=number, has_side_effects=True, vmem_limit_bytes=58 * 2**20
        ),
        cost_estimate=pl.CostEstimate(flops=10**10, bytes_accessed=3 * 10**8, transcendentals=0),
    )(block_all.reshape(1, seq), block_all.reshape(seq, 1), d_mix, spread, mixed, lse, cosines, sines, *behind)


def norm_parts(values):
    mean = jnp.mean(values, axis=-1, keepdims=True)
    spread = jnp.mean(values * values, axis=-1, keepdims=True) - mean * mean
    return mean, lax.rsqrt(spread + epsilon)


def after_attention(total, c, ins, outs):
    stream, gain, shift = ins
    (after_ref,) = outs
    after = stream[c].astype(jnp.float32) + total
    after_ref[c] = after
    values = after.astype(jnp.bfloat16).astype(jnp.float32)
    mean, inverse = norm_parts(values)
    return ((values - mean) * inverse * gain[...] + shift[...]).astype(jnp.bfloat16)


def after_hidden(total, c, ins, outs):
    (after,) = ins
    return (after[c] + total).astype(jnp.bfloat16)


def behind_norm(total, c, ins, outs):
    grad, values_ref, gain = ins
    grad_ref, sums = outs
    values = values_ref[c].astype(jnp.bfloat16).astype(jnp.float32)
    mean, inverse = norm_parts(values)
    centred = (values - mean) * inverse
    scaled = total * gain[...]
    back = inverse * (
        scaled
        - jnp.mean(scaled, axis=-1, keepdims=True)
        - centred * jnp.mean(scaled * centred, axis=-1, keepdims=True)
    )
    given = grad[c] + back
    grad_ref[c] = given
    here = [jnp.sum(total * centred, axis=0, keepdims=True), jnp.sum(total, axis=0, keepdims=True)]

    @pl.when(c == 0)
    def _():
        sums[...] = jnp.zeros_like(sums)

    sums[...] += jnp.concatenate(here, axis=0)
    return given.astype(jnp.bfloat16)


def relay_kernel(middle, n_ins, n_outs, layers, n_after, polish, n, chunks, lag, spread, partial, *refs):
    ins, carry, refs = refs[:n_ins], refs[n_ins : n_ins + len(layers)], refs[n_ins + len(layers) + n_after :]
    whole, outs, refs = refs[0], refs[1 : 1 + n_outs], refs[1 + n_outs :]
    carried, refs = refs[: len(layers)], refs[len(layers) :]
    if polish:
        ins, (gain, shift) = ins[:-2], ins[-2:]
        outs, polished = outs[:-1], outs[-1]
    if spread:
        outs, all_sums = outs[:-1], outs[-1]
    arrived, outgoing, total, sum_sent, sum_got, block_sent, block_got, carry_sent, carry_got, last_sent, last_got = refs
    section, i = lax.axis_index("section"), lax.axis_index("col")
    width = whole.shape[-1]
    first, last = i == 0, i == n - 1

    barrier = pltpu.get_barrier_semaphore()

    def greet(**place):
        pl.semaphore_signal(barrier, 1, device_id=place, device_id_type=pl.DeviceIdType.MESH)

    if spread:
        for d in range(1, 2 * n):
            greet(section=lax.rem(section + d // n, 2), col=lax.rem(i + d, n))
        pl.semaphore_wait(barrier, 2 * n - 1)
    else:
        greet(section=1 - section)

        @pl.when(i > 0)
        def _():
            greet(col=i - 1)

        @pl.when(i < n - 1)
        def _():
            greet(col=i + 1)

        @pl.when(first | last)
        def _():
            pl.semaphore_wait(barrier, 2)

        @pl.when((i > 0) & (i < n - 1))
        def _():
            pl.semaphore_wait(barrier, 3)

    def carry_copy(k):
        return remote(carry[k], carried[k], carry_sent.at[k], carry_got.at[k], "section", layers[k])

    for k, layer in enumerate(layers):
        @pl.when(section != layer)
        def _(k=k):
            carry_copy(k).start()

    def remote_col(source, target, sent, got, device):
        return remote(source, target, sent, got, "col", device)

    def sum_copy(c, j, right):
        slot = j + 1 if right else j
        return remote_col(
            outgoing.at[c, j], arrived.at[c, slot], sum_sent.at[c, j], sum_got.at[c, slot], i + 1 if right else i - 1
        )

    def block_copy(c, o, right, own=False):
        sent = n if own and not right else o
        return remote_col(whole.at[c, o], whole.at[c, o], block_sent.at[c, sent], block_got.at[0, c, o], i + 1 if right else i - 1)

    def slice_copy(c, d):
        to = lax.rem(i + d, n)
        return pltpu.make_async_remote_copy(
            src_ref=outgoing.at[c, i, :, pl.ds(pl.multiple_of(to * width, 128), width)],
            dst_ref=whole.at[section, c, i],
            send_sem=block_sent.at[c, d],
            recv_sem=block_got.at[section, c, i],
            device_id={"section": 0, "col": to},
            device_id_type=pl.DeviceIdType.MESH,
        )

    def arrive(c, slot):
        remote_col(outgoing.at[c, 0], arrived.at[c, slot], sum_sent.at[c, 0], sum_got.at[c, slot], i).wait_recv()

    def work(c, o):
        if polish:
            values = whole[c, o].astype(jnp.float32)
            mean, inverse = norm_parts(values)
            polished[c, o] = ((values - mean) * inverse * gain[...] + shift[...]).astype(jnp.bfloat16)

    def sums_copy(d):
        to = lax.rem(i + d, n)
        return pltpu.make_async_remote_copy(
            src_ref=outs[-1].at[:, pl.ds(pl.multiple_of(to * width, 128), width)],
            dst_ref=all_sums.at[section, i],
            send_sem=last_sent.at[d],
            recv_sem=last_got.at[section, i],
            device_id={"section": 0, "col": to},
            device_id_type=pl.DeviceIdType.MESH,
        )

    def sums_arrive(s, o):
        return pltpu.make_async_remote_copy(
            src_ref=outs[-1].at[:, pl.ds(0, width)],
            dst_ref=all_sums.at[s, o],
            send_sem=last_sent.at[0],
            recv_sem=last_got.at[s, o],
            device_id={"section": 0, "col": o},
            device_id_type=pl.DeviceIdType.MESH,
        )

    def middle_slot(k):
        return jnp.maximum(lag * k + n - 1 - k, lag * (n - 1 - k) + k)

    def at(now, slot, allowed):
        since = now - slot
        c = jnp.maximum(since, 0) // n
        return c, allowed & (since >= 0) & (lax.rem(jnp.maximum(since, 0), n) == 0) & (since < n * chunks)

    def step(now, carry):
        for j in range(n - 1, 0, -1):
            c, due = at(now, lag * i + n - 1 - j, i < j)

            @pl.when(due & first)
            def _(c=c, j=j):
                outgoing[c, j] = partial[c, j]

            @pl.when(due & (i > 0))
            def _(c=c, j=j):
                arrive(c, j + 1)
                both = arrived[c, j + 1].astype(jnp.float32) + partial[c, j].astype(jnp.float32)
                outgoing[c, j] = both.astype(jnp.bfloat16)

            @pl.when(due)
            def _(c=c, j=j):
                sum_copy(c, j, True).start()

        for j in range(n - 1):
            c, due = at(now, lag * (n - 1 - i) + j, i > j)

            @pl.when(due & last)
            def _(c=c, j=j):
                outgoing[c, j] = partial[c, j]

            @pl.when(due & (i < n - 1))
            def _(c=c, j=j):
                arrive(c, j)
                both = arrived[c, j].astype(jnp.float32) + partial[c, j].astype(jnp.float32)
                outgoing[c, j] = both.astype(jnp.bfloat16)

            @pl.when(due)
            def _(c=c, j=j):
                sum_copy(c, j, False).start()

        c, due = at(now, middle_slot(i), i >= 0)

        @pl.when(due)
        def _():
            total[...] = partial[c, i].astype(jnp.float32)

        @pl.when(due & (i > 0))
        def _():
            arrive(c, i + 1)
            total[...] += arrived[c, i + 1].astype(jnp.float32)

        @pl.when(due & (i < n - 1))
        def _():
            arrive(c, i)
            total[...] += arrived[c, i].astype(jnp.float32)

        @pl.when(due)
        def _():
            block = middle(total[...], c, ins, outs)
            if spread:
                outgoing[c, i] = block
                for d in range(1, n):
                    slice_copy(c, d).start()

                @pl.when(section == 0)
                def _():
                    whole[0, c, i] = outgoing[c, i, :, pl.ds(pl.multiple_of(i * width, 128), width)]

                @pl.when(section != 0)
                def _():
                    slice_copy(c, 0).start()

            else:
                whole[c, i] = block
                work(c, i)

        if spread:
            return carry

        @pl.when(due & (i < n - 1))
        def _():
            block_copy(c, i, True, own=True).start()

        @pl.when(due & (i > 0))
        def _():
            block_copy(c, i, False, own=True).start()

        for o in range(n - 1):
            c, due = at(now, middle_slot(o) + lag * (i - o), i > o)

            @pl.when(due)
            def _(c=c, o=o):
                block_copy(c, o, True).wait_recv()

            @pl.when(due & (i < n - 1))
            def _(c=c, o=o):
                block_copy(c, o, True).start()

            @pl.when(due)
            def _(c=c, o=o):
                work(c, o)

        for o in range(1, n):
            c, due = at(now, middle_slot(o) + lag * (o - i), i < o)

            @pl.when(due)
            def _(c=c, o=o):
                block_copy(c, o, False).wait_recv()

            @pl.when(due & (i > 0))
            def _(c=c, o=o):
                block_copy(c, o, False).start()

            @pl.when(due)
            def _(c=c, o=o):
                work(c, o)

        return carry

    lax.fori_loop(0, n * (chunks - 1) + 2 * lag * (n - 1) + 1, step, 0)

    if spread:
        for d in range(1, n):
            sums_copy(d).start()

        @pl.when(section == 0)
        def _():
            all_sums[0, i] = outs[-1][:, pl.ds(pl.multiple_of(i * width, 128), width)]

        @pl.when(section != 0)
        def _():
            sums_copy(0).start()

    def slice_arrives(c, s, o):
        return pltpu.make_async_remote_copy(
            src_ref=outgoing.at[c, 0, :, pl.ds(0, width)],
            dst_ref=whole.at[s, c, o],
            send_sem=block_sent.at[c, 0],
            recv_sem=block_got.at[s, c, o],
            device_id={"section": 0, "col": o},
            device_id_type=pl.DeviceIdType.MESH,
        )

    def settle(c, carry):
        for j in range(n):
            @pl.when(j != i)
            def _(j=j):
                sum_copy(c, j, True).wait_send()

        if spread:
            for d in range(1, n):
                slice_copy(c, d).wait_send()

            @pl.when(section != 0)
            def _():
                slice_copy(c, 0).wait_send()

            for s in range(2):
                for o in range(n):
                    @pl.when((section == 0) & ((s == 1) | (o != i)))
                    def _(s=s, o=o):
                        slice_arrives(c, s, o).wait_recv()

            return carry
        for o in range(n):
            @pl.when((o <= i) & (i < n - 1))
            def _(o=o):
                block_copy(c, o, True).wait_send()

            @pl.when((o > i) & (i > 0))
            def _(o=o):
                block_copy(c, o, True).wait_send()

        @pl.when(i > 0)
        def _():
            block_copy(c, i, False, own=True).wait_send()

        return carry

    lax.fori_loop(0, chunks, settle, 0)
    if spread:
        for d in range(1, n):
            sums_copy(d).wait_send()

        @pl.when(section != 0)
        def _():
            sums_copy(0).wait_send()

        for s in range(2):
            for o in range(n):
                @pl.when((section == 0) & ((s == 1) | (o != i)))
                def _(s=s, o=o):
                    sums_arrive(s, o).wait_recv()

    for k, layer in enumerate(layers):
        @pl.when(section != layer)
        def _(k=k):
            carry_copy(k).wait_send()

        @pl.when(section == layer)
        def _(k=k):
            carry_copy(k).wait_recv()


def relay(middle, number, partial, ins, outs, n, spread=False, carry=(), behind=(), polish=(), lag=3, rows=RELAY_ROWS):
    tokens, features = partial.shape
    owned = tokens // n
    chunks = owned // rows
    blocks = lambda values: values.reshape(chunks, rows, features) if values.shape[0] == owned else values
    ins = [blocks(values) for values in ins] + list(polish)
    outs = list(outs) + ([(tokens, features)] if polish else []) + ([(2, n, 2, features // n)] if spread else [])
    out_shapes = [
        jax.ShapeDtypeStruct(
            (2, chunks, n, rows, features // n) if spread else (chunks, n, rows, features), jnp.bfloat16
        )
    ] + [
        jax.ShapeDtypeStruct((chunks, n, rows, features), jnp.bfloat16)
        if shape[0] == tokens
        else jax.ShapeDtypeStruct((chunks, rows, features) if shape[0] == owned else shape, jnp.float32)
        for shape in outs
    ]
    vmem, anywhere = pl.BlockSpec(memory_space=pltpu.VMEM), pl.BlockSpec(memory_space=pl.ANY)
    layers = tuple(layer for layer, _ in carry)
    carry = [values for _, values in carry]
    whole, *rest = pl.pallas_call(
        functools.partial(relay_kernel, middle, len(ins), len(outs), layers, len(behind), bool(polish), n, chunks, lag, spread),
        in_specs=[vmem] * (1 + len(ins)) + [anywhere] * (len(carry) + len(behind)),
        out_specs=[vmem] * len(out_shapes) + [anywhere] * len(carry),
        out_shape=out_shapes + [jax.ShapeDtypeStruct(values.shape, values.dtype) for values in carry],
        scratch_shapes=[
            pltpu.VMEM((chunks, n + 1, rows, features), jnp.bfloat16),
            pltpu.VMEM((chunks, n, rows, features), jnp.bfloat16),
            pltpu.VMEM((rows, features), jnp.float32),
            pltpu.SemaphoreType.DMA((chunks, n)),
            pltpu.SemaphoreType.DMA((chunks, n + 1)),
            pltpu.SemaphoreType.DMA((chunks, n + 1)),
            pltpu.SemaphoreType.DMA((2 if spread else 1, chunks, n)),
            pltpu.SemaphoreType.DMA((max(1, len(carry)),)),
            pltpu.SemaphoreType.DMA((max(1, len(carry)),)),
            pltpu.SemaphoreType.DMA((n,)),
            pltpu.SemaphoreType.DMA((2, n)),
        ],
        compiler_params=pltpu.CompilerParams(
            collective_id=number, has_side_effects=True, vmem_limit_bytes=56 * 2**20
        ),
        cost_estimate=pl.CostEstimate(flops=0, bytes_accessed=35 * 10**7, transcendentals=0),
    )(partial.reshape(chunks, n, rows, features), *ins, *carry, *behind)
    shapes = {(chunks, rows, features): (owned, features), (chunks, n, rows, features): (tokens, features)}
    rest = [values.reshape(shapes.get(values.shape, values.shape)) for values in rest]
    return [whole.reshape((2, tokens, -1) if spread else (tokens, -1))] + rest


def gather_kernel(n, chunks, lag, own, small, angles, whole, smalls, normed, cosines, sines, sent, got, small_sent, small_got):
    section, i = lax.axis_index("section"), lax.axis_index("col")
    rows, width = own.shape[0] // chunks, own.shape[1]
    others = [(s, d) for s in range(2) for d in range(n) if (s, d) != (0, 0)]
    place = lambda s, d: {"section": lax.rem(section + s, 2), "col": lax.rem(i + d, n)}
    barrier = pltpu.get_barrier_semaphore()
    for s, d in others:
        pl.semaphore_signal(barrier, 1, device_id=place(s, d), device_id_type=pl.DeviceIdType.MESH)
    pl.semaphore_wait(barrier, len(others))

    def small_copy(s, d):
        return pltpu.make_async_remote_copy(
            src_ref=small,
            dst_ref=smalls.at[section, i],
            send_sem=small_sent.at[s, d],
            recv_sem=small_got.at[section, i],
            device_id=place(s, d),
            device_id_type=pl.DeviceIdType.MESH,
        )

    for s, d in others:
        small_copy(s, d).start()
    smalls[section, i] = small[...]

    def small_arrives(s, d):
        from_s, from_d = lax.rem(section + s, 2), lax.rem(i + d, n)
        return pltpu.make_async_remote_copy(
            src_ref=small,
            dst_ref=smalls.at[from_s, from_d],
            send_sem=small_sent.at[s, d],
            recv_sem=small_got.at[from_s, from_d],
            device_id=place(s, d),
            device_id_type=pl.DeviceIdType.MESH,
        )

    def norm(c):
        here = pl.ds(pl.multiple_of(c * rows, rows), rows)
        values = whole[here, :].astype(jnp.float32)
        mean, inverse = norm_parts(values)
        for o in range(n):
            part = slice(o * width, (o + 1) * width)
            gain, shift = smalls[0, o, 0:1, :], smalls[0, o, 2:3, :]
            normed[here, part] = ((values[:, part] - mean) * inverse * gain + shift).astype(jnp.bfloat16)

    def block(c, o, right, mine=False):
        part = whole.at[pl.ds(pl.multiple_of(c * rows, rows), rows), columns(o, width)]
        return remote(
            part, part, sent.at[c, n if mine and not right else o], got.at[c, o], "col", i + 1 if right else i - 1
        )

    def at(now, slot, allowed):
        since = jnp.maximum(now - slot, 0)
        return since // (n - 1), allowed & (now >= slot) & (lax.rem(since, n - 1) == 0) & (since < (n - 1) * chunks)

    def step(now, carry):
        c, due = at(now, 0, i >= 0)

        @pl.when(due)
        def _():
            here = pl.ds(pl.multiple_of(c * rows, rows), rows)
            whole[here, columns(i, width)] = own[here, :]

        @pl.when(due & (i < n - 1))
        def _():
            block(c, i, True, True).start()

        @pl.when(due & (i > 0))
        def _():
            block(c, i, False, True).start()

        for o in range(n):
            c, due = at(now, lag * jnp.abs(i - o), i != o)

            @pl.when(due)
            def _(c=c, o=o):
                block(c, o, True).wait_recv()

            @pl.when(due & (i > o) & (i < n - 1))
            def _(c=c, o=o):
                block(c, o, True).start()

            @pl.when(due & (i < o) & (i > 0))
            def _(c=c, o=o):
                block(c, o, False).start()

        c, due = at(now, lag * (n - 1), i >= 0)

        @pl.when(due)
        def _():
            norm(c)

        return carry

    turns = angles.shape[0] // 2
    lane = lax.broadcasted_iota(jnp.int32, (turns, LANES), 1)
    place_of = lax.broadcasted_iota(jnp.int32, (turns, LANES), 0)
    turned = lane % HEAD_DIM < 2 * turns
    picked = jnp.where(turned & (lane % turns == place_of), 1.0, 0.0)
    sign = jnp.where(lane % HEAD_DIM < turns, -1.0, 1.0)

    def spread_out(table, pick):
        return lax.dot_general(
            table, pick, (((0,), (0,)), ((), ())), precision=lax.Precision.HIGHEST, preferred_element_type=jnp.float32
        )

    still = jnp.where(turned[:1], 0.0, 1.0)
    cosines[...] = spread_out(angles[:turns, :], picked) + still
    sines[...] = spread_out(angles[turns:, :], picked * sign)
    for s, d in others:
        small_arrives(s, d).wait_recv()

    lax.fori_loop(0, (n - 1) * (chunks - 1) + lag * (n - 1) + 1, step, 0)

    def settle(c, carry):
        for o in range(n):
            @pl.when(((o <= i) & (i < n - 1)) | ((o > i) & (i > 0)))
            def _(o=o):
                block(c, o, True).wait_send()

        @pl.when(i > 0)
        def _():
            block(c, i, False, True).wait_send()

        return carry

    lax.fori_loop(0, chunks, settle, 0)
    for s, d in others:
        small_copy(s, d).wait_send()


def gathered(number, own, small, angles, n, lag=3, rows=64):
    tokens, width = own.shape
    chunks = tokens // rows
    vmem = pl.BlockSpec(memory_space=pltpu.VMEM)
    return pl.pallas_call(
        functools.partial(gather_kernel, n, chunks, lag),
        in_specs=[vmem] * 3,
        out_specs=[vmem] * 5,
        out_shape=[
            jax.ShapeDtypeStruct((tokens, n * width), own.dtype),
            jax.ShapeDtypeStruct((2, n) + small.shape, small.dtype),
            jax.ShapeDtypeStruct((tokens, n * width), own.dtype),
            jax.ShapeDtypeStruct((angles.shape[1], LANES), jnp.float32),
            jax.ShapeDtypeStruct((angles.shape[1], LANES), jnp.float32),
        ],
        scratch_shapes=[
            pltpu.SemaphoreType.DMA((chunks, n + 1)),
            pltpu.SemaphoreType.DMA((chunks, n)),
            pltpu.SemaphoreType.DMA((2, n)),
            pltpu.SemaphoreType.DMA((2, n)),
        ],
        compiler_params=pltpu.CompilerParams(
            collective_id=number, has_side_effects=True, vmem_limit_bytes=40 * 2**20
        ),
        cost_estimate=pl.CostEstimate(flops=0, bytes_accessed=25 * 10**7, transcendentals=0),
    )(own, small, angles)


def rotary_angles(positions):
    half_dims = ROT // 2
    inverse_freq = 1.0 / 10000.0 ** (jnp.arange(half_dims, dtype=jnp.float32) * 2.0 / ROT)
    angles = positions.astype(jnp.float32)[None, :] * inverse_freq[:, None]
    return jnp.concatenate([jnp.cos(angles), jnp.sin(angles)])


def product(left, right):
    return jnp.dot(left, right, preferred_element_type=jnp.float32)


def per_device(
    inputs,
    cotangent,
    block_ids,
    norm_gains,
    norm_shifts,
    qkv_weight,
    qkv_bias,
    out_weight,
    gate_up_weight,
    down_weight,
):
    section = lax.axis_index("section")
    row = lax.axis_index("row")
    col = lax.axis_index("col")
    rows_axis = lax.axis_size("row")
    cols_axis = lax.axis_size("col")
    tokens, width = inputs.shape[1:]
    owned = tokens // cols_axis
    units = down_weight.shape[2]
    seq = tokens * rows_axis
    both = ("section", "row")
    whole_lanes = width == rows_axis * LANES
    heads = LANES // HEAD_DIM if whole_lanes else 1
    copies = 1 if whole_lanes else rows_axis * HEAD_DIM // width

    def expand(values):
        if whole_lanes:
            return values
        values = values.reshape(tokens, -1, width // HEAD_DIM, HEAD_DIM)
        values = jnp.pad(jnp.repeat(values, copies, axis=2), ((0, 0), (0, 0), (0, 0), (0, LANES - HEAD_DIM)))
        return values.reshape(tokens, -1)

    def contract(values):
        if whole_lanes:
            return values
        values = values.reshape(tokens, -1, rows_axis, LANES)[:, :, ::copies, :HEAD_DIM]
        return values.reshape(tokens, -1)

    def weights_of(block):
        block = block[0].reshape(block.shape[1], -1)
        return lax.all_gather(block, both, axis=0, tiled=True).reshape(2, D, -1)

    def mine(values):
        blocks = values.reshape(owned // RELAY_ROWS, cols_axis, RELAY_ROWS, -1)
        return lax.dynamic_index_in_dim(blocks, col, 1, keepdims=False).reshape(owned, -1)

    def my_features(values):
        return lax.dynamic_slice_in_dim(values, col * width, width, 1)

    own_small = jnp.concatenate([norm_gains[0], norm_shifts[0], qkv_bias[0], jnp.zeros((1, width), jnp.float32)])
    angles = rotary_angles(jnp.arange(seq, dtype=jnp.int32))
    stream, small, normed, cosines, sines = gathered(
        7, lax.dynamic_index_in_dim(inputs, section, 0, keepdims=False), own_small, angles, cols_axis
    )
    whole_small = small.transpose(0, 2, 1, 3).reshape(2, own_small.shape[0], D)
    gains, shifts = whole_small[:, :2], whole_small[:, 2:4]
    bias = lax.dynamic_index_in_dim(small, col, 1, keepdims=False)[:, 4:7].reshape(2, -1)

    qkv_w = weights_of(qkv_weight)
    out_w = weights_of(out_weight)
    gate_up_w = weights_of(gate_up_weight)
    down_w = weights_of(down_weight)

    ids = lax.dynamic_index_in_dim(block_ids, section, 0, keepdims=False)
    kept = []
    hidden_out = []
    waited = []
    for layer in range(2):
        qkv = product(normed, qkv_w[layer]) + bias[layer]
        if layer == 1:
            here = section + jnp.where(hidden_out[0][0, 0] == hidden_out[0][0, 0], 0, 1)
            branch = lax.all_gather(
                lax.dynamic_index_in_dim(cotangent, here, 0, keepdims=False), "col", axis=1, tiled=True
            )
            waited = [branch]
        spread, mixed, log_sums, attn_mix = attend(8, expand(qkv), ids, cosines, sines, heads, rows_axis)
        attn_mix = contract(attn_mix)
        normed_two, after = relay(
            after_attention,
            layer,
            product(attn_mix, out_w[layer].T).astype(jnp.bfloat16),
            [mine(stream), gains[layer, 1:], shifts[layer, 1:]],
            [(owned, D)],
            cols_axis,
            behind=waited,
        )
        gate_up = product(normed_two, gate_up_w[layer])
        gate, up = gate_up[:, :units], gate_up[:, units:]
        hidden = (jax.nn.silu(gate) * up).astype(jnp.bfloat16)
        kept.append((stream, normed, spread, mixed, log_sums, attn_mix, after, normed_two, gate_up, hidden))
        partial = product(hidden, down_w[layer].T)
        if layer == 0:
            stream, normed = relay(
                after_hidden,
                2,
                partial.astype(jnp.bfloat16),
                [after],
                [],
                cols_axis,
                polish=(gains[1, :1], shifts[1, :1]),
            )
            hidden_out.append(my_features(stream))
        else:
            blocks = partial.reshape(owned // RELAY_ROWS, cols_axis, RELAY_ROWS, D)
            owner = lax.broadcasted_iota(jnp.int32, blocks.shape, 1) == col
            blocks = blocks + jnp.where(owner, after.reshape(-1, 1, RELAY_ROWS, D), 0.0)
            result = blocks.reshape(tokens, D).astype(jnp.bfloat16)

    grad = mine(branch).astype(jnp.float32)
    weight_sums = [[], []]
    small_sums = []
    bias_grads = [None, None]
    input_out = [None, None]
    input_got = [None, None]
    hidden_got = [None, None]

    def collect(layer, term):
        weight_sums[layer].append(lax.psum_scatter(term, "row", scatter_dimension=0, tiled=True))
        return weight_sums[layer][-1]

    arrived = [[None] * 4, [None] * 4]
    def together(*values):
        return lax.optimization_barrier(values)

    for layer in (1, 0):
        stream, normed, spread, mixed, log_sums, attn_mix, after, normed_two, gate_up, hidden = kept[layer]
        gate, up = gate_up[:, :units], gate_up[:, units:]
        d_hidden = product(branch, down_w[layer])
        sig = jax.nn.sigmoid(gate)
        d_gate = d_hidden * up * sig * (1.0 + gate * (1.0 - sig))
        d_up = d_hidden * gate * sig
        d_gate_up = jnp.concatenate([d_gate, d_up], axis=1).astype(jnp.bfloat16)
        partial, down_term, gate_up_term = together(
            dot_last(d_gate_up, gate_up_w[layer]).astype(jnp.bfloat16),
            dot_first(branch, hidden).astype(jnp.bfloat16),
            dot_first(normed_two, d_gate_up).astype(jnp.bfloat16),
        )
        down_sum, gate_up_sum = collect(layer, down_term), collect(layer, gate_up_term)
        grad_attn, d_after, sums_two, *got = relay(
            behind_norm,
            3 + layer,
            partial,
            [grad, after, gains[layer, 1:]],
            [(owned, D), (2, D)],
            cols_axis,
            carry=[]
            if layer == 1
            else [(0, hidden_out[0]), (1, hidden_out[1]), (1, input_out[1]), (1, weight_sums[1][2]), (1, weight_sums[1][3])],
            behind=[] if layer == 1 else [down_sum],
        )
        if layer == 1:
            result = jnp.where(d_after[0, 0] == d_after[0, 0], result, 0)
            hidden_out.append(lax.psum_scatter(result, "col", scatter_dimension=1, tiled=True))
        else:
            hidden_got[0], hidden_got[1], input_got[1], arrived[1][2], arrived[1][3] = got
        small_sums += [sums_two]
        d_mix, out_term = together(
            product(grad_attn, out_w[layer]).astype(jnp.bfloat16), dot_first(grad_attn, attn_mix).astype(jnp.bfloat16)
        )
        out_sum = collect(layer, out_term)
        d_qkv = contract(
            attend_back(
                9,
                expand(d_mix),
                spread,
                mixed,
                log_sums,
                ids,
                cosines,
                sines,
                heads,
                rows_axis,
                behind=[down_sum, gate_up_sum],
            )
        )
        partial, qkv_term, bias_grads[layer] = together(
            dot_last(d_qkv, qkv_w[layer]).astype(jnp.bfloat16),
            dot_first(normed, d_qkv).astype(jnp.bfloat16),
            jnp.sum(d_qkv.astype(jnp.float32), axis=0),
        )
        qkv_sum = collect(layer, qkv_term)
        if layer == 0:
            early_sums = lax.psum_scatter(jnp.stack(small_sums), "col", scatter_dimension=2, tiled=True)
            early = jnp.concatenate([early_sums.reshape(6, -1), bias_grads[1].reshape(3, -1), bias_grads[0].reshape(3, -1)])
            early = jnp.sum(lax.all_gather(early, both, axis=0), axis=0)
        branch, grad, sums_one, *got = relay(
            behind_norm,
            5 + layer,
            partial,
            [d_after, mine(stream), gains[layer, :1]],
            [(owned, D), (2, D)],
            cols_axis,
            spread=layer == 0,
            carry=[(layer, down_sum), (layer, gate_up_sum)] + ([(0, out_sum)] if layer == 0 else []),
            behind=[hidden_out[1]] if layer == 1 else [early_sums],
        )
        if layer == 0:
            late_sums, *got = got
        arrived[layer][: len(got)] = got
        small_sums += [sums_one]
        input_out[layer] = my_features(branch) if layer == 1 else branch

    arrived[0][3] = lax.ppermute(weight_sums[0][3], "section", [(1, 0)])
    hidden_states = jnp.where(
        section == 0, jnp.stack([hidden_out[0], hidden_got[0]]), jnp.stack([hidden_got[1], hidden_out[1]])
    )
    input_grads = jnp.where(section == 0, input_out[0], jnp.stack([input_got[1], input_out[1]])).astype(jnp.float32)
    down_grad, gate_up_grad, out_grad, qkv_grad = (
        jnp.where(section == 0, first, second).astype(jnp.float32)
        + jnp.where(section == 0, first_got, second_got).astype(jnp.float32)
        for first, second, first_got, second_got in zip(*weight_sums, *arrived)
    )
    last = lax.psum(jnp.sum(late_sums, axis=(0, 1)), "row")
    norm_sums = jnp.where(section == 0, jnp.stack([last, early[4:6]]), jnp.stack([early[2:4], early[0:2]]))
    bias_sum = jnp.where(section == 0, early[9:12], early[6:9])
    return (
        hidden_states[None],
        input_grads[None],
        norm_sums[:, 0][None],
        norm_sums[:, 1][None],
        qkv_grad.reshape(qkv_weight.shape),
        bias_sum.reshape(qkv_bias.shape),
        out_grad[None],
        gate_up_grad.reshape(gate_up_weight.shape),
        down_grad[None],
    )


def solution(mesh):
    in_specs = (
        P(None, "row", "col"),
        P(None, "row", "col"),
        P(),
        P("section", None, "col"),
        P("section", None, "col"),
        P("section", "row", None, "col"),
        P("section", None, "col"),
        P("section", "row", "col"),
        P("section", "row", None, "col"),
        P("section", "row", "col"),
    )
    out_specs = (
        P("section", None, "row", "col"),
        P("section", None, "row", "col"),
        P("section", None, "col"),
        P("section", None, "col"),
        P("section", "row", None, "col"),
        P("section", None, "col"),
        P("section", "row", "col"),
        P("section", "row", None, "col"),
        P("section", "row", "col"),
    )
    return jax.shard_map(
        per_device, mesh=mesh, in_specs=in_specs, out_specs=out_specs, check_vma=False
    )
```

```python
import functools

import jax
import jax.numpy as jnp
from jax import lax
from jax.experimental import pallas as pl
from jax.experimental.pallas import tpu as pltpu
from jax.sharding import PartitionSpec as P

D = 2048
HEADS = 32
HEAD_DIM = 64
ROT = 16
LANES = 128
REACH = 256
RELAY_ROWS = 16


epsilon = 1e-05


def dot_last(a, b):
    return lax.dot_general(a, b, (((1,), (1,)), ((), ())), preferred_element_type=jnp.float32)


def dot_first(a, b):
    return lax.dot_general(a, b, (((0,), (0,)), ((), ())), preferred_element_type=jnp.float32)


def lanes_of(rows, head):
    lane = lax.broadcasted_iota(jnp.int32, (rows, LANES), 1)
    return lane // HEAD_DIM == head


def spin(x, cosines, sines):
    lane = lax.broadcasted_iota(jnp.int32, x.shape, 1)
    ahead, behind = pltpu.roll(x, LANES - ROT // 2, 1), pltpu.roll(x, ROT // 2, 1)
    return x * cosines + jnp.where(lane % ROT < ROT // 2, ahead, behind) * sines


def meet(axis, n):
    me = lax.axis_index(axis)
    barrier = pltpu.get_barrier_semaphore()
    for d in range(1, n):
        pl.semaphore_signal(
            barrier, 1, device_id={axis: lax.rem(me + d, n)}, device_id_type=pl.DeviceIdType.MESH
        )
    pl.semaphore_wait(barrier, n - 1)


def remote(source, target, sent, got, axis, device):
    return pltpu.make_async_remote_copy(
        src_ref=source,
        dst_ref=target,
        send_sem=sent,
        recv_sem=got,
        device_id={axis: device},
        device_id_type=pl.DeviceIdType.MESH,
    )


def columns(which, size=LANES):
    return pl.ds(pl.multiple_of(which * size, size), size)


def attend_kernel(
    heads, n, bq, bk, bid_q, bid_k, qkv, cosines, sines,
    spread, mixed, lse_ref, mix, vone, scores, leaving, qkv_sent, qkv_got, mix_sent, mix_got,
):
    me = lax.axis_index("row")
    tokens = qkv.shape[0]
    seq = n * tokens
    here = pl.ds(pl.multiple_of(me * tokens, tokens), tokens)
    low = jnp.bfloat16
    meet("row", n)

    def parts(t):
        cos, sin = cosines[here, :], sines[here, :]
        query = spin(qkv[:, columns(t)], cos, sin).astype(low) * jnp.asarray(HEAD_DIM**-0.5, low)
        key = spin(qkv[:, columns(n + t)], cos, sin).astype(low)
        return query.astype(low), key, qkv[:, columns(2 * n + t)].astype(low)

    def leave(d):
        to = lax.rem(me + d, n)
        return remote(leaving.at[d - 1], spread.at[:, here], qkv_sent.at[d - 1], qkv_got.at[me], "row", to)

    for d in range(1, n):
        for k, part in enumerate(parts(lax.rem(me + d, n))):
            leaving[d - 1, k] = part
        leave(d).start()
    for k, part in enumerate(parts(me)):
        spread[k, here, :] = part

    def come(row):
        @pl.when(row != me)
        def _():
            there = pl.ds(row * tokens, tokens)
            remote(leaving.at[0], spread.at[:, there], qkv_sent.at[0], qkv_got.at[row], "row", me).wait_recv()

        there = pl.ds(row * tokens, tokens)
        for h in range(heads):
            vone[h, there, :] = jnp.where(lanes_of(tokens, h), spread[2, there, :], jnp.ones((), low))

    def mix_copy(i, device):
        rows = pl.ds(lax.rem(i, tokens // bq) * bq, bq)
        return remote(
            mixed.at[pl.ds(i * bq, bq)], mix.at[rows, columns(me)], mix_sent.at[i], mix_got.at[me, lax.rem(i, tokens // bq)], "row", device
        )

    def block(i, carry):
        rows = pl.ds(pl.multiple_of(i * bq, bq), bq)
        q = spread[0, rows, :]
        bid = bid_q[rows, :]
        free = i * (bq // bk)
        last = jnp.minimum(((i + 1) * bq + REACH + bk - 1) // bk, seq // bk)
        qs = [jnp.where(lanes_of(bq, h), q, jnp.zeros((), low)) for h in range(heads)]

        def score(t, tops, hide):
            span = pl.ds(pl.multiple_of(t * bk, bk), bk)
            keys = spread[1, span, :]
            if hide:
                visible = bid_k[:, span] <= bid
            found = []
            for h in range(heads):
                s = dot_last(qs[h], keys)
                if hide:
                    s = jnp.where(visible, s, -1e30)
                scores[h, :, span] = s
                top = tops[h]
                for c in range(bk // LANES):
                    top = jnp.maximum(top, s[:, c * LANES : (c + 1) * LANES])
                found.append(top)
            return tuple(found)

        tops = tuple(jnp.full((bq, LANES), -1e30, jnp.float32) for _ in range(heads))
        tops = lax.fori_loop(0, free, lambda t, c: score(t, c, False), tops)
        tops = lax.fori_loop(free, last, lambda t, c: score(t, c, True), tops)
        tops = [jnp.max(top, axis=1, keepdims=True) for top in tops]

        def gather(t, sums):
            span = pl.ds(pl.multiple_of(t * bk, bk), bk)
            found = []
            for h in range(heads):
                p = jnp.exp(scores[h, :, span] - tops[h]).astype(low)
                found.append(sums[h] + jnp.dot(p, vone[h, span, :], preferred_element_type=jnp.float32))
            return tuple(found)

        sums = tuple(jnp.zeros((bq, LANES), jnp.float32) for _ in range(heads))
        sums = lax.fori_loop(0, last, gather, sums)
        outcome = jnp.zeros((bq, LANES), jnp.float32)
        lse = jnp.zeros((bq, LANES), jnp.float32)
        for h in range(heads):
            totals = pltpu.roll(sums[h], HEAD_DIM, 1)
            outcome = jnp.where(lanes_of(bq, h), sums[h] / totals, outcome)
            lse = jnp.where(lanes_of(bq, h), tops[h] + jnp.log(totals), lse)
        mixed[rows, :] = outcome.astype(low)
        lse_ref[:, rows] = lse.T
        return carry

    per_row = tokens // bq
    for row in range(n):
        if row == 0:
            come(0)
        if row + 1 < n:
            come(row + 1)

        def run(half, carry, row=row):
            i = row * per_row + half
            block(i, 0)

            @pl.when(row == me)
            def _():
                mix[pl.ds(pl.multiple_of(half * bq, bq), bq), columns(me)] = mixed[pl.ds(pl.multiple_of(i * bq, bq), bq), :]

            @pl.when(row != me)
            def _():
                mix_copy(i, row).start()

            return carry

        lax.fori_loop(0, per_row, run, 0)

    for d in range(1, n):
        leave(d).wait_send()
    for i in range(n * per_row):
        @pl.when(i // per_row != me)
        def _(i=i):
            mix_copy(i, me).wait_send()

    for row in range(n):
        @pl.when(row != me)
        def _(row=row):
            for half in range(per_row):
                rows = pl.ds(half * bq, bq)
                remote(
                    mixed.at[pl.ds(0, bq)], mix.at[rows, columns(row)], mix_sent.at[0], mix_got.at[row, half], "row", me
                ).wait_recv()


def attend(number, qkv, block_all, cosines, sines, heads, n, bq=512, bk=512):
    tokens = qkv.shape[0]
    bq, bk = min(bq, tokens), min(bk, tokens)
    seq = n * tokens
    vmem = pl.BlockSpec(memory_space=pltpu.VMEM)
    low = jnp.bfloat16
    return pl.pallas_call(
        functools.partial(attend_kernel, heads, n, bq, bk),
        in_specs=[vmem] * 5,
        out_specs=[vmem] * 4,
        out_shape=[
            jax.ShapeDtypeStruct((3, seq, LANES), low),
            jax.ShapeDtypeStruct((seq, LANES), low),
            jax.ShapeDtypeStruct((LANES, seq), jnp.float32),
            jax.ShapeDtypeStruct((tokens, n * LANES), low),
        ],
        scratch_shapes=[
            pltpu.VMEM((heads, seq, LANES), low),
            pltpu.VMEM((heads, bq, seq), jnp.float32),
            pltpu.VMEM((n - 1, 3, tokens, LANES), low),
            pltpu.SemaphoreType.DMA((n - 1,)),
            pltpu.SemaphoreType.DMA((n,)),
            pltpu.SemaphoreType.DMA((seq // bq,)),
            pltpu.SemaphoreType.DMA((n, tokens // bq)),
        ],
        compiler_params=pltpu.CompilerParams(
            collective_id=number, has_side_effects=True, vmem_limit_bytes=58 * 2**20
        ),
        cost_estimate=pl.CostEstimate(flops=10**10, bytes_accessed=2 * 10**8, transcendentals=0),
    )(block_all.reshape(seq, 1), block_all.reshape(1, seq), qkv, cosines, sines)


def attend_back_kernel(
    heads, n, bq, bk, layer, bid_q, bid_k, d_mix, spread, mixed, lse_ref, cosines, sines, carry, *refs
):
    d_qkv, carried, grads, kone, dk_acc, dv_acc, leaving, g_sent, g_got, back_sent, back_got, carry_sent, carry_got = refs
    section = lax.axis_index("section")
    me = lax.axis_index("row")
    tokens = d_mix.shape[0]
    seq = n * tokens
    per_row = tokens // bq
    blocks = n * per_row
    low = jnp.bfloat16
    zero = jnp.zeros((), low)
    here = pl.ds(pl.multiple_of(me * tokens, tokens), tokens)
    barrier = pltpu.get_barrier_semaphore()
    pl.semaphore_signal(barrier, 1, device_id={"section": 1 - section}, device_id_type=pl.DeviceIdType.MESH)
    for d in range(1, n):
        pl.semaphore_signal(barrier, 1, device_id={"row": lax.rem(me + d, n)}, device_id_type=pl.DeviceIdType.MESH)
    pl.semaphore_wait(barrier, n)
    carry_copy = remote(carry, carried, carry_sent, carry_got, "section", layer)

    def give(d):
        to = lax.rem(me + d, n)
        return remote(d_mix.at[:, columns(to)], grads.at[here], g_sent.at[d - 1], g_got.at[me], "row", to)

    for d in range(1, n):
        give(d).start()

    @pl.when(section != layer)
    def _():
        carry_copy.start()

    grads[here, :] = d_mix[:, columns(me)]
    for h in range(heads):
        kone[h] = jnp.where(lanes_of(seq, h), spread[1], zero)
    dk_acc[...] = jnp.zeros_like(dk_acc)
    dv_acc[...] = jnp.zeros_like(dv_acc)

    def tile(t, dq, hide, stuff):
        qs, gs, lses, deltas, bid = stuff
        span = pl.ds(pl.multiple_of(t * bk, bk), bk)
        keys, values = spread[1, span, :], spread[2, span, :]
        dv, dk = dv_acc[span, :], dk_acc[span, :]
        if hide:
            visible = bid_k[span, :] <= bid
        for h in range(heads):
            s = dot_last(keys, qs[h])
            if hide:
                s = jnp.where(visible, s, -1e30)
            p = jnp.exp(s - lses[h])
            dp = dot_last(values, gs[h])
            ds = (p * (dp - deltas[h])).astype(low)
            dv = dv + jnp.dot(p.astype(low), gs[h], preferred_element_type=jnp.float32)
            dk = dk + jnp.dot(ds, qs[h], preferred_element_type=jnp.float32)
            dq = dq + dot_first(ds, kone[h, span, :])
        dv_acc[span, :] = dv
        dk_acc[span, :] = dk
        return dq

    def block(i):
        rows = pl.ds(pl.multiple_of(i * bq, bq), bq)
        q, g = spread[0, rows, :], grads[rows, :]
        product = (g.astype(jnp.float32) * mixed[rows, :].astype(jnp.float32)).T
        span = lambda h: slice(h * HEAD_DIM, (h + 1) * HEAD_DIM)
        deltas = [jnp.sum(product[span(h)], axis=0, keepdims=True) for h in range(heads)]
        lses = [lse_ref[h * HEAD_DIM : h * HEAD_DIM + 1, rows] for h in range(heads)]
        qs = [jnp.where(lanes_of(bq, h), q, zero) for h in range(heads)]
        gs = [jnp.where(lanes_of(bq, h), g, zero) for h in range(heads)]
        stuff = (qs, gs, lses, deltas, bid_q[:, rows])
        free = i * (bq // bk)
        last = jnp.minimum(((i + 1) * bq + REACH + bk - 1) // bk, seq // bk)
        dq = jnp.zeros((bq, LANES), jnp.float32)
        dq = lax.fori_loop(0, free, lambda t, c: tile(t, c, False, stuff), dq)
        dq = lax.fori_loop(free, last, lambda t, c: tile(t, c, True, stuff), dq)
        return spin(dq * (HEAD_DIM**-0.5), cosines[rows, :], -sines[rows, :]).astype(low)

    def back_copy(k, i, device):
        half = lax.rem(i, per_row)
        rows = pl.ds(pl.multiple_of(half * bq, bq), bq)
        return remote(
            leaving.at[k, pl.ds(pl.multiple_of(i * bq, bq), bq)],
            d_qkv.at[rows, columns(k * n + me)],
            back_sent.at[k, i],
            back_got.at[k, me, half],
            "row",
            device,
        )

    def send(k, i, values):
        row = i // per_row
        half = lax.rem(i, per_row)

        @pl.when(row == me)
        def _():
            d_qkv[pl.ds(pl.multiple_of(half * bq, bq), bq), columns(k * n + me)] = values

        @pl.when(row != me)
        def _():
            leaving[k, pl.ds(pl.multiple_of(i * bq, bq), bq), :] = values
            back_copy(k, i, row).start()

    def keys_done(i):
        rows = pl.ds(pl.multiple_of(i * bq, bq), bq)
        send(1, i, spin(dk_acc[rows, :], cosines[rows, :], -sines[rows, :]).astype(low))
        send(2, i, dv_acc[rows, :].astype(low))

    for row in range(n - 1, -1, -1):
        @pl.when(row != me)
        def _(row=row):
            there = pl.ds(row * tokens, tokens)
            remote(d_mix.at[:, columns(0)], grads.at[there], g_sent.at[0], g_got.at[row], "row", me).wait_recv()

        def run(step, carry, row=row):
            i = row * per_row + per_row - 1 - step
            send(0, i, block(i))

            @pl.when(i + 1 < blocks)
            def _():
                keys_done(i + 1)

            return carry

        lax.fori_loop(0, per_row, run, 0)
    keys_done(0)

    for d in range(1, n):
        give(d).wait_send()

    def settle(i, carry):
        @pl.when(i // per_row != me)
        def _():
            half = lax.rem(i, per_row)
            rows = pl.ds(pl.multiple_of(half * bq, bq), bq)
            for k in range(3):
                back_copy(k, i, me).wait_send()
                remote(
                    leaving.at[k, pl.ds(0, bq)],
                    d_qkv.at[rows, columns(k * n + i // per_row)],
                    back_sent.at[k, 0],
                    back_got.at[k, i // per_row, half],
                    "row",
                    me,
                ).wait_recv()

        return carry

    lax.fori_loop(0, blocks, settle, 0)

    @pl.when(section != layer)
    def _():
        carry_copy.wait_send()

    @pl.when(section == layer)
    def _():
        carry_copy.wait_recv()


def attend_back(number, d_mix, spread, mixed, lse, block_all, cosines, sines, heads, n, layer, carry, bq=512, bk=512):
    tokens = d_mix.shape[0]
    bq, bk = min(bq, tokens), min(bk, tokens)
    seq = n * tokens
    vmem = pl.BlockSpec(memory_space=pltpu.VMEM)
    low = jnp.bfloat16
    return pl.pallas_call(
        functools.partial(attend_back_kernel, heads, n, bq, bk, layer),
        in_specs=[vmem] * 8 + [pl.BlockSpec(memory_space=pl.ANY)],
        out_specs=[vmem, pl.BlockSpec(memory_space=pl.ANY)],
        out_shape=[jax.ShapeDtypeStruct((tokens, 3 * n * LANES), low), jax.ShapeDtypeStruct(carry.shape, carry.dtype)],
        scratch_shapes=[
            pltpu.VMEM((seq, LANES), low),
            pltpu.VMEM((heads, seq, LANES), low),
            pltpu.VMEM((seq, LANES), jnp.float32),
            pltpu.VMEM((seq, LANES), jnp.float32),
            pltpu.VMEM((3, seq, LANES), low),
            pltpu.SemaphoreType.DMA((n - 1,)),
            pltpu.SemaphoreType.DMA((n,)),
            pltpu.SemaphoreType.DMA((3, seq // bq)),
            pltpu.SemaphoreType.DMA((3, n, tokens // bq)),
            pltpu.SemaphoreType.DMA,
            pltpu.SemaphoreType.DMA,
        ],
        compiler_params=pltpu.CompilerParams(
            collective_id=number, has_side_effects=True, vmem_limit_bytes=58 * 2**20
        ),
        cost_estimate=pl.CostEstimate(flops=10**10, bytes_accessed=3 * 10**8, transcendentals=0),
    )(block_all.reshape(1, seq), block_all.reshape(seq, 1), d_mix, spread, mixed, lse, cosines, sines, carry)


def norm_parts(values):
    mean = jnp.mean(values, axis=-1, keepdims=True)
    spread = jnp.mean(values * values, axis=-1, keepdims=True) - mean * mean
    return mean, lax.rsqrt(spread + epsilon)


def after_attention(total, c, ins, outs):
    stream, gain, shift = ins
    (after_ref,) = outs
    after = stream[c].astype(jnp.float32) + total
    after_ref[c] = after
    values = after.astype(jnp.bfloat16).astype(jnp.float32)
    mean, inverse = norm_parts(values)
    return ((values - mean) * inverse * gain[...] + shift[...]).astype(jnp.bfloat16)


def after_hidden(total, c, ins, outs):
    (after,) = ins
    return (after[c] + total).astype(jnp.bfloat16)


def behind_norm(total, c, ins, outs):
    grad, values_ref, gain = ins
    grad_ref, sums = outs
    values = values_ref[c].astype(jnp.bfloat16).astype(jnp.float32)
    mean, inverse = norm_parts(values)
    centred = (values - mean) * inverse
    scaled = total * gain[...]
    back = inverse * (
        scaled
        - jnp.mean(scaled, axis=-1, keepdims=True)
        - centred * jnp.mean(scaled * centred, axis=-1, keepdims=True)
    )
    given = grad[c] + back
    grad_ref[c] = given
    here = [jnp.sum(total * centred, axis=0, keepdims=True), jnp.sum(total, axis=0, keepdims=True)]

    @pl.when(c == 0)
    def _():
        sums[...] = jnp.zeros_like(sums)

    sums[...] += jnp.concatenate(here, axis=0)
    return given.astype(jnp.bfloat16)


def relay_kernel(middle, n_ins, n_outs, layers, n_after, polish, n, chunks, lag, spread, partial, *refs):
    ins, carry, refs = refs[:n_ins], refs[n_ins : n_ins + len(layers)], refs[n_ins + len(layers) + n_after :]
    whole, outs, refs = refs[0], refs[1 : 1 + n_outs], refs[1 + n_outs :]
    carried, refs = refs[: len(layers)], refs[len(layers) :]
    if polish:
        ins, (gain, shift) = ins[:-2], ins[-2:]
        outs, polished = outs[:-1], outs[-1]
    if spread:
        outs, all_sums = outs[:-1], outs[-1]
    arrived, outgoing, total, sum_sent, sum_got, block_sent, block_got, carry_sent, carry_got, last_sent, last_got = refs
    section, i = lax.axis_index("section"), lax.axis_index("col")
    width = whole.shape[-1]
    first, last = i == 0, i == n - 1

    barrier = pltpu.get_barrier_semaphore()

    def greet(**place):
        pl.semaphore_signal(barrier, 1, device_id=place, device_id_type=pl.DeviceIdType.MESH)

    if spread:
        for d in range(1, 2 * n):
            greet(section=lax.rem(section + d // n, 2), col=lax.rem(i + d, n))
        pl.semaphore_wait(barrier, 2 * n - 1)
    else:
        greet(section=1 - section)

        @pl.when(i > 0)
        def _():
            greet(col=i - 1)

        @pl.when(i < n - 1)
        def _():
            greet(col=i + 1)

        @pl.when(first | last)
        def _():
            pl.semaphore_wait(barrier, 2)

        @pl.when((i > 0) & (i < n - 1))
        def _():
            pl.semaphore_wait(barrier, 3)

    def carry_copy(k):
        return remote(carry[k], carried[k], carry_sent.at[k], carry_got.at[k], "section", layers[k])

    for k, layer in enumerate(layers):
        @pl.when(section != layer)
        def _(k=k):
            carry_copy(k).start()

    def remote_col(source, target, sent, got, device):
        return remote(source, target, sent, got, "col", device)

    def sum_copy(c, j, right):
        slot = j + 1 if right else j
        return remote_col(
            outgoing.at[c, j], arrived.at[c, slot], sum_sent.at[c, j], sum_got.at[c, slot], i + 1 if right else i - 1
        )

    def block_copy(c, o, right, own=False):
        sent = n if own and not right else o
        return remote_col(whole.at[c, o], whole.at[c, o], block_sent.at[c, sent], block_got.at[0, c, o], i + 1 if right else i - 1)

    def slice_copy(c, d):
        to = lax.rem(i + d, n)
        return pltpu.make_async_remote_copy(
            src_ref=outgoing.at[c, i, :, pl.ds(pl.multiple_of(to * width, 128), width)],
            dst_ref=whole.at[section, c, i],
            send_sem=block_sent.at[c, d],
            recv_sem=block_got.at[section, c, i],
            device_id={"section": 0, "col": to},
            device_id_type=pl.DeviceIdType.MESH,
        )

    def arrive(c, slot):
        remote_col(outgoing.at[c, 0], arrived.at[c, slot], sum_sent.at[c, 0], sum_got.at[c, slot], i).wait_recv()

    def work(c, o):
        if polish:
            values = whole[c, o].astype(jnp.float32)
            mean, inverse = norm_parts(values)
            polished[c, o] = ((values - mean) * inverse * gain[...] + shift[...]).astype(jnp.bfloat16)

    def sums_copy(d):
        to = lax.rem(i + d, n)
        return pltpu.make_async_remote_copy(
            src_ref=outs[-1].at[:, pl.ds(pl.multiple_of(to * width, 128), width)],
            dst_ref=all_sums.at[section, i],
            send_sem=last_sent.at[d],
            recv_sem=last_got.at[section, i],
            device_id={"section": 0, "col": to},
            device_id_type=pl.DeviceIdType.MESH,
        )

    def sums_arrive(s, o):
        return pltpu.make_async_remote_copy(
            src_ref=outs[-1].at[:, pl.ds(0, width)],
            dst_ref=all_sums.at[s, o],
            send_sem=last_sent.at[0],
            recv_sem=last_got.at[s, o],
            device_id={"section": 0, "col": o},
            device_id_type=pl.DeviceIdType.MESH,
        )

    def middle_slot(k):
        return jnp.maximum(lag * k + n - 1 - k, lag * (n - 1 - k) + k)

    def at(now, slot, allowed):
        since = now - slot
        c = jnp.maximum(since, 0) // n
        return c, allowed & (since >= 0) & (lax.rem(jnp.maximum(since, 0), n) == 0) & (since < n * chunks)

    def step(now, carry):
        for j in range(n - 1, 0, -1):
            c, due = at(now, lag * i + n - 1 - j, i < j)

            @pl.when(due & first)
            def _(c=c, j=j):
                outgoing[c, j] = partial[c, j]

            @pl.when(due & (i > 0))
            def _(c=c, j=j):
                arrive(c, j + 1)
                both = arrived[c, j + 1].astype(jnp.float32) + partial[c, j].astype(jnp.float32)
                outgoing[c, j] = both.astype(jnp.bfloat16)

            @pl.when(due)
            def _(c=c, j=j):
                sum_copy(c, j, True).start()

        for j in range(n - 1):
            c, due = at(now, lag * (n - 1 - i) + j, i > j)

            @pl.when(due & last)
            def _(c=c, j=j):
                outgoing[c, j] = partial[c, j]

            @pl.when(due & (i < n - 1))
            def _(c=c, j=j):
                arrive(c, j)
                both = arrived[c, j].astype(jnp.float32) + partial[c, j].astype(jnp.float32)
                outgoing[c, j] = both.astype(jnp.bfloat16)

            @pl.when(due)
            def _(c=c, j=j):
                sum_copy(c, j, False).start()

        c, due = at(now, middle_slot(i), i >= 0)

        @pl.when(due)
        def _():
            total[...] = partial[c, i].astype(jnp.float32)

        @pl.when(due & (i > 0))
        def _():
            arrive(c, i + 1)
            total[...] += arrived[c, i + 1].astype(jnp.float32)

        @pl.when(due & (i < n - 1))
        def _():
            arrive(c, i)
            total[...] += arrived[c, i].astype(jnp.float32)

        @pl.when(due)
        def _():
            block = middle(total[...], c, ins, outs)
            if spread:
                outgoing[c, i] = block
                for d in range(1, n):
                    slice_copy(c, d).start()

                @pl.when(section == 0)
                def _():
                    whole[0, c, i] = outgoing[c, i, :, pl.ds(pl.multiple_of(i * width, 128), width)]

                @pl.when(section != 0)
                def _():
                    slice_copy(c, 0).start()

            else:
                whole[c, i] = block
                work(c, i)

        if spread:
            return carry

        @pl.when(due & (i < n - 1))
        def _():
            block_copy(c, i, True, own=True).start()

        @pl.when(due & (i > 0))
        def _():
            block_copy(c, i, False, own=True).start()

        for o in range(n - 1):
            c, due = at(now, middle_slot(o) + lag * (i - o), i > o)

            @pl.when(due)
            def _(c=c, o=o):
                block_copy(c, o, True).wait_recv()

            @pl.when(due & (i < n - 1))
            def _(c=c, o=o):
                block_copy(c, o, True).start()

            @pl.when(due)
            def _(c=c, o=o):
                work(c, o)

        for o in range(1, n):
            c, due = at(now, middle_slot(o) + lag * (o - i), i < o)

            @pl.when(due)
            def _(c=c, o=o):
                block_copy(c, o, False).wait_recv()

            @pl.when(due & (i > 0))
            def _(c=c, o=o):
                block_copy(c, o, False).start()

            @pl.when(due)
            def _(c=c, o=o):
                work(c, o)

        return carry

    lax.fori_loop(0, n * (chunks - 1) + 2 * lag * (n - 1) + 1, step, 0)

    if spread:
        for d in range(1, n):
            sums_copy(d).start()

        @pl.when(section == 0)
        def _():
            all_sums[0, i] = outs[-1][:, pl.ds(pl.multiple_of(i * width, 128), width)]

        @pl.when(section != 0)
        def _():
            sums_copy(0).start()

    def slice_arrives(c, s, o):
        return pltpu.make_async_remote_copy(
            src_ref=outgoing.at[c, 0, :, pl.ds(0, width)],
            dst_ref=whole.at[s, c, o],
            send_sem=block_sent.at[c, 0],
            recv_sem=block_got.at[s, c, o],
            device_id={"section": 0, "col": o},
            device_id_type=pl.DeviceIdType.MESH,
        )

    def settle(c, carry):
        for j in range(n):
            @pl.when(j != i)
            def _(j=j):
                sum_copy(c, j, True).wait_send()

        if spread:
            for d in range(1, n):
                slice_copy(c, d).wait_send()

            @pl.when(section != 0)
            def _():
                slice_copy(c, 0).wait_send()

            for s in range(2):
                for o in range(n):
                    @pl.when((section == 0) & ((s == 1) | (o != i)))
                    def _(s=s, o=o):
                        slice_arrives(c, s, o).wait_recv()

            return carry
        for o in range(n):
            @pl.when((o <= i) & (i < n - 1))
            def _(o=o):
                block_copy(c, o, True).wait_send()

            @pl.when((o > i) & (i > 0))
            def _(o=o):
                block_copy(c, o, True).wait_send()

        @pl.when(i > 0)
        def _():
            block_copy(c, i, False, own=True).wait_send()

        return carry

    lax.fori_loop(0, chunks, settle, 0)
    if spread:
        for d in range(1, n):
            sums_copy(d).wait_send()

        @pl.when(section != 0)
        def _():
            sums_copy(0).wait_send()

        for s in range(2):
            for o in range(n):
                @pl.when((section == 0) & ((s == 1) | (o != i)))
                def _(s=s, o=o):
                    sums_arrive(s, o).wait_recv()

    for k, layer in enumerate(layers):
        @pl.when(section != layer)
        def _(k=k):
            carry_copy(k).wait_send()

        @pl.when(section == layer)
        def _(k=k):
            carry_copy(k).wait_recv()


def relay(middle, number, partial, ins, outs, n, spread=False, carry=(), behind=(), polish=(), lag=3, rows=RELAY_ROWS):
    tokens, features = partial.shape
    owned = tokens // n
    chunks = owned // rows
    blocks = lambda values: values.reshape(chunks, rows, features) if values.shape[0] == owned else values
    ins = [blocks(values) for values in ins] + list(polish)
    outs = list(outs) + ([(tokens, features)] if polish else []) + ([(2, n, 2, features // n)] if spread else [])
    out_shapes = [
        jax.ShapeDtypeStruct(
            (2, chunks, n, rows, features // n) if spread else (chunks, n, rows, features), jnp.bfloat16
        )
    ] + [
        jax.ShapeDtypeStruct((chunks, n, rows, features), jnp.bfloat16)
        if shape[0] == tokens
        else jax.ShapeDtypeStruct((chunks, rows, features) if shape[0] == owned else shape, jnp.float32)
        for shape in outs
    ]
    vmem, anywhere = pl.BlockSpec(memory_space=pltpu.VMEM), pl.BlockSpec(memory_space=pl.ANY)
    layers = tuple(layer for layer, _ in carry)
    carry = [values for _, values in carry]
    whole, *rest = pl.pallas_call(
        functools.partial(relay_kernel, middle, len(ins), len(outs), layers, len(behind), bool(polish), n, chunks, lag, spread),
        in_specs=[vmem] * (1 + len(ins)) + [anywhere] * (len(carry) + len(behind)),
        out_specs=[vmem] * len(out_shapes) + [anywhere] * len(carry),
        out_shape=out_shapes + [jax.ShapeDtypeStruct(values.shape, values.dtype) for values in carry],
        scratch_shapes=[
            pltpu.VMEM((chunks, n + 1, rows, features), jnp.bfloat16),
            pltpu.VMEM((chunks, n, rows, features), jnp.bfloat16),
            pltpu.VMEM((rows, features), jnp.float32),
            pltpu.SemaphoreType.DMA((chunks, n)),
            pltpu.SemaphoreType.DMA((chunks, n + 1)),
            pltpu.SemaphoreType.DMA((chunks, n + 1)),
            pltpu.SemaphoreType.DMA((2 if spread else 1, chunks, n)),
            pltpu.SemaphoreType.DMA((max(1, len(carry)),)),
            pltpu.SemaphoreType.DMA((max(1, len(carry)),)),
            pltpu.SemaphoreType.DMA((n,)),
            pltpu.SemaphoreType.DMA((2, n)),
        ],
        compiler_params=pltpu.CompilerParams(
            collective_id=number, has_side_effects=True, vmem_limit_bytes=56 * 2**20
        ),
        cost_estimate=pl.CostEstimate(flops=0, bytes_accessed=35 * 10**7, transcendentals=0),
    )(partial.reshape(chunks, n, rows, features), *ins, *carry, *behind)
    shapes = {(chunks, rows, features): (owned, features), (chunks, n, rows, features): (tokens, features)}
    rest = [values.reshape(shapes.get(values.shape, values.shape)) for values in rest]
    return [whole.reshape((2, tokens, -1) if spread else (tokens, -1))] + rest


def gather_kernel(n, chunks, lag, own, small, angles, whole, smalls, normed, cosines, sines, sent, got, small_sent, small_got):
    section, i = lax.axis_index("section"), lax.axis_index("col")
    rows, width = own.shape[0] // chunks, own.shape[1]
    others = [(s, d) for s in range(2) for d in range(n) if (s, d) != (0, 0)]
    place = lambda s, d: {"section": lax.rem(section + s, 2), "col": lax.rem(i + d, n)}
    barrier = pltpu.get_barrier_semaphore()
    for s, d in others:
        pl.semaphore_signal(barrier, 1, device_id=place(s, d), device_id_type=pl.DeviceIdType.MESH)
    pl.semaphore_wait(barrier, len(others))

    def small_copy(s, d):
        return pltpu.make_async_remote_copy(
            src_ref=small,
            dst_ref=smalls.at[section, i],
            send_sem=small_sent.at[s, d],
            recv_sem=small_got.at[section, i],
            device_id=place(s, d),
            device_id_type=pl.DeviceIdType.MESH,
        )

    for s, d in others:
        small_copy(s, d).start()
    smalls[section, i] = small[...]

    def small_arrives(s, d):
        from_s, from_d = lax.rem(section + s, 2), lax.rem(i + d, n)
        return pltpu.make_async_remote_copy(
            src_ref=small,
            dst_ref=smalls.at[from_s, from_d],
            send_sem=small_sent.at[s, d],
            recv_sem=small_got.at[from_s, from_d],
            device_id=place(s, d),
            device_id_type=pl.DeviceIdType.MESH,
        )

    def norm(c):
        here = pl.ds(pl.multiple_of(c * rows, rows), rows)
        values = whole[here, :].astype(jnp.float32)
        mean, inverse = norm_parts(values)
        for o in range(n):
            part = slice(o * width, (o + 1) * width)
            gain, shift = smalls[0, o, 0:1, :], smalls[0, o, 2:3, :]
            normed[here, part] = ((values[:, part] - mean) * inverse * gain + shift).astype(jnp.bfloat16)

    def block(c, o, right, mine=False):
        part = whole.at[pl.ds(pl.multiple_of(c * rows, rows), rows), columns(o, width)]
        return remote(
            part, part, sent.at[c, n if mine and not right else o], got.at[c, o], "col", i + 1 if right else i - 1
        )

    def at(now, slot, allowed):
        since = jnp.maximum(now - slot, 0)
        return since // (n - 1), allowed & (now >= slot) & (lax.rem(since, n - 1) == 0) & (since < (n - 1) * chunks)

    def step(now, carry):
        c, due = at(now, 0, i >= 0)

        @pl.when(due)
        def _():
            here = pl.ds(pl.multiple_of(c * rows, rows), rows)
            whole[here, columns(i, width)] = own[here, :]

        @pl.when(due & (i < n - 1))
        def _():
            block(c, i, True, True).start()

        @pl.when(due & (i > 0))
        def _():
            block(c, i, False, True).start()

        for o in range(n):
            c, due = at(now, lag * jnp.abs(i - o), i != o)

            @pl.when(due)
            def _(c=c, o=o):
                block(c, o, True).wait_recv()

            @pl.when(due & (i > o) & (i < n - 1))
            def _(c=c, o=o):
                block(c, o, True).start()

            @pl.when(due & (i < o) & (i > 0))
            def _(c=c, o=o):
                block(c, o, False).start()

        c, due = at(now, lag * (n - 1), i >= 0)

        @pl.when(due)
        def _():
            norm(c)

        return carry

    turns = angles.shape[0] // 2
    lane = lax.broadcasted_iota(jnp.int32, (turns, LANES), 1)
    place_of = lax.broadcasted_iota(jnp.int32, (turns, LANES), 0)
    turned = lane % HEAD_DIM < 2 * turns
    picked = jnp.where(turned & (lane % turns == place_of), 1.0, 0.0)
    sign = jnp.where(lane % HEAD_DIM < turns, -1.0, 1.0)

    def spread_out(table, pick):
        return lax.dot_general(
            table, pick, (((0,), (0,)), ((), ())), precision=lax.Precision.HIGHEST, preferred_element_type=jnp.float32
        )

    still = jnp.where(turned[:1], 0.0, 1.0)
    cosines[...] = spread_out(angles[:turns, :], picked) + still
    sines[...] = spread_out(angles[turns:, :], picked * sign)
    for s, d in others:
        small_arrives(s, d).wait_recv()

    lax.fori_loop(0, (n - 1) * (chunks - 1) + lag * (n - 1) + 1, step, 0)

    def settle(c, carry):
        for o in range(n):
            @pl.when(((o <= i) & (i < n - 1)) | ((o > i) & (i > 0)))
            def _(o=o):
                block(c, o, True).wait_send()

        @pl.when(i > 0)
        def _():
            block(c, i, False, True).wait_send()

        return carry

    lax.fori_loop(0, chunks, settle, 0)
    for s, d in others:
        small_copy(s, d).wait_send()


def gathered(number, own, small, angles, n, lag=3, rows=64):
    tokens, width = own.shape
    chunks = tokens // rows
    vmem = pl.BlockSpec(memory_space=pltpu.VMEM)
    return pl.pallas_call(
        functools.partial(gather_kernel, n, chunks, lag),
        in_specs=[vmem] * 3,
        out_specs=[vmem] * 5,
        out_shape=[
            jax.ShapeDtypeStruct((tokens, n * width), own.dtype),
            jax.ShapeDtypeStruct((2, n) + small.shape, small.dtype),
            jax.ShapeDtypeStruct((tokens, n * width), own.dtype),
            jax.ShapeDtypeStruct((angles.shape[1], LANES), jnp.float32),
            jax.ShapeDtypeStruct((angles.shape[1], LANES), jnp.float32),
        ],
        scratch_shapes=[
            pltpu.SemaphoreType.DMA((chunks, n + 1)),
            pltpu.SemaphoreType.DMA((chunks, n)),
            pltpu.SemaphoreType.DMA((2, n)),
            pltpu.SemaphoreType.DMA((2, n)),
        ],
        compiler_params=pltpu.CompilerParams(
            collective_id=number, has_side_effects=True, vmem_limit_bytes=40 * 2**20
        ),
        cost_estimate=pl.CostEstimate(flops=0, bytes_accessed=25 * 10**7, transcendentals=0),
    )(own, small, angles)


def rotary_angles(positions):
    half_dims = ROT // 2
    inverse_freq = 1.0 / 10000.0 ** (jnp.arange(half_dims, dtype=jnp.float32) * 2.0 / ROT)
    angles = positions.astype(jnp.float32)[None, :] * inverse_freq[:, None]
    return jnp.concatenate([jnp.cos(angles), jnp.sin(angles)])


def product(left, right):
    return jnp.dot(left, right, preferred_element_type=jnp.float32)


def per_device(
    inputs,
    cotangent,
    block_ids,
    norm_gains,
    norm_shifts,
    qkv_weight,
    qkv_bias,
    out_weight,
    gate_up_weight,
    down_weight,
):
    section = lax.axis_index("section")
    row = lax.axis_index("row")
    col = lax.axis_index("col")
    rows_axis = lax.axis_size("row")
    cols_axis = lax.axis_size("col")
    tokens, width = inputs.shape[1:]
    owned = tokens // cols_axis
    units = down_weight.shape[2]
    seq = tokens * rows_axis
    both = ("section", "row")
    whole_lanes = width == rows_axis * LANES
    heads = LANES // HEAD_DIM if whole_lanes else 1
    copies = 1 if whole_lanes else rows_axis * HEAD_DIM // width

    def expand(values):
        if whole_lanes:
            return values
        values = values.reshape(tokens, -1, width // HEAD_DIM, HEAD_DIM)
        values = jnp.pad(jnp.repeat(values, copies, axis=2), ((0, 0), (0, 0), (0, 0), (0, LANES - HEAD_DIM)))
        return values.reshape(tokens, -1)

    def contract(values):
        if whole_lanes:
            return values
        values = values.reshape(tokens, -1, rows_axis, LANES)[:, :, ::copies, :HEAD_DIM]
        return values.reshape(tokens, -1)

    def weights_of(block):
        block = block[0].reshape(block.shape[1], -1)
        return lax.all_gather(block, both, axis=0, tiled=True).reshape(2, D, -1)

    def mine(values):
        blocks = values.reshape(owned // RELAY_ROWS, cols_axis, RELAY_ROWS, -1)
        return lax.dynamic_index_in_dim(blocks, col, 1, keepdims=False).reshape(owned, -1)

    def my_features(values):
        return lax.dynamic_slice_in_dim(values, col * width, width, 1)

    own_small = jnp.concatenate([norm_gains[0], norm_shifts[0], qkv_bias[0], jnp.zeros((1, width), jnp.float32)])
    angles = rotary_angles(jnp.arange(seq, dtype=jnp.int32))
    stream, small, normed, cosines, sines = gathered(
        7, lax.dynamic_index_in_dim(inputs, section, 0, keepdims=False), own_small, angles, cols_axis
    )
    whole_small = small.transpose(0, 2, 1, 3).reshape(2, own_small.shape[0], D)
    gains, shifts = whole_small[:, :2], whole_small[:, 2:4]
    bias = lax.dynamic_index_in_dim(small, col, 1, keepdims=False)[:, 4:7].reshape(2, -1)

    qkv_w = weights_of(qkv_weight)
    out_w = weights_of(out_weight)
    gate_up_w = weights_of(gate_up_weight)
    down_w = weights_of(down_weight)

    ids = lax.dynamic_index_in_dim(block_ids, section, 0, keepdims=False)
    kept = []
    hidden_out = []
    waited = []
    for layer in range(2):
        qkv = product(normed, qkv_w[layer]) + bias[layer]
        if layer == 1:
            here = section + jnp.where(hidden_out[0][0, 0] == hidden_out[0][0, 0], 0, 1)
            branch = lax.all_gather(
                lax.dynamic_index_in_dim(cotangent, here, 0, keepdims=False), "col", axis=1, tiled=True
            )
            waited = [branch]
        spread, mixed, log_sums, attn_mix = attend(8, expand(qkv), ids, cosines, sines, heads, rows_axis)
        attn_mix = contract(attn_mix)
        normed_two, after = relay(
            after_attention,
            layer,
            product(attn_mix, out_w[layer].T).astype(jnp.bfloat16),
            [mine(stream), gains[layer, 1:], shifts[layer, 1:]],
            [(owned, D)],
            cols_axis,
            behind=waited,
        )
        gate_up = product(normed_two, gate_up_w[layer])
        gate, up = gate_up[:, :units], gate_up[:, units:]
        hidden = (jax.nn.silu(gate) * up).astype(jnp.bfloat16)
        kept.append((stream, normed, spread, mixed, log_sums, attn_mix, after, normed_two, gate_up, hidden))
        partial = product(hidden, down_w[layer].T)
        if layer == 0:
            stream, normed = relay(
                after_hidden,
                2,
                partial.astype(jnp.bfloat16),
                [after],
                [],
                cols_axis,
                polish=(gains[1, :1], shifts[1, :1]),
            )
            hidden_out.append(my_features(stream))
        else:
            blocks = partial.reshape(owned // RELAY_ROWS, cols_axis, RELAY_ROWS, D)
            owner = lax.broadcasted_iota(jnp.int32, blocks.shape, 1) == col
            blocks = blocks + jnp.where(owner, after.reshape(-1, 1, RELAY_ROWS, D), 0.0)
            result = blocks.reshape(tokens, D).astype(jnp.bfloat16)

    grad = mine(branch).astype(jnp.float32)
    weight_sums = [[], []]
    small_sums = []
    bias_grads = [None, None]
    input_out = [None, None]
    input_got = [None, None]
    hidden_got = [None, None]

    def collect(layer, term):
        weight_sums[layer].append(lax.psum_scatter(term, "row", scatter_dimension=0, tiled=True))
        return weight_sums[layer][-1]

    arrived = [[None] * 4, [None] * 4]
    def together(*values):
        return lax.optimization_barrier(values)

    for layer in (1, 0):
        stream, normed, spread, mixed, log_sums, attn_mix, after, normed_two, gate_up, hidden = kept[layer]
        gate, up = gate_up[:, :units], gate_up[:, units:]
        d_hidden = product(branch, down_w[layer])
        sig = jax.nn.sigmoid(gate)
        d_gate = d_hidden * up * sig * (1.0 + gate * (1.0 - sig))
        d_up = d_hidden * gate * sig
        d_gate_up = jnp.concatenate([d_gate, d_up], axis=1).astype(jnp.bfloat16)
        partial, down_term, gate_up_term = together(
            dot_last(d_gate_up, gate_up_w[layer]).astype(jnp.bfloat16),
            dot_first(branch, hidden).astype(jnp.bfloat16),
            dot_first(normed_two, d_gate_up).astype(jnp.bfloat16),
        )
        down_sum, gate_up_sum = collect(layer, down_term), collect(layer, gate_up_term)
        grad_attn, d_after, sums_two, *got = relay(
            behind_norm,
            3 + layer,
            partial,
            [grad, after, gains[layer, 1:]],
            [(owned, D), (2, D)],
            cols_axis,
            carry=[]
            if layer == 1
            else [(0, hidden_out[0]), (1, hidden_out[1]), (1, input_out[1]), (1, weight_sums[1][2]), (1, weight_sums[1][3])],
            behind=[] if layer == 1 else [weight_sums[1][0]],
        )
        if layer == 1:
            result = jnp.where(d_after[0, 0] == d_after[0, 0], result, 0)
            hidden_out.append(lax.psum_scatter(result, "col", scatter_dimension=1, tiled=True))
        else:
            hidden_got[0], hidden_got[1], input_got[1], arrived[1][2], arrived[1][3] = got
        small_sums += [sums_two]
        d_mix, out_term = together(
            product(grad_attn, out_w[layer]).astype(jnp.bfloat16), dot_first(grad_attn, attn_mix).astype(jnp.bfloat16)
        )
        out_sum = collect(layer, out_term)
        d_qkv, arrived[layer][1] = attend_back(
            9 + layer,
            expand(d_mix),
            spread,
            mixed,
            log_sums,
            ids,
            cosines,
            sines,
            heads,
            rows_axis,
            layer,
            gate_up_sum,
        )
        d_qkv = contract(d_qkv)
        partial, qkv_term, bias_grads[layer] = together(
            dot_last(d_qkv, qkv_w[layer]).astype(jnp.bfloat16),
            dot_first(normed, d_qkv).astype(jnp.bfloat16),
            jnp.sum(d_qkv.astype(jnp.float32), axis=0),
        )
        qkv_sum = collect(layer, qkv_term)
        if layer == 0:
            early_sums = lax.psum_scatter(jnp.stack(small_sums), "col", scatter_dimension=2, tiled=True)
            early = jnp.concatenate([early_sums.reshape(6, -1), bias_grads[1].reshape(3, -1), bias_grads[0].reshape(3, -1)])
            early = jnp.sum(lax.all_gather(early, both, axis=0), axis=0)
        branch, grad, sums_one, *got = relay(
            behind_norm,
            5 + layer,
            partial,
            [d_after, mine(stream), gains[layer, :1]],
            [(owned, D), (2, D)],
            cols_axis,
            spread=layer == 0,
            carry=[] if layer == 1 else [(0, down_sum), (0, out_sum), (1, weight_sums[1][0])],
            behind=[hidden_out[1]] if layer == 1 else [early_sums],
        )
        if layer == 0:
            late_sums, arrived[0][0], arrived[0][2], arrived[1][0] = got
        small_sums += [sums_one]
        input_out[layer] = my_features(branch) if layer == 1 else branch

    arrived[0][3] = lax.ppermute(weight_sums[0][3], "section", [(1, 0)])
    hidden_states = jnp.where(
        section == 0, jnp.stack([hidden_out[0], hidden_got[0]]), jnp.stack([hidden_got[1], hidden_out[1]])
    )
    input_grads = jnp.where(section == 0, input_out[0], jnp.stack([input_got[1], input_out[1]])).astype(jnp.float32)
    down_grad, gate_up_grad, out_grad, qkv_grad = (
        jnp.where(section == 0, first, second).astype(jnp.float32)
        + jnp.where(section == 0, first_got, second_got).astype(jnp.float32)
        for first, second, first_got, second_got in zip(*weight_sums, *arrived)
    )
    last = lax.psum(jnp.sum(late_sums, axis=(0, 1)), "row")
    norm_sums = jnp.where(section == 0, jnp.stack([last, early[4:6]]), jnp.stack([early[2:4], early[0:2]]))
    bias_sum = jnp.where(section == 0, early[9:12], early[6:9])
    return (
        hidden_states[None],
        input_grads[None],
        norm_sums[:, 0][None],
        norm_sums[:, 1][None],
        qkv_grad.reshape(qkv_weight.shape),
        bias_sum.reshape(qkv_bias.shape),
        out_grad[None],
        gate_up_grad.reshape(gate_up_weight.shape),
        down_grad[None],
    )


def solution(mesh):
    in_specs = (
        P(None, "row", "col"),
        P(None, "row", "col"),
        P(),
        P("section", None, "col"),
        P("section", None, "col"),
        P("section", "row", None, "col"),
        P("section", None, "col"),
        P("section", "row", "col"),
        P("section", "row", None, "col"),
        P("section", "row", "col"),
    )
    out_specs = (
        P("section", None, "row", "col"),
        P("section", None, "row", "col"),
        P("section", None, "col"),
        P("section", None, "col"),
        P("section", "row", None, "col"),
        P("section", None, "col"),
        P("section", "row", "col"),
        P("section", "row", None, "col"),
        P("section", "row", "col"),
    )
    return jax.shard_map(
        per_device, mesh=mesh, in_specs=in_specs, out_specs=out_specs, check_vma=False
    )
```

```python
import functools

import jax
import jax.numpy as jnp
from jax import lax
from jax.experimental import pallas as pl
from jax.experimental.pallas import tpu as pltpu
from jax.sharding import PartitionSpec as P

D = 2048
HEADS = 32
HEAD_DIM = 64
ROT = 16
LANES = 128
REACH = 256
RELAY_ROWS = 16


epsilon = 1e-05


def dot_last(a, b):
    return lax.dot_general(a, b, (((1,), (1,)), ((), ())), preferred_element_type=jnp.float32)


def dot_first(a, b):
    return lax.dot_general(a, b, (((0,), (0,)), ((), ())), preferred_element_type=jnp.float32)


def lanes_of(rows, head):
    lane = lax.broadcasted_iota(jnp.int32, (rows, LANES), 1)
    return lane // HEAD_DIM == head


def spin(x, cosines, sines):
    lane = lax.broadcasted_iota(jnp.int32, x.shape, 1)
    ahead, behind = pltpu.roll(x, LANES - ROT // 2, 1), pltpu.roll(x, ROT // 2, 1)
    return x * cosines + jnp.where(lane % ROT < ROT // 2, ahead, behind) * sines


def meet(axis, n):
    me = lax.axis_index(axis)
    barrier = pltpu.get_barrier_semaphore()
    for d in range(1, n):
        pl.semaphore_signal(
            barrier, 1, device_id={axis: lax.rem(me + d, n)}, device_id_type=pl.DeviceIdType.MESH
        )
    pl.semaphore_wait(barrier, n - 1)


def remote(source, target, sent, got, axis, device):
    return pltpu.make_async_remote_copy(
        src_ref=source,
        dst_ref=target,
        send_sem=sent,
        recv_sem=got,
        device_id={axis: device},
        device_id_type=pl.DeviceIdType.MESH,
    )


def columns(which, size=LANES):
    return pl.ds(pl.multiple_of(which * size, size), size)


def attend_kernel(heads, n, bq, bk, given, bid_q, bid_k, *refs):
    me = lax.axis_index("row")
    if given:
        spread, mixed, lse_ref, mix, vone, scores, mix_sent, mix_got = refs
    else:
        qkv, cosines, sines, spread, mixed, lse_ref, mix, vone, scores, mix_sent, mix_got = refs[:11]
        leaving, qkv_sent, qkv_got = refs[11:]
    tokens = mix.shape[0]
    seq = n * tokens
    here = pl.ds(pl.multiple_of(me * tokens, tokens), tokens)
    low = jnp.bfloat16
    meet("row", n)

    def parts(t):
        cos, sin = cosines[here, :], sines[here, :]
        query = spin(qkv[:, columns(t)], cos, sin).astype(low) * jnp.asarray(HEAD_DIM**-0.5, low)
        key = spin(qkv[:, columns(n + t)], cos, sin).astype(low)
        return query.astype(low), key, qkv[:, columns(2 * n + t)].astype(low)

    def leave(d):
        to = lax.rem(me + d, n)
        return remote(leaving.at[d - 1], spread.at[:, here], qkv_sent.at[d - 1], qkv_got.at[me], "row", to)

    if not given:
        for d in range(1, n):
            for k, part in enumerate(parts(lax.rem(me + d, n))):
                leaving[d - 1, k] = part
            leave(d).start()
        for k, part in enumerate(parts(me)):
            spread[k, here, :] = part

    def come(row):
        if not given:
            @pl.when(row != me)
            def _():
                there = pl.ds(row * tokens, tokens)
                remote(leaving.at[0], spread.at[:, there], qkv_sent.at[0], qkv_got.at[row], "row", me).wait_recv()

        there = pl.ds(row * tokens, tokens)
        for h in range(heads):
            vone[h, there, :] = jnp.where(lanes_of(tokens, h), spread[2, there, :], jnp.ones((), low))

    def mix_copy(i, device):
        rows = pl.ds(lax.rem(i, tokens // bq) * bq, bq)
        return remote(
            mixed.at[pl.ds(i * bq, bq)], mix.at[rows, columns(me)], mix_sent.at[i], mix_got.at[me, lax.rem(i, tokens // bq)], "row", device
        )

    def block(i, carry):
        rows = pl.ds(pl.multiple_of(i * bq, bq), bq)
        q = spread[0, rows, :]
        bid = bid_q[rows, :]
        free = i * (bq // bk)
        last = jnp.minimum(((i + 1) * bq + REACH + bk - 1) // bk, seq // bk)
        qs = [jnp.where(lanes_of(bq, h), q, jnp.zeros((), low)) for h in range(heads)]

        def score(t, tops, hide):
            span = pl.ds(pl.multiple_of(t * bk, bk), bk)
            keys = spread[1, span, :]
            if hide:
                visible = bid_k[:, span] <= bid
            found = []
            for h in range(heads):
                s = dot_last(qs[h], keys)
                if hide:
                    s = jnp.where(visible, s, -1e30)
                scores[h, :, span] = s
                top = tops[h]
                for c in range(bk // LANES):
                    top = jnp.maximum(top, s[:, c * LANES : (c + 1) * LANES])
                found.append(top)
            return tuple(found)

        tops = tuple(jnp.full((bq, LANES), -1e30, jnp.float32) for _ in range(heads))
        tops = lax.fori_loop(0, free, lambda t, c: score(t, c, False), tops)
        tops = lax.fori_loop(free, last, lambda t, c: score(t, c, True), tops)
        tops = [jnp.max(top, axis=1, keepdims=True) for top in tops]

        def gather(t, sums):
            span = pl.ds(pl.multiple_of(t * bk, bk), bk)
            found = []
            for h in range(heads):
                p = jnp.exp(scores[h, :, span] - tops[h]).astype(low)
                found.append(sums[h] + jnp.dot(p, vone[h, span, :], preferred_element_type=jnp.float32))
            return tuple(found)

        sums = tuple(jnp.zeros((bq, LANES), jnp.float32) for _ in range(heads))
        sums = lax.fori_loop(0, last, gather, sums)
        outcome = jnp.zeros((bq, LANES), jnp.float32)
        lse = jnp.zeros((bq, LANES), jnp.float32)
        for h in range(heads):
            totals = pltpu.roll(sums[h], HEAD_DIM, 1)
            outcome = jnp.where(lanes_of(bq, h), sums[h] / totals, outcome)
            lse = jnp.where(lanes_of(bq, h), tops[h] + jnp.log(totals), lse)
        mixed[rows, :] = outcome.astype(low)
        lse_ref[:, rows] = lse.T
        return carry

    per_row = tokens // bq
    for row in range(n):
        if row == 0:
            come(0)
        if row + 1 < n:
            come(row + 1)

        def run(half, carry, row=row):
            i = row * per_row + half
            block(i, 0)

            @pl.when(row == me)
            def _():
                mix[pl.ds(pl.multiple_of(half * bq, bq), bq), columns(me)] = mixed[pl.ds(pl.multiple_of(i * bq, bq), bq), :]

            @pl.when(row != me)
            def _():
                mix_copy(i, row).start()

            return carry

        lax.fori_loop(0, per_row, run, 0)

    if not given:
        for d in range(1, n):
            leave(d).wait_send()
    for i in range(n * per_row):
        @pl.when(i // per_row != me)
        def _(i=i):
            mix_copy(i, me).wait_send()

    for row in range(n):
        @pl.when(row != me)
        def _(row=row):
            for half in range(per_row):
                rows = pl.ds(half * bq, bq)
                remote(
                    mixed.at[pl.ds(0, bq)], mix.at[rows, columns(row)], mix_sent.at[0], mix_got.at[row, half], "row", me
                ).wait_recv()


def attend(number, block_all, heads, n, tokens, qkv=None, cosines=None, sines=None, spread=None, bq=512, bk=512):
    bq, bk = min(bq, tokens), min(bk, tokens)
    seq = n * tokens
    vmem = pl.BlockSpec(memory_space=pltpu.VMEM)
    low = jnp.bfloat16
    given = spread is not None
    operands = [spread] if given else [qkv, cosines, sines]
    out_shape = [
        jax.ShapeDtypeStruct((3, seq, LANES), low),
        jax.ShapeDtypeStruct((seq, LANES), low),
        jax.ShapeDtypeStruct((LANES, seq), jnp.float32),
        jax.ShapeDtypeStruct((tokens, n * LANES), low),
    ][given:]
    exchange = [
        pltpu.VMEM((n - 1, 3, tokens, LANES), low),
        pltpu.SemaphoreType.DMA((n - 1,)),
        pltpu.SemaphoreType.DMA((n,)),
    ]
    found = pl.pallas_call(
        functools.partial(attend_kernel, heads, n, bq, bk, given),
        in_specs=[vmem] * (2 + len(operands)),
        out_specs=[vmem] * len(out_shape),
        out_shape=out_shape,
        scratch_shapes=[
            pltpu.VMEM((heads, seq, LANES), low),
            pltpu.VMEM((heads, bq, seq), jnp.float32),
            pltpu.SemaphoreType.DMA((seq // bq,)),
            pltpu.SemaphoreType.DMA((n, tokens // bq)),
        ]
        + ([] if given else exchange),
        compiler_params=pltpu.CompilerParams(
            collective_id=number, has_side_effects=True, vmem_limit_bytes=58 * 2**20
        ),
        cost_estimate=pl.CostEstimate(flops=10**10, bytes_accessed=2 * 10**8, transcendentals=0),
    )(block_all.reshape(seq, 1), block_all.reshape(1, seq), *operands)
    return [spread] + list(found) if given else found


def attend_back_kernel(
    heads, n, bq, bk, layer, bid_q, bid_k, grads, spread, mixed, lse_ref, cosines, sines, carry, *refs
):
    d_qkv, carried, kone, dk_acc, dv_acc, leaving, back_sent, back_got, carry_sent, carry_got = refs
    section = lax.axis_index("section")
    me = lax.axis_index("row")
    seq = grads.shape[0]
    tokens = seq // n
    per_row = tokens // bq
    blocks = n * per_row
    low = jnp.bfloat16
    zero = jnp.zeros((), low)
    barrier = pltpu.get_barrier_semaphore()
    pl.semaphore_signal(barrier, 1, device_id={"section": 1 - section}, device_id_type=pl.DeviceIdType.MESH)
    for d in range(1, n):
        pl.semaphore_signal(barrier, 1, device_id={"row": lax.rem(me + d, n)}, device_id_type=pl.DeviceIdType.MESH)
    pl.semaphore_wait(barrier, n)
    carry_copy = remote(carry, carried, carry_sent, carry_got, "section", layer)

    @pl.when(section != layer)
    def _():
        carry_copy.start()

    for h in range(heads):
        kone[h] = jnp.where(lanes_of(seq, h), spread[1], zero)
    dk_acc[...] = jnp.zeros_like(dk_acc)
    dv_acc[...] = jnp.zeros_like(dv_acc)

    def tile(t, dq, hide, stuff):
        qs, gs, lses, deltas, bid = stuff
        span = pl.ds(pl.multiple_of(t * bk, bk), bk)
        keys, values = spread[1, span, :], spread[2, span, :]
        dv, dk = dv_acc[span, :], dk_acc[span, :]
        if hide:
            visible = bid_k[span, :] <= bid
        for h in range(heads):
            s = dot_last(keys, qs[h])
            if hide:
                s = jnp.where(visible, s, -1e30)
            p = jnp.exp(s - lses[h])
            dp = dot_last(values, gs[h])
            ds = (p * (dp - deltas[h])).astype(low)
            dv = dv + jnp.dot(p.astype(low), gs[h], preferred_element_type=jnp.float32)
            dk = dk + jnp.dot(ds, qs[h], preferred_element_type=jnp.float32)
            dq = dq + dot_first(ds, kone[h, span, :])
        dv_acc[span, :] = dv
        dk_acc[span, :] = dk
        return dq

    def block(i):
        rows = pl.ds(pl.multiple_of(i * bq, bq), bq)
        q, g = spread[0, rows, :], grads[rows, :]
        product = (g.astype(jnp.float32) * mixed[rows, :].astype(jnp.float32)).T
        span = lambda h: slice(h * HEAD_DIM, (h + 1) * HEAD_DIM)
        deltas = [jnp.sum(product[span(h)], axis=0, keepdims=True) for h in range(heads)]
        lses = [lse_ref[h * HEAD_DIM : h * HEAD_DIM + 1, rows] for h in range(heads)]
        qs = [jnp.where(lanes_of(bq, h), q, zero) for h in range(heads)]
        gs = [jnp.where(lanes_of(bq, h), g, zero) for h in range(heads)]
        stuff = (qs, gs, lses, deltas, bid_q[:, rows])
        free = i * (bq // bk)
        last = jnp.minimum(((i + 1) * bq + REACH + bk - 1) // bk, seq // bk)
        dq = jnp.zeros((bq, LANES), jnp.float32)
        dq = lax.fori_loop(0, free, lambda t, c: tile(t, c, False, stuff), dq)
        dq = lax.fori_loop(free, last, lambda t, c: tile(t, c, True, stuff), dq)
        return spin(dq * (HEAD_DIM**-0.5), cosines[rows, :], -sines[rows, :]).astype(low)

    def back_copy(k, i, device):
        half = lax.rem(i, per_row)
        rows = pl.ds(pl.multiple_of(half * bq, bq), bq)
        return remote(
            leaving.at[k, pl.ds(pl.multiple_of(i * bq, bq), bq)],
            d_qkv.at[rows, columns(k * n + me)],
            back_sent.at[k, i],
            back_got.at[k, me, half],
            "row",
            device,
        )

    def send(k, i, values):
        row = i // per_row
        half = lax.rem(i, per_row)

        @pl.when(row == me)
        def _():
            d_qkv[pl.ds(pl.multiple_of(half * bq, bq), bq), columns(k * n + me)] = values

        @pl.when(row != me)
        def _():
            leaving[k, pl.ds(pl.multiple_of(i * bq, bq), bq), :] = values
            back_copy(k, i, row).start()

    def keys_done(i):
        rows = pl.ds(pl.multiple_of(i * bq, bq), bq)
        send(1, i, spin(dk_acc[rows, :], cosines[rows, :], -sines[rows, :]).astype(low))
        send(2, i, dv_acc[rows, :].astype(low))

    for row in range(n - 1, -1, -1):
        def run(step, carry, row=row):
            i = row * per_row + per_row - 1 - step
            send(0, i, block(i))

            @pl.when(i + 1 < blocks)
            def _():
                keys_done(i + 1)

            return carry

        lax.fori_loop(0, per_row, run, 0)
    keys_done(0)

    def settle(i, carry):
        @pl.when(i // per_row != me)
        def _():
            half = lax.rem(i, per_row)
            rows = pl.ds(pl.multiple_of(half * bq, bq), bq)
            for k in range(3):
                back_copy(k, i, me).wait_send()
                remote(
                    leaving.at[k, pl.ds(0, bq)],
                    d_qkv.at[rows, columns(k * n + i // per_row)],
                    back_sent.at[k, 0],
                    back_got.at[k, i // per_row, half],
                    "row",
                    me,
                ).wait_recv()

        return carry

    lax.fori_loop(0, blocks, settle, 0)

    @pl.when(section != layer)
    def _():
        carry_copy.wait_send()

    @pl.when(section == layer)
    def _():
        carry_copy.wait_recv()


def attend_back(number, grads, spread, mixed, lse, block_all, cosines, sines, heads, n, layer, carry, bq=512, bk=512):
    seq = grads.shape[0]
    tokens = seq // n
    bq, bk = min(bq, tokens), min(bk, tokens)
    vmem = pl.BlockSpec(memory_space=pltpu.VMEM)
    low = jnp.bfloat16
    return pl.pallas_call(
        functools.partial(attend_back_kernel, heads, n, bq, bk, layer),
        in_specs=[vmem] * 8 + [pl.BlockSpec(memory_space=pl.ANY)],
        out_specs=[vmem, pl.BlockSpec(memory_space=pl.ANY)],
        out_shape=[jax.ShapeDtypeStruct((tokens, 3 * n * LANES), low), jax.ShapeDtypeStruct(carry.shape, carry.dtype)],
        scratch_shapes=[
            pltpu.VMEM((heads, seq, LANES), low),
            pltpu.VMEM((seq, LANES), jnp.float32),
            pltpu.VMEM((seq, LANES), jnp.float32),
            pltpu.VMEM((3, seq, LANES), low),
            pltpu.SemaphoreType.DMA((3, seq // bq)),
            pltpu.SemaphoreType.DMA((3, n, tokens // bq)),
            pltpu.SemaphoreType.DMA,
            pltpu.SemaphoreType.DMA,
        ],
        compiler_params=pltpu.CompilerParams(
            collective_id=number, has_side_effects=True, vmem_limit_bytes=58 * 2**20
        ),
        cost_estimate=pl.CostEstimate(flops=10**10, bytes_accessed=3 * 10**8, transcendentals=0),
    )(block_all.reshape(1, seq), block_all.reshape(seq, 1), grads, spread, mixed, lse, cosines, sines, carry)


def norm_parts(values):
    mean = jnp.mean(values, axis=-1, keepdims=True)
    spread = jnp.mean(values * values, axis=-1, keepdims=True) - mean * mean
    return mean, lax.rsqrt(spread + epsilon)


def after_attention(total, c, ins, outs):
    stream, gain, shift = ins
    (after_ref,) = outs
    after = stream[c].astype(jnp.float32) + total
    after_ref[c] = after
    values = after.astype(jnp.bfloat16).astype(jnp.float32)
    mean, inverse = norm_parts(values)
    return ((values - mean) * inverse * gain[...] + shift[...]).astype(jnp.bfloat16)


def after_hidden(total, c, ins, outs):
    (after,) = ins
    return (after[c] + total).astype(jnp.bfloat16)


def behind_norm(total, c, ins, outs):
    grad, values_ref, gain = ins
    grad_ref, sums = outs
    values = values_ref[c].astype(jnp.bfloat16).astype(jnp.float32)
    mean, inverse = norm_parts(values)
    centred = (values - mean) * inverse
    scaled = total * gain[...]
    back = inverse * (
        scaled
        - jnp.mean(scaled, axis=-1, keepdims=True)
        - centred * jnp.mean(scaled * centred, axis=-1, keepdims=True)
    )
    given = grad[c] + back
    grad_ref[c] = given
    here = [jnp.sum(total * centred, axis=0, keepdims=True), jnp.sum(total, axis=0, keepdims=True)]

    @pl.when(c == 0)
    def _():
        sums[...] = jnp.zeros_like(sums)

    sums[...] += jnp.concatenate(here, axis=0)
    return given.astype(jnp.bfloat16)


def relay_kernel(
    middle, n_ins, n_outs, layers, n_after, polish, parts, n_row, n, chunks, lag, spread, partial, *refs
):
    ins, carry, refs = refs[:n_ins], refs[n_ins : n_ins + len(layers)], refs[n_ins + len(layers) + n_after :]
    whole, outs, refs = refs[0], refs[1 : 1 + n_outs], refs[1 + n_outs :]
    carried, refs = refs[: len(layers)], refs[len(layers) :]
    if parts:
        ins, (weight, bias, cosines, sines) = ins[:-4], ins[-4:]
        outs, landed = outs[:-1], outs[-1]
        *refs, projected, leaving, part_sent, part_got = refs
    if polish:
        ins, (gain, shift) = ins[:-2], ins[-2:]
        outs, polished = outs[:-1], outs[-1]
    if spread:
        outs, all_sums = outs[:-1], outs[-1]
    arrived, outgoing, total, sum_sent, sum_got, block_sent, block_got, carry_sent, carry_got, last_sent, last_got = refs
    section, i = lax.axis_index("section"), lax.axis_index("col")
    width = whole.shape[-1]
    first, last = i == 0, i == n - 1

    barrier = pltpu.get_barrier_semaphore()

    def greet(**place):
        pl.semaphore_signal(barrier, 1, device_id=place, device_id_type=pl.DeviceIdType.MESH)

    if spread:
        for d in range(1, 2 * n):
            greet(section=lax.rem(section + d // n, 2), col=lax.rem(i + d, n))
        pl.semaphore_wait(barrier, 2 * n - 1)
    else:
        greet(section=1 - section)
        me = lax.axis_index("row")
        row_peers = n_row - 1 if parts else 0
        for d in range(1, row_peers + 1):
            greet(row=lax.rem(me + d, n_row))

        @pl.when(i > 0)
        def _():
            greet(col=i - 1)

        @pl.when(i < n - 1)
        def _():
            greet(col=i + 1)

        @pl.when(first | last)
        def _():
            pl.semaphore_wait(barrier, 2 + row_peers)

        @pl.when((i > 0) & (i < n - 1))
        def _():
            pl.semaphore_wait(barrier, 3 + row_peers)

    def carry_copy(k):
        return remote(carry[k], carried[k], carry_sent.at[k], carry_got.at[k], "section", layers[k])

    for k, layer in enumerate(layers):
        @pl.when(section != layer)
        def _(k=k):
            carry_copy(k).start()

    def remote_col(source, target, sent, got, device):
        return remote(source, target, sent, got, "col", device)

    def sum_copy(c, j, right):
        slot = j + 1 if right else j
        return remote_col(
            outgoing.at[c, j], arrived.at[c, slot], sum_sent.at[c, j], sum_got.at[c, slot], i + 1 if right else i - 1
        )

    def block_copy(c, o, right, own=False):
        sent = n if own and not right else o
        return remote_col(whole.at[c, o], whole.at[c, o], block_sent.at[c, sent], block_got.at[0, c, o], i + 1 if right else i - 1)

    def slice_copy(c, d):
        to = lax.rem(i + d, n)
        return pltpu.make_async_remote_copy(
            src_ref=outgoing.at[c, i, :, pl.ds(pl.multiple_of(to * width, 128), width)],
            dst_ref=whole.at[section, c, i],
            send_sem=block_sent.at[c, d],
            recv_sem=block_got.at[section, c, i],
            device_id={"section": 0, "col": to},
            device_id_type=pl.DeviceIdType.MESH,
        )

    def arrive(c, slot):
        remote_col(outgoing.at[c, 0], arrived.at[c, slot], sum_sent.at[c, 0], sum_got.at[c, slot], i).wait_recv()

    def work(c, o):
        if polish:
            values = whole[c, o].astype(jnp.float32)
            mean, inverse = norm_parts(values)
            polished[c, o] = ((values - mean) * inverse * gain[...] + shift[...]).astype(jnp.bfloat16)

    rows = whole.shape[-2]
    per = max(1, min(chunks, LANES // (n * rows)))
    many = per * n * rows
    tokens = chunks * n * rows

    def part_rows(source, b):
        return pl.ds(pl.multiple_of(source * tokens + b * many, many), many)

    def part_copy(b, d):
        to = lax.rem(me + d, n_row)
        return remote(
            leaving.at[d - 1, :, part_rows(0, b)],
            landed.at[:, part_rows(me, b)],
            part_sent.at[d - 1, b],
            part_got.at[me, b],
            "row",
            to,
        )

    def project(b):
        values = (polished if polish else whole)[pl.ds(b * per, per)].reshape(many, whole.shape[-1])
        projected[...] = jnp.dot(values, weight[...], preferred_element_type=jnp.float32) + bias[...]
        here = part_rows(me, b)

        def part(k, t):
            found = projected[:, columns(k * n_row + t)]
            if parts == 3 and k < 2:
                found = spin(found, cosines[here, :], sines[here, :])
            found = found.astype(jnp.bfloat16)
            if parts == 3 and k == 0:
                found = (found * jnp.asarray(HEAD_DIM**-0.5, jnp.bfloat16)).astype(jnp.bfloat16)
            return found

        for d in range(1, n_row):
            for k in range(parts):
                leaving[d - 1, k, part_rows(0, b), :] = part(k, lax.rem(me + d, n_row))
            part_copy(b, d).start()
        for k in range(parts):
            landed[k, here, :] = part(k, me)

    def sums_copy(d):
        to = lax.rem(i + d, n)
        return pltpu.make_async_remote_copy(
            src_ref=outs[-1].at[:, pl.ds(pl.multiple_of(to * width, 128), width)],
            dst_ref=all_sums.at[section, i],
            send_sem=last_sent.at[d],
            recv_sem=last_got.at[section, i],
            device_id={"section": 0, "col": to},
            device_id_type=pl.DeviceIdType.MESH,
        )

    def sums_arrive(s, o):
        return pltpu.make_async_remote_copy(
            src_ref=outs[-1].at[:, pl.ds(0, width)],
            dst_ref=all_sums.at[s, o],
            send_sem=last_sent.at[0],
            recv_sem=last_got.at[s, o],
            device_id={"section": 0, "col": o},
            device_id_type=pl.DeviceIdType.MESH,
        )

    def middle_slot(k):
        return jnp.maximum(lag * k + n - 1 - k, lag * (n - 1 - k) + k)

    def at(now, slot, allowed):
        since = now - slot
        c = jnp.maximum(since, 0) // n
        return c, allowed & (since >= 0) & (lax.rem(jnp.maximum(since, 0), n) == 0) & (since < n * chunks)

    def step(now, carry):
        for j in range(n - 1, 0, -1):
            c, due = at(now, lag * i + n - 1 - j, i < j)

            @pl.when(due & first)
            def _(c=c, j=j):
                outgoing[c, j] = partial[c, j]

            @pl.when(due & (i > 0))
            def _(c=c, j=j):
                arrive(c, j + 1)
                both = arrived[c, j + 1].astype(jnp.float32) + partial[c, j].astype(jnp.float32)
                outgoing[c, j] = both.astype(jnp.bfloat16)

            @pl.when(due)
            def _(c=c, j=j):
                sum_copy(c, j, True).start()

        for j in range(n - 1):
            c, due = at(now, lag * (n - 1 - i) + j, i > j)

            @pl.when(due & last)
            def _(c=c, j=j):
                outgoing[c, j] = partial[c, j]

            @pl.when(due & (i < n - 1))
            def _(c=c, j=j):
                arrive(c, j)
                both = arrived[c, j].astype(jnp.float32) + partial[c, j].astype(jnp.float32)
                outgoing[c, j] = both.astype(jnp.bfloat16)

            @pl.when(due)
            def _(c=c, j=j):
                sum_copy(c, j, False).start()

        c, due = at(now, middle_slot(i), i >= 0)

        @pl.when(due)
        def _():
            total[...] = partial[c, i].astype(jnp.float32)

        @pl.when(due & (i > 0))
        def _():
            arrive(c, i + 1)
            total[...] += arrived[c, i + 1].astype(jnp.float32)

        @pl.when(due & (i < n - 1))
        def _():
            arrive(c, i)
            total[...] += arrived[c, i].astype(jnp.float32)

        @pl.when(due)
        def _():
            block = middle(total[...], c, ins, outs)
            if spread:
                outgoing[c, i] = block
                for d in range(1, n):
                    slice_copy(c, d).start()

                @pl.when(section == 0)
                def _():
                    whole[0, c, i] = outgoing[c, i, :, pl.ds(pl.multiple_of(i * width, 128), width)]

                @pl.when(section != 0)
                def _():
                    slice_copy(c, 0).start()

            else:
                whole[c, i] = block
                work(c, i)

        if spread:
            return carry

        @pl.when(due & (i < n - 1))
        def _():
            block_copy(c, i, True, own=True).start()

        @pl.when(due & (i > 0))
        def _():
            block_copy(c, i, False, own=True).start()

        for o in range(n - 1):
            c, due = at(now, middle_slot(o) + lag * (i - o), i > o)

            @pl.when(due)
            def _(c=c, o=o):
                block_copy(c, o, True).wait_recv()

            @pl.when(due & (i < n - 1))
            def _(c=c, o=o):
                block_copy(c, o, True).start()

            @pl.when(due)
            def _(c=c, o=o):
                work(c, o)

        for o in range(1, n):
            c, due = at(now, middle_slot(o) + lag * (o - i), i < o)

            @pl.when(due)
            def _(c=c, o=o):
                block_copy(c, o, False).wait_recv()

            @pl.when(due & (i > 0))
            def _(c=c, o=o):
                block_copy(c, o, False).start()

            @pl.when(due)
            def _(c=c, o=o):
                work(c, o)

        if parts:
            since = now - (n * (per - 1) + 2 * lag * (n - 1))

            @pl.when((since >= 0) & (lax.rem(jnp.maximum(since, 0), n * per) == 0))
            def _():
                project(jnp.maximum(since, 0) // (n * per))

        return carry

    lax.fori_loop(0, n * (chunks - 1) + 2 * lag * (n - 1) + 1, step, 0)

    if spread:
        for d in range(1, n):
            sums_copy(d).start()

        @pl.when(section == 0)
        def _():
            all_sums[0, i] = outs[-1][:, pl.ds(pl.multiple_of(i * width, 128), width)]

        @pl.when(section != 0)
        def _():
            sums_copy(0).start()

    def slice_arrives(c, s, o):
        return pltpu.make_async_remote_copy(
            src_ref=outgoing.at[c, 0, :, pl.ds(0, width)],
            dst_ref=whole.at[s, c, o],
            send_sem=block_sent.at[c, 0],
            recv_sem=block_got.at[s, c, o],
            device_id={"section": 0, "col": o},
            device_id_type=pl.DeviceIdType.MESH,
        )

    def settle(c, carry):
        for j in range(n):
            @pl.when(j != i)
            def _(j=j):
                sum_copy(c, j, True).wait_send()

        if spread:
            for d in range(1, n):
                slice_copy(c, d).wait_send()

            @pl.when(section != 0)
            def _():
                slice_copy(c, 0).wait_send()

            for s in range(2):
                for o in range(n):
                    @pl.when((section == 0) & ((s == 1) | (o != i)))
                    def _(s=s, o=o):
                        slice_arrives(c, s, o).wait_recv()

            return carry
        for o in range(n):
            @pl.when((o <= i) & (i < n - 1))
            def _(o=o):
                block_copy(c, o, True).wait_send()

            @pl.when((o > i) & (i > 0))
            def _(o=o):
                block_copy(c, o, True).wait_send()

        @pl.when(i > 0)
        def _():
            block_copy(c, i, False, own=True).wait_send()

        return carry

    lax.fori_loop(0, chunks, settle, 0)
    if spread:
        for d in range(1, n):
            sums_copy(d).wait_send()

        @pl.when(section != 0)
        def _():
            sums_copy(0).wait_send()

        for s in range(2):
            for o in range(n):
                @pl.when((section == 0) & ((s == 1) | (o != i)))
                def _(s=s, o=o):
                    sums_arrive(s, o).wait_recv()

    if parts:
        def settle_parts(b, carry):
            for d in range(1, n_row):
                part_copy(b, d).wait_send()
                source = lax.rem(me + d, n_row)
                remote(
                    leaving.at[0, :, part_rows(0, b)],
                    landed.at[:, part_rows(source, b)],
                    part_sent.at[0, b],
                    part_got.at[source, b],
                    "row",
                    source,
                ).wait_recv()
            return carry

        lax.fori_loop(0, chunks // per, settle_parts, 0)

    for k, layer in enumerate(layers):
        @pl.when(section != layer)
        def _(k=k):
            carry_copy(k).wait_send()

        @pl.when(section == layer)
        def _(k=k):
            carry_copy(k).wait_recv()


def relay(middle, number, partial, ins, outs, n, spread=False, carry=(), behind=(), polish=(), project=(), n_row=1, lag=3, rows=RELAY_ROWS):
    tokens, features = partial.shape
    owned = tokens // n
    chunks = owned // rows
    blocks = lambda values: values.reshape(chunks, rows, features) if values.shape[0] == owned else values
    ins = [blocks(values) for values in ins] + list(polish) + list(project)
    parts = project[0].shape[1] // (n_row * LANES) if project else 0
    batches = chunks // max(1, min(chunks, LANES // (n * rows)))
    outs = list(outs) + ([(tokens, features)] if polish else []) + ([(parts, n_row * tokens, LANES)] if parts else []) + ([(2, n, 2, features // n)] if spread else [])
    out_shapes = [
        jax.ShapeDtypeStruct(
            (2, chunks, n, rows, features // n) if spread else (chunks, n, rows, features), jnp.bfloat16
        )
    ] + [
        jax.ShapeDtypeStruct((chunks, n, rows, features), jnp.bfloat16)
        if shape[0] == tokens
        else jax.ShapeDtypeStruct(shape, jnp.bfloat16)
        if shape[-1] == LANES
        else jax.ShapeDtypeStruct((chunks, rows, features) if shape[0] == owned else shape, jnp.float32)
        for shape in outs
    ]
    vmem, anywhere = pl.BlockSpec(memory_space=pltpu.VMEM), pl.BlockSpec(memory_space=pl.ANY)
    layers = tuple(layer for layer, _ in carry)
    carry = [values for _, values in carry]
    whole, *rest = pl.pallas_call(
        functools.partial(relay_kernel, middle, len(ins), len(outs), layers, len(behind), bool(polish), parts, n_row, n, chunks, lag, spread),
        in_specs=[vmem] * (1 + len(ins)) + [anywhere] * (len(carry) + len(behind)),
        out_specs=[vmem] * len(out_shapes) + [anywhere] * len(carry),
        out_shape=out_shapes + [jax.ShapeDtypeStruct(values.shape, values.dtype) for values in carry],
        scratch_shapes=[
            pltpu.VMEM((chunks, n + 1, rows, features), jnp.bfloat16),
            pltpu.VMEM((chunks, n, rows, features), jnp.bfloat16),
            pltpu.VMEM((rows, features), jnp.float32),
            pltpu.SemaphoreType.DMA((chunks, n)),
            pltpu.SemaphoreType.DMA((chunks, n + 1)),
            pltpu.SemaphoreType.DMA((chunks, n + 1)),
            pltpu.SemaphoreType.DMA((2 if spread else 1, chunks, n)),
            pltpu.SemaphoreType.DMA((max(1, len(carry)),)),
            pltpu.SemaphoreType.DMA((max(1, len(carry)),)),
            pltpu.SemaphoreType.DMA((n,)),
            pltpu.SemaphoreType.DMA((2, n)),
        ]
        + (
            [
                pltpu.VMEM((tokens // batches, project[0].shape[1]), jnp.float32),
                pltpu.VMEM((n_row - 1, parts, tokens, LANES), jnp.bfloat16),
                pltpu.SemaphoreType.DMA((n_row - 1, batches)),
                pltpu.SemaphoreType.DMA((n_row, batches)),
            ]
            if parts
            else []
        ),
        compiler_params=pltpu.CompilerParams(
            collective_id=number, has_side_effects=True, vmem_limit_bytes=56 * 2**20
        ),
        cost_estimate=pl.CostEstimate(flops=0, bytes_accessed=35 * 10**7, transcendentals=0),
    )(partial.reshape(chunks, n, rows, features), *ins, *carry, *behind)
    shapes = {(chunks, rows, features): (owned, features), (chunks, n, rows, features): (tokens, features)}
    rest = [values.reshape(shapes.get(values.shape, values.shape)) for values in rest]
    return [whole.reshape((2, tokens, -1) if spread else (tokens, -1))] + rest


def gather_kernel(n, chunks, lag, own, small, angles, whole, smalls, normed, cosines, sines, sent, got, small_sent, small_got):
    section, i = lax.axis_index("section"), lax.axis_index("col")
    rows, width = own.shape[0] // chunks, own.shape[1]
    others = [(s, d) for s in range(2) for d in range(n) if (s, d) != (0, 0)]
    place = lambda s, d: {"section": lax.rem(section + s, 2), "col": lax.rem(i + d, n)}
    barrier = pltpu.get_barrier_semaphore()
    for s, d in others:
        pl.semaphore_signal(barrier, 1, device_id=place(s, d), device_id_type=pl.DeviceIdType.MESH)
    pl.semaphore_wait(barrier, len(others))

    def small_copy(s, d):
        return pltpu.make_async_remote_copy(
            src_ref=small,
            dst_ref=smalls.at[section, i],
            send_sem=small_sent.at[s, d],
            recv_sem=small_got.at[section, i],
            device_id=place(s, d),
            device_id_type=pl.DeviceIdType.MESH,
        )

    for s, d in others:
        small_copy(s, d).start()
    smalls[section, i] = small[...]

    def small_arrives(s, d):
        from_s, from_d = lax.rem(section + s, 2), lax.rem(i + d, n)
        return pltpu.make_async_remote_copy(
            src_ref=small,
            dst_ref=smalls.at[from_s, from_d],
            send_sem=small_sent.at[s, d],
            recv_sem=small_got.at[from_s, from_d],
            device_id=place(s, d),
            device_id_type=pl.DeviceIdType.MESH,
        )

    def norm(c):
        here = pl.ds(pl.multiple_of(c * rows, rows), rows)
        values = whole[here, :].astype(jnp.float32)
        mean, inverse = norm_parts(values)
        for o in range(n):
            part = slice(o * width, (o + 1) * width)
            gain, shift = smalls[0, o, 0:1, :], smalls[0, o, 2:3, :]
            normed[here, part] = ((values[:, part] - mean) * inverse * gain + shift).astype(jnp.bfloat16)

    def block(c, o, right, mine=False):
        part = whole.at[pl.ds(pl.multiple_of(c * rows, rows), rows), columns(o, width)]
        return remote(
            part, part, sent.at[c, n if mine and not right else o], got.at[c, o], "col", i + 1 if right else i - 1
        )

    def at(now, slot, allowed):
        since = jnp.maximum(now - slot, 0)
        return since // (n - 1), allowed & (now >= slot) & (lax.rem(since, n - 1) == 0) & (since < (n - 1) * chunks)

    def step(now, carry):
        c, due = at(now, 0, i >= 0)

        @pl.when(due)
        def _():
            here = pl.ds(pl.multiple_of(c * rows, rows), rows)
            whole[here, columns(i, width)] = own[here, :]

        @pl.when(due & (i < n - 1))
        def _():
            block(c, i, True, True).start()

        @pl.when(due & (i > 0))
        def _():
            block(c, i, False, True).start()

        for o in range(n):
            c, due = at(now, lag * jnp.abs(i - o), i != o)

            @pl.when(due)
            def _(c=c, o=o):
                block(c, o, True).wait_recv()

            @pl.when(due & (i > o) & (i < n - 1))
            def _(c=c, o=o):
                block(c, o, True).start()

            @pl.when(due & (i < o) & (i > 0))
            def _(c=c, o=o):
                block(c, o, False).start()

        c, due = at(now, lag * (n - 1), i >= 0)

        @pl.when(due)
        def _():
            norm(c)

        return carry

    turns = angles.shape[0] // 2
    lane = lax.broadcasted_iota(jnp.int32, (turns, LANES), 1)
    place_of = lax.broadcasted_iota(jnp.int32, (turns, LANES), 0)
    turned = lane % HEAD_DIM < 2 * turns
    picked = jnp.where(turned & (lane % turns == place_of), 1.0, 0.0)
    sign = jnp.where(lane % HEAD_DIM < turns, -1.0, 1.0)

    def spread_out(table, pick):
        return lax.dot_general(
            table, pick, (((0,), (0,)), ((), ())), precision=lax.Precision.HIGHEST, preferred_element_type=jnp.float32
        )

    still = jnp.where(turned[:1], 0.0, 1.0)
    cosines[...] = spread_out(angles[:turns, :], picked) + still
    sines[...] = spread_out(angles[turns:, :], picked * sign)
    for s, d in others:
        small_arrives(s, d).wait_recv()

    lax.fori_loop(0, (n - 1) * (chunks - 1) + lag * (n - 1) + 1, step, 0)

    def settle(c, carry):
        for o in range(n):
            @pl.when(((o <= i) & (i < n - 1)) | ((o > i) & (i > 0)))
            def _(o=o):
                block(c, o, True).wait_send()

        @pl.when(i > 0)
        def _():
            block(c, i, False, True).wait_send()

        return carry

    lax.fori_loop(0, chunks, settle, 0)
    for s, d in others:
        small_copy(s, d).wait_send()


def gathered(number, own, small, angles, n, lag=3, rows=64):
    tokens, width = own.shape
    chunks = tokens // rows
    vmem = pl.BlockSpec(memory_space=pltpu.VMEM)
    return pl.pallas_call(
        functools.partial(gather_kernel, n, chunks, lag),
        in_specs=[vmem] * 3,
        out_specs=[vmem] * 5,
        out_shape=[
            jax.ShapeDtypeStruct((tokens, n * width), own.dtype),
            jax.ShapeDtypeStruct((2, n) + small.shape, small.dtype),
            jax.ShapeDtypeStruct((tokens, n * width), own.dtype),
            jax.ShapeDtypeStruct((angles.shape[1], LANES), jnp.float32),
            jax.ShapeDtypeStruct((angles.shape[1], LANES), jnp.float32),
        ],
        scratch_shapes=[
            pltpu.SemaphoreType.DMA((chunks, n + 1)),
            pltpu.SemaphoreType.DMA((chunks, n)),
            pltpu.SemaphoreType.DMA((2, n)),
            pltpu.SemaphoreType.DMA((2, n)),
        ],
        compiler_params=pltpu.CompilerParams(
            collective_id=number, has_side_effects=True, vmem_limit_bytes=40 * 2**20
        ),
        cost_estimate=pl.CostEstimate(flops=0, bytes_accessed=25 * 10**7, transcendentals=0),
    )(own, small, angles)


def rotary_angles(positions):
    half_dims = ROT // 2
    inverse_freq = 1.0 / 10000.0 ** (jnp.arange(half_dims, dtype=jnp.float32) * 2.0 / ROT)
    angles = positions.astype(jnp.float32)[None, :] * inverse_freq[:, None]
    return jnp.concatenate([jnp.cos(angles), jnp.sin(angles)])


def product(left, right):
    return jnp.dot(left, right, preferred_element_type=jnp.float32)


def per_device(
    inputs,
    cotangent,
    block_ids,
    norm_gains,
    norm_shifts,
    qkv_weight,
    qkv_bias,
    out_weight,
    gate_up_weight,
    down_weight,
):
    section = lax.axis_index("section")
    row = lax.axis_index("row")
    col = lax.axis_index("col")
    rows_axis = lax.axis_size("row")
    cols_axis = lax.axis_size("col")
    tokens, width = inputs.shape[1:]
    owned = tokens // cols_axis
    units = down_weight.shape[2]
    seq = tokens * rows_axis
    both = ("section", "row")
    whole_lanes = width == rows_axis * LANES
    heads = LANES // HEAD_DIM if whole_lanes else 1
    copies = 1 if whole_lanes else rows_axis * HEAD_DIM // width

    def expand(values):
        if whole_lanes:
            return values
        rows = values.shape[0]
        values = values.reshape(rows, -1, width // HEAD_DIM, HEAD_DIM)
        values = jnp.pad(jnp.repeat(values, copies, axis=2), ((0, 0), (0, 0), (0, 0), (0, LANES - HEAD_DIM)))
        return values.reshape(rows, -1)

    def contract(values):
        if whole_lanes:
            return values
        values = values.reshape(tokens, -1, rows_axis, LANES)[:, :, ::copies, :HEAD_DIM]
        return values.reshape(tokens, -1)

    def weights_of(block):
        block = block[0].reshape(block.shape[1], -1)
        return lax.all_gather(block, both, axis=0, tiled=True).reshape(2, D, -1)

    def mine(values):
        blocks = values.reshape(owned // RELAY_ROWS, cols_axis, RELAY_ROWS, -1)
        return lax.dynamic_index_in_dim(blocks, col, 1, keepdims=False).reshape(owned, -1)

    def my_features(values):
        return lax.dynamic_slice_in_dim(values, col * width, width, 1)

    own_small = jnp.concatenate([norm_gains[0], norm_shifts[0], qkv_bias[0], jnp.zeros((1, width), jnp.float32)])
    angles = rotary_angles(jnp.arange(seq, dtype=jnp.int32))
    stream, small, normed, cosines, sines = gathered(
        7, lax.dynamic_index_in_dim(inputs, section, 0, keepdims=False), own_small, angles, cols_axis
    )
    whole_small = small.transpose(0, 2, 1, 3).reshape(2, own_small.shape[0], D)
    gains, shifts = whole_small[:, :2], whole_small[:, 2:4]
    bias = lax.dynamic_index_in_dim(small, col, 1, keepdims=False)[:, 4:7].reshape(2, -1)

    qkv_w = weights_of(qkv_weight)
    out_w = weights_of(out_weight)
    gate_up_w = weights_of(gate_up_weight)
    down_w = weights_of(down_weight)

    ids = lax.dynamic_index_in_dim(block_ids, section, 0, keepdims=False)
    kept = []
    hidden_out = []
    waited = []
    for layer in range(2):
        if layer == 0:
            qkv = expand(product(normed, qkv_w[0]) + bias[0])
            spread, mixed, log_sums, attn_mix = attend(
                8, ids, heads, rows_axis, tokens, qkv=qkv, cosines=cosines, sines=sines
            )
        else:
            here = section + jnp.where(hidden_out[0][0, 0] == hidden_out[0][0, 0], 0, 1)
            branch = lax.all_gather(
                lax.dynamic_index_in_dim(cotangent, here, 0, keepdims=False), "col", axis=1, tiled=True
            )
            waited = [branch]
            spread, mixed, log_sums, attn_mix = attend(9, ids, heads, rows_axis, tokens, spread=spread)
        attn_mix = contract(attn_mix)
        normed_two, after = relay(
            after_attention,
            layer,
            product(attn_mix, out_w[layer].T).astype(jnp.bfloat16),
            [mine(stream), gains[layer, 1:], shifts[layer, 1:]],
            [(owned, D)],
            cols_axis,
            behind=waited,
        )
        gate_up = product(normed_two, gate_up_w[layer])
        gate, up = gate_up[:, :units], gate_up[:, units:]
        hidden = (jax.nn.silu(gate) * up).astype(jnp.bfloat16)
        kept.append((stream, normed, spread, mixed, log_sums, attn_mix, after, normed_two, gate_up, hidden))
        partial = product(hidden, down_w[layer].T)
        if layer == 0:
            stream, normed, spread = relay(
                after_hidden,
                2,
                partial.astype(jnp.bfloat16),
                [after],
                [],
                cols_axis,
                polish=(gains[1, :1], shifts[1, :1]),
                project=(expand(qkv_w[1]), expand(bias[1:]), cosines, sines),
                n_row=rows_axis,
            )
            hidden_out.append(my_features(stream))
        else:
            blocks = partial.reshape(owned // RELAY_ROWS, cols_axis, RELAY_ROWS, D)
            owner = lax.broadcasted_iota(jnp.int32, blocks.shape, 1) == col
            blocks = blocks + jnp.where(owner, after.reshape(-1, 1, RELAY_ROWS, D), 0.0)
            result = blocks.reshape(tokens, D).astype(jnp.bfloat16)

    grad = mine(branch).astype(jnp.float32)
    weight_sums = [[], []]
    small_sums = []
    bias_grads = [None, None]
    input_out = [None, None]
    input_got = [None, None]
    hidden_got = [None, None]

    def collect(layer, term):
        weight_sums[layer].append(lax.psum_scatter(term, "row", scatter_dimension=0, tiled=True))
        return weight_sums[layer][-1]

    arrived = [[None] * 4, [None] * 4]
    no_table = jnp.zeros((8, LANES), jnp.float32)

    def together(*values):
        return lax.optimization_barrier(values)

    for layer in (1, 0):
        stream, normed, spread, mixed, log_sums, attn_mix, after, normed_two, gate_up, hidden = kept[layer]
        gate, up = gate_up[:, :units], gate_up[:, units:]
        d_hidden = product(branch, down_w[layer])
        sig = jax.nn.sigmoid(gate)
        d_gate = d_hidden * up * sig * (1.0 + gate * (1.0 - sig))
        d_up = d_hidden * gate * sig
        d_gate_up = jnp.concatenate([d_gate, d_up], axis=1).astype(jnp.bfloat16)
        partial, down_term, gate_up_term = together(
            dot_last(d_gate_up, gate_up_w[layer]).astype(jnp.bfloat16),
            dot_first(branch, hidden).astype(jnp.bfloat16),
            dot_first(normed_two, d_gate_up).astype(jnp.bfloat16),
        )
        down_sum, gate_up_sum = collect(layer, down_term), collect(layer, gate_up_term)
        grad_attn, d_after, sums_two, spread_grad, *got = relay(
            behind_norm,
            3 + layer,
            partial,
            [grad, after, gains[layer, 1:]],
            [(owned, D), (2, D)],
            cols_axis,
            carry=[]
            if layer == 1
            else [(0, hidden_out[0]), (1, hidden_out[1]), (1, input_out[1]), (1, weight_sums[1][2]), (1, weight_sums[1][3])],
            behind=[] if layer == 1 else [weight_sums[1][0]],
            project=(expand(out_w[layer]), jnp.zeros((1, rows_axis * LANES), jnp.float32), no_table, no_table),
            n_row=rows_axis,
        )
        if layer == 1:
            result = jnp.where(d_after[0, 0] == d_after[0, 0], result, 0)
            hidden_out.append(lax.psum_scatter(result, "col", scatter_dimension=1, tiled=True))
        else:
            hidden_got[0], hidden_got[1], input_got[1], arrived[1][2], arrived[1][3] = got
        small_sums += [sums_two]
        out_term = dot_first(grad_attn, attn_mix).astype(jnp.bfloat16)
        out_sum = collect(layer, out_term)
        d_qkv, arrived[layer][1] = attend_back(
            10 + layer,
            spread_grad[0],
            spread,
            mixed,
            log_sums,
            ids,
            cosines,
            sines,
            heads,
            rows_axis,
            layer,
            gate_up_sum,
        )
        d_qkv = contract(d_qkv)
        partial, qkv_term, bias_grads[layer] = together(
            dot_last(d_qkv, qkv_w[layer]).astype(jnp.bfloat16),
            dot_first(normed, d_qkv).astype(jnp.bfloat16),
            jnp.sum(d_qkv.astype(jnp.float32), axis=0),
        )
        qkv_sum = collect(layer, qkv_term)
        if layer == 0:
            early_sums = lax.psum_scatter(jnp.stack(small_sums), "col", scatter_dimension=2, tiled=True)
            early = jnp.concatenate([early_sums.reshape(6, -1), bias_grads[1].reshape(3, -1), bias_grads[0].reshape(3, -1)])
            early = jnp.sum(lax.all_gather(early, both, axis=0), axis=0)
        branch, grad, sums_one, *got = relay(
            behind_norm,
            5 + layer,
            partial,
            [d_after, mine(stream), gains[layer, :1]],
            [(owned, D), (2, D)],
            cols_axis,
            spread=layer == 0,
            carry=[] if layer == 1 else [(0, down_sum), (0, out_sum), (1, weight_sums[1][0])],
            behind=[hidden_out[1]] if layer == 1 else [early_sums],
        )
        if layer == 0:
            late_sums, arrived[0][0], arrived[0][2], arrived[1][0] = got
        small_sums += [sums_one]
        input_out[layer] = my_features(branch) if layer == 1 else branch

    arrived[0][3] = lax.ppermute(weight_sums[0][3], "section", [(1, 0)])
    hidden_states = jnp.where(
        section == 0, jnp.stack([hidden_out[0], hidden_got[0]]), jnp.stack([hidden_got[1], hidden_out[1]])
    )
    input_grads = jnp.where(section == 0, input_out[0], jnp.stack([input_got[1], input_out[1]])).astype(jnp.float32)
    down_grad, gate_up_grad, out_grad, qkv_grad = (
        jnp.where(section == 0, first, second).astype(jnp.float32)
        + jnp.where(section == 0, first_got, second_got).astype(jnp.float32)
        for first, second, first_got, second_got in zip(*weight_sums, *arrived)
    )
    last = lax.psum(jnp.sum(late_sums, axis=(0, 1)), "row")
    norm_sums = jnp.where(section == 0, jnp.stack([last, early[4:6]]), jnp.stack([early[2:4], early[0:2]]))
    bias_sum = jnp.where(section == 0, early[9:12], early[6:9])
    return (
        hidden_states[None],
        input_grads[None],
        norm_sums[:, 0][None],
        norm_sums[:, 1][None],
        qkv_grad.reshape(qkv_weight.shape),
        bias_sum.reshape(qkv_bias.shape),
        out_grad[None],
        gate_up_grad.reshape(gate_up_weight.shape),
        down_grad[None],
    )


def solution(mesh):
    in_specs = (
        P(None, "row", "col"),
        P(None, "row", "col"),
        P(),
        P("section", None, "col"),
        P("section", None, "col"),
        P("section", "row", None, "col"),
        P("section", None, "col"),
        P("section", "row", "col"),
        P("section", "row", None, "col"),
        P("section", "row", "col"),
    )
    out_specs = (
        P("section", None, "row", "col"),
        P("section", None, "row", "col"),
        P("section", None, "col"),
        P("section", None, "col"),
        P("section", "row", None, "col"),
        P("section", None, "col"),
        P("section", "row", "col"),
        P("section", "row", None, "col"),
        P("section", "row", "col"),
    )
    return jax.shard_map(
        per_device, mesh=mesh, in_specs=in_specs, out_specs=out_specs, check_vma=False
    )
```

```python
import functools

import jax
import jax.numpy as jnp
from jax import lax
from jax.experimental import pallas as pl
from jax.experimental.pallas import tpu as pltpu
from jax.sharding import PartitionSpec as P

D = 2048
HEADS = 32
HEAD_DIM = 64
ROT = 16
LANES = 128
REACH = 256
RELAY_ROWS = 16


epsilon = 1e-05


def dot_last(a, b):
    return lax.dot_general(a, b, (((1,), (1,)), ((), ())), preferred_element_type=jnp.float32)


def dot_first(a, b):
    return lax.dot_general(a, b, (((0,), (0,)), ((), ())), preferred_element_type=jnp.float32)


def lanes_of(rows, head):
    lane = lax.broadcasted_iota(jnp.int32, (rows, LANES), 1)
    return lane // HEAD_DIM == head


def spin(x, cosines, sines):
    lane = lax.broadcasted_iota(jnp.int32, x.shape, 1)
    ahead, behind = pltpu.roll(x, LANES - ROT // 2, 1), pltpu.roll(x, ROT // 2, 1)
    return x * cosines + jnp.where(lane % ROT < ROT // 2, ahead, behind) * sines


def meet(axis, n):
    me = lax.axis_index(axis)
    barrier = pltpu.get_barrier_semaphore()
    for d in range(1, n):
        pl.semaphore_signal(
            barrier, 1, device_id={axis: lax.rem(me + d, n)}, device_id_type=pl.DeviceIdType.MESH
        )
    pl.semaphore_wait(barrier, n - 1)


def remote(source, target, sent, got, axis, device):
    return pltpu.make_async_remote_copy(
        src_ref=source,
        dst_ref=target,
        send_sem=sent,
        recv_sem=got,
        device_id={axis: device},
        device_id_type=pl.DeviceIdType.MESH,
    )


def columns(which, size=LANES):
    return pl.ds(pl.multiple_of(which * size, size), size)


def attend_kernel(heads, n, bq, given, bid_q, bid_k, *refs):
    me = lax.axis_index("row")
    if given:
        spread, mixed, lse_ref, mix, vone, scores, mix_sent, mix_got = refs
    else:
        qkv, cosines, sines, spread, mixed, lse_ref, mix, vone, scores, mix_sent, mix_got = refs[:11]
        leaving, qkv_sent, qkv_got = refs[11:]
    tokens = mix.shape[0]
    seq = n * tokens
    here = pl.ds(pl.multiple_of(me * tokens, tokens), tokens)
    low = jnp.bfloat16
    meet("row", n)

    def parts(t):
        cos, sin = cosines[here, :], sines[here, :]
        query = spin(qkv[:, columns(t)], cos, sin).astype(low) * jnp.asarray(HEAD_DIM**-0.5, low)
        key = spin(qkv[:, columns(n + t)], cos, sin).astype(low)
        return query.astype(low), key, qkv[:, columns(2 * n + t)].astype(low)

    def leave(d):
        to = lax.rem(me + d, n)
        return remote(leaving.at[d - 1], spread.at[:, here], qkv_sent.at[d - 1], qkv_got.at[me], "row", to)

    if not given:
        for d in range(1, n):
            for k, part in enumerate(parts(lax.rem(me + d, n))):
                leaving[d - 1, k] = part
            leave(d).start()
        for k, part in enumerate(parts(me)):
            spread[k, here, :] = part

    def come(row):
        if not given:
            @pl.when(row != me)
            def _():
                there = pl.ds(row * tokens, tokens)
                remote(leaving.at[0], spread.at[:, there], qkv_sent.at[0], qkv_got.at[row], "row", me).wait_recv()

        there = pl.ds(row * tokens, tokens)
        for h in range(heads):
            vone[h, there, :] = jnp.where(lanes_of(tokens, h), spread[2, there, :], jnp.ones((), low))

    def mix_copy(i, device):
        rows = pl.ds(lax.rem(i, tokens // bq) * bq, bq)
        return remote(
            mixed.at[pl.ds(i * bq, bq)], mix.at[rows, columns(me)], mix_sent.at[i], mix_got.at[me, lax.rem(i, tokens // bq)], "row", device
        )

    def block(i, carry):
        rows = pl.ds(pl.multiple_of(i * bq, bq), bq)
        q = spread[0, rows, :]
        bid = bid_q[rows, :]
        begin = i * bq
        ahead = jnp.where(begin + bq < seq, 1, 0)
        qs = [jnp.where(lanes_of(bq, h), q, jnp.zeros((), low)) for h in range(heads)]

        def score(start, size, tops, hide):
            span = pl.ds(pl.multiple_of(start, REACH), size)
            keys = spread[1, span, :]
            if hide:
                visible = bid_k[:, span] <= bid
            found = []
            for h in range(heads):
                s = dot_last(qs[h], keys)
                if hide:
                    s = jnp.where(visible, s, -1e30)
                scores[h, :, span] = s
                top = tops[h]
                for c in range(size // LANES):
                    top = jnp.maximum(top, s[:, c * LANES : (c + 1) * LANES])
                found.append(top)
            return tuple(found)

        tops = tuple(jnp.full((bq, LANES), -1e30, jnp.float32) for _ in range(heads))
        tops = lax.fori_loop(0, i // 2, lambda t, c: score(2 * t * bq, 2 * bq, c, False), tops)
        tops = lax.fori_loop(i // 2 * 2, i, lambda t, c: score(t * bq, bq, c, False), tops)
        tops = score(begin, bq, tops, True)
        tops = lax.fori_loop(0, ahead, lambda t, c: score(begin + bq, REACH, c, True), tops)
        tops = [jnp.max(top, axis=1, keepdims=True) for top in tops]

        def gather(start, size, sums):
            span = pl.ds(pl.multiple_of(start, REACH), size)
            found = []
            for h in range(heads):
                p = jnp.exp(scores[h, :, span] - tops[h]).astype(low)
                found.append(sums[h] + jnp.dot(p, vone[h, span, :], preferred_element_type=jnp.float32))
            return tuple(found)

        sums = tuple(jnp.zeros((bq, LANES), jnp.float32) for _ in range(heads))
        sums = lax.fori_loop(0, (i + 1) // 2, lambda t, c: gather(2 * t * bq, 2 * bq, c), sums)
        sums = lax.fori_loop((i + 1) // 2 * 2, i + 1, lambda t, c: gather(t * bq, bq, c), sums)
        sums = lax.fori_loop(0, ahead, lambda t, c: gather(begin + bq, REACH, c), sums)
        outcome = jnp.zeros((bq, LANES), jnp.float32)
        lse = jnp.zeros((bq, LANES), jnp.float32)
        for h in range(heads):
            totals = pltpu.roll(sums[h], HEAD_DIM, 1)
            outcome = jnp.where(lanes_of(bq, h), sums[h] / totals, outcome)
            lse = jnp.where(lanes_of(bq, h), tops[h] + jnp.log(totals), lse)
        mixed[rows, :] = outcome.astype(low)
        lse_ref[:, rows] = lse.T
        return carry

    per_row = tokens // bq
    for row in range(n):
        if row == 0:
            come(0)
        if row + 1 < n:
            come(row + 1)

        def run(half, carry, row=row):
            i = row * per_row + half
            block(i, 0)

            @pl.when(row == me)
            def _():
                mix[pl.ds(pl.multiple_of(half * bq, bq), bq), columns(me)] = mixed[pl.ds(pl.multiple_of(i * bq, bq), bq), :]

            @pl.when(row != me)
            def _():
                mix_copy(i, row).start()

            return carry

        lax.fori_loop(0, per_row, run, 0)

    if not given:
        for d in range(1, n):
            leave(d).wait_send()
    for i in range(n * per_row):
        @pl.when(i // per_row != me)
        def _(i=i):
            mix_copy(i, me).wait_send()

    for row in range(n):
        @pl.when(row != me)
        def _(row=row):
            for half in range(per_row):
                rows = pl.ds(half * bq, bq)
                remote(
                    mixed.at[pl.ds(0, bq)], mix.at[rows, columns(row)], mix_sent.at[0], mix_got.at[row, half], "row", me
                ).wait_recv()


def attend(number, block_all, heads, n, tokens, qkv=None, cosines=None, sines=None, spread=None, bq=512):
    bq = min(bq, tokens)
    seq = n * tokens
    vmem = pl.BlockSpec(memory_space=pltpu.VMEM)
    low = jnp.bfloat16
    given = spread is not None
    operands = [spread] if given else [qkv, cosines, sines]
    out_shape = [
        jax.ShapeDtypeStruct((3, seq, LANES), low),
        jax.ShapeDtypeStruct((seq, LANES), low),
        jax.ShapeDtypeStruct((LANES, seq), jnp.float32),
        jax.ShapeDtypeStruct((tokens, n * LANES), low),
    ][given:]
    exchange = [
        pltpu.VMEM((n - 1, 3, tokens, LANES), low),
        pltpu.SemaphoreType.DMA((n - 1,)),
        pltpu.SemaphoreType.DMA((n,)),
    ]
    found = pl.pallas_call(
        functools.partial(attend_kernel, heads, n, bq, given),
        in_specs=[vmem] * (2 + len(operands)),
        out_specs=[vmem] * len(out_shape),
        out_shape=out_shape,
        scratch_shapes=[
            pltpu.VMEM((heads, seq, LANES), low),
            pltpu.VMEM((heads, bq, seq), jnp.float32),
            pltpu.SemaphoreType.DMA((seq // bq,)),
            pltpu.SemaphoreType.DMA((n, tokens // bq)),
        ]
        + ([] if given else exchange),
        compiler_params=pltpu.CompilerParams(
            collective_id=number, has_side_effects=True, vmem_limit_bytes=58 * 2**20
        ),
        cost_estimate=pl.CostEstimate(flops=10**10, bytes_accessed=2 * 10**8, transcendentals=0),
    )(block_all.reshape(seq, 1), block_all.reshape(1, seq), *operands)
    return [spread] + list(found) if given else found


def attend_back_kernel(
    heads, n, bq, layer, bid_q, bid_k, d_mix, spread, mixed, lse_ref, cosines, sines, carry, *refs
):
    d_qkv, carried, grads, kone, dk_acc, dv_acc, leaving, g_sent, g_got, back_sent, back_got, carry_sent, carry_got = refs
    section = lax.axis_index("section")
    me = lax.axis_index("row")
    tokens = d_mix.shape[0]
    seq = n * tokens
    per_row = tokens // bq
    blocks = n * per_row
    low = jnp.bfloat16
    zero = jnp.zeros((), low)
    here = pl.ds(pl.multiple_of(me * tokens, tokens), tokens)
    barrier = pltpu.get_barrier_semaphore()
    pl.semaphore_signal(barrier, 1, device_id={"section": 1 - section}, device_id_type=pl.DeviceIdType.MESH)
    for d in range(1, n):
        pl.semaphore_signal(barrier, 1, device_id={"row": lax.rem(me + d, n)}, device_id_type=pl.DeviceIdType.MESH)
    pl.semaphore_wait(barrier, n)
    carry_copy = remote(carry, carried, carry_sent, carry_got, "section", layer)

    def give(d):
        to = lax.rem(me + d, n)
        return remote(d_mix.at[:, columns(to)], grads.at[here], g_sent.at[d - 1], g_got.at[me], "row", to)

    for d in range(1, n):
        give(d).start()

    @pl.when(section != layer)
    def _():
        carry_copy.start()

    grads[here, :] = d_mix[:, columns(me)]
    for h in range(heads):
        kone[h] = jnp.where(lanes_of(seq, h), spread[1], zero).T
    dk_acc[...] = jnp.zeros_like(dk_acc)
    dv_acc[...] = jnp.zeros_like(dv_acc)

    def tile(start, size, dq, hide, stuff):
        qs, gs, lses, deltas, bid = stuff
        span = pl.ds(pl.multiple_of(start, REACH), size)
        keys, values = spread[1, span, :], spread[2, span, :]
        dv, dk = dv_acc[span, :], dk_acc[span, :]
        if hide:
            visible = bid_k[span, :] <= bid
        for h in range(heads):
            s = dot_last(keys, qs[h])
            if hide:
                s = jnp.where(visible, s, -1e30)
            p = jnp.exp(s - lses[h])
            dp = dot_last(values, gs[h])
            ds = (p * (dp - deltas[h])).astype(low)
            dv = dv + jnp.dot(p.astype(low), gs[h], preferred_element_type=jnp.float32)
            dk = dk + jnp.dot(ds, qs[h], preferred_element_type=jnp.float32)
            dq = dq + jnp.dot(kone[h, :, span], ds, preferred_element_type=jnp.float32)
        dv_acc[span, :] = dv
        dk_acc[span, :] = dk
        return dq

    def block(i):
        rows = pl.ds(pl.multiple_of(i * bq, bq), bq)
        q, g = spread[0, rows, :], grads[rows, :]
        product = (g.astype(jnp.float32) * mixed[rows, :].astype(jnp.float32)).T
        span = lambda h: slice(h * HEAD_DIM, (h + 1) * HEAD_DIM)
        deltas = [jnp.sum(product[span(h)], axis=0, keepdims=True) for h in range(heads)]
        lses = [lse_ref[h * HEAD_DIM : h * HEAD_DIM + 1, rows] for h in range(heads)]
        qs = [jnp.where(lanes_of(bq, h), q, zero) for h in range(heads)]
        gs = [jnp.where(lanes_of(bq, h), g, zero) for h in range(heads)]
        stuff = (qs, gs, lses, deltas, bid_q[:, rows])
        begin = i * bq
        ahead = jnp.where(begin + bq < seq, 1, 0)
        dq = jnp.zeros((LANES, bq), jnp.float32)
        dq = lax.fori_loop(0, i, lambda t, c: tile(t * bq, bq, c, False, stuff), dq)
        dq = tile(begin, bq, dq, True, stuff)
        dq = lax.fori_loop(0, ahead, lambda t, c: tile(begin + bq, REACH, c, True, stuff), dq)
        return spin(dq.T * (HEAD_DIM**-0.5), cosines[rows, :], -sines[rows, :]).astype(low)

    def back_copy(k, i, device):
        half = lax.rem(i, per_row)
        rows = pl.ds(pl.multiple_of(half * bq, bq), bq)
        return remote(
            leaving.at[k, pl.ds(pl.multiple_of(i * bq, bq), bq)],
            d_qkv.at[rows, columns(k * n + me)],
            back_sent.at[k, i],
            back_got.at[k, me, half],
            "row",
            device,
        )

    def send(k, i, values):
        row = i // per_row
        half = lax.rem(i, per_row)

        @pl.when(row == me)
        def _():
            d_qkv[pl.ds(pl.multiple_of(half * bq, bq), bq), columns(k * n + me)] = values

        @pl.when(row != me)
        def _():
            leaving[k, pl.ds(pl.multiple_of(i * bq, bq), bq), :] = values
            back_copy(k, i, row).start()

    def keys_done(i):
        rows = pl.ds(pl.multiple_of(i * bq, bq), bq)
        send(1, i, spin(dk_acc[rows, :], cosines[rows, :], -sines[rows, :]).astype(low))
        send(2, i, dv_acc[rows, :].astype(low))

    for row in range(n - 1, -1, -1):
        @pl.when(row != me)
        def _(row=row):
            there = pl.ds(row * tokens, tokens)
            remote(d_mix.at[:, columns(0)], grads.at[there], g_sent.at[0], g_got.at[row], "row", me).wait_recv()

        def run(step, carry, row=row):
            i = row * per_row + per_row - 1 - step
            send(0, i, block(i))

            @pl.when(i + 1 < blocks)
            def _():
                keys_done(i + 1)

            return carry

        lax.fori_loop(0, per_row, run, 0)
    keys_done(0)

    for d in range(1, n):
        give(d).wait_send()

    def settle(i, carry):
        @pl.when(i // per_row != me)
        def _():
            half = lax.rem(i, per_row)
            rows = pl.ds(pl.multiple_of(half * bq, bq), bq)
            for k in range(3):
                back_copy(k, i, me).wait_send()
                remote(
                    leaving.at[k, pl.ds(0, bq)],
                    d_qkv.at[rows, columns(k * n + i // per_row)],
                    back_sent.at[k, 0],
                    back_got.at[k, i // per_row, half],
                    "row",
                    me,
                ).wait_recv()

        return carry

    lax.fori_loop(0, blocks, settle, 0)

    @pl.when(section != layer)
    def _():
        carry_copy.wait_send()

    @pl.when(section == layer)
    def _():
        carry_copy.wait_recv()


def attend_back(number, d_mix, spread, mixed, lse, block_all, cosines, sines, heads, n, layer, carry, bq=512):
    tokens = d_mix.shape[0]
    bq = min(bq, tokens)
    seq = n * tokens
    vmem = pl.BlockSpec(memory_space=pltpu.VMEM)
    low = jnp.bfloat16
    return pl.pallas_call(
        functools.partial(attend_back_kernel, heads, n, bq, layer),
        in_specs=[vmem] * 8 + [pl.BlockSpec(memory_space=pl.ANY)],
        out_specs=[vmem, pl.BlockSpec(memory_space=pl.ANY)],
        out_shape=[jax.ShapeDtypeStruct((tokens, 3 * n * LANES), low), jax.ShapeDtypeStruct(carry.shape, carry.dtype)],
        scratch_shapes=[
            pltpu.VMEM((seq, LANES), low),
            pltpu.VMEM((heads, LANES, seq), low),
            pltpu.VMEM((seq, LANES), jnp.float32),
            pltpu.VMEM((seq, LANES), jnp.float32),
            pltpu.VMEM((3, seq, LANES), low),
            pltpu.SemaphoreType.DMA((n - 1,)),
            pltpu.SemaphoreType.DMA((n,)),
            pltpu.SemaphoreType.DMA((3, seq // bq)),
            pltpu.SemaphoreType.DMA((3, n, tokens // bq)),
            pltpu.SemaphoreType.DMA,
            pltpu.SemaphoreType.DMA,
        ],
        compiler_params=pltpu.CompilerParams(
            collective_id=number, has_side_effects=True, vmem_limit_bytes=58 * 2**20
        ),
        cost_estimate=pl.CostEstimate(flops=10**10, bytes_accessed=3 * 10**8, transcendentals=0),
    )(block_all.reshape(1, seq), block_all.reshape(seq, 1), d_mix, spread, mixed, lse, cosines, sines, carry)


def norm_parts(values):
    mean = jnp.mean(values, axis=-1, keepdims=True)
    spread = jnp.mean(values * values, axis=-1, keepdims=True) - mean * mean
    return mean, lax.rsqrt(spread + epsilon)


def after_attention(total, c, ins, outs):
    stream, gain, shift = ins
    (after_ref,) = outs
    after = stream[c].astype(jnp.float32) + total
    after_ref[c] = after
    values = after.astype(jnp.bfloat16).astype(jnp.float32)
    mean, inverse = norm_parts(values)
    return ((values - mean) * inverse * gain[...] + shift[...]).astype(jnp.bfloat16)


def after_hidden(total, c, ins, outs):
    (after,) = ins
    return (after[c] + total).astype(jnp.bfloat16)


def behind_norm(total, c, ins, outs):
    grad, values_ref, gain = ins
    grad_ref, sums = outs
    values = values_ref[c].astype(jnp.bfloat16).astype(jnp.float32)
    mean, inverse = norm_parts(values)
    centred = (values - mean) * inverse
    scaled = total * gain[...]
    back = inverse * (
        scaled
        - jnp.mean(scaled, axis=-1, keepdims=True)
        - centred * jnp.mean(scaled * centred, axis=-1, keepdims=True)
    )
    given = grad[c] + back
    grad_ref[c] = given
    here = [jnp.sum(total * centred, axis=0, keepdims=True), jnp.sum(total, axis=0, keepdims=True)]

    @pl.when(c == 0)
    def _():
        sums[...] = jnp.zeros_like(sums)

    sums[...] += jnp.concatenate(here, axis=0)
    return given.astype(jnp.bfloat16)


def relay_kernel(
    middle, n_ins, n_outs, layers, n_after, polish, parts, n_row, n, chunks, lag, spread, partial, *refs
):
    ins, carry, refs = refs[:n_ins], refs[n_ins : n_ins + len(layers)], refs[n_ins + len(layers) + n_after :]
    whole, outs, refs = refs[0], refs[1 : 1 + n_outs], refs[1 + n_outs :]
    carried, refs = refs[: len(layers)], refs[len(layers) :]
    if parts:
        ins, (weights, bias, cosines, sines) = ins[:-4], ins[-4:]
        outs, landed = outs[:-1], outs[-1]
        *refs, leaving, part_sent, part_got, weight, weight_got = refs
        weight_copy = pltpu.make_async_copy(weights.at[pl.ds(weight.shape[0], weight.shape[0])], weight, weight_got)
        weight_copy.start()
    if polish:
        ins, (gain, shift) = ins[:-2], ins[-2:]
        outs, polished = outs[:-1], outs[-1]
    if spread:
        outs, all_sums = outs[:-1], outs[-1]
    arrived, outgoing, total, sum_sent, sum_got, block_sent, block_got, carry_sent, carry_got, last_sent, last_got = refs
    section, i = lax.axis_index("section"), lax.axis_index("col")
    width = whole.shape[-1]
    first, last = i == 0, i == n - 1

    barrier = pltpu.get_barrier_semaphore()

    def greet(**place):
        pl.semaphore_signal(barrier, 1, device_id=place, device_id_type=pl.DeviceIdType.MESH)

    if spread:
        for d in range(1, 2 * n):
            greet(section=lax.rem(section + d // n, 2), col=lax.rem(i + d, n))
        pl.semaphore_wait(barrier, 2 * n - 1)
    else:
        greet(section=1 - section)
        me = lax.axis_index("row")
        row_peers = n_row - 1 if parts else 0
        for d in range(1, row_peers + 1):
            greet(row=lax.rem(me + d, n_row))

        @pl.when(i > 0)
        def _():
            greet(col=i - 1)

        @pl.when(i < n - 1)
        def _():
            greet(col=i + 1)

        @pl.when(first | last)
        def _():
            pl.semaphore_wait(barrier, 2 + row_peers)

        @pl.when((i > 0) & (i < n - 1))
        def _():
            pl.semaphore_wait(barrier, 3 + row_peers)

    def carry_copy(k):
        return remote(carry[k], carried[k], carry_sent.at[k], carry_got.at[k], "section", layers[k])

    for k, layer in enumerate(layers):
        @pl.when(section != layer)
        def _(k=k):
            carry_copy(k).start()

    def remote_col(source, target, sent, got, device):
        return remote(source, target, sent, got, "col", device)

    def sum_copy(c, j, right):
        slot = j + 1 if right else j
        return remote_col(
            outgoing.at[c, j], arrived.at[c, slot], sum_sent.at[c, j], sum_got.at[c, slot], i + 1 if right else i - 1
        )

    def block_copy(c, o, right, own=False):
        sent = n if own and not right else o
        return remote_col(whole.at[c, o], whole.at[c, o], block_sent.at[c, sent], block_got.at[0, c, o], i + 1 if right else i - 1)

    def slice_copy(c, d):
        to = lax.rem(i + d, n)
        return pltpu.make_async_remote_copy(
            src_ref=outgoing.at[c, i, :, pl.ds(pl.multiple_of(to * width, 128), width)],
            dst_ref=whole.at[section, c, i],
            send_sem=block_sent.at[c, d],
            recv_sem=block_got.at[section, c, i],
            device_id={"section": 0, "col": to},
            device_id_type=pl.DeviceIdType.MESH,
        )

    def arrive(c, slot):
        remote_col(outgoing.at[c, 0], arrived.at[c, slot], sum_sent.at[c, 0], sum_got.at[c, slot], i).wait_recv()

    def work(c, o):
        if polish:
            values = whole[c, o].astype(jnp.float32)
            mean, inverse = norm_parts(values)
            polished[c, o] = ((values - mean) * inverse * gain[...] + shift[...]).astype(jnp.bfloat16)

    rows = whole.shape[-2]
    per = max(1, min(chunks, LANES // (n * rows)))
    many = per * n * rows
    unit = max(1, n * per // n_row)
    tokens = chunks * n * rows

    def part_rows(source, b):
        return pl.ds(pl.multiple_of(source * tokens + b * many, many), many)

    def part_copy(b, d):
        to = lax.rem(me + d, n_row)
        return remote(
            leaving.at[d - 1, :, part_rows(0, b)],
            landed.at[:, part_rows(me, b)],
            part_sent.at[d - 1, b],
            part_got.at[me, b],
            "row",
            to,
        )

    def project(b, d):
        values = (polished if polish else whole)[pl.ds(b * per, per)].reshape(many, whole.shape[-1])
        here, there = part_rows(me, b), part_rows(0, b)
        t = lax.rem(me + d, n_row)
        for k in range(parts):
            column = columns(k * n_row + t)
            found = jnp.dot(values, weight[:, column], preferred_element_type=jnp.float32) + bias[:, column]
            if parts == 3 and k < 2:
                found = spin(found, cosines[here, :], sines[here, :])
            found = found.astype(jnp.bfloat16)
            if parts == 3 and k == 0:
                found = (found * jnp.asarray(HEAD_DIM**-0.5, jnp.bfloat16)).astype(jnp.bfloat16)

            @pl.when(d > 0)
            def _(k=k, found=found):
                leaving[d - 1, k, there, :] = found

            @pl.when(d == 0)
            def _(k=k, found=found):
                landed[k, here, :] = found

        @pl.when(d > 0)
        def _():
            part_copy(b, d).start()

    def sums_copy(d):
        to = lax.rem(i + d, n)
        return pltpu.make_async_remote_copy(
            src_ref=outs[-1].at[:, pl.ds(pl.multiple_of(to * width, 128), width)],
            dst_ref=all_sums.at[section, i],
            send_sem=last_sent.at[d],
            recv_sem=last_got.at[section, i],
            device_id={"section": 0, "col": to},
            device_id_type=pl.DeviceIdType.MESH,
        )

    def sums_arrive(s, o):
        return pltpu.make_async_remote_copy(
            src_ref=outs[-1].at[:, pl.ds(0, width)],
            dst_ref=all_sums.at[s, o],
            send_sem=last_sent.at[0],
            recv_sem=last_got.at[s, o],
            device_id={"section": 0, "col": o},
            device_id_type=pl.DeviceIdType.MESH,
        )

    def middle_slot(k):
        return jnp.maximum(lag * k + n - 1 - k, lag * (n - 1 - k) + k)

    def at(now, slot, allowed):
        since = now - slot
        c = jnp.maximum(since, 0) // n
        return c, allowed & (since >= 0) & (lax.rem(jnp.maximum(since, 0), n) == 0) & (since < n * chunks)

    def step(now, carry):
        for j in range(n - 1, 0, -1):
            c, due = at(now, lag * i + n - 1 - j, i < j)

            @pl.when(due & first)
            def _(c=c, j=j):
                outgoing[c, j] = partial[c, j]

            @pl.when(due & (i > 0))
            def _(c=c, j=j):
                arrive(c, j + 1)
                both = arrived[c, j + 1].astype(jnp.float32) + partial[c, j].astype(jnp.float32)
                outgoing[c, j] = both.astype(jnp.bfloat16)

            @pl.when(due)
            def _(c=c, j=j):
                sum_copy(c, j, True).start()

        for j in range(n - 1):
            c, due = at(now, lag * (n - 1 - i) + j, i > j)

            @pl.when(due & last)
            def _(c=c, j=j):
                outgoing[c, j] = partial[c, j]

            @pl.when(due & (i < n - 1))
            def _(c=c, j=j):
                arrive(c, j)
                both = arrived[c, j].astype(jnp.float32) + partial[c, j].astype(jnp.float32)
                outgoing[c, j] = both.astype(jnp.bfloat16)

            @pl.when(due)
            def _(c=c, j=j):
                sum_copy(c, j, False).start()

        c, due = at(now, middle_slot(i), i >= 0)

        @pl.when(due)
        def _():
            total[...] = partial[c, i].astype(jnp.float32)

        @pl.when(due & (i > 0))
        def _():
            arrive(c, i + 1)
            total[...] += arrived[c, i + 1].astype(jnp.float32)

        @pl.when(due & (i < n - 1))
        def _():
            arrive(c, i)
            total[...] += arrived[c, i].astype(jnp.float32)

        @pl.when(due)
        def _():
            block = middle(total[...], c, ins, outs)
            if spread:
                outgoing[c, i] = block
                for d in range(1, n):
                    slice_copy(c, d).start()

                @pl.when(section == 0)
                def _():
                    whole[0, c, i] = outgoing[c, i, :, pl.ds(pl.multiple_of(i * width, 128), width)]

                @pl.when(section != 0)
                def _():
                    slice_copy(c, 0).start()

            else:
                whole[c, i] = block
                work(c, i)

        if spread:
            return carry

        @pl.when(due & (i < n - 1))
        def _():
            block_copy(c, i, True, own=True).start()

        @pl.when(due & (i > 0))
        def _():
            block_copy(c, i, False, own=True).start()

        for o in range(n - 1):
            c, due = at(now, middle_slot(o) + lag * (i - o), i > o)

            @pl.when(due)
            def _(c=c, o=o):
                block_copy(c, o, True).wait_recv()

            @pl.when(due & (i < n - 1))
            def _(c=c, o=o):
                block_copy(c, o, True).start()

            @pl.when(due)
            def _(c=c, o=o):
                work(c, o)

        for o in range(1, n):
            c, due = at(now, middle_slot(o) + lag * (o - i), i < o)

            @pl.when(due)
            def _(c=c, o=o):
                block_copy(c, o, False).wait_recv()

            @pl.when(due & (i > 0))
            def _(c=c, o=o):
                block_copy(c, o, False).start()

            @pl.when(due)
            def _(c=c, o=o):
                work(c, o)

        if parts:
            since = now - (n * (per - 1) + 2 * lag * (n - 1))
            given = jnp.maximum(since, 0)
            turn = lax.rem(given, n * per) // unit

            @pl.when(since == 0)
            def _():
                weight_copy.wait()

            @pl.when((since >= 0) & (lax.rem(given, unit) == 0) & (turn < n_row) & (given < n * chunks))
            def _():
                project(given // (n * per), lax.rem(turn + 1, n_row))

        return carry

    steps = n * (chunks - 1) + 2 * lag * (n - 1) + 1
    lax.fori_loop(0, steps + (unit * (n_row - 1) if parts else 0), step, 0)

    if spread:
        for d in range(1, n):
            sums_copy(d).start()

        @pl.when(section == 0)
        def _():
            all_sums[0, i] = outs[-1][:, pl.ds(pl.multiple_of(i * width, 128), width)]

        @pl.when(section != 0)
        def _():
            sums_copy(0).start()

    def slice_arrives(c, s, o):
        return pltpu.make_async_remote_copy(
            src_ref=outgoing.at[c, 0, :, pl.ds(0, width)],
            dst_ref=whole.at[s, c, o],
            send_sem=block_sent.at[c, 0],
            recv_sem=block_got.at[s, c, o],
            device_id={"section": 0, "col": o},
            device_id_type=pl.DeviceIdType.MESH,
        )

    def settle(c, carry):
        for j in range(n):
            @pl.when(j != i)
            def _(j=j):
                sum_copy(c, j, True).wait_send()

        if spread:
            for d in range(1, n):
                slice_copy(c, d).wait_send()

            @pl.when(section != 0)
            def _():
                slice_copy(c, 0).wait_send()

            for s in range(2):
                for o in range(n):
                    @pl.when((section == 0) & ((s == 1) | (o != i)))
                    def _(s=s, o=o):
                        slice_arrives(c, s, o).wait_recv()

            return carry
        for o in range(n):
            @pl.when((o <= i) & (i < n - 1))
            def _(o=o):
                block_copy(c, o, True).wait_send()

            @pl.when((o > i) & (i > 0))
            def _(o=o):
                block_copy(c, o, True).wait_send()

        @pl.when(i > 0)
        def _():
            block_copy(c, i, False, own=True).wait_send()

        return carry

    lax.fori_loop(0, chunks, settle, 0)
    if spread:
        for d in range(1, n):
            sums_copy(d).wait_send()

        @pl.when(section != 0)
        def _():
            sums_copy(0).wait_send()

        for s in range(2):
            for o in range(n):
                @pl.when((section == 0) & ((s == 1) | (o != i)))
                def _(s=s, o=o):
                    sums_arrive(s, o).wait_recv()

    if parts:
        def settle_parts(b, carry):
            for d in range(1, n_row):
                part_copy(b, d).wait_send()
                source = lax.rem(me + d, n_row)
                remote(
                    leaving.at[0, :, part_rows(0, b)],
                    landed.at[:, part_rows(source, b)],
                    part_sent.at[0, b],
                    part_got.at[source, b],
                    "row",
                    source,
                ).wait_recv()
            return carry

        lax.fori_loop(0, chunks // per, settle_parts, 0)

    for k, layer in enumerate(layers):
        @pl.when(section != layer)
        def _(k=k):
            carry_copy(k).wait_send()

        @pl.when(section == layer)
        def _(k=k):
            carry_copy(k).wait_recv()


def relay(middle, number, partial, ins, outs, n, spread=False, carry=(), behind=(), polish=(), project=(), n_row=1, lag=3, rows=RELAY_ROWS):
    tokens, features = partial.shape
    owned = tokens // n
    chunks = owned // rows
    blocks = lambda values: values.reshape(chunks, rows, features) if values.shape[0] == owned else values
    ins = [blocks(values) for values in ins] + list(polish) + list(project)
    parts = project[0].shape[1] // (n_row * LANES) if project else 0
    batches = chunks // max(1, min(chunks, LANES // (n * rows)))
    outs = list(outs) + ([(tokens, features)] if polish else []) + ([(parts, n_row * tokens, LANES)] if parts else []) + ([(2, n, 2, features // n)] if spread else [])
    out_shapes = [
        jax.ShapeDtypeStruct(
            (2, chunks, n, rows, features // n) if spread else (chunks, n, rows, features), jnp.bfloat16
        )
    ] + [
        jax.ShapeDtypeStruct((chunks, n, rows, features), jnp.bfloat16)
        if shape[0] == tokens
        else jax.ShapeDtypeStruct(shape, jnp.bfloat16)
        if shape[-1] == LANES
        else jax.ShapeDtypeStruct((chunks, rows, features) if shape[0] == owned else shape, jnp.float32)
        for shape in outs
    ]
    vmem, anywhere = pl.BlockSpec(memory_space=pltpu.VMEM), pl.BlockSpec(memory_space=pl.ANY)
    specs = [vmem] * (1 + len(ins))
    if project:
        specs[-4] = anywhere
    layers = tuple(layer for layer, _ in carry)
    carry = [values for _, values in carry]
    whole, *rest = pl.pallas_call(
        functools.partial(relay_kernel, middle, len(ins), len(outs), layers, len(behind), bool(polish), parts, n_row, n, chunks, lag, spread),
        in_specs=specs + [anywhere] * (len(carry) + len(behind)),
        out_specs=[vmem] * len(out_shapes) + [anywhere] * len(carry),
        out_shape=out_shapes + [jax.ShapeDtypeStruct(values.shape, values.dtype) for values in carry],
        scratch_shapes=[
            pltpu.VMEM((chunks, n + 1, rows, features), jnp.bfloat16),
            pltpu.VMEM((chunks, n, rows, features), jnp.bfloat16),
            pltpu.VMEM((rows, features), jnp.float32),
            pltpu.SemaphoreType.DMA((chunks, n)),
            pltpu.SemaphoreType.DMA((chunks, n + 1)),
            pltpu.SemaphoreType.DMA((chunks, n + 1)),
            pltpu.SemaphoreType.DMA((2 if spread else 1, chunks, n)),
            pltpu.SemaphoreType.DMA((max(1, len(carry)),)),
            pltpu.SemaphoreType.DMA((max(1, len(carry)),)),
            pltpu.SemaphoreType.DMA((n,)),
            pltpu.SemaphoreType.DMA((2, n)),
        ]
        + (
            [
                pltpu.VMEM((n_row - 1, parts, tokens, LANES), jnp.bfloat16),
                pltpu.SemaphoreType.DMA((n_row - 1, batches)),
                pltpu.SemaphoreType.DMA((n_row, batches)),
                pltpu.VMEM((features, project[0].shape[1]), jnp.bfloat16),
                pltpu.SemaphoreType.DMA,
            ]
            if parts
            else []
        ),
        compiler_params=pltpu.CompilerParams(
            collective_id=number, has_side_effects=True, vmem_limit_bytes=56 * 2**20
        ),
        cost_estimate=pl.CostEstimate(flops=0, bytes_accessed=35 * 10**7, transcendentals=0),
    )(partial.reshape(chunks, n, rows, features), *ins, *carry, *behind)
    shapes = {(chunks, rows, features): (owned, features), (chunks, n, rows, features): (tokens, features)}
    rest = [values.reshape(shapes.get(values.shape, values.shape)) for values in rest]
    return [whole.reshape((2, tokens, -1) if spread else (tokens, -1))] + rest


def gather_kernel(n, chunks, lag, own, small, angles, whole, smalls, normed, cosines, sines, sent, got, small_sent, small_got):
    section, i = lax.axis_index("section"), lax.axis_index("col")
    rows, width = own.shape[0] // chunks, own.shape[1]
    others = [(s, d) for s in range(2) for d in range(n) if (s, d) != (0, 0)]
    place = lambda s, d: {"section": lax.rem(section + s, 2), "col": lax.rem(i + d, n)}
    barrier = pltpu.get_barrier_semaphore()
    for s, d in others:
        pl.semaphore_signal(barrier, 1, device_id=place(s, d), device_id_type=pl.DeviceIdType.MESH)
    pl.semaphore_wait(barrier, len(others))

    def small_copy(s, d):
        return pltpu.make_async_remote_copy(
            src_ref=small,
            dst_ref=smalls.at[section, i],
            send_sem=small_sent.at[s, d],
            recv_sem=small_got.at[section, i],
            device_id=place(s, d),
            device_id_type=pl.DeviceIdType.MESH,
        )

    for s, d in others:
        small_copy(s, d).start()
    smalls[section, i] = small[...]

    def small_arrives(s, d):
        from_s, from_d = lax.rem(section + s, 2), lax.rem(i + d, n)
        return pltpu.make_async_remote_copy(
            src_ref=small,
            dst_ref=smalls.at[from_s, from_d],
            send_sem=small_sent.at[s, d],
            recv_sem=small_got.at[from_s, from_d],
            device_id=place(s, d),
            device_id_type=pl.DeviceIdType.MESH,
        )

    def norm(c):
        here = pl.ds(pl.multiple_of(c * rows, rows), rows)
        values = whole[here, :].astype(jnp.float32)
        mean, inverse = norm_parts(values)
        for o in range(n):
            part = slice(o * width, (o + 1) * width)
            gain, shift = smalls[0, o, 0:1, :], smalls[0, o, 2:3, :]
            normed[here, part] = ((values[:, part] - mean) * inverse * gain + shift).astype(jnp.bfloat16)

    def block(c, o, right, mine=False):
        part = whole.at[pl.ds(pl.multiple_of(c * rows, rows), rows), columns(o, width)]
        return remote(
            part, part, sent.at[c, n if mine and not right else o], got.at[c, o], "col", i + 1 if right else i - 1
        )

    def at(now, slot, allowed):
        since = jnp.maximum(now - slot, 0)
        return since // (n - 1), allowed & (now >= slot) & (lax.rem(since, n - 1) == 0) & (since < (n - 1) * chunks)

    def step(now, carry):
        c, due = at(now, 0, i >= 0)

        @pl.when(due)
        def _():
            here = pl.ds(pl.multiple_of(c * rows, rows), rows)
            whole[here, columns(i, width)] = own[here, :]

        @pl.when(due & (i < n - 1))
        def _():
            block(c, i, True, True).start()

        @pl.when(due & (i > 0))
        def _():
            block(c, i, False, True).start()

        for o in range(n):
            c, due = at(now, lag * jnp.abs(i - o), i != o)

            @pl.when(due)
            def _(c=c, o=o):
                block(c, o, True).wait_recv()

            @pl.when(due & (i > o) & (i < n - 1))
            def _(c=c, o=o):
                block(c, o, True).start()

            @pl.when(due & (i < o) & (i > 0))
            def _(c=c, o=o):
                block(c, o, False).start()

        c, due = at(now, lag * (n - 1), i >= 0)

        @pl.when(due)
        def _():
            norm(c)

        return carry

    turns = angles.shape[0] // 2
    lane = lax.broadcasted_iota(jnp.int32, (turns, LANES), 1)
    place_of = lax.broadcasted_iota(jnp.int32, (turns, LANES), 0)
    turned = lane % HEAD_DIM < 2 * turns
    picked = jnp.where(turned & (lane % turns == place_of), 1.0, 0.0)
    sign = jnp.where(lane % HEAD_DIM < turns, -1.0, 1.0)

    def spread_out(table, pick):
        return lax.dot_general(
            table, pick, (((0,), (0,)), ((), ())), precision=lax.Precision.HIGHEST, preferred_element_type=jnp.float32
        )

    still = jnp.where(turned[:1], 0.0, 1.0)
    cosines[...] = spread_out(angles[:turns, :], picked) + still
    sines[...] = spread_out(angles[turns:, :], picked * sign)
    for s, d in others:
        small_arrives(s, d).wait_recv()

    lax.fori_loop(0, (n - 1) * (chunks - 1) + lag * (n - 1) + 1, step, 0)

    def settle(c, carry):
        for o in range(n):
            @pl.when(((o <= i) & (i < n - 1)) | ((o > i) & (i > 0)))
            def _(o=o):
                block(c, o, True).wait_send()

        @pl.when(i > 0)
        def _():
            block(c, i, False, True).wait_send()

        return carry

    lax.fori_loop(0, chunks, settle, 0)
    for s, d in others:
        small_copy(s, d).wait_send()


def gathered(number, own, small, angles, n, lag=3, rows=64):
    tokens, width = own.shape
    chunks = tokens // rows
    vmem = pl.BlockSpec(memory_space=pltpu.VMEM)
    return pl.pallas_call(
        functools.partial(gather_kernel, n, chunks, lag),
        in_specs=[vmem] * 3,
        out_specs=[vmem] * 5,
        out_shape=[
            jax.ShapeDtypeStruct((tokens, n * width), own.dtype),
            jax.ShapeDtypeStruct((2, n) + small.shape, small.dtype),
            jax.ShapeDtypeStruct((tokens, n * width), own.dtype),
            jax.ShapeDtypeStruct((angles.shape[1], LANES), jnp.float32),
            jax.ShapeDtypeStruct((angles.shape[1], LANES), jnp.float32),
        ],
        scratch_shapes=[
            pltpu.SemaphoreType.DMA((chunks, n + 1)),
            pltpu.SemaphoreType.DMA((chunks, n)),
            pltpu.SemaphoreType.DMA((2, n)),
            pltpu.SemaphoreType.DMA((2, n)),
        ],
        compiler_params=pltpu.CompilerParams(
            collective_id=number, has_side_effects=True, vmem_limit_bytes=40 * 2**20
        ),
        cost_estimate=pl.CostEstimate(flops=0, bytes_accessed=25 * 10**7, transcendentals=0),
    )(own, small, angles)


def rotary_angles(positions):
    half_dims = ROT // 2
    inverse_freq = 1.0 / 10000.0 ** (jnp.arange(half_dims, dtype=jnp.float32) * 2.0 / ROT)
    angles = positions.astype(jnp.float32)[None, :] * inverse_freq[:, None]
    return jnp.concatenate([jnp.cos(angles), jnp.sin(angles)])


def product(left, right):
    return jnp.dot(left, right, preferred_element_type=jnp.float32)


def per_device(
    inputs,
    cotangent,
    block_ids,
    norm_gains,
    norm_shifts,
    qkv_weight,
    qkv_bias,
    out_weight,
    gate_up_weight,
    down_weight,
):
    section = lax.axis_index("section")
    row = lax.axis_index("row")
    col = lax.axis_index("col")
    rows_axis = lax.axis_size("row")
    cols_axis = lax.axis_size("col")
    tokens, width = inputs.shape[1:]
    owned = tokens // cols_axis
    units = down_weight.shape[2]
    seq = tokens * rows_axis
    both = ("section", "row")
    whole_lanes = width == rows_axis * LANES
    heads = LANES // HEAD_DIM if whole_lanes else 1
    copies = 1 if whole_lanes else rows_axis * HEAD_DIM // width

    def expand(values):
        if whole_lanes:
            return values
        rows = values.shape[0]
        values = values.reshape(rows, -1, width // HEAD_DIM, HEAD_DIM)
        values = jnp.pad(jnp.repeat(values, copies, axis=2), ((0, 0), (0, 0), (0, 0), (0, LANES - HEAD_DIM)))
        return values.reshape(rows, -1)

    def contract(values):
        if whole_lanes:
            return values
        values = values.reshape(tokens, -1, rows_axis, LANES)[:, :, ::copies, :HEAD_DIM]
        return values.reshape(tokens, -1)

    def weights_of(block):
        block = block[0].reshape(block.shape[1], -1)
        return lax.all_gather(block, both, axis=0, tiled=True).reshape(2, D, -1)

    def mine(values):
        blocks = values.reshape(owned // RELAY_ROWS, cols_axis, RELAY_ROWS, -1)
        return lax.dynamic_index_in_dim(blocks, col, 1, keepdims=False).reshape(owned, -1)

    def my_features(values):
        return lax.dynamic_slice_in_dim(values, col * width, width, 1)

    own_small = jnp.concatenate([norm_gains[0], norm_shifts[0], qkv_bias[0], jnp.zeros((1, width), jnp.float32)])
    angles = rotary_angles(jnp.arange(seq, dtype=jnp.int32))
    stream, small, normed, cosines, sines = gathered(
        7, lax.dynamic_index_in_dim(inputs, section, 0, keepdims=False), own_small, angles, cols_axis
    )
    whole_small = small.transpose(0, 2, 1, 3).reshape(2, own_small.shape[0], D)
    gains, shifts = whole_small[:, :2], whole_small[:, 2:4]
    bias = lax.dynamic_index_in_dim(small, col, 1, keepdims=False)[:, 4:7].reshape(2, -1)

    qkv_w = weights_of(qkv_weight)
    out_w = weights_of(out_weight)
    gate_up_w = weights_of(gate_up_weight)
    down_w = weights_of(down_weight)

    ids = lax.dynamic_index_in_dim(block_ids, section, 0, keepdims=False)
    kept = []
    hidden_out = []
    waited = []
    for layer in range(2):
        if layer == 0:
            qkv = expand(product(normed, qkv_w[0]) + bias[0])
            spread, mixed, log_sums, attn_mix = attend(
                8, ids, heads, rows_axis, tokens, qkv=qkv, cosines=cosines, sines=sines
            )
        else:
            here = section + jnp.where(hidden_out[0][0, 0] == hidden_out[0][0, 0], 0, 1)
            branch = lax.all_gather(
                lax.dynamic_index_in_dim(cotangent, here, 0, keepdims=False), "col", axis=1, tiled=True
            )
            waited = [branch]
            spread, mixed, log_sums, attn_mix = attend(9, ids, heads, rows_axis, tokens, spread=spread)
        attn_mix = contract(attn_mix)
        normed_two, after = relay(
            after_attention,
            layer,
            product(attn_mix, out_w[layer].T).astype(jnp.bfloat16),
            [mine(stream), gains[layer, 1:], shifts[layer, 1:]],
            [(owned, D)],
            cols_axis,
            behind=waited,
        )
        gate_up = product(normed_two, gate_up_w[layer])
        gate, up = gate_up[:, :units], gate_up[:, units:]
        hidden = (jax.nn.silu(gate) * up).astype(jnp.bfloat16)
        kept.append((stream, normed, spread, mixed, log_sums, attn_mix, after, normed_two, gate_up, hidden))
        partial = product(hidden, down_w[layer].T)
        if layer == 0:
            stream, normed, spread = relay(
                after_hidden,
                2,
                partial.astype(jnp.bfloat16),
                [after],
                [],
                cols_axis,
                polish=(gains[1, :1], shifts[1, :1]),
                project=(expand(qkv_w.reshape(2 * D, -1)), expand(bias[1:]), cosines, sines),
                n_row=rows_axis,
            )
            hidden_out.append(my_features(stream))
        else:
            blocks = partial.reshape(owned // RELAY_ROWS, cols_axis, RELAY_ROWS, D)
            owner = lax.broadcasted_iota(jnp.int32, blocks.shape, 1) == col
            blocks = blocks + jnp.where(owner, after.reshape(-1, 1, RELAY_ROWS, D), 0.0)
            result = blocks.reshape(tokens, D).astype(jnp.bfloat16)

    grad = mine(branch).astype(jnp.float32)
    weight_sums = [[], []]
    small_sums = []
    bias_grads = [None, None]
    input_out = [None, None]
    input_got = [None, None]
    hidden_got = [None, None]

    def collect(layer, term):
        weight_sums[layer].append(lax.psum_scatter(term, "row", scatter_dimension=0, tiled=True))
        return weight_sums[layer][-1]

    arrived = [[None] * 4, [None] * 4]
    def together(*values):
        return lax.optimization_barrier(values)

    for layer in (1, 0):
        stream, normed, spread, mixed, log_sums, attn_mix, after, normed_two, gate_up, hidden = kept[layer]
        gate, up = gate_up[:, :units], gate_up[:, units:]
        d_hidden = product(branch, down_w[layer])
        sig = jax.nn.sigmoid(gate)
        d_gate = d_hidden * up * sig * (1.0 + gate * (1.0 - sig))
        d_up = d_hidden * gate * sig
        d_gate_up = jnp.concatenate([d_gate, d_up], axis=1).astype(jnp.bfloat16)
        partial, down_term, gate_up_term = together(
            dot_last(d_gate_up, gate_up_w[layer]).astype(jnp.bfloat16),
            dot_first(branch, hidden).astype(jnp.bfloat16),
            dot_first(normed_two, d_gate_up).astype(jnp.bfloat16),
        )
        down_sum, gate_up_sum = collect(layer, down_term), collect(layer, gate_up_term)
        grad_attn, d_after, sums_two, *got = relay(
            behind_norm,
            3 + layer,
            partial,
            [grad, after, gains[layer, 1:]],
            [(owned, D), (2, D)],
            cols_axis,
            carry=[]
            if layer == 1
            else [(0, hidden_out[0]), (1, hidden_out[1]), (1, input_out[1]), (1, weight_sums[1][2]), (1, weight_sums[1][3])],
            behind=[] if layer == 1 else [weight_sums[1][0]],
        )
        if layer == 1:
            result = jnp.where(d_after[0, 0] == d_after[0, 0], result, 0)
            hidden_out.append(lax.psum_scatter(result, "col", scatter_dimension=1, tiled=True))
        else:
            hidden_got[0], hidden_got[1], input_got[1], arrived[1][2], arrived[1][3] = got
        small_sums += [sums_two]
        d_mix, out_term = together(
            product(grad_attn, out_w[layer]).astype(jnp.bfloat16), dot_first(grad_attn, attn_mix).astype(jnp.bfloat16)
        )
        out_sum = collect(layer, out_term)
        d_qkv, arrived[layer][1] = attend_back(
            10 + layer,
            expand(d_mix),
            spread,
            mixed,
            log_sums,
            ids,
            cosines,
            sines,
            heads,
            rows_axis,
            layer,
            gate_up_sum,
        )
        d_qkv = contract(d_qkv)
        partial, qkv_term, bias_grads[layer] = together(
            dot_last(d_qkv, qkv_w[layer]).astype(jnp.bfloat16),
            dot_first(normed, d_qkv).astype(jnp.bfloat16),
            jnp.sum(d_qkv.astype(jnp.float32), axis=0),
        )
        qkv_sum = collect(layer, qkv_term)
        if layer == 0:
            early_sums = lax.psum_scatter(jnp.stack(small_sums), "col", scatter_dimension=2, tiled=True)
            early = jnp.concatenate([early_sums.reshape(6, -1), bias_grads[1].reshape(3, -1), bias_grads[0].reshape(3, -1)])
            early = jnp.sum(lax.all_gather(early, both, axis=0), axis=0)
        branch, grad, sums_one, *got = relay(
            behind_norm,
            5 + layer,
            partial,
            [d_after, mine(stream), gains[layer, :1]],
            [(owned, D), (2, D)],
            cols_axis,
            spread=layer == 0,
            carry=[] if layer == 1 else [(0, down_sum), (0, out_sum), (1, weight_sums[1][0])],
            behind=[hidden_out[1]] if layer == 1 else [early_sums],
        )
        if layer == 0:
            late_sums, arrived[0][0], arrived[0][2], arrived[1][0] = got
        small_sums += [sums_one]
        input_out[layer] = my_features(branch) if layer == 1 else branch

    arrived[0][3] = lax.ppermute(weight_sums[0][3], "section", [(1, 0)])
    hidden_states = jnp.where(
        section == 0, jnp.stack([hidden_out[0], hidden_got[0]]), jnp.stack([hidden_got[1], hidden_out[1]])
    )
    input_grads = jnp.where(section == 0, input_out[0], jnp.stack([input_got[1], input_out[1]])).astype(jnp.float32)
    down_grad, gate_up_grad, out_grad, qkv_grad = (
        jnp.where(section == 0, first, second).astype(jnp.float32)
        + jnp.where(section == 0, first_got, second_got).astype(jnp.float32)
        for first, second, first_got, second_got in zip(*weight_sums, *arrived)
    )
    last = lax.psum(jnp.sum(late_sums, axis=(0, 1)), "row")
    norm_sums = jnp.where(section == 0, jnp.stack([last, early[4:6]]), jnp.stack([early[2:4], early[0:2]]))
    bias_sum = jnp.where(section == 0, early[9:12], early[6:9])
    return (
        hidden_states[None],
        input_grads[None],
        norm_sums[:, 0][None],
        norm_sums[:, 1][None],
        qkv_grad.reshape(qkv_weight.shape),
        bias_sum.reshape(qkv_bias.shape),
        out_grad[None],
        gate_up_grad.reshape(gate_up_weight.shape),
        down_grad[None],
    )


def solution(mesh):
    in_specs = (
        P(None, "row", "col"),
        P(None, "row", "col"),
        P(),
        P("section", None, "col"),
        P("section", None, "col"),
        P("section", "row", None, "col"),
        P("section", None, "col"),
        P("section", "row", "col"),
        P("section", "row", None, "col"),
        P("section", "row", "col"),
    )
    out_specs = (
        P("section", None, "row", "col"),
        P("section", None, "row", "col"),
        P("section", None, "col"),
        P("section", None, "col"),
        P("section", "row", None, "col"),
        P("section", None, "col"),
        P("section", "row", "col"),
        P("section", "row", None, "col"),
        P("section", "row", "col"),
    )
    return jax.shard_map(
        per_device, mesh=mesh, in_specs=in_specs, out_specs=out_specs, check_vma=False
    )
```

```python
import functools

import jax
import jax.numpy as jnp
from jax import lax
from jax.experimental import pallas as pl
from jax.experimental.pallas import tpu as pltpu
from jax.sharding import PartitionSpec as P

D = 2048
HEADS = 32
HEAD_DIM = 64
ROT = 16
LANES = 128
REACH = 256
RELAY_ROWS = 16


epsilon = 1e-05


def dot_last(a, b):
    return lax.dot_general(a, b, (((1,), (1,)), ((), ())), preferred_element_type=jnp.float32)


def dot_first(a, b):
    return lax.dot_general(a, b, (((0,), (0,)), ((), ())), preferred_element_type=jnp.float32)


def lanes_of(rows, head):
    lane = lax.broadcasted_iota(jnp.int32, (rows, LANES), 1)
    return lane // HEAD_DIM == head


def spin(x, cosines, sines):
    lane = lax.broadcasted_iota(jnp.int32, x.shape, 1)
    ahead, behind = pltpu.roll(x, LANES - ROT // 2, 1), pltpu.roll(x, ROT // 2, 1)
    return x * cosines + jnp.where(lane % ROT < ROT // 2, ahead, behind) * sines


def meet(axis, n):
    me = lax.axis_index(axis)
    barrier = pltpu.get_barrier_semaphore()
    for d in range(1, n):
        pl.semaphore_signal(
            barrier, 1, device_id={axis: lax.rem(me + d, n)}, device_id_type=pl.DeviceIdType.MESH
        )
    pl.semaphore_wait(barrier, n - 1)


def remote(source, target, sent, got, axis, device):
    return pltpu.make_async_remote_copy(
        src_ref=source,
        dst_ref=target,
        send_sem=sent,
        recv_sem=got,
        device_id={axis: device},
        device_id_type=pl.DeviceIdType.MESH,
    )


def columns(which, size=LANES):
    return pl.ds(pl.multiple_of(which * size, size), size)


def attend_kernel(heads, n, bq, given, bid_q, bid_k, *refs):
    me = lax.axis_index("row")
    if given:
        spread, mixed, lse_ref, mix, vone, scores, mix_sent, mix_got = refs
    else:
        qkv, cosines, sines, spread, mixed, lse_ref, mix, vone, scores, mix_sent, mix_got = refs[:11]
        leaving, qkv_sent, qkv_got = refs[11:]
    tokens = mix.shape[0]
    seq = n * tokens
    here = pl.ds(pl.multiple_of(me * tokens, tokens), tokens)
    low = jnp.bfloat16
    meet("row", n)

    def parts(t):
        cos, sin = cosines[here, :], sines[here, :]
        query = spin(qkv[:, columns(t)], cos, sin).astype(low) * jnp.asarray(HEAD_DIM**-0.5, low)
        key = spin(qkv[:, columns(n + t)], cos, sin).astype(low)
        return query.astype(low), key, qkv[:, columns(2 * n + t)].astype(low)

    def leave(d):
        to = lax.rem(me + d, n)
        return remote(leaving.at[d - 1], spread.at[:, here], qkv_sent.at[d - 1], qkv_got.at[me], "row", to)

    if not given:
        for d in range(1, n):
            for k, part in enumerate(parts(lax.rem(me + d, n))):
                leaving[d - 1, k] = part
            leave(d).start()
        for k, part in enumerate(parts(me)):
            spread[k, here, :] = part

    def come(row):
        if not given:
            @pl.when(row != me)
            def _():
                there = pl.ds(row * tokens, tokens)
                remote(leaving.at[0], spread.at[:, there], qkv_sent.at[0], qkv_got.at[row], "row", me).wait_recv()

        there = pl.ds(row * tokens, tokens)
        for h in range(heads):
            vone[h, there, :] = jnp.where(lanes_of(tokens, h), spread[2, there, :], jnp.ones((), low))

    def mix_copy(i, device):
        rows = pl.ds(lax.rem(i, tokens // bq) * bq, bq)
        return remote(
            mixed.at[pl.ds(i * bq, bq)], mix.at[rows, columns(me)], mix_sent.at[i], mix_got.at[me, lax.rem(i, tokens // bq)], "row", device
        )

    def block(i, carry):
        rows = pl.ds(pl.multiple_of(i * bq, bq), bq)
        q = spread[0, rows, :]
        bid = bid_q[rows, :]
        begin = i * bq
        ahead = jnp.where(begin + bq < seq, 1, 0)
        qs = [jnp.where(lanes_of(bq, h), q, jnp.zeros((), low)) for h in range(heads)]

        def score(start, size, tops, hide):
            span = pl.ds(pl.multiple_of(start, REACH), size)
            keys = spread[1, span, :]
            if hide:
                visible = bid_k[:, span] <= bid
            found = []
            for h in range(heads):
                s = dot_last(qs[h], keys)
                if hide:
                    s = jnp.where(visible, s, -1e30)
                scores[h, :, span] = s
                top = tops[h]
                for c in range(size // LANES):
                    top = jnp.maximum(top, s[:, c * LANES : (c + 1) * LANES])
                found.append(top)
            return tuple(found)

        tops = tuple(jnp.full((bq, LANES), -1e30, jnp.float32) for _ in range(heads))
        tops = lax.fori_loop(0, i // 2, lambda t, c: score(2 * t * bq, 2 * bq, c, False), tops)
        tops = lax.fori_loop(i // 2 * 2, i, lambda t, c: score(t * bq, bq, c, False), tops)
        tops = score(begin, bq, tops, True)
        tops = lax.fori_loop(0, ahead, lambda t, c: score(begin + bq, REACH, c, True), tops)
        tops = [jnp.max(top, axis=1, keepdims=True) for top in tops]

        def gather(start, size, sums):
            span = pl.ds(pl.multiple_of(start, REACH), size)
            found = []
            for h in range(heads):
                p = jnp.exp(scores[h, :, span] - tops[h]).astype(low)
                found.append(sums[h] + jnp.dot(p, vone[h, span, :], preferred_element_type=jnp.float32))
            return tuple(found)

        sums = tuple(jnp.zeros((bq, LANES), jnp.float32) for _ in range(heads))
        sums = lax.fori_loop(0, (i + 1) // 2, lambda t, c: gather(2 * t * bq, 2 * bq, c), sums)
        sums = lax.fori_loop((i + 1) // 2 * 2, i + 1, lambda t, c: gather(t * bq, bq, c), sums)
        sums = lax.fori_loop(0, ahead, lambda t, c: gather(begin + bq, REACH, c), sums)
        outcome = jnp.zeros((bq, LANES), jnp.float32)
        lse = jnp.zeros((bq, LANES), jnp.float32)
        for h in range(heads):
            totals = pltpu.roll(sums[h], HEAD_DIM, 1)
            outcome = jnp.where(lanes_of(bq, h), sums[h] / totals, outcome)
            lse = jnp.where(lanes_of(bq, h), tops[h] + jnp.log(totals), lse)
        mixed[rows, :] = outcome.astype(low)
        lse_ref[:, rows] = lse.T
        return carry

    per_row = tokens // bq
    for row in range(n):
        if row == 0:
            come(0)
        if row + 1 < n:
            come(row + 1)

        def run(half, carry, row=row):
            i = row * per_row + half
            block(i, 0)

            @pl.when(row == me)
            def _():
                mix[pl.ds(pl.multiple_of(half * bq, bq), bq), columns(me)] = mixed[pl.ds(pl.multiple_of(i * bq, bq), bq), :]

            @pl.when(row != me)
            def _():
                mix_copy(i, row).start()

            return carry

        lax.fori_loop(0, per_row, run, 0)

    if not given:
        for d in range(1, n):
            leave(d).wait_send()
    for i in range(n * per_row):
        @pl.when(i // per_row != me)
        def _(i=i):
            mix_copy(i, me).wait_send()

    for row in range(n):
        @pl.when(row != me)
        def _(row=row):
            for half in range(per_row):
                rows = pl.ds(half * bq, bq)
                remote(
                    mixed.at[pl.ds(0, bq)], mix.at[rows, columns(row)], mix_sent.at[0], mix_got.at[row, half], "row", me
                ).wait_recv()


def attend(number, block_all, heads, n, tokens, qkv=None, cosines=None, sines=None, spread=None, bq=512):
    bq = min(bq, tokens)
    seq = n * tokens
    vmem = pl.BlockSpec(memory_space=pltpu.VMEM)
    low = jnp.bfloat16
    given = spread is not None
    operands = [spread] if given else [qkv, cosines, sines]
    out_shape = [
        jax.ShapeDtypeStruct((3, seq, LANES), low),
        jax.ShapeDtypeStruct((seq, LANES), low),
        jax.ShapeDtypeStruct((LANES, seq), jnp.float32),
        jax.ShapeDtypeStruct((tokens, n * LANES), low),
    ][given:]
    exchange = [
        pltpu.VMEM((n - 1, 3, tokens, LANES), low),
        pltpu.SemaphoreType.DMA((n - 1,)),
        pltpu.SemaphoreType.DMA((n,)),
    ]
    found = pl.pallas_call(
        functools.partial(attend_kernel, heads, n, bq, given),
        in_specs=[vmem] * (2 + len(operands)),
        out_specs=[vmem] * len(out_shape),
        out_shape=out_shape,
        scratch_shapes=[
            pltpu.VMEM((heads, seq, LANES), low),
            pltpu.VMEM((heads, bq, seq), jnp.float32),
            pltpu.SemaphoreType.DMA((seq // bq,)),
            pltpu.SemaphoreType.DMA((n, tokens // bq)),
        ]
        + ([] if given else exchange),
        compiler_params=pltpu.CompilerParams(
            collective_id=number, has_side_effects=True, vmem_limit_bytes=58 * 2**20
        ),
        cost_estimate=pl.CostEstimate(flops=10**10, bytes_accessed=2 * 10**8, transcendentals=0),
    )(block_all.reshape(seq, 1), block_all.reshape(1, seq), *operands)
    return [spread] + list(found) if given else found


def attend_back_kernel(
    heads, n, bq, layer, bid_q, bid_k, d_mix, spread, mixed, lse_ref, cosines, sines, carry, *refs
):
    d_qkv, carried, grads, kone, dk_acc, dv_acc, leaving, g_sent, g_got, back_sent, back_got, carry_sent, carry_got = refs
    section = lax.axis_index("section")
    me = lax.axis_index("row")
    tokens = d_mix.shape[0]
    seq = n * tokens
    per_row = tokens // bq
    blocks = n * per_row
    low = jnp.bfloat16
    zero = jnp.zeros((), low)
    here = pl.ds(pl.multiple_of(me * tokens, tokens), tokens)
    barrier = pltpu.get_barrier_semaphore()
    pl.semaphore_signal(barrier, 1, device_id={"section": 1 - section}, device_id_type=pl.DeviceIdType.MESH)
    for d in range(1, n):
        pl.semaphore_signal(barrier, 1, device_id={"row": lax.rem(me + d, n)}, device_id_type=pl.DeviceIdType.MESH)
    pl.semaphore_wait(barrier, n)
    carry_copy = remote(carry, carried, carry_sent, carry_got, "section", layer)

    def give(d):
        to = lax.rem(me + d, n)
        return remote(d_mix.at[:, columns(to)], grads.at[here], g_sent.at[d - 1], g_got.at[me], "row", to)

    for d in range(1, n):
        give(d).start()

    @pl.when(section != layer)
    def _():
        carry_copy.start()

    grads[here, :] = d_mix[:, columns(me)]
    for h in range(heads):
        kone[h] = jnp.where(lanes_of(seq, h), spread[1], zero).T
    dk_acc[...] = jnp.zeros_like(dk_acc)
    dv_acc[...] = jnp.zeros_like(dv_acc)

    def tile(start, size, dq, hide, stuff):
        qs, gs, lses, deltas, bid = stuff
        span = pl.ds(pl.multiple_of(start, REACH), size)
        keys, values = spread[1, span, :], spread[2, span, :]
        dv, dk = dv_acc[span, :], dk_acc[span, :]
        if hide:
            visible = bid_k[span, :] <= bid
        for h in range(heads):
            s = dot_last(keys, qs[h])
            if hide:
                s = jnp.where(visible, s, -1e30)
            p = jnp.exp(s - lses[h])
            dp = dot_last(values, gs[h])
            ds = (p * (dp - deltas[h])).astype(low)
            dv = dv + jnp.dot(p.astype(low), gs[h], preferred_element_type=jnp.float32)
            dk = dk + jnp.dot(ds, qs[h], preferred_element_type=jnp.float32)
            dq = dq + jnp.dot(kone[h, :, span], ds, preferred_element_type=jnp.float32)
        dv_acc[span, :] = dv
        dk_acc[span, :] = dk
        return dq

    def block(i):
        rows = pl.ds(pl.multiple_of(i * bq, bq), bq)
        q, g = spread[0, rows, :], grads[rows, :]
        product = (g.astype(jnp.float32) * mixed[rows, :].astype(jnp.float32)).T
        span = lambda h: slice(h * HEAD_DIM, (h + 1) * HEAD_DIM)
        deltas = [jnp.sum(product[span(h)], axis=0, keepdims=True) for h in range(heads)]
        lses = [lse_ref[h * HEAD_DIM : h * HEAD_DIM + 1, rows] for h in range(heads)]
        qs = [jnp.where(lanes_of(bq, h), q, zero) for h in range(heads)]
        gs = [jnp.where(lanes_of(bq, h), g, zero) for h in range(heads)]
        stuff = (qs, gs, lses, deltas, bid_q[:, rows])
        begin = i * bq
        ahead = jnp.where(begin + bq < seq, 1, 0)
        dq = jnp.zeros((LANES, bq), jnp.float32)
        dq = lax.fori_loop(0, i, lambda t, c: tile(t * bq, bq, c, False, stuff), dq)
        dq = tile(begin, bq, dq, True, stuff)
        dq = lax.fori_loop(0, ahead, lambda t, c: tile(begin + bq, REACH, c, True, stuff), dq)
        return spin(dq.T * (HEAD_DIM**-0.5), cosines[rows, :], -sines[rows, :]).astype(low)

    def back_copy(k, i, device):
        half = lax.rem(i, per_row)
        rows = pl.ds(pl.multiple_of(half * bq, bq), bq)
        return remote(
            leaving.at[k, pl.ds(pl.multiple_of(i * bq, bq), bq)],
            d_qkv.at[rows, columns(k * n + me)],
            back_sent.at[k, i],
            back_got.at[k, me, half],
            "row",
            device,
        )

    def send(k, i, values):
        row = i // per_row
        half = lax.rem(i, per_row)

        @pl.when(row == me)
        def _():
            d_qkv[pl.ds(pl.multiple_of(half * bq, bq), bq), columns(k * n + me)] = values

        @pl.when(row != me)
        def _():
            leaving[k, pl.ds(pl.multiple_of(i * bq, bq), bq), :] = values
            back_copy(k, i, row).start()

    def keys_done(i):
        rows = pl.ds(pl.multiple_of(i * bq, bq), bq)
        send(1, i, spin(dk_acc[rows, :], cosines[rows, :], -sines[rows, :]).astype(low))
        send(2, i, dv_acc[rows, :].astype(low))

    for row in range(n - 1, -1, -1):
        @pl.when(row != me)
        def _(row=row):
            there = pl.ds(row * tokens, tokens)
            remote(d_mix.at[:, columns(0)], grads.at[there], g_sent.at[0], g_got.at[row], "row", me).wait_recv()

        def run(step, carry, row=row):
            i = row * per_row + per_row - 1 - step
            send(0, i, block(i))

            @pl.when(i + 1 < blocks)
            def _():
                keys_done(i + 1)

            return carry

        lax.fori_loop(0, per_row, run, 0)
    keys_done(0)

    for d in range(1, n):
        give(d).wait_send()

    def settle(i, carry):
        @pl.when(i // per_row != me)
        def _():
            half = lax.rem(i, per_row)
            rows = pl.ds(pl.multiple_of(half * bq, bq), bq)
            for k in range(3):
                back_copy(k, i, me).wait_send()
                remote(
                    leaving.at[k, pl.ds(0, bq)],
                    d_qkv.at[rows, columns(k * n + i // per_row)],
                    back_sent.at[k, 0],
                    back_got.at[k, i // per_row, half],
                    "row",
                    me,
                ).wait_recv()

        return carry

    lax.fori_loop(0, blocks, settle, 0)

    @pl.when(section != layer)
    def _():
        carry_copy.wait_send()

    @pl.when(section == layer)
    def _():
        carry_copy.wait_recv()


def attend_back(number, d_mix, spread, mixed, lse, block_all, cosines, sines, heads, n, layer, carry, bq=512):
    tokens = d_mix.shape[0]
    bq = min(bq, tokens)
    seq = n * tokens
    vmem = pl.BlockSpec(memory_space=pltpu.VMEM)
    low = jnp.bfloat16
    return pl.pallas_call(
        functools.partial(attend_back_kernel, heads, n, bq, layer),
        in_specs=[vmem] * 8 + [pl.BlockSpec(memory_space=pl.ANY)],
        out_specs=[vmem, pl.BlockSpec(memory_space=pl.ANY)],
        out_shape=[jax.ShapeDtypeStruct((tokens, 3 * n * LANES), low), jax.ShapeDtypeStruct(carry.shape, carry.dtype)],
        scratch_shapes=[
            pltpu.VMEM((seq, LANES), low),
            pltpu.VMEM((heads, LANES, seq), low),
            pltpu.VMEM((seq, LANES), jnp.float32),
            pltpu.VMEM((seq, LANES), jnp.float32),
            pltpu.VMEM((3, seq, LANES), low),
            pltpu.SemaphoreType.DMA((n - 1,)),
            pltpu.SemaphoreType.DMA((n,)),
            pltpu.SemaphoreType.DMA((3, seq // bq)),
            pltpu.SemaphoreType.DMA((3, n, tokens // bq)),
            pltpu.SemaphoreType.DMA,
            pltpu.SemaphoreType.DMA,
        ],
        compiler_params=pltpu.CompilerParams(
            collective_id=number, has_side_effects=True, vmem_limit_bytes=58 * 2**20
        ),
        cost_estimate=pl.CostEstimate(flops=10**10, bytes_accessed=3 * 10**8, transcendentals=0),
    )(block_all.reshape(1, seq), block_all.reshape(seq, 1), d_mix, spread, mixed, lse, cosines, sines, carry)


def norm_parts(values):
    mean = jnp.mean(values, axis=-1, keepdims=True)
    spread = jnp.mean(values * values, axis=-1, keepdims=True) - mean * mean
    return mean, lax.rsqrt(spread + epsilon)


def after_attention(total, c, ins, outs):
    stream, gain, shift = ins
    (after_ref,) = outs
    after = stream[c].astype(jnp.float32) + total
    after_ref[c] = after
    values = after.astype(jnp.bfloat16).astype(jnp.float32)
    mean, inverse = norm_parts(values)
    return ((values - mean) * inverse * gain[...] + shift[...]).astype(jnp.bfloat16)


def after_hidden(total, c, ins, outs):
    (after,) = ins
    return (after[c] + total).astype(jnp.bfloat16)


def behind_norm(total, c, ins, outs):
    grad, values_ref, gain = ins
    grad_ref, sums = outs
    values = values_ref[c].astype(jnp.bfloat16).astype(jnp.float32)
    mean, inverse = norm_parts(values)
    centred = (values - mean) * inverse
    scaled = total * gain[...]
    back = inverse * (
        scaled
        - jnp.mean(scaled, axis=-1, keepdims=True)
        - centred * jnp.mean(scaled * centred, axis=-1, keepdims=True)
    )
    given = grad[c] + back
    grad_ref[c] = given
    here = [jnp.sum(total * centred, axis=0, keepdims=True), jnp.sum(total, axis=0, keepdims=True)]

    @pl.when(c == 0)
    def _():
        sums[...] = jnp.zeros_like(sums)

    sums[...] += jnp.concatenate(here, axis=0)
    return given.astype(jnp.bfloat16)


def relay_kernel(
    middle, n_ins, n_outs, layers, n_after, polish, parts, n_row, n, chunks, lag, spread, partial, *refs
):
    ins, carry, refs = refs[:n_ins], refs[n_ins : n_ins + len(layers)], refs[n_ins + len(layers) + n_after :]
    whole, outs, refs = refs[0], refs[1 : 1 + n_outs], refs[1 + n_outs :]
    carried, refs = refs[: len(layers)], refs[len(layers) :]
    if parts:
        ins, (weights, bias, cosines, sines) = ins[:-4], ins[-4:]
        outs, landed = outs[:-1], outs[-1]
        *refs, leaving, part_sent, part_got, weight, weight_got = refs
        weight_copy = pltpu.make_async_copy(weights.at[pl.ds(weight.shape[0], weight.shape[0])], weight, weight_got)
        weight_copy.start()
    if polish:
        ins, (gain, shift) = ins[:-2], ins[-2:]
        outs, polished = outs[:-1], outs[-1]
    if spread:
        outs, all_sums = outs[:-1], outs[-1]
    arrived, outgoing, total, sum_sent, sum_got, block_sent, block_got, carry_sent, carry_got, last_sent, last_got = refs
    section, i = lax.axis_index("section"), lax.axis_index("col")
    width = whole.shape[-1]
    first, last = i == 0, i == n - 1

    barrier = pltpu.get_barrier_semaphore()

    def greet(**place):
        pl.semaphore_signal(barrier, 1, device_id=place, device_id_type=pl.DeviceIdType.MESH)

    if spread:
        for d in range(1, 2 * n):
            greet(section=lax.rem(section + d // n, 2), col=lax.rem(i + d, n))
        pl.semaphore_wait(barrier, 2 * n - 1)
    else:
        greet(section=1 - section)
        me = lax.axis_index("row")
        row_peers = n_row - 1 if parts else 0
        for d in range(1, row_peers + 1):
            greet(row=lax.rem(me + d, n_row))

        @pl.when(i > 0)
        def _():
            greet(col=i - 1)

        @pl.when(i < n - 1)
        def _():
            greet(col=i + 1)

        @pl.when(first | last)
        def _():
            pl.semaphore_wait(barrier, 2 + row_peers)

        @pl.when((i > 0) & (i < n - 1))
        def _():
            pl.semaphore_wait(barrier, 3 + row_peers)

    def carry_copy(k):
        return remote(carry[k], carried[k], carry_sent.at[k], carry_got.at[k], "section", layers[k])

    for k, layer in enumerate(layers):
        @pl.when(section != layer)
        def _(k=k):
            carry_copy(k).start()

    def remote_col(source, target, sent, got, device):
        return remote(source, target, sent, got, "col", device)

    def sum_copy(c, j, right):
        slot = j + 1 if right else j
        return remote_col(
            outgoing.at[c, j], arrived.at[c, slot], sum_sent.at[c, j], sum_got.at[c, slot], i + 1 if right else i - 1
        )

    def block_copy(c, o, right, own=False):
        sent = n if own and not right else o
        return remote_col(whole.at[c, o], whole.at[c, o], block_sent.at[c, sent], block_got.at[0, c, o], i + 1 if right else i - 1)

    def slice_copy(c, d):
        to = lax.rem(i + d, n)
        return pltpu.make_async_remote_copy(
            src_ref=outgoing.at[c, i, :, pl.ds(pl.multiple_of(to * width, 128), width)],
            dst_ref=whole.at[section, c, i],
            send_sem=block_sent.at[c, d],
            recv_sem=block_got.at[section, c, i],
            device_id={"section": 0, "col": to},
            device_id_type=pl.DeviceIdType.MESH,
        )

    def arrive(c, slot):
        remote_col(outgoing.at[c, 0], arrived.at[c, slot], sum_sent.at[c, 0], sum_got.at[c, slot], i).wait_recv()

    def work(c, o):
        if polish:
            values = whole[c, o].astype(jnp.float32)
            mean, inverse = norm_parts(values)
            polished[c, o] = ((values - mean) * inverse * gain[...] + shift[...]).astype(jnp.bfloat16)

    rows = whole.shape[-2]
    per = max(1, min(chunks, LANES // (n * rows)))
    many = per * n * rows
    unit = max(1, n * per // n_row)
    tokens = chunks * n * rows

    def part_rows(source, b):
        return pl.ds(pl.multiple_of(source * tokens + b * many, many), many)

    def part_copy(b, d):
        to = lax.rem(me + d, n_row)
        return remote(
            leaving.at[d - 1, :, part_rows(0, b)],
            landed.at[:, part_rows(me, b)],
            part_sent.at[d - 1, b],
            part_got.at[me, b],
            "row",
            to,
        )

    def project(b, d):
        values = (polished if polish else whole)[pl.ds(b * per, per)].reshape(many, whole.shape[-1])
        here, there = part_rows(me, b), part_rows(0, b)
        t = lax.rem(me + d, n_row)
        for k in range(parts):
            column = columns(k * n_row + t)
            found = jnp.dot(values, weight[:, column], preferred_element_type=jnp.float32) + bias[:, column]
            if parts == 3 and k < 2:
                found = spin(found, cosines[here, :], sines[here, :])
            found = found.astype(jnp.bfloat16)
            if parts == 3 and k == 0:
                found = (found * jnp.asarray(HEAD_DIM**-0.5, jnp.bfloat16)).astype(jnp.bfloat16)

            @pl.when(d > 0)
            def _(k=k, found=found):
                leaving[d - 1, k, there, :] = found

            @pl.when(d == 0)
            def _(k=k, found=found):
                landed[k, here, :] = found

        @pl.when(d > 0)
        def _():
            part_copy(b, d).start()

    def sums_copy(d):
        to = lax.rem(i + d, n)
        return pltpu.make_async_remote_copy(
            src_ref=outs[-1].at[:, pl.ds(pl.multiple_of(to * width, 128), width)],
            dst_ref=all_sums.at[section, i],
            send_sem=last_sent.at[d],
            recv_sem=last_got.at[section, i],
            device_id={"section": 0, "col": to},
            device_id_type=pl.DeviceIdType.MESH,
        )

    def sums_arrive(s, o):
        return pltpu.make_async_remote_copy(
            src_ref=outs[-1].at[:, pl.ds(0, width)],
            dst_ref=all_sums.at[s, o],
            send_sem=last_sent.at[0],
            recv_sem=last_got.at[s, o],
            device_id={"section": 0, "col": o},
            device_id_type=pl.DeviceIdType.MESH,
        )

    def middle_slot(k):
        return jnp.maximum(lag * k + n - 1 - k, lag * (n - 1 - k) + k)

    def at(now, slot, allowed):
        since = now - slot
        c = jnp.maximum(since, 0) // n
        return c, allowed & (since >= 0) & (lax.rem(jnp.maximum(since, 0), n) == 0) & (since < n * chunks)

    def step(now, carry):
        for j in range(n - 1, 0, -1):
            c, due = at(now, lag * i + n - 1 - j, i < j)

            @pl.when(due & first)
            def _(c=c, j=j):
                outgoing[c, j] = partial[c, j]

            @pl.when(due & (i > 0))
            def _(c=c, j=j):
                arrive(c, j + 1)
                both = arrived[c, j + 1].astype(jnp.float32) + partial[c, j].astype(jnp.float32)
                outgoing[c, j] = both.astype(jnp.bfloat16)

            @pl.when(due)
            def _(c=c, j=j):
                sum_copy(c, j, True).start()

        for j in range(n - 1):
            c, due = at(now, lag * (n - 1 - i) + j, i > j)

            @pl.when(due & last)
            def _(c=c, j=j):
                outgoing[c, j] = partial[c, j]

            @pl.when(due & (i < n - 1))
            def _(c=c, j=j):
                arrive(c, j)
                both = arrived[c, j].astype(jnp.float32) + partial[c, j].astype(jnp.float32)
                outgoing[c, j] = both.astype(jnp.bfloat16)

            @pl.when(due)
            def _(c=c, j=j):
                sum_copy(c, j, False).start()

        c, due = at(now, middle_slot(i), i >= 0)

        @pl.when(due)
        def _():
            total[...] = partial[c, i].astype(jnp.float32)

        @pl.when(due & (i > 0))
        def _():
            arrive(c, i + 1)
            total[...] += arrived[c, i + 1].astype(jnp.float32)

        @pl.when(due & (i < n - 1))
        def _():
            arrive(c, i)
            total[...] += arrived[c, i].astype(jnp.float32)

        @pl.when(due)
        def _():
            block = middle(total[...], c, ins, outs)
            if spread:
                outgoing[c, i] = block
                for d in range(1, n):
                    slice_copy(c, d).start()

                @pl.when(section == 0)
                def _():
                    whole[0, c, i] = outgoing[c, i, :, pl.ds(pl.multiple_of(i * width, 128), width)]

                @pl.when(section != 0)
                def _():
                    slice_copy(c, 0).start()

            else:
                whole[c, i] = block
                work(c, i)

        if spread:
            return carry

        @pl.when(due & (i < n - 1))
        def _():
            block_copy(c, i, True, own=True).start()

        @pl.when(due & (i > 0))
        def _():
            block_copy(c, i, False, own=True).start()

        for o in range(n - 1):
            c, due = at(now, middle_slot(o) + lag * (i - o), i > o)

            @pl.when(due)
            def _(c=c, o=o):
                block_copy(c, o, True).wait_recv()

            @pl.when(due & (i < n - 1))
            def _(c=c, o=o):
                block_copy(c, o, True).start()

            @pl.when(due)
            def _(c=c, o=o):
                work(c, o)

        for o in range(1, n):
            c, due = at(now, middle_slot(o) + lag * (o - i), i < o)

            @pl.when(due)
            def _(c=c, o=o):
                block_copy(c, o, False).wait_recv()

            @pl.when(due & (i > 0))
            def _(c=c, o=o):
                block_copy(c, o, False).start()

            @pl.when(due)
            def _(c=c, o=o):
                work(c, o)

        if parts:
            since = now - (n * (per - 1) + 2 * lag * (n - 1))
            given = jnp.maximum(since, 0)
            turn = lax.rem(given, n * per) // unit

            @pl.when(since == 0)
            def _():
                weight_copy.wait()

            @pl.when((since >= 0) & (lax.rem(given, unit) == 0) & (turn < n_row) & (given < n * chunks))
            def _():
                project(given // (n * per), lax.rem(turn + 1, n_row))

        return carry

    steps = n * (chunks - 1) + 2 * lag * (n - 1) + 1
    lax.fori_loop(0, steps + (unit * (n_row - 1) if parts else 0), step, 0)

    if spread:
        for d in range(1, n):
            sums_copy(d).start()

        @pl.when(section == 0)
        def _():
            all_sums[0, i] = outs[-1][:, pl.ds(pl.multiple_of(i * width, 128), width)]

        @pl.when(section != 0)
        def _():
            sums_copy(0).start()

    def slice_arrives(c, s, o):
        return pltpu.make_async_remote_copy(
            src_ref=outgoing.at[c, 0, :, pl.ds(0, width)],
            dst_ref=whole.at[s, c, o],
            send_sem=block_sent.at[c, 0],
            recv_sem=block_got.at[s, c, o],
            device_id={"section": 0, "col": o},
            device_id_type=pl.DeviceIdType.MESH,
        )

    def settle(c, carry):
        for j in range(n):
            @pl.when(j != i)
            def _(j=j):
                sum_copy(c, j, True).wait_send()

        if spread:
            for d in range(1, n):
                slice_copy(c, d).wait_send()

            @pl.when(section != 0)
            def _():
                slice_copy(c, 0).wait_send()

            for s in range(2):
                for o in range(n):
                    @pl.when((section == 0) & ((s == 1) | (o != i)))
                    def _(s=s, o=o):
                        slice_arrives(c, s, o).wait_recv()

            return carry
        for o in range(n):
            @pl.when((o <= i) & (i < n - 1))
            def _(o=o):
                block_copy(c, o, True).wait_send()

            @pl.when((o > i) & (i > 0))
            def _(o=o):
                block_copy(c, o, True).wait_send()

        @pl.when(i > 0)
        def _():
            block_copy(c, i, False, own=True).wait_send()

        return carry

    lax.fori_loop(0, chunks, settle, 0)
    if spread:
        for d in range(1, n):
            sums_copy(d).wait_send()

        @pl.when(section != 0)
        def _():
            sums_copy(0).wait_send()

        for s in range(2):
            for o in range(n):
                @pl.when((section == 0) & ((s == 1) | (o != i)))
                def _(s=s, o=o):
                    sums_arrive(s, o).wait_recv()

    if parts:
        def settle_parts(b, carry):
            for d in range(1, n_row):
                part_copy(b, d).wait_send()
                source = lax.rem(me + d, n_row)
                remote(
                    leaving.at[0, :, part_rows(0, b)],
                    landed.at[:, part_rows(source, b)],
                    part_sent.at[0, b],
                    part_got.at[source, b],
                    "row",
                    source,
                ).wait_recv()
            return carry

        lax.fori_loop(0, chunks // per, settle_parts, 0)

    for k, layer in enumerate(layers):
        @pl.when(section != layer)
        def _(k=k):
            carry_copy(k).wait_send()

        @pl.when(section == layer)
        def _(k=k):
            carry_copy(k).wait_recv()


def relay(middle, number, partial, ins, outs, n, spread=False, carry=(), behind=(), polish=(), project=(), n_row=1, lag=3, rows=RELAY_ROWS):
    tokens, features = partial.shape
    owned = tokens // n
    chunks = owned // rows
    blocks = lambda values: values.reshape(chunks, rows, features) if values.shape[0] == owned else values
    ins = [blocks(values) for values in ins] + list(polish) + list(project)
    parts = project[0].shape[1] // (n_row * LANES) if project else 0
    batches = chunks // max(1, min(chunks, LANES // (n * rows)))
    outs = list(outs) + ([(tokens, features)] if polish else []) + ([(parts, n_row * tokens, LANES)] if parts else []) + ([(2, n, 2, features // n)] if spread else [])
    out_shapes = [
        jax.ShapeDtypeStruct(
            (2, chunks, n, rows, features // n) if spread else (chunks, n, rows, features), jnp.bfloat16
        )
    ] + [
        jax.ShapeDtypeStruct((chunks, n, rows, features), jnp.bfloat16)
        if shape[0] == tokens
        else jax.ShapeDtypeStruct(shape, jnp.bfloat16)
        if shape[-1] == LANES
        else jax.ShapeDtypeStruct((chunks, rows, features) if shape[0] == owned else shape, jnp.float32)
        for shape in outs
    ]
    vmem, anywhere = pl.BlockSpec(memory_space=pltpu.VMEM), pl.BlockSpec(memory_space=pl.ANY)
    specs = [vmem] * (1 + len(ins))
    if project:
        specs[-4] = anywhere
    layers = tuple(layer for layer, _ in carry)
    carry = [values for _, values in carry]
    whole, *rest = pl.pallas_call(
        functools.partial(relay_kernel, middle, len(ins), len(outs), layers, len(behind), bool(polish), parts, n_row, n, chunks, lag, spread),
        in_specs=specs + [anywhere] * (len(carry) + len(behind)),
        out_specs=[vmem] * len(out_shapes) + [anywhere] * len(carry),
        out_shape=out_shapes + [jax.ShapeDtypeStruct(values.shape, values.dtype) for values in carry],
        scratch_shapes=[
            pltpu.VMEM((chunks, n + 1, rows, features), jnp.bfloat16),
            pltpu.VMEM((chunks, n, rows, features), jnp.bfloat16),
            pltpu.VMEM((rows, features), jnp.float32),
            pltpu.SemaphoreType.DMA((chunks, n)),
            pltpu.SemaphoreType.DMA((chunks, n + 1)),
            pltpu.SemaphoreType.DMA((chunks, n + 1)),
            pltpu.SemaphoreType.DMA((2 if spread else 1, chunks, n)),
            pltpu.SemaphoreType.DMA((max(1, len(carry)),)),
            pltpu.SemaphoreType.DMA((max(1, len(carry)),)),
            pltpu.SemaphoreType.DMA((n,)),
            pltpu.SemaphoreType.DMA((2, n)),
        ]
        + (
            [
                pltpu.VMEM((n_row - 1, parts, tokens, LANES), jnp.bfloat16),
                pltpu.SemaphoreType.DMA((n_row - 1, batches)),
                pltpu.SemaphoreType.DMA((n_row, batches)),
                pltpu.VMEM((features, project[0].shape[1]), jnp.bfloat16),
                pltpu.SemaphoreType.DMA,
            ]
            if parts
            else []
        ),
        compiler_params=pltpu.CompilerParams(
            collective_id=number, has_side_effects=True, vmem_limit_bytes=56 * 2**20
        ),
        cost_estimate=pl.CostEstimate(flops=0, bytes_accessed=35 * 10**7, transcendentals=0),
    )(partial.reshape(chunks, n, rows, features), *ins, *carry, *behind)
    shapes = {(chunks, rows, features): (owned, features), (chunks, n, rows, features): (tokens, features)}
    rest = [values.reshape(shapes.get(values.shape, values.shape)) for values in rest]
    return [whole.reshape((2, tokens, -1) if spread else (tokens, -1))] + rest


def gather_kernel(n, chunks, lag, own, small, angles, whole, smalls, normed, cosines, sines, sent, got, small_sent, small_got):
    section, i = lax.axis_index("section"), lax.axis_index("col")
    rows, width = own.shape[0] // chunks, own.shape[1]
    others = [(s, d) for s in range(2) for d in range(n) if (s, d) != (0, 0)]
    place = lambda s, d: {"section": lax.rem(section + s, 2), "col": lax.rem(i + d, n)}
    barrier = pltpu.get_barrier_semaphore()
    for s, d in others:
        pl.semaphore_signal(barrier, 1, device_id=place(s, d), device_id_type=pl.DeviceIdType.MESH)
    pl.semaphore_wait(barrier, len(others))

    def small_copy(s, d):
        return pltpu.make_async_remote_copy(
            src_ref=small,
            dst_ref=smalls.at[section, i],
            send_sem=small_sent.at[s, d],
            recv_sem=small_got.at[section, i],
            device_id=place(s, d),
            device_id_type=pl.DeviceIdType.MESH,
        )

    for s, d in others:
        small_copy(s, d).start()
    smalls[section, i] = small[...]

    def small_arrives(s, d):
        from_s, from_d = lax.rem(section + s, 2), lax.rem(i + d, n)
        return pltpu.make_async_remote_copy(
            src_ref=small,
            dst_ref=smalls.at[from_s, from_d],
            send_sem=small_sent.at[s, d],
            recv_sem=small_got.at[from_s, from_d],
            device_id=place(s, d),
            device_id_type=pl.DeviceIdType.MESH,
        )

    def norm(c):
        here = pl.ds(pl.multiple_of(c * rows, rows), rows)
        values = whole[here, :].astype(jnp.float32)
        mean, inverse = norm_parts(values)
        for o in range(n):
            part = slice(o * width, (o + 1) * width)
            gain, shift = smalls[0, o, 0:1, :], smalls[0, o, 2:3, :]
            normed[here, part] = ((values[:, part] - mean) * inverse * gain + shift).astype(jnp.bfloat16)

    def block(c, o, right, mine=False):
        part = whole.at[pl.ds(pl.multiple_of(c * rows, rows), rows), columns(o, width)]
        return remote(
            part, part, sent.at[c, n if mine and not right else o], got.at[c, o], "col", i + 1 if right else i - 1
        )

    def at(now, slot, allowed):
        since = jnp.maximum(now - slot, 0)
        return since // (n - 1), allowed & (now >= slot) & (lax.rem(since, n - 1) == 0) & (since < (n - 1) * chunks)

    def step(now, carry):
        c, due = at(now, 0, i >= 0)

        @pl.when(due)
        def _():
            here = pl.ds(pl.multiple_of(c * rows, rows), rows)
            whole[here, columns(i, width)] = own[here, :]

        @pl.when(due & (i < n - 1))
        def _():
            block(c, i, True, True).start()

        @pl.when(due & (i > 0))
        def _():
            block(c, i, False, True).start()

        for o in range(n):
            c, due = at(now, lag * jnp.abs(i - o), i != o)

            @pl.when(due)
            def _(c=c, o=o):
                block(c, o, True).wait_recv()

            @pl.when(due & (i > o) & (i < n - 1))
            def _(c=c, o=o):
                block(c, o, True).start()

            @pl.when(due & (i < o) & (i > 0))
            def _(c=c, o=o):
                block(c, o, False).start()

        c, due = at(now, lag * (n - 1), i >= 0)

        @pl.when(due)
        def _():
            norm(c)

        return carry

    turns = angles.shape[0] // 2
    lane = lax.broadcasted_iota(jnp.int32, (turns, LANES), 1)
    place_of = lax.broadcasted_iota(jnp.int32, (turns, LANES), 0)
    turned = lane % HEAD_DIM < 2 * turns
    picked = jnp.where(turned & (lane % turns == place_of), 1.0, 0.0)
    sign = jnp.where(lane % HEAD_DIM < turns, -1.0, 1.0)

    def spread_out(table, pick):
        return lax.dot_general(
            table, pick, (((0,), (0,)), ((), ())), precision=lax.Precision.HIGHEST, preferred_element_type=jnp.float32
        )

    still = jnp.where(turned[:1], 0.0, 1.0)
    cosines[...] = spread_out(angles[:turns, :], picked) + still
    sines[...] = spread_out(angles[turns:, :], picked * sign)
    for s, d in others:
        small_arrives(s, d).wait_recv()

    lax.fori_loop(0, (n - 1) * (chunks - 1) + lag * (n - 1) + 1, step, 0)

    def settle(c, carry):
        for o in range(n):
            @pl.when(((o <= i) & (i < n - 1)) | ((o > i) & (i > 0)))
            def _(o=o):
                block(c, o, True).wait_send()

        @pl.when(i > 0)
        def _():
            block(c, i, False, True).wait_send()

        return carry

    lax.fori_loop(0, chunks, settle, 0)
    for s, d in others:
        small_copy(s, d).wait_send()


def gathered(number, own, small, angles, n, lag=3, rows=64):
    tokens, width = own.shape
    chunks = tokens // rows
    vmem = pl.BlockSpec(memory_space=pltpu.VMEM)
    return pl.pallas_call(
        functools.partial(gather_kernel, n, chunks, lag),
        in_specs=[vmem] * 3,
        out_specs=[vmem] * 5,
        out_shape=[
            jax.ShapeDtypeStruct((tokens, n * width), own.dtype),
            jax.ShapeDtypeStruct((2, n) + small.shape, small.dtype),
            jax.ShapeDtypeStruct((tokens, n * width), own.dtype),
            jax.ShapeDtypeStruct((angles.shape[1], LANES), jnp.float32),
            jax.ShapeDtypeStruct((angles.shape[1], LANES), jnp.float32),
        ],
        scratch_shapes=[
            pltpu.SemaphoreType.DMA((chunks, n + 1)),
            pltpu.SemaphoreType.DMA((chunks, n)),
            pltpu.SemaphoreType.DMA((2, n)),
            pltpu.SemaphoreType.DMA((2, n)),
        ],
        compiler_params=pltpu.CompilerParams(
            collective_id=number, has_side_effects=True, vmem_limit_bytes=40 * 2**20
        ),
        cost_estimate=pl.CostEstimate(flops=0, bytes_accessed=25 * 10**7, transcendentals=0),
    )(own, small, angles)


def rotary_angles(positions):
    half_dims = ROT // 2
    inverse_freq = 1.0 / 10000.0 ** (jnp.arange(half_dims, dtype=jnp.float32) * 2.0 / ROT)
    angles = positions.astype(jnp.float32)[None, :] * inverse_freq[:, None]
    return jnp.concatenate([jnp.cos(angles), jnp.sin(angles)])


def hold(values, behind):
    anywhere = pl.BlockSpec(memory_space=pl.ANY)
    return pl.pallas_call(
        lambda *refs: None,
        in_specs=[anywhere] * (1 + len(behind)),
        out_specs=anywhere,
        out_shape=jax.ShapeDtypeStruct(values.shape, values.dtype),
        input_output_aliases={0: 0},
    )(values, *behind)


def product(left, right):
    return jnp.dot(left, right, preferred_element_type=jnp.float32)


def per_device(
    inputs,
    cotangent,
    block_ids,
    norm_gains,
    norm_shifts,
    qkv_weight,
    qkv_bias,
    out_weight,
    gate_up_weight,
    down_weight,
):
    section = lax.axis_index("section")
    row = lax.axis_index("row")
    col = lax.axis_index("col")
    rows_axis = lax.axis_size("row")
    cols_axis = lax.axis_size("col")
    tokens, width = inputs.shape[1:]
    owned = tokens // cols_axis
    units = down_weight.shape[2]
    seq = tokens * rows_axis
    both = ("section", "row")
    whole_lanes = width == rows_axis * LANES
    heads = LANES // HEAD_DIM if whole_lanes else 1
    copies = 1 if whole_lanes else rows_axis * HEAD_DIM // width

    def expand(values):
        if whole_lanes:
            return values
        rows = values.shape[0]
        values = values.reshape(rows, -1, width // HEAD_DIM, HEAD_DIM)
        values = jnp.pad(jnp.repeat(values, copies, axis=2), ((0, 0), (0, 0), (0, 0), (0, LANES - HEAD_DIM)))
        return values.reshape(rows, -1)

    def contract(values):
        if whole_lanes:
            return values
        values = values.reshape(tokens, -1, rows_axis, LANES)[:, :, ::copies, :HEAD_DIM]
        return values.reshape(tokens, -1)

    def weights_of(block):
        block = block[0].reshape(block.shape[1], -1)
        return lax.all_gather(block, both, axis=0, tiled=True).reshape(2, D, -1)

    def mine(values):
        blocks = values.reshape(owned // RELAY_ROWS, cols_axis, RELAY_ROWS, -1)
        return lax.dynamic_index_in_dim(blocks, col, 1, keepdims=False).reshape(owned, -1)

    def my_features(values):
        return lax.dynamic_slice_in_dim(values, col * width, width, 1)

    own_small = jnp.concatenate([norm_gains[0], norm_shifts[0], qkv_bias[0], jnp.zeros((1, width), jnp.float32)])
    angles = rotary_angles(jnp.arange(seq, dtype=jnp.int32))
    stream, small, normed, cosines, sines = gathered(
        7, lax.dynamic_index_in_dim(inputs, section, 0, keepdims=False), own_small, angles, cols_axis
    )
    whole_small = small.transpose(0, 2, 1, 3).reshape(2, own_small.shape[0], D)
    gains, shifts = whole_small[:, :2], whole_small[:, 2:4]
    bias = lax.dynamic_index_in_dim(small, col, 1, keepdims=False)[:, 4:7].reshape(2, -1)

    qkv_w = weights_of(qkv_weight)
    out_w = weights_of(out_weight)
    gate_up_w = weights_of(gate_up_weight)
    down_w = weights_of(down_weight)

    ids = lax.dynamic_index_in_dim(block_ids, section, 0, keepdims=False)
    kept = []
    hidden_out = []

    def gathered_half(which, half):
        values = lax.dynamic_index_in_dim(cotangent, which, 0, keepdims=False)
        values = values[half * (tokens // 2) : (half + 1) * (tokens // 2)]
        return lax.all_gather(values, "col", axis=1, tiled=True)

    first_half = gathered_half(section, 0)
    waited = [first_half]
    for layer in range(2):
        if layer == 0:
            qkv = expand(product(normed, qkv_w[0]) + bias[0])
            spread, mixed, log_sums, attn_mix = attend(
                8, ids, heads, rows_axis, tokens, qkv=qkv, cosines=cosines, sines=sines
            )
        else:
            here = section + jnp.where(hidden_out[0][0, 0] == hidden_out[0][0, 0], 0, 1)
            second_half = gathered_half(here, 1)
            waited = [second_half]
            spread, mixed, log_sums, attn_mix = attend(9, ids, heads, rows_axis, tokens, spread=spread)
        attn_mix = contract(attn_mix)
        normed_two, after = relay(
            after_attention,
            layer,
            product(attn_mix, out_w[layer].T).astype(jnp.bfloat16),
            [mine(stream), gains[layer, 1:], shifts[layer, 1:]],
            [(owned, D)],
            cols_axis,
            behind=waited,
        )
        gate_up = product(normed_two, gate_up_w[layer])
        gate, up = gate_up[:, :units], gate_up[:, units:]
        hidden = (jax.nn.silu(gate) * up).astype(jnp.bfloat16)
        kept.append((stream, normed, spread, mixed, log_sums, attn_mix, after, normed_two, gate_up, hidden))
        partial = product(hidden, down_w[layer].T)
        if layer == 0:
            stream, normed, spread = relay(
                after_hidden,
                2,
                partial.astype(jnp.bfloat16),
                [after],
                [],
                cols_axis,
                polish=(gains[1, :1], shifts[1, :1]),
                project=(expand(qkv_w.reshape(2 * D, -1)), expand(bias[1:]), cosines, sines),
                n_row=rows_axis,
            )
            hidden_out.append(my_features(stream))
        else:
            blocks = partial.reshape(owned // RELAY_ROWS, cols_axis, RELAY_ROWS, D)
            owner = lax.broadcasted_iota(jnp.int32, blocks.shape, 1) == col
            blocks = blocks + jnp.where(owner, after.reshape(-1, 1, RELAY_ROWS, D), 0.0)
            result = blocks.reshape(tokens, D).astype(jnp.bfloat16)

    branch = jnp.concatenate([first_half, second_half])
    grad = mine(branch).astype(jnp.float32)
    weight_sums = [[], []]
    small_sums = []
    bias_grads = [None, None]
    input_out = [None, None]
    input_got = [None, None]
    hidden_got = [None, None]

    def collect(layer, term):
        weight_sums[layer].append(lax.psum_scatter(term, "row", scatter_dimension=0, tiled=True))
        return weight_sums[layer][-1]

    arrived = [[None] * 3, [None] * 3]
    def together(*values):
        return lax.optimization_barrier(values)

    for layer in (1, 0):
        stream, normed, spread, mixed, log_sums, attn_mix, after, normed_two, gate_up, hidden = kept[layer]
        gate, up = gate_up[:, :units], gate_up[:, units:]
        d_hidden = product(branch, down_w[layer])
        sig = jax.nn.sigmoid(gate)
        d_gate = d_hidden * up * sig * (1.0 + gate * (1.0 - sig))
        d_up = d_hidden * gate * sig
        d_gate_up = jnp.concatenate([d_gate, d_up], axis=1).astype(jnp.bfloat16)
        partial, down_term, gate_up_term = together(
            dot_last(d_gate_up, gate_up_w[layer]).astype(jnp.bfloat16),
            dot_first(branch, hidden).astype(jnp.bfloat16),
            dot_first(normed_two, d_gate_up).astype(jnp.bfloat16),
        )
        down_sum, gate_up_sum = collect(layer, down_term), collect(layer, gate_up_term)
        grad_attn, d_after, sums_two, *got = relay(
            behind_norm,
            3 + layer,
            partial,
            [grad, after, gains[layer, 1:]],
            [(owned, D), (2, D)],
            cols_axis,
            carry=[]
            if layer == 1
            else [(0, hidden_out[0]), (1, hidden_out[1]), (1, input_out[1]), (1, weight_sums[1][2])],
            behind=[] if layer == 1 else [weight_sums[1][0]],
        )
        if layer == 1:
            result = jnp.where(d_after[0, 0] == d_after[0, 0], result, 0)
            hidden_out.append(lax.psum_scatter(result, "col", scatter_dimension=1, tiled=True))
        else:
            hidden_got[0], hidden_got[1], input_got[1], arrived[1][2] = got
        small_sums += [sums_two]
        d_mix, out_term = together(
            product(grad_attn, out_w[layer]).astype(jnp.bfloat16), dot_first(grad_attn, attn_mix).astype(jnp.bfloat16)
        )
        out_sum = collect(layer, out_term)
        d_qkv, arrived[layer][1] = attend_back(
            10 + layer,
            expand(d_mix) if layer == 1 else hold(expand(d_mix), [down_sum]),
            spread,
            mixed,
            log_sums,
            ids,
            cosines,
            sines,
            heads,
            rows_axis,
            layer,
            gate_up_sum,
        )
        d_qkv = contract(d_qkv)
        partial, qkv_term, bias_grads[layer] = together(
            dot_last(d_qkv, qkv_w[layer]).astype(jnp.bfloat16),
            dot_first(normed, d_qkv).astype(jnp.bfloat16),
            jnp.sum(d_qkv.astype(jnp.float32), axis=0),
        )
        if layer == 1:
            qkv_terms = jnp.pad(qkv_term, ((D, 0), (0, 0)))
        else:
            qkv_terms = lax.dynamic_update_slice(qkv_terms, qkv_term, (0, 0))
            qkv_grad = lax.psum_scatter(qkv_terms, both, scatter_dimension=0, tiled=True).astype(jnp.float32)
        if layer == 0:
            early_sums = lax.psum_scatter(jnp.stack(small_sums), "col", scatter_dimension=2, tiled=True)
            early = jnp.concatenate([early_sums.reshape(6, -1), bias_grads[1].reshape(3, -1), bias_grads[0].reshape(3, -1)])
            early = jnp.sum(lax.all_gather(early, both, axis=0), axis=0)
        branch, grad, sums_one, *got = relay(
            behind_norm,
            5 + layer,
            partial,
            [d_after, mine(stream), gains[layer, :1]],
            [(owned, D), (2, D)],
            cols_axis,
            spread=layer == 0,
            carry=[] if layer == 1 else [(0, down_sum), (0, out_sum), (1, weight_sums[1][0])],
            behind=[hidden_out[1]] if layer == 1 else [early_sums],
        )
        if layer == 0:
            late_sums, arrived[0][0], arrived[0][2], arrived[1][0] = got
        small_sums += [sums_one]
        input_out[layer] = my_features(branch) if layer == 1 else branch

    hidden_states = jnp.where(
        section == 0, jnp.stack([hidden_out[0], hidden_got[0]]), jnp.stack([hidden_got[1], hidden_out[1]])
    )
    input_grads = jnp.where(section == 0, input_out[0], jnp.stack([input_got[1], input_out[1]])).astype(jnp.float32)
    down_grad, gate_up_grad, out_grad = (
        jnp.where(section == 0, first, second).astype(jnp.float32)
        + jnp.where(section == 0, first_got, second_got).astype(jnp.float32)
        for first, second, first_got, second_got in zip(*weight_sums, *arrived)
    )
    last = lax.psum(jnp.sum(late_sums, axis=(0, 1)), "row")
    norm_sums = jnp.where(section == 0, jnp.stack([last, early[4:6]]), jnp.stack([early[2:4], early[0:2]]))
    bias_sum = jnp.where(section == 0, early[9:12], early[6:9])
    return (
        hidden_states[None],
        input_grads[None],
        norm_sums[:, 0][None],
        norm_sums[:, 1][None],
        qkv_grad.reshape(qkv_weight.shape),
        bias_sum.reshape(qkv_bias.shape),
        out_grad[None],
        gate_up_grad.reshape(gate_up_weight.shape),
        down_grad[None],
    )


def solution(mesh):
    in_specs = (
        P(None, "row", "col"),
        P(None, "row", "col"),
        P(),
        P("section", None, "col"),
        P("section", None, "col"),
        P("section", "row", None, "col"),
        P("section", None, "col"),
        P("section", "row", "col"),
        P("section", "row", None, "col"),
        P("section", "row", "col"),
    )
    out_specs = (
        P("section", None, "row", "col"),
        P("section", None, "row", "col"),
        P("section", None, "col"),
        P("section", None, "col"),
        P("section", "row", None, "col"),
        P("section", None, "col"),
        P("section", "row", "col"),
        P("section", "row", None, "col"),
        P("section", "row", "col"),
    )
    return jax.shard_map(
        per_device, mesh=mesh, in_specs=in_specs, out_specs=out_specs, check_vma=False
    )
```

```python
import functools

import jax
import jax.numpy as jnp
from jax import lax
from jax.experimental import pallas as pl
from jax.experimental.pallas import tpu as pltpu
from jax.sharding import PartitionSpec as P

D = 2048
HEADS = 32
HEAD_DIM = 64
ROT = 16
LANES = 128
REACH = 256
RELAY_ROWS = 16


epsilon = 1e-05


def dot_last(a, b):
    return lax.dot_general(a, b, (((1,), (1,)), ((), ())), preferred_element_type=jnp.float32)


def dot_first(a, b):
    return lax.dot_general(a, b, (((0,), (0,)), ((), ())), preferred_element_type=jnp.float32)


def lanes_of(rows, head):
    lane = lax.broadcasted_iota(jnp.int32, (rows, LANES), 1)
    return lane // HEAD_DIM == head


def spin(x, cosines, sines):
    lane = lax.broadcasted_iota(jnp.int32, x.shape, 1)
    ahead, behind = pltpu.roll(x, LANES - ROT // 2, 1), pltpu.roll(x, ROT // 2, 1)
    return x * cosines + jnp.where(lane % ROT < ROT // 2, ahead, behind) * sines


def meet(axis, n):
    me = lax.axis_index(axis)
    barrier = pltpu.get_barrier_semaphore()
    for d in range(1, n):
        pl.semaphore_signal(
            barrier, 1, device_id={axis: lax.rem(me + d, n)}, device_id_type=pl.DeviceIdType.MESH
        )
    pl.semaphore_wait(barrier, n - 1)


def remote(source, target, sent, got, axis, device):
    return pltpu.make_async_remote_copy(
        src_ref=source,
        dst_ref=target,
        send_sem=sent,
        recv_sem=got,
        device_id={axis: device},
        device_id_type=pl.DeviceIdType.MESH,
    )


def columns(which, size=LANES):
    return pl.ds(pl.multiple_of(which * size, size), size)


def attend_kernel(heads, n, bq, given, bid_q, bid_k, *refs):
    me = lax.axis_index("row")
    if given:
        spread, mixed, lse_ref, mix, vone, scores, mix_sent, mix_got = refs
    else:
        qkv, cosines, sines, spread, mixed, lse_ref, mix, vone, scores, mix_sent, mix_got = refs[:11]
        leaving, qkv_sent, qkv_got = refs[11:]
    tokens = mix.shape[0]
    seq = n * tokens
    here = pl.ds(pl.multiple_of(me * tokens, tokens), tokens)
    low = jnp.bfloat16
    meet("row", n)

    def parts(t):
        cos, sin = cosines[here, :], sines[here, :]
        query = spin(qkv[:, columns(t)], cos, sin).astype(low) * jnp.asarray(HEAD_DIM**-0.5, low)
        key = spin(qkv[:, columns(n + t)], cos, sin).astype(low)
        return query.astype(low), key, qkv[:, columns(2 * n + t)].astype(low)

    def leave(d):
        to = lax.rem(me + d, n)
        return remote(leaving.at[d - 1], spread.at[:, here], qkv_sent.at[d - 1], qkv_got.at[me], "row", to)

    if not given:
        for d in range(1, n):
            for k, part in enumerate(parts(lax.rem(me + d, n))):
                leaving[d - 1, k] = part
            leave(d).start()
        for k, part in enumerate(parts(me)):
            spread[k, here, :] = part

    def come(row):
        if not given:
            @pl.when(row != me)
            def _():
                there = pl.ds(row * tokens, tokens)
                remote(leaving.at[0], spread.at[:, there], qkv_sent.at[0], qkv_got.at[row], "row", me).wait_recv()

        there = pl.ds(row * tokens, tokens)
        for h in range(heads):
            vone[h, there, :] = jnp.where(lanes_of(tokens, h), spread[2, there, :], jnp.ones((), low))

    def mix_copy(i, device):
        rows = pl.ds(lax.rem(i, tokens // bq) * bq, bq)
        return remote(
            mixed.at[pl.ds(i * bq, bq)], mix.at[rows, columns(me)], mix_sent.at[i], mix_got.at[me, lax.rem(i, tokens // bq)], "row", device
        )

    def block(i, carry):
        rows = pl.ds(pl.multiple_of(i * bq, bq), bq)
        q = spread[0, rows, :]
        bid = bid_q[rows, :]
        begin = i * bq
        ahead = jnp.where(begin + bq < seq, 1, 0)
        qs = [jnp.where(lanes_of(bq, h), q, jnp.zeros((), low)) for h in range(heads)]

        def score(start, size, tops, hide):
            span = pl.ds(pl.multiple_of(start, REACH), size)
            keys = spread[1, span, :]
            if hide:
                visible = bid_k[:, span] <= bid
            found = []
            for h in range(heads):
                s = dot_last(qs[h], keys)
                if hide:
                    s = jnp.where(visible, s, -1e30)
                scores[h, :, span] = s
                top = tops[h]
                for c in range(size // LANES):
                    top = jnp.maximum(top, s[:, c * LANES : (c + 1) * LANES])
                found.append(top)
            return tuple(found)

        tops = tuple(jnp.full((bq, LANES), -1e30, jnp.float32) for _ in range(heads))
        tops = lax.fori_loop(0, i // 2, lambda t, c: score(2 * t * bq, 2 * bq, c, False), tops)
        tops = lax.fori_loop(i // 2 * 2, i, lambda t, c: score(t * bq, bq, c, False), tops)
        tops = score(begin, bq, tops, True)
        tops = lax.fori_loop(0, ahead, lambda t, c: score(begin + bq, REACH, c, True), tops)
        tops = [jnp.max(top, axis=1, keepdims=True) for top in tops]

        def gather(start, size, sums):
            span = pl.ds(pl.multiple_of(start, REACH), size)
            found = []
            for h in range(heads):
                p = jnp.exp(scores[h, :, span] - tops[h]).astype(low)
                found.append(sums[h] + jnp.dot(p, vone[h, span, :], preferred_element_type=jnp.float32))
            return tuple(found)

        sums = tuple(jnp.zeros((bq, LANES), jnp.float32) for _ in range(heads))
        sums = lax.fori_loop(0, (i + 1) // 2, lambda t, c: gather(2 * t * bq, 2 * bq, c), sums)
        sums = lax.fori_loop((i + 1) // 2 * 2, i + 1, lambda t, c: gather(t * bq, bq, c), sums)
        sums = lax.fori_loop(0, ahead, lambda t, c: gather(begin + bq, REACH, c), sums)
        outcome = jnp.zeros((bq, LANES), jnp.float32)
        lse = jnp.zeros((bq, LANES), jnp.float32)
        for h in range(heads):
            totals = pltpu.roll(sums[h], HEAD_DIM, 1)
            outcome = jnp.where(lanes_of(bq, h), sums[h] / totals, outcome)
            lse = jnp.where(lanes_of(bq, h), tops[h] + jnp.log(totals), lse)
        mixed[rows, :] = outcome.astype(low)
        lse_ref[:, rows] = lse.T
        return carry

    per_row = tokens // bq
    for row in range(n):
        if row == 0:
            come(0)
        if row + 1 < n:
            come(row + 1)

        def run(half, carry, row=row):
            i = row * per_row + half
            block(i, 0)

            @pl.when(row == me)
            def _():
                mix[pl.ds(pl.multiple_of(half * bq, bq), bq), columns(me)] = mixed[pl.ds(pl.multiple_of(i * bq, bq), bq), :]

            @pl.when(row != me)
            def _():
                mix_copy(i, row).start()

            return carry

        lax.fori_loop(0, per_row, run, 0)

    if not given:
        for d in range(1, n):
            leave(d).wait_send()
    for i in range(n * per_row):
        @pl.when(i // per_row != me)
        def _(i=i):
            mix_copy(i, me).wait_send()

    for row in range(n):
        @pl.when(row != me)
        def _(row=row):
            for half in range(per_row):
                rows = pl.ds(half * bq, bq)
                remote(
                    mixed.at[pl.ds(0, bq)], mix.at[rows, columns(row)], mix_sent.at[0], mix_got.at[row, half], "row", me
                ).wait_recv()


def attend(number, block_all, heads, n, tokens, qkv=None, cosines=None, sines=None, spread=None, bq=512):
    bq = min(bq, tokens)
    seq = n * tokens
    vmem = pl.BlockSpec(memory_space=pltpu.VMEM)
    low = jnp.bfloat16
    given = spread is not None
    operands = [spread] if given else [qkv, cosines, sines]
    out_shape = [
        jax.ShapeDtypeStruct((3, seq, LANES), low),
        jax.ShapeDtypeStruct((seq, LANES), low),
        jax.ShapeDtypeStruct((LANES, seq), jnp.float32),
        jax.ShapeDtypeStruct((tokens, n * LANES), low),
    ][given:]
    exchange = [
        pltpu.VMEM((n - 1, 3, tokens, LANES), low),
        pltpu.SemaphoreType.DMA((n - 1,)),
        pltpu.SemaphoreType.DMA((n,)),
    ]
    found = pl.pallas_call(
        functools.partial(attend_kernel, heads, n, bq, given),
        in_specs=[vmem] * (2 + len(operands)),
        out_specs=[vmem] * len(out_shape),
        out_shape=out_shape,
        scratch_shapes=[
            pltpu.VMEM((heads, seq, LANES), low),
            pltpu.VMEM((heads, bq, seq), jnp.float32),
            pltpu.SemaphoreType.DMA((seq // bq,)),
            pltpu.SemaphoreType.DMA((n, tokens // bq)),
        ]
        + ([] if given else exchange),
        compiler_params=pltpu.CompilerParams(
            collective_id=number, has_side_effects=True, vmem_limit_bytes=58 * 2**20
        ),
        cost_estimate=pl.CostEstimate(flops=10**10, bytes_accessed=2 * 10**8, transcendentals=0),
    )(block_all.reshape(seq, 1), block_all.reshape(1, seq), *operands)
    return [spread] + list(found) if given else found


def attend_back_kernel(
    heads, n, bq, layer, bid_q, bid_k, d_mix, spread, mixed, lse_ref, cosines, sines, carry, *refs
):
    d_qkv, carried, grads, kone, dk_acc, dv_acc, leaving, g_sent, g_got, back_sent, back_got, carry_sent, carry_got = refs
    section = lax.axis_index("section")
    me = lax.axis_index("row")
    tokens = d_mix.shape[0]
    seq = n * tokens
    per_row = tokens // bq
    blocks = n * per_row
    low = jnp.bfloat16
    zero = jnp.zeros((), low)
    here = pl.ds(pl.multiple_of(me * tokens, tokens), tokens)
    barrier = pltpu.get_barrier_semaphore()
    pl.semaphore_signal(barrier, 1, device_id={"section": 1 - section}, device_id_type=pl.DeviceIdType.MESH)
    for d in range(1, n):
        pl.semaphore_signal(barrier, 1, device_id={"row": lax.rem(me + d, n)}, device_id_type=pl.DeviceIdType.MESH)
    pl.semaphore_wait(barrier, n)
    carry_copy = remote(carry, carried, carry_sent, carry_got, "section", layer)

    def give(d):
        to = lax.rem(me + d, n)
        return remote(d_mix.at[:, columns(to)], grads.at[here], g_sent.at[d - 1], g_got.at[me], "row", to)

    for d in range(1, n):
        give(d).start()

    @pl.when(section != layer)
    def _():
        carry_copy.start()

    grads[here, :] = d_mix[:, columns(me)]
    for h in range(heads):
        kone[h] = jnp.where(lanes_of(seq, h), spread[1], zero).T
    dk_acc[...] = jnp.zeros_like(dk_acc)
    dv_acc[...] = jnp.zeros_like(dv_acc)

    def tile(start, size, dq, hide, stuff):
        qs, gs, lses, deltas, bid = stuff
        span = pl.ds(pl.multiple_of(start, REACH), size)
        keys, values = spread[1, span, :], spread[2, span, :]
        dv, dk = dv_acc[span, :], dk_acc[span, :]
        if hide:
            visible = bid_k[span, :] <= bid
        for h in range(heads):
            s = dot_last(keys, qs[h])
            if hide:
                s = jnp.where(visible, s, -1e30)
            p = jnp.exp(s - lses[h])
            dp = dot_last(values, gs[h])
            ds = (p * (dp - deltas[h])).astype(low)
            dv = dv + jnp.dot(p.astype(low), gs[h], preferred_element_type=jnp.float32)
            dk = dk + jnp.dot(ds, qs[h], preferred_element_type=jnp.float32)
            dq = dq + jnp.dot(kone[h, :, span], ds, preferred_element_type=jnp.float32)
        dv_acc[span, :] = dv
        dk_acc[span, :] = dk
        return dq

    def block(i):
        rows = pl.ds(pl.multiple_of(i * bq, bq), bq)
        q, g = spread[0, rows, :], grads[rows, :]
        product = (g.astype(jnp.float32) * mixed[rows, :].astype(jnp.float32)).T
        span = lambda h: slice(h * HEAD_DIM, (h + 1) * HEAD_DIM)
        deltas = [jnp.sum(product[span(h)], axis=0, keepdims=True) for h in range(heads)]
        lses = [lse_ref[h * HEAD_DIM : h * HEAD_DIM + 1, rows] for h in range(heads)]
        qs = [jnp.where(lanes_of(bq, h), q, zero) for h in range(heads)]
        gs = [jnp.where(lanes_of(bq, h), g, zero) for h in range(heads)]
        stuff = (qs, gs, lses, deltas, bid_q[:, rows])
        begin = i * bq
        ahead = jnp.where(begin + bq < seq, 1, 0)
        dq = jnp.zeros((LANES, bq), jnp.float32)
        dq = lax.fori_loop(0, i, lambda t, c: tile(t * bq, bq, c, False, stuff), dq)
        dq = tile(begin, bq, dq, True, stuff)
        dq = lax.fori_loop(0, ahead, lambda t, c: tile(begin + bq, REACH, c, True, stuff), dq)
        return spin(dq.T * (HEAD_DIM**-0.5), cosines[rows, :], -sines[rows, :]).astype(low)

    def back_copy(k, i, device):
        half = lax.rem(i, per_row)
        rows = pl.ds(pl.multiple_of(half * bq, bq), bq)
        return remote(
            leaving.at[k, pl.ds(pl.multiple_of(i * bq, bq), bq)],
            d_qkv.at[rows, columns(k * n + me)],
            back_sent.at[k, i],
            back_got.at[k, me, half],
            "row",
            device,
        )

    def send(k, i, values):
        row = i // per_row
        half = lax.rem(i, per_row)

        @pl.when(row == me)
        def _():
            d_qkv[pl.ds(pl.multiple_of(half * bq, bq), bq), columns(k * n + me)] = values

        @pl.when(row != me)
        def _():
            leaving[k, pl.ds(pl.multiple_of(i * bq, bq), bq), :] = values
            back_copy(k, i, row).start()

    def keys_done(i):
        rows = pl.ds(pl.multiple_of(i * bq, bq), bq)
        send(1, i, spin(dk_acc[rows, :], cosines[rows, :], -sines[rows, :]).astype(low))
        send(2, i, dv_acc[rows, :].astype(low))

    for row in range(n - 1, -1, -1):
        @pl.when(row != me)
        def _(row=row):
            there = pl.ds(row * tokens, tokens)
            remote(d_mix.at[:, columns(0)], grads.at[there], g_sent.at[0], g_got.at[row], "row", me).wait_recv()

        def run(step, carry, row=row):
            i = row * per_row + per_row - 1 - step
            send(0, i, block(i))

            @pl.when(i + 1 < blocks)
            def _():
                keys_done(i + 1)

            return carry

        lax.fori_loop(0, per_row, run, 0)
    keys_done(0)

    for d in range(1, n):
        give(d).wait_send()

    def settle(i, carry):
        @pl.when(i // per_row != me)
        def _():
            half = lax.rem(i, per_row)
            rows = pl.ds(pl.multiple_of(half * bq, bq), bq)
            for k in range(3):
                back_copy(k, i, me).wait_send()
                remote(
                    leaving.at[k, pl.ds(0, bq)],
                    d_qkv.at[rows, columns(k * n + i // per_row)],
                    back_sent.at[k, 0],
                    back_got.at[k, i // per_row, half],
                    "row",
                    me,
                ).wait_recv()

        return carry

    lax.fori_loop(0, blocks, settle, 0)

    @pl.when(section != layer)
    def _():
        carry_copy.wait_send()

    @pl.when(section == layer)
    def _():
        carry_copy.wait_recv()


def attend_back(number, d_mix, spread, mixed, lse, block_all, cosines, sines, heads, n, layer, carry, bq=512):
    tokens = d_mix.shape[0]
    bq = min(bq, tokens)
    seq = n * tokens
    vmem = pl.BlockSpec(memory_space=pltpu.VMEM)
    low = jnp.bfloat16
    return pl.pallas_call(
        functools.partial(attend_back_kernel, heads, n, bq, layer),
        in_specs=[vmem] * 8 + [pl.BlockSpec(memory_space=pl.ANY)],
        out_specs=[vmem, pl.BlockSpec(memory_space=pl.ANY)],
        out_shape=[jax.ShapeDtypeStruct((tokens, 3 * n * LANES), low), jax.ShapeDtypeStruct(carry.shape, carry.dtype)],
        scratch_shapes=[
            pltpu.VMEM((seq, LANES), low),
            pltpu.VMEM((heads, LANES, seq), low),
            pltpu.VMEM((seq, LANES), jnp.float32),
            pltpu.VMEM((seq, LANES), jnp.float32),
            pltpu.VMEM((3, seq, LANES), low),
            pltpu.SemaphoreType.DMA((n - 1,)),
            pltpu.SemaphoreType.DMA((n,)),
            pltpu.SemaphoreType.DMA((3, seq // bq)),
            pltpu.SemaphoreType.DMA((3, n, tokens // bq)),
            pltpu.SemaphoreType.DMA,
            pltpu.SemaphoreType.DMA,
        ],
        compiler_params=pltpu.CompilerParams(
            collective_id=number, has_side_effects=True, vmem_limit_bytes=58 * 2**20
        ),
        cost_estimate=pl.CostEstimate(flops=10**10, bytes_accessed=3 * 10**8, transcendentals=0),
    )(block_all.reshape(1, seq), block_all.reshape(seq, 1), d_mix, spread, mixed, lse, cosines, sines, carry)


def norm_parts(values):
    mean = jnp.mean(values, axis=-1, keepdims=True)
    spread = jnp.mean(values * values, axis=-1, keepdims=True) - mean * mean
    return mean, lax.rsqrt(spread + epsilon)


def after_attention(total, c, ins, outs):
    stream, gain, shift = ins
    (after_ref,) = outs
    after = stream[c].astype(jnp.float32) + total
    after_ref[c] = after
    values = after.astype(jnp.bfloat16).astype(jnp.float32)
    mean, inverse = norm_parts(values)
    return ((values - mean) * inverse * gain[...] + shift[...]).astype(jnp.bfloat16)


def after_hidden(total, c, ins, outs):
    (after,) = ins
    return (after[c] + total).astype(jnp.bfloat16)


def behind_norm(total, c, ins, outs):
    grad, values_ref, gain = ins
    grad_ref, sums = outs
    values = values_ref[c].astype(jnp.bfloat16).astype(jnp.float32)
    mean, inverse = norm_parts(values)
    centred = (values - mean) * inverse
    scaled = total * gain[...]
    back = inverse * (
        scaled
        - jnp.mean(scaled, axis=-1, keepdims=True)
        - centred * jnp.mean(scaled * centred, axis=-1, keepdims=True)
    )
    given = grad[c] + back
    grad_ref[c] = given
    here = [jnp.sum(total * centred, axis=0, keepdims=True), jnp.sum(total, axis=0, keepdims=True)]

    @pl.when(c == 0)
    def _():
        sums[...] = jnp.zeros_like(sums)

    sums[...] += jnp.concatenate(here, axis=0)
    return given.astype(jnp.bfloat16)


def relay_kernel(
    middle, n_ins, n_outs, layers, n_after, polish, parts, n_row, n, chunks, lag, spread, partial, *refs
):
    ins, carry, refs = refs[:n_ins], refs[n_ins : n_ins + len(layers)], refs[n_ins + len(layers) + n_after :]
    whole, outs, refs = refs[0], refs[1 : 1 + n_outs], refs[1 + n_outs :]
    carried, refs = refs[: len(layers)], refs[len(layers) :]
    if parts:
        ins, (weights, bias, cosines, sines) = ins[:-4], ins[-4:]
        outs, landed = outs[:-1], outs[-1]
        *refs, leaving, part_sent, part_got, weight, weight_got = refs
        weight_copy = pltpu.make_async_copy(weights.at[pl.ds(weight.shape[0], weight.shape[0])], weight, weight_got)
        weight_copy.start()
    if polish:
        ins, (gain, shift) = ins[:-2], ins[-2:]
        outs, polished = outs[:-1], outs[-1]
    if spread:
        outs, all_sums = outs[:-1], outs[-1]
    arrived, outgoing, total, sum_sent, sum_got, block_sent, block_got, carry_sent, carry_got, last_sent, last_got = refs
    section, i = lax.axis_index("section"), lax.axis_index("col")
    width = whole.shape[-1]
    first, last = i == 0, i == n - 1

    barrier = pltpu.get_barrier_semaphore()

    def greet(**place):
        pl.semaphore_signal(barrier, 1, device_id=place, device_id_type=pl.DeviceIdType.MESH)

    if spread:
        for d in range(1, 2 * n):
            greet(section=lax.rem(section + d // n, 2), col=lax.rem(i + d, n))
        pl.semaphore_wait(barrier, 2 * n - 1)
    else:
        greet(section=1 - section)
        me = lax.axis_index("row")
        row_peers = n_row - 1 if parts else 0
        for d in range(1, row_peers + 1):
            greet(row=lax.rem(me + d, n_row))

        @pl.when(i > 0)
        def _():
            greet(col=i - 1)

        @pl.when(i < n - 1)
        def _():
            greet(col=i + 1)

        @pl.when(first | last)
        def _():
            pl.semaphore_wait(barrier, 2 + row_peers)

        @pl.when((i > 0) & (i < n - 1))
        def _():
            pl.semaphore_wait(barrier, 3 + row_peers)

    def carry_copy(k):
        return remote(carry[k], carried[k], carry_sent.at[k], carry_got.at[k], "section", layers[k])

    for k, layer in enumerate(layers):
        @pl.when(section != layer)
        def _(k=k):
            carry_copy(k).start()

    def remote_col(source, target, sent, got, device):
        return remote(source, target, sent, got, "col", device)

    def sum_copy(c, j, right):
        slot = j + 1 if right else j
        return remote_col(
            outgoing.at[c, j], arrived.at[c, slot], sum_sent.at[c, j], sum_got.at[c, slot], i + 1 if right else i - 1
        )

    def block_copy(c, o, right, own=False):
        sent = n if own and not right else o
        return remote_col(whole.at[c, o], whole.at[c, o], block_sent.at[c, sent], block_got.at[0, c, o], i + 1 if right else i - 1)

    def slice_copy(c, d):
        to = lax.rem(i + d, n)
        return pltpu.make_async_remote_copy(
            src_ref=outgoing.at[c, i, :, pl.ds(pl.multiple_of(to * width, 128), width)],
            dst_ref=whole.at[section, c, i],
            send_sem=block_sent.at[c, d],
            recv_sem=block_got.at[section, c, i],
            device_id={"section": 0, "col": to},
            device_id_type=pl.DeviceIdType.MESH,
        )

    def arrive(c, slot):
        remote_col(outgoing.at[c, 0], arrived.at[c, slot], sum_sent.at[c, 0], sum_got.at[c, slot], i).wait_recv()

    def work(c, o):
        if polish:
            values = whole[c, o].astype(jnp.float32)
            mean, inverse = norm_parts(values)
            polished[c, o] = ((values - mean) * inverse * gain[...] + shift[...]).astype(jnp.bfloat16)

    rows = whole.shape[-2]
    per = max(1, min(chunks, LANES // (n * rows)))
    many = per * n * rows
    unit = max(1, n * per // n_row)
    tokens = chunks * n * rows

    def part_rows(source, b):
        return pl.ds(pl.multiple_of(source * tokens + b * many, many), many)

    def part_copy(b, d):
        to = lax.rem(me + d, n_row)
        return remote(
            leaving.at[d - 1, :, part_rows(0, b)],
            landed.at[:, part_rows(me, b)],
            part_sent.at[d - 1, b],
            part_got.at[me, b],
            "row",
            to,
        )

    def project(b, d):
        values = (polished if polish else whole)[pl.ds(b * per, per)].reshape(many, whole.shape[-1])
        here, there = part_rows(me, b), part_rows(0, b)
        t = lax.rem(me + d, n_row)
        for k in range(parts):
            column = columns(k * n_row + t)
            found = jnp.dot(values, weight[:, column], preferred_element_type=jnp.float32) + bias[:, column]
            if parts == 3 and k < 2:
                found = spin(found, cosines[here, :], sines[here, :])
            found = found.astype(jnp.bfloat16)
            if parts == 3 and k == 0:
                found = (found * jnp.asarray(HEAD_DIM**-0.5, jnp.bfloat16)).astype(jnp.bfloat16)

            @pl.when(d > 0)
            def _(k=k, found=found):
                leaving[d - 1, k, there, :] = found

            @pl.when(d == 0)
            def _(k=k, found=found):
                landed[k, here, :] = found

        @pl.when(d > 0)
        def _():
            part_copy(b, d).start()

    def sums_copy(d):
        to = lax.rem(i + d, n)
        return pltpu.make_async_remote_copy(
            src_ref=outs[-1].at[:, pl.ds(pl.multiple_of(to * width, 128), width)],
            dst_ref=all_sums.at[section, i],
            send_sem=last_sent.at[d],
            recv_sem=last_got.at[section, i],
            device_id={"section": 0, "col": to},
            device_id_type=pl.DeviceIdType.MESH,
        )

    def sums_arrive(s, o):
        return pltpu.make_async_remote_copy(
            src_ref=outs[-1].at[:, pl.ds(0, width)],
            dst_ref=all_sums.at[s, o],
            send_sem=last_sent.at[0],
            recv_sem=last_got.at[s, o],
            device_id={"section": 0, "col": o},
            device_id_type=pl.DeviceIdType.MESH,
        )

    def middle_slot(k):
        return jnp.maximum(lag * k + n - 1 - k, lag * (n - 1 - k) + k)

    def at(now, slot, allowed):
        since = now - slot
        c = jnp.maximum(since, 0) // n
        return c, allowed & (since >= 0) & (lax.rem(jnp.maximum(since, 0), n) == 0) & (since < n * chunks)

    def step(now, carry):
        for j in range(n - 1, 0, -1):
            c, due = at(now, lag * i + n - 1 - j, i < j)

            @pl.when(due & first)
            def _(c=c, j=j):
                outgoing[c, j] = partial[c, j]

            @pl.when(due & (i > 0))
            def _(c=c, j=j):
                arrive(c, j + 1)
                both = arrived[c, j + 1].astype(jnp.float32) + partial[c, j].astype(jnp.float32)
                outgoing[c, j] = both.astype(jnp.bfloat16)

            @pl.when(due)
            def _(c=c, j=j):
                sum_copy(c, j, True).start()

        for j in range(n - 1):
            c, due = at(now, lag * (n - 1 - i) + j, i > j)

            @pl.when(due & last)
            def _(c=c, j=j):
                outgoing[c, j] = partial[c, j]

            @pl.when(due & (i < n - 1))
            def _(c=c, j=j):
                arrive(c, j)
                both = arrived[c, j].astype(jnp.float32) + partial[c, j].astype(jnp.float32)
                outgoing[c, j] = both.astype(jnp.bfloat16)

            @pl.when(due)
            def _(c=c, j=j):
                sum_copy(c, j, False).start()

        c, due = at(now, middle_slot(i), i >= 0)

        @pl.when(due)
        def _():
            total[...] = partial[c, i].astype(jnp.float32)

        @pl.when(due & (i > 0))
        def _():
            arrive(c, i + 1)
            total[...] += arrived[c, i + 1].astype(jnp.float32)

        @pl.when(due & (i < n - 1))
        def _():
            arrive(c, i)
            total[...] += arrived[c, i].astype(jnp.float32)

        @pl.when(due)
        def _():
            block = middle(total[...], c, ins, outs)
            if spread:
                outgoing[c, i] = block
                for d in range(1, n):
                    slice_copy(c, d).start()

                @pl.when(section == 0)
                def _():
                    whole[0, c, i] = outgoing[c, i, :, pl.ds(pl.multiple_of(i * width, 128), width)]

                @pl.when(section != 0)
                def _():
                    slice_copy(c, 0).start()

            else:
                whole[c, i] = block
                work(c, i)

        if spread:
            return carry

        @pl.when(due & (i < n - 1))
        def _():
            block_copy(c, i, True, own=True).start()

        @pl.when(due & (i > 0))
        def _():
            block_copy(c, i, False, own=True).start()

        for o in range(n - 1):
            c, due = at(now, middle_slot(o) + lag * (i - o), i > o)

            @pl.when(due)
            def _(c=c, o=o):
                block_copy(c, o, True).wait_recv()

            @pl.when(due & (i < n - 1))
            def _(c=c, o=o):
                block_copy(c, o, True).start()

            @pl.when(due)
            def _(c=c, o=o):
                work(c, o)

        for o in range(1, n):
            c, due = at(now, middle_slot(o) + lag * (o - i), i < o)

            @pl.when(due)
            def _(c=c, o=o):
                block_copy(c, o, False).wait_recv()

            @pl.when(due & (i > 0))
            def _(c=c, o=o):
                block_copy(c, o, False).start()

            @pl.when(due)
            def _(c=c, o=o):
                work(c, o)

        if parts:
            since = now - (n * (per - 1) + 2 * lag * (n - 1))
            given = jnp.maximum(since, 0)
            turn = lax.rem(given, n * per) // unit

            @pl.when(since == 0)
            def _():
                weight_copy.wait()

            @pl.when((since >= 0) & (lax.rem(given, unit) == 0) & (turn < n_row) & (given < n * chunks))
            def _():
                project(given // (n * per), lax.rem(turn + 1, n_row))

        return carry

    steps = n * (chunks - 1) + 2 * lag * (n - 1) + 1
    lax.fori_loop(0, steps + (unit * (n_row - 1) if parts else 0), step, 0)

    if spread:
        for d in range(1, n):
            sums_copy(d).start()

        @pl.when(section == 0)
        def _():
            all_sums[0, i] = outs[-1][:, pl.ds(pl.multiple_of(i * width, 128), width)]

        @pl.when(section != 0)
        def _():
            sums_copy(0).start()

    def slice_arrives(c, s, o):
        return pltpu.make_async_remote_copy(
            src_ref=outgoing.at[c, 0, :, pl.ds(0, width)],
            dst_ref=whole.at[s, c, o],
            send_sem=block_sent.at[c, 0],
            recv_sem=block_got.at[s, c, o],
            device_id={"section": 0, "col": o},
            device_id_type=pl.DeviceIdType.MESH,
        )

    def settle(c, carry):
        for j in range(n):
            @pl.when(j != i)
            def _(j=j):
                sum_copy(c, j, True).wait_send()

        if spread:
            for d in range(1, n):
                slice_copy(c, d).wait_send()

            @pl.when(section != 0)
            def _():
                slice_copy(c, 0).wait_send()

            for s in range(2):
                for o in range(n):
                    @pl.when((section == 0) & ((s == 1) | (o != i)))
                    def _(s=s, o=o):
                        slice_arrives(c, s, o).wait_recv()

            return carry
        for o in range(n):
            @pl.when((o <= i) & (i < n - 1))
            def _(o=o):
                block_copy(c, o, True).wait_send()

            @pl.when((o > i) & (i > 0))
            def _(o=o):
                block_copy(c, o, True).wait_send()

        @pl.when(i > 0)
        def _():
            block_copy(c, i, False, own=True).wait_send()

        return carry

    lax.fori_loop(0, chunks, settle, 0)
    if spread:
        for d in range(1, n):
            sums_copy(d).wait_send()

        @pl.when(section != 0)
        def _():
            sums_copy(0).wait_send()

        for s in range(2):
            for o in range(n):
                @pl.when((section == 0) & ((s == 1) | (o != i)))
                def _(s=s, o=o):
                    sums_arrive(s, o).wait_recv()

    if parts:
        def settle_parts(b, carry):
            for d in range(1, n_row):
                part_copy(b, d).wait_send()
                source = lax.rem(me + d, n_row)
                remote(
                    leaving.at[0, :, part_rows(0, b)],
                    landed.at[:, part_rows(source, b)],
                    part_sent.at[0, b],
                    part_got.at[source, b],
                    "row",
                    source,
                ).wait_recv()
            return carry

        lax.fori_loop(0, chunks // per, settle_parts, 0)

    for k, layer in enumerate(layers):
        @pl.when(section != layer)
        def _(k=k):
            carry_copy(k).wait_send()

        @pl.when(section == layer)
        def _(k=k):
            carry_copy(k).wait_recv()


def relay(middle, number, partial, ins, outs, n, spread=False, carry=(), behind=(), polish=(), project=(), n_row=1, lag=3, rows=RELAY_ROWS):
    tokens, features = partial.shape
    owned = tokens // n
    chunks = owned // rows
    blocks = lambda values: values.reshape(chunks, rows, features) if values.shape[0] == owned else values
    ins = [blocks(values) for values in ins] + list(polish) + list(project)
    parts = project[0].shape[1] // (n_row * LANES) if project else 0
    batches = chunks // max(1, min(chunks, LANES // (n * rows)))
    outs = list(outs) + ([(tokens, features)] if polish else []) + ([(parts, n_row * tokens, LANES)] if parts else []) + ([(2, n, 2, features // n)] if spread else [])
    out_shapes = [
        jax.ShapeDtypeStruct(
            (2, chunks, n, rows, features // n) if spread else (chunks, n, rows, features), jnp.bfloat16
        )
    ] + [
        jax.ShapeDtypeStruct((chunks, n, rows, features), jnp.bfloat16)
        if shape[0] == tokens
        else jax.ShapeDtypeStruct(shape, jnp.bfloat16)
        if shape[-1] == LANES
        else jax.ShapeDtypeStruct((chunks, rows, features) if shape[0] == owned else shape, jnp.float32)
        for shape in outs
    ]
    vmem, anywhere = pl.BlockSpec(memory_space=pltpu.VMEM), pl.BlockSpec(memory_space=pl.ANY)
    specs = [vmem] * (1 + len(ins))
    if project:
        specs[-4] = anywhere
    layers = tuple(layer for layer, _ in carry)
    carry = [values for _, values in carry]
    whole, *rest = pl.pallas_call(
        functools.partial(relay_kernel, middle, len(ins), len(outs), layers, len(behind), bool(polish), parts, n_row, n, chunks, lag, spread),
        in_specs=specs + [anywhere] * (len(carry) + len(behind)),
        out_specs=[vmem] * len(out_shapes) + [anywhere] * len(carry),
        out_shape=out_shapes + [jax.ShapeDtypeStruct(values.shape, values.dtype) for values in carry],
        scratch_shapes=[
            pltpu.VMEM((chunks, n + 1, rows, features), jnp.bfloat16),
            pltpu.VMEM((chunks, n, rows, features), jnp.bfloat16),
            pltpu.VMEM((rows, features), jnp.float32),
            pltpu.SemaphoreType.DMA((chunks, n)),
            pltpu.SemaphoreType.DMA((chunks, n + 1)),
            pltpu.SemaphoreType.DMA((chunks, n + 1)),
            pltpu.SemaphoreType.DMA((2 if spread else 1, chunks, n)),
            pltpu.SemaphoreType.DMA((max(1, len(carry)),)),
            pltpu.SemaphoreType.DMA((max(1, len(carry)),)),
            pltpu.SemaphoreType.DMA((n,)),
            pltpu.SemaphoreType.DMA((2, n)),
        ]
        + (
            [
                pltpu.VMEM((n_row - 1, parts, tokens, LANES), jnp.bfloat16),
                pltpu.SemaphoreType.DMA((n_row - 1, batches)),
                pltpu.SemaphoreType.DMA((n_row, batches)),
                pltpu.VMEM((features, project[0].shape[1]), jnp.bfloat16),
                pltpu.SemaphoreType.DMA,
            ]
            if parts
            else []
        ),
        compiler_params=pltpu.CompilerParams(
            collective_id=number, has_side_effects=True, vmem_limit_bytes=56 * 2**20
        ),
        cost_estimate=pl.CostEstimate(flops=0, bytes_accessed=35 * 10**7, transcendentals=0),
    )(partial.reshape(chunks, n, rows, features), *ins, *carry, *behind)
    shapes = {(chunks, rows, features): (owned, features), (chunks, n, rows, features): (tokens, features)}
    rest = [values.reshape(shapes.get(values.shape, values.shape)) for values in rest]
    return [whole.reshape((2, tokens, -1) if spread else (tokens, -1))] + rest


def gather_kernel(n, chunks, lag, own, small, angles, whole, smalls, normed, cosines, sines, sent, got, small_sent, small_got):
    section, i = lax.axis_index("section"), lax.axis_index("col")
    rows, width = own.shape[0] // chunks, own.shape[1]
    others = [(s, d) for s in range(2) for d in range(n) if (s, d) != (0, 0)]
    place = lambda s, d: {"section": lax.rem(section + s, 2), "col": lax.rem(i + d, n)}
    barrier = pltpu.get_barrier_semaphore()
    for s, d in others:
        pl.semaphore_signal(barrier, 1, device_id=place(s, d), device_id_type=pl.DeviceIdType.MESH)
    pl.semaphore_wait(barrier, len(others))

    def small_copy(s, d):
        return pltpu.make_async_remote_copy(
            src_ref=small,
            dst_ref=smalls.at[section, i],
            send_sem=small_sent.at[s, d],
            recv_sem=small_got.at[section, i],
            device_id=place(s, d),
            device_id_type=pl.DeviceIdType.MESH,
        )

    for s, d in others:
        small_copy(s, d).start()
    smalls[section, i] = small[...]

    def small_arrives(s, d):
        from_s, from_d = lax.rem(section + s, 2), lax.rem(i + d, n)
        return pltpu.make_async_remote_copy(
            src_ref=small,
            dst_ref=smalls.at[from_s, from_d],
            send_sem=small_sent.at[s, d],
            recv_sem=small_got.at[from_s, from_d],
            device_id=place(s, d),
            device_id_type=pl.DeviceIdType.MESH,
        )

    def norm(c):
        here = pl.ds(pl.multiple_of(c * rows, rows), rows)
        values = whole[here, :].astype(jnp.float32)
        mean, inverse = norm_parts(values)
        for o in range(n):
            part = slice(o * width, (o + 1) * width)
            gain, shift = smalls[0, o, 0:1, :], smalls[0, o, 2:3, :]
            normed[here, part] = ((values[:, part] - mean) * inverse * gain + shift).astype(jnp.bfloat16)

    def block(c, o, right, mine=False):
        part = whole.at[pl.ds(pl.multiple_of(c * rows, rows), rows), columns(o, width)]
        return remote(
            part, part, sent.at[c, n if mine and not right else o], got.at[c, o], "col", i + 1 if right else i - 1
        )

    def at(now, slot, allowed):
        since = jnp.maximum(now - slot, 0)
        return since // (n - 1), allowed & (now >= slot) & (lax.rem(since, n - 1) == 0) & (since < (n - 1) * chunks)

    def step(now, carry):
        c, due = at(now, 0, i >= 0)

        @pl.when(due)
        def _():
            here = pl.ds(pl.multiple_of(c * rows, rows), rows)
            whole[here, columns(i, width)] = own[here, :]

        @pl.when(due & (i < n - 1))
        def _():
            block(c, i, True, True).start()

        @pl.when(due & (i > 0))
        def _():
            block(c, i, False, True).start()

        for o in range(n):
            c, due = at(now, lag * jnp.abs(i - o), i != o)

            @pl.when(due)
            def _(c=c, o=o):
                block(c, o, True).wait_recv()

            @pl.when(due & (i > o) & (i < n - 1))
            def _(c=c, o=o):
                block(c, o, True).start()

            @pl.when(due & (i < o) & (i > 0))
            def _(c=c, o=o):
                block(c, o, False).start()

        c, due = at(now, lag * (n - 1), i >= 0)

        @pl.when(due)
        def _():
            norm(c)

        return carry

    turns = angles.shape[0] // 2
    lane = lax.broadcasted_iota(jnp.int32, (turns, LANES), 1)
    place_of = lax.broadcasted_iota(jnp.int32, (turns, LANES), 0)
    turned = lane % HEAD_DIM < 2 * turns
    picked = jnp.where(turned & (lane % turns == place_of), 1.0, 0.0)
    sign = jnp.where(lane % HEAD_DIM < turns, -1.0, 1.0)

    def spread_out(table, pick):
        return lax.dot_general(
            table, pick, (((0,), (0,)), ((), ())), precision=lax.Precision.HIGHEST, preferred_element_type=jnp.float32
        )

    still = jnp.where(turned[:1], 0.0, 1.0)
    cosines[...] = spread_out(angles[:turns, :], picked) + still
    sines[...] = spread_out(angles[turns:, :], picked * sign)
    for s, d in others:
        small_arrives(s, d).wait_recv()

    lax.fori_loop(0, (n - 1) * (chunks - 1) + lag * (n - 1) + 1, step, 0)

    def settle(c, carry):
        for o in range(n):
            @pl.when(((o <= i) & (i < n - 1)) | ((o > i) & (i > 0)))
            def _(o=o):
                block(c, o, True).wait_send()

        @pl.when(i > 0)
        def _():
            block(c, i, False, True).wait_send()

        return carry

    lax.fori_loop(0, chunks, settle, 0)
    for s, d in others:
        small_copy(s, d).wait_send()


def gathered(number, own, small, angles, n, lag=3, rows=64):
    tokens, width = own.shape
    chunks = tokens // rows
    vmem = pl.BlockSpec(memory_space=pltpu.VMEM)
    return pl.pallas_call(
        functools.partial(gather_kernel, n, chunks, lag),
        in_specs=[vmem] * 3,
        out_specs=[vmem] * 5,
        out_shape=[
            jax.ShapeDtypeStruct((tokens, n * width), own.dtype),
            jax.ShapeDtypeStruct((2, n) + small.shape, small.dtype),
            jax.ShapeDtypeStruct((tokens, n * width), own.dtype),
            jax.ShapeDtypeStruct((angles.shape[1], LANES), jnp.float32),
            jax.ShapeDtypeStruct((angles.shape[1], LANES), jnp.float32),
        ],
        scratch_shapes=[
            pltpu.SemaphoreType.DMA((chunks, n + 1)),
            pltpu.SemaphoreType.DMA((chunks, n)),
            pltpu.SemaphoreType.DMA((2, n)),
            pltpu.SemaphoreType.DMA((2, n)),
        ],
        compiler_params=pltpu.CompilerParams(
            collective_id=number, has_side_effects=True, vmem_limit_bytes=40 * 2**20
        ),
        cost_estimate=pl.CostEstimate(flops=0, bytes_accessed=25 * 10**7, transcendentals=0),
    )(own, small, angles)


def ffn_kernel(units, values, weight, down, gate_up, hidden, partial):
    both = jnp.dot(values[...], weight[...], preferred_element_type=jnp.float32)
    gate_up[...] = both
    gate, up = both[:, :units], both[:, units:]
    found = (gate * (1.0 / (1.0 + jnp.exp(-gate))) * up).astype(jnp.bfloat16)
    hidden[...] = found
    partial[...] = dot_last(found, down[...]).astype(partial.dtype)


def ffn_back_kernel(units, branch, gate_up, weight, down, d_gate_up, partial):
    d_hidden = jnp.dot(branch[...], down[...], preferred_element_type=jnp.float32)
    gate, up = gate_up[:, :units], gate_up[:, units:]
    sig = 1.0 / (1.0 + jnp.exp(-gate))
    d_gate_up[:, :units] = (d_hidden * up * sig * (1.0 + gate * (1.0 - sig))).astype(jnp.bfloat16)
    d_gate_up[:, units:] = (d_hidden * gate * sig).astype(jnp.bfloat16)
    partial[...] = dot_last(d_gate_up[...], weight[...]).astype(partial.dtype)


def ffn_call(kernel, layer, inputs, weight, down, outs, rows=256):
    tokens = inputs[0].shape[0]
    units = down.shape[1]
    by_rows = lambda width: pl.BlockSpec((rows, width), lambda i: (i, 0))
    once = lambda width: pl.BlockSpec((D, width), lambda i: (layer, 0), pipeline_mode=pl.Buffered(1))
    return pl.pallas_call(
        functools.partial(kernel, units),
        grid=(tokens // rows,),
        in_specs=[by_rows(values.shape[1]) for values in inputs] + [once(2 * units), once(units)],
        out_specs=[by_rows(width) for width, _ in outs],
        out_shape=[jax.ShapeDtypeStruct((tokens, width), kind) for width, kind in outs],
        compiler_params=pltpu.CompilerParams(vmem_limit_bytes=58 * 2**20),
        cost_estimate=pl.CostEstimate(flops=6 * tokens * D * units, bytes_accessed=4 * 10**7, transcendentals=0),
    )(*inputs, weight, down)


def rotary_angles(positions):
    half_dims = ROT // 2
    inverse_freq = 1.0 / 10000.0 ** (jnp.arange(half_dims, dtype=jnp.float32) * 2.0 / ROT)
    angles = positions.astype(jnp.float32)[None, :] * inverse_freq[:, None]
    return jnp.concatenate([jnp.cos(angles), jnp.sin(angles)])


def product(left, right):
    return jnp.dot(left, right, preferred_element_type=jnp.float32)


def per_device(
    inputs,
    cotangent,
    block_ids,
    norm_gains,
    norm_shifts,
    qkv_weight,
    qkv_bias,
    out_weight,
    gate_up_weight,
    down_weight,
):
    section = lax.axis_index("section")
    row = lax.axis_index("row")
    col = lax.axis_index("col")
    rows_axis = lax.axis_size("row")
    cols_axis = lax.axis_size("col")
    tokens, width = inputs.shape[1:]
    owned = tokens // cols_axis
    units = down_weight.shape[2]
    seq = tokens * rows_axis
    both = ("section", "row")
    whole_lanes = width == rows_axis * LANES
    heads = LANES // HEAD_DIM if whole_lanes else 1
    copies = 1 if whole_lanes else rows_axis * HEAD_DIM // width

    def expand(values):
        if whole_lanes:
            return values
        rows = values.shape[0]
        values = values.reshape(rows, -1, width // HEAD_DIM, HEAD_DIM)
        values = jnp.pad(jnp.repeat(values, copies, axis=2), ((0, 0), (0, 0), (0, 0), (0, LANES - HEAD_DIM)))
        return values.reshape(rows, -1)

    def contract(values):
        if whole_lanes:
            return values
        values = values.reshape(tokens, -1, rows_axis, LANES)[:, :, ::copies, :HEAD_DIM]
        return values.reshape(tokens, -1)

    def weights_of(block):
        block = block[0].reshape(block.shape[1], -1)
        return lax.all_gather(block, both, axis=0, tiled=True).reshape(2, D, -1)

    def mine(values):
        blocks = values.reshape(owned // RELAY_ROWS, cols_axis, RELAY_ROWS, -1)
        return lax.dynamic_index_in_dim(blocks, col, 1, keepdims=False).reshape(owned, -1)

    def my_features(values):
        return lax.dynamic_slice_in_dim(values, col * width, width, 1)

    own_small = jnp.concatenate([norm_gains[0], norm_shifts[0], qkv_bias[0], jnp.zeros((1, width), jnp.float32)])
    angles = rotary_angles(jnp.arange(seq, dtype=jnp.int32))
    stream, small, normed, cosines, sines = gathered(
        7, lax.dynamic_index_in_dim(inputs, section, 0, keepdims=False), own_small, angles, cols_axis
    )
    whole_small = small.transpose(0, 2, 1, 3).reshape(2, own_small.shape[0], D)
    gains, shifts = whole_small[:, :2], whole_small[:, 2:4]
    bias = lax.dynamic_index_in_dim(small, col, 1, keepdims=False)[:, 4:7].reshape(2, -1)

    qkv_w = weights_of(qkv_weight)
    out_w = weights_of(out_weight)
    gate_up_w = weights_of(gate_up_weight)
    down_w = weights_of(down_weight)

    ids = lax.dynamic_index_in_dim(block_ids, section, 0, keepdims=False)
    def feed_forward(layer, values):
        kind = jnp.bfloat16 if layer == 0 else jnp.float32
        if units % LANES == 0:
            outs = [(2 * units, jnp.float32), (units, jnp.bfloat16), (D, kind)]
            return ffn_call(ffn_kernel, layer, [values], all_gate_up, all_down, outs)
        gate_up = product(values, gate_up_w[layer])
        hidden = (jax.nn.silu(gate_up[:, :units]) * gate_up[:, units:]).astype(jnp.bfloat16)
        return gate_up, hidden, dot_last(hidden, down_w[layer]).astype(kind)

    def feed_back(layer, branch, gate_up):
        if units % LANES == 0:
            outs = [(2 * units, jnp.bfloat16), (D, jnp.bfloat16)]
            return ffn_call(ffn_back_kernel, layer, [branch, gate_up], all_gate_up, all_down, outs)
        gate, up = gate_up[:, :units], gate_up[:, units:]
        d_hidden = product(branch, down_w[layer])
        sig = jax.nn.sigmoid(gate)
        d_gate = d_hidden * up * sig * (1.0 + gate * (1.0 - sig))
        d_up = d_hidden * gate * sig
        d_gate_up = jnp.concatenate([d_gate, d_up], axis=1).astype(jnp.bfloat16)
        return d_gate_up, dot_last(d_gate_up, gate_up_w[layer]).astype(jnp.bfloat16)

    all_gate_up, all_down = gate_up_w.reshape(2 * D, -1), down_w.reshape(2 * D, -1)
    kept = []
    hidden_out = []

    def gathered_half(which, half):
        values = lax.dynamic_index_in_dim(cotangent, which, 0, keepdims=False)
        values = values[half * (tokens // 2) : (half + 1) * (tokens // 2)]
        return lax.all_gather(values, "col", axis=1, tiled=True)

    first_half = gathered_half(section, 0)
    waited = [first_half]
    for layer in range(2):
        if layer == 0:
            qkv = expand(product(normed, qkv_w[0]) + bias[0])
            spread, mixed, log_sums, attn_mix = attend(
                8, ids, heads, rows_axis, tokens, qkv=qkv, cosines=cosines, sines=sines
            )
        else:
            here = section + jnp.where(hidden_out[0][0, 0] == hidden_out[0][0, 0], 0, 1)
            second_half = gathered_half(here, 1)
            waited = [second_half]
            spread, mixed, log_sums, attn_mix = attend(9, ids, heads, rows_axis, tokens, spread=spread)
        attn_mix = contract(attn_mix)
        normed_two, after = relay(
            after_attention,
            layer,
            product(attn_mix, out_w[layer].T).astype(jnp.bfloat16),
            [mine(stream), gains[layer, 1:], shifts[layer, 1:]],
            [(owned, D)],
            cols_axis,
            behind=waited,
        )
        gate_up, hidden, partial = feed_forward(layer, normed_two)
        kept.append((stream, normed, spread, mixed, log_sums, attn_mix, after, normed_two, gate_up, hidden))
        if layer == 0:
            stream, normed, spread = relay(
                after_hidden,
                2,
                partial.astype(jnp.bfloat16),
                [after],
                [],
                cols_axis,
                polish=(gains[1, :1], shifts[1, :1]),
                project=(expand(qkv_w.reshape(2 * D, -1)), expand(bias[1:]), cosines, sines),
                n_row=rows_axis,
            )
            hidden_out.append(my_features(stream))
        else:
            blocks = partial.reshape(owned // RELAY_ROWS, cols_axis, RELAY_ROWS, D)
            owner = lax.broadcasted_iota(jnp.int32, blocks.shape, 1) == col
            blocks = blocks + jnp.where(owner, after.reshape(-1, 1, RELAY_ROWS, D), 0.0)
            result = blocks.reshape(tokens, D).astype(jnp.bfloat16)

    branch = jnp.concatenate([first_half, second_half])
    grad = mine(branch).astype(jnp.float32)
    weight_sums = [[], []]
    small_sums = []
    bias_grads = [None, None]
    input_out = [None, None]
    input_got = [None, None]
    hidden_got = [None, None]

    def collect(layer, term):
        weight_sums[layer].append(lax.psum_scatter(term, "row", scatter_dimension=0, tiled=True))
        return weight_sums[layer][-1]

    arrived = [[None] * 3, [None] * 3]
    def together(*values):
        return lax.optimization_barrier(values)

    for layer in (1, 0):
        stream, normed, spread, mixed, log_sums, attn_mix, after, normed_two, gate_up, hidden = kept[layer]
        d_gate_up, partial = feed_back(layer, branch, gate_up)
        partial, down_term, gate_up_term = together(
            partial,
            dot_first(branch, hidden).astype(jnp.bfloat16),
            dot_first(normed_two, d_gate_up).astype(jnp.bfloat16),
        )
        down_sum, gate_up_sum = collect(layer, down_term), collect(layer, gate_up_term)
        grad_attn, d_after, sums_two, *got = relay(
            behind_norm,
            3 + layer,
            partial,
            [grad, after, gains[layer, 1:]],
            [(owned, D), (2, D)],
            cols_axis,
            carry=[]
            if layer == 1
            else [(0, hidden_out[0]), (1, hidden_out[1]), (1, input_out[1]), (1, weight_sums[1][2])],
            behind=[] if layer == 1 else [weight_sums[1][0]],
        )
        if layer == 1:
            result = jnp.where(d_after[0, 0] == d_after[0, 0], result, 0)
            hidden_out.append(lax.psum_scatter(result, "col", scatter_dimension=1, tiled=True))
        else:
            hidden_got[0], hidden_got[1], input_got[1], arrived[1][2] = got
        small_sums += [sums_two]
        d_mix, out_term = together(
            product(grad_attn, out_w[layer]).astype(jnp.bfloat16), dot_first(grad_attn, attn_mix).astype(jnp.bfloat16)
        )
        out_sum = collect(layer, out_term)
        d_qkv, arrived[layer][1] = attend_back(
            10 + layer,
            expand(d_mix),
            spread,
            mixed,
            log_sums,
            ids,
            cosines,
            sines,
            heads,
            rows_axis,
            layer,
            gate_up_sum,
        )
        d_qkv = contract(d_qkv)
        partial, qkv_term, bias_grads[layer] = together(
            dot_last(d_qkv, qkv_w[layer]).astype(jnp.bfloat16),
            dot_first(normed, d_qkv).astype(jnp.bfloat16),
            jnp.sum(d_qkv.astype(jnp.float32), axis=0),
        )
        if layer == 1:
            qkv_terms = jnp.pad(qkv_term, ((D, 0), (0, 0)))
        else:
            qkv_terms = lax.dynamic_update_slice(qkv_terms, qkv_term, (0, 0))
            qkv_grad = lax.psum_scatter(qkv_terms, both, scatter_dimension=0, tiled=True).astype(jnp.float32)
        if layer == 0:
            early_sums = lax.psum_scatter(jnp.stack(small_sums), "col", scatter_dimension=2, tiled=True)
            early = jnp.concatenate([early_sums.reshape(6, -1), bias_grads[1].reshape(3, -1), bias_grads[0].reshape(3, -1)])
            early = jnp.sum(lax.all_gather(early, both, axis=0), axis=0)
        branch, grad, sums_one, *got = relay(
            behind_norm,
            5 + layer,
            partial,
            [d_after, mine(stream), gains[layer, :1]],
            [(owned, D), (2, D)],
            cols_axis,
            spread=layer == 0,
            carry=[] if layer == 1 else [(0, down_sum), (0, out_sum), (1, weight_sums[1][0])],
            behind=[hidden_out[1]] if layer == 1 else [early_sums],
        )
        if layer == 0:
            late_sums, arrived[0][0], arrived[0][2], arrived[1][0] = got
        small_sums += [sums_one]
        input_out[layer] = my_features(branch) if layer == 1 else branch

    hidden_states = jnp.where(
        section == 0, jnp.stack([hidden_out[0], hidden_got[0]]), jnp.stack([hidden_got[1], hidden_out[1]])
    )
    input_grads = jnp.where(section == 0, input_out[0], jnp.stack([input_got[1], input_out[1]])).astype(jnp.float32)
    down_grad, gate_up_grad, out_grad = (
        jnp.where(section == 0, first, second).astype(jnp.float32)
        + jnp.where(section == 0, first_got, second_got).astype(jnp.float32)
        for first, second, first_got, second_got in zip(*weight_sums, *arrived)
    )
    last = lax.psum(jnp.sum(late_sums, axis=(0, 1)), "row")
    norm_sums = jnp.where(section == 0, jnp.stack([last, early[4:6]]), jnp.stack([early[2:4], early[0:2]]))
    bias_sum = jnp.where(section == 0, early[9:12], early[6:9])
    return (
        hidden_states[None],
        input_grads[None],
        norm_sums[:, 0][None],
        norm_sums[:, 1][None],
        qkv_grad.reshape(qkv_weight.shape),
        bias_sum.reshape(qkv_bias.shape),
        out_grad[None],
        gate_up_grad.reshape(gate_up_weight.shape),
        down_grad[None],
    )


def solution(mesh):
    in_specs = (
        P(None, "row", "col"),
        P(None, "row", "col"),
        P(),
        P("section", None, "col"),
        P("section", None, "col"),
        P("section", "row", None, "col"),
        P("section", None, "col"),
        P("section", "row", "col"),
        P("section", "row", None, "col"),
        P("section", "row", "col"),
    )
    out_specs = (
        P("section", None, "row", "col"),
        P("section", None, "row", "col"),
        P("section", None, "col"),
        P("section", None, "col"),
        P("section", "row", None, "col"),
        P("section", None, "col"),
        P("section", "row", "col"),
        P("section", "row", None, "col"),
        P("section", "row", "col"),
    )
    return jax.shard_map(
        per_device, mesh=mesh, in_specs=in_specs, out_specs=out_specs, check_vma=False
    )
```

```python
import functools

import jax
import jax.numpy as jnp
from jax import lax
from jax.experimental import pallas as pl
from jax.experimental.pallas import tpu as pltpu
from jax.sharding import PartitionSpec as P

D = 2048
HEADS = 32
HEAD_DIM = 64
ROT = 16
LANES = 128
REACH = 256
RELAY_ROWS = 16


epsilon = 1e-05


def dot_last(a, b):
    return lax.dot_general(a, b, (((1,), (1,)), ((), ())), preferred_element_type=jnp.float32)


def dot_first(a, b):
    return lax.dot_general(a, b, (((0,), (0,)), ((), ())), preferred_element_type=jnp.float32)


def lanes_of(rows, head):
    lane = lax.broadcasted_iota(jnp.int32, (rows, LANES), 1)
    return lane // HEAD_DIM == head


def spin(x, cosines, sines):
    lane = lax.broadcasted_iota(jnp.int32, x.shape, 1)
    ahead, behind = pltpu.roll(x, LANES - ROT // 2, 1), pltpu.roll(x, ROT // 2, 1)
    return x * cosines + jnp.where(lane % ROT < ROT // 2, ahead, behind) * sines


def meet(axis, n):
    me = lax.axis_index(axis)
    barrier = pltpu.get_barrier_semaphore()
    for d in range(1, n):
        pl.semaphore_signal(
            barrier, 1, device_id={axis: lax.rem(me + d, n)}, device_id_type=pl.DeviceIdType.MESH
        )
    pl.semaphore_wait(barrier, n - 1)


def remote(source, target, sent, got, axis, device):
    return pltpu.make_async_remote_copy(
        src_ref=source,
        dst_ref=target,
        send_sem=sent,
        recv_sem=got,
        device_id={axis: device},
        device_id_type=pl.DeviceIdType.MESH,
    )


def columns(which, size=LANES):
    return pl.ds(pl.multiple_of(which * size, size), size)


def attend_kernel(heads, n, bq, given, bid_q, bid_k, *refs):
    me = lax.axis_index("row")
    if given:
        spread, mixed, lse_ref, mix, vone, scores, mix_sent, mix_got = refs
    else:
        qkv, cosines, sines, spread, mixed, lse_ref, mix, vone, scores, mix_sent, mix_got = refs[:11]
        leaving, qkv_sent, qkv_got = refs[11:]
    tokens = mix.shape[0]
    seq = n * tokens
    here = pl.ds(pl.multiple_of(me * tokens, tokens), tokens)
    low = jnp.bfloat16
    meet("row", n)

    def parts(t):
        cos, sin = cosines[here, :], sines[here, :]
        query = spin(qkv[:, columns(t)], cos, sin).astype(low) * jnp.asarray(HEAD_DIM**-0.5, low)
        key = spin(qkv[:, columns(n + t)], cos, sin).astype(low)
        return query.astype(low), key, qkv[:, columns(2 * n + t)].astype(low)

    def leave(d):
        to = lax.rem(me + d, n)
        return remote(leaving.at[d - 1], spread.at[:, here], qkv_sent.at[d - 1], qkv_got.at[me], "row", to)

    if not given:
        for d in range(1, n):
            for k, part in enumerate(parts(lax.rem(me + d, n))):
                leaving[d - 1, k] = part
            leave(d).start()
        for k, part in enumerate(parts(me)):
            spread[k, here, :] = part

    def come(row):
        if not given:
            @pl.when(row != me)
            def _():
                there = pl.ds(row * tokens, tokens)
                remote(leaving.at[0], spread.at[:, there], qkv_sent.at[0], qkv_got.at[row], "row", me).wait_recv()

        there = pl.ds(row * tokens, tokens)
        for h in range(heads):
            vone[h, there, :] = jnp.where(lanes_of(tokens, h), spread[2, there, :], jnp.ones((), low))

    def mix_copy(i, device):
        rows = pl.ds(lax.rem(i, tokens // bq) * bq, bq)
        return remote(
            mixed.at[pl.ds(i * bq, bq)], mix.at[rows, columns(me)], mix_sent.at[i], mix_got.at[me, lax.rem(i, tokens // bq)], "row", device
        )

    def block(i, carry):
        rows = pl.ds(pl.multiple_of(i * bq, bq), bq)
        q = spread[0, rows, :]
        bid = bid_q[rows, :]
        begin = i * bq
        ahead = jnp.where(begin + bq < seq, 1, 0)
        qs = [jnp.where(lanes_of(bq, h), q, jnp.zeros((), low)) for h in range(heads)]

        def score(start, size, tops, hide):
            span = pl.ds(pl.multiple_of(start, REACH), size)
            keys = spread[1, span, :]
            if hide:
                visible = bid_k[:, span] <= bid
            found = []
            for h in range(heads):
                s = dot_last(qs[h], keys)
                if hide:
                    s = jnp.where(visible, s, -1e30)
                scores[h, :, span] = s
                top = tops[h]
                for c in range(size // LANES):
                    top = jnp.maximum(top, s[:, c * LANES : (c + 1) * LANES])
                found.append(top)
            return tuple(found)

        tops = tuple(jnp.full((bq, LANES), -1e30, jnp.float32) for _ in range(heads))
        tops = lax.fori_loop(0, i // 2, lambda t, c: score(2 * t * bq, 2 * bq, c, False), tops)
        tops = lax.fori_loop(i // 2 * 2, i, lambda t, c: score(t * bq, bq, c, False), tops)
        tops = score(begin, bq, tops, True)
        tops = lax.fori_loop(0, ahead, lambda t, c: score(begin + bq, REACH, c, True), tops)
        tops = [jnp.max(top, axis=1, keepdims=True) for top in tops]

        def gather(start, size, sums):
            span = pl.ds(pl.multiple_of(start, REACH), size)
            found = []
            for h in range(heads):
                p = jnp.exp(scores[h, :, span] - tops[h]).astype(low)
                found.append(sums[h] + jnp.dot(p, vone[h, span, :], preferred_element_type=jnp.float32))
            return tuple(found)

        sums = tuple(jnp.zeros((bq, LANES), jnp.float32) for _ in range(heads))
        sums = lax.fori_loop(0, (i + 1) // 2, lambda t, c: gather(2 * t * bq, 2 * bq, c), sums)
        sums = lax.fori_loop((i + 1) // 2 * 2, i + 1, lambda t, c: gather(t * bq, bq, c), sums)
        sums = lax.fori_loop(0, ahead, lambda t, c: gather(begin + bq, REACH, c), sums)
        outcome = jnp.zeros((bq, LANES), jnp.float32)
        lse = jnp.zeros((bq, LANES), jnp.float32)
        for h in range(heads):
            totals = pltpu.roll(sums[h], HEAD_DIM, 1)
            outcome = jnp.where(lanes_of(bq, h), sums[h] / totals, outcome)
            lse = jnp.where(lanes_of(bq, h), tops[h] + jnp.log(totals), lse)
        mixed[rows, :] = outcome.astype(low)
        lse_ref[:, rows] = lse.T
        return carry

    per_row = tokens // bq
    for row in range(n):
        if row == 0:
            come(0)
        if row + 1 < n:
            come(row + 1)

        def run(half, carry, row=row):
            i = row * per_row + half
            block(i, 0)

            @pl.when(row == me)
            def _():
                mix[pl.ds(pl.multiple_of(half * bq, bq), bq), columns(me)] = mixed[pl.ds(pl.multiple_of(i * bq, bq), bq), :]

            @pl.when(row != me)
            def _():
                mix_copy(i, row).start()

            return carry

        lax.fori_loop(0, per_row, run, 0)

    if not given:
        for d in range(1, n):
            leave(d).wait_send()
    for i in range(n * per_row):
        @pl.when(i // per_row != me)
        def _(i=i):
            mix_copy(i, me).wait_send()

    for row in range(n):
        @pl.when(row != me)
        def _(row=row):
            for half in range(per_row):
                rows = pl.ds(half * bq, bq)
                remote(
                    mixed.at[pl.ds(0, bq)], mix.at[rows, columns(row)], mix_sent.at[0], mix_got.at[row, half], "row", me
                ).wait_recv()


def attend(number, block_all, heads, n, tokens, qkv=None, cosines=None, sines=None, spread=None, bq=512):
    bq = min(bq, tokens)
    seq = n * tokens
    vmem = pl.BlockSpec(memory_space=pltpu.VMEM)
    low = jnp.bfloat16
    given = spread is not None
    operands = [spread] if given else [qkv, cosines, sines]
    out_shape = [
        jax.ShapeDtypeStruct((3, seq, LANES), low),
        jax.ShapeDtypeStruct((seq, LANES), low),
        jax.ShapeDtypeStruct((LANES, seq), jnp.float32),
        jax.ShapeDtypeStruct((tokens, n * LANES), low),
    ][given:]
    exchange = [
        pltpu.VMEM((n - 1, 3, tokens, LANES), low),
        pltpu.SemaphoreType.DMA((n - 1,)),
        pltpu.SemaphoreType.DMA((n,)),
    ]
    found = pl.pallas_call(
        functools.partial(attend_kernel, heads, n, bq, given),
        in_specs=[vmem] * (2 + len(operands)),
        out_specs=[vmem] * len(out_shape),
        out_shape=out_shape,
        scratch_shapes=[
            pltpu.VMEM((heads, seq, LANES), low),
            pltpu.VMEM((heads, bq, seq), jnp.float32),
            pltpu.SemaphoreType.DMA((seq // bq,)),
            pltpu.SemaphoreType.DMA((n, tokens // bq)),
        ]
        + ([] if given else exchange),
        compiler_params=pltpu.CompilerParams(
            collective_id=number, has_side_effects=True, vmem_limit_bytes=58 * 2**20
        ),
        cost_estimate=pl.CostEstimate(flops=10**10, bytes_accessed=2 * 10**8, transcendentals=0),
    )(block_all.reshape(seq, 1), block_all.reshape(1, seq), *operands)
    return [spread] + list(found) if given else found


def attend_back_kernel(
    heads, n, bq, layer, bid_q, bid_k, d_mix, spread, mixed, lse_ref, cosines, sines, carry, *refs
):
    d_qkv, carried, grads, kone, dk_acc, dv_acc, leaving, g_sent, g_got, back_sent, back_got, carry_sent, carry_got = refs
    section = lax.axis_index("section")
    me = lax.axis_index("row")
    tokens = d_mix.shape[0]
    seq = n * tokens
    per_row = tokens // bq
    blocks = n * per_row
    low = jnp.bfloat16
    zero = jnp.zeros((), low)
    here = pl.ds(pl.multiple_of(me * tokens, tokens), tokens)
    barrier = pltpu.get_barrier_semaphore()
    pl.semaphore_signal(barrier, 1, device_id={"section": 1 - section}, device_id_type=pl.DeviceIdType.MESH)
    for d in range(1, n):
        pl.semaphore_signal(barrier, 1, device_id={"row": lax.rem(me + d, n)}, device_id_type=pl.DeviceIdType.MESH)
    pl.semaphore_wait(barrier, n)
    carry_copy = remote(carry, carried, carry_sent, carry_got, "section", layer)

    def give(d):
        to = lax.rem(me + d, n)
        return remote(d_mix.at[:, columns(to)], grads.at[here], g_sent.at[d - 1], g_got.at[me], "row", to)

    for d in range(1, n):
        give(d).start()

    @pl.when(section != layer)
    def _():
        carry_copy.start()

    grads[here, :] = d_mix[:, columns(me)]
    for h in range(heads):
        kone[h] = jnp.where(lanes_of(seq, h), spread[1], zero).T
    dk_acc[...] = jnp.zeros_like(dk_acc)
    dv_acc[...] = jnp.zeros_like(dv_acc)

    def tile(start, size, dq, hide, stuff):
        qs, gs, lses, deltas, bid = stuff
        span = pl.ds(pl.multiple_of(start, REACH), size)
        keys, values = spread[1, span, :], spread[2, span, :]
        dv, dk = dv_acc[span, :], dk_acc[span, :]
        if hide:
            visible = bid_k[span, :] <= bid
        for h in range(heads):
            s = dot_last(keys, qs[h])
            if hide:
                s = jnp.where(visible, s, -1e30)
            p = jnp.exp(s - lses[h])
            dp = dot_last(values, gs[h])
            ds = (p * (dp - deltas[h])).astype(low)
            dv = dv + jnp.dot(p.astype(low), gs[h], preferred_element_type=jnp.float32)
            dk = dk + jnp.dot(ds, qs[h], preferred_element_type=jnp.float32)
            dq = dq + jnp.dot(kone[h, :, span], ds, preferred_element_type=jnp.float32)
        dv_acc[span, :] = dv
        dk_acc[span, :] = dk
        return dq

    def block(i):
        rows = pl.ds(pl.multiple_of(i * bq, bq), bq)
        q, g = spread[0, rows, :], grads[rows, :]
        product = (g.astype(jnp.float32) * mixed[rows, :].astype(jnp.float32)).T
        span = lambda h: slice(h * HEAD_DIM, (h + 1) * HEAD_DIM)
        deltas = [jnp.sum(product[span(h)], axis=0, keepdims=True) for h in range(heads)]
        lses = [lse_ref[h * HEAD_DIM : h * HEAD_DIM + 1, rows] for h in range(heads)]
        qs = [jnp.where(lanes_of(bq, h), q, zero) for h in range(heads)]
        gs = [jnp.where(lanes_of(bq, h), g, zero) for h in range(heads)]
        stuff = (qs, gs, lses, deltas, bid_q[:, rows])
        begin = i * bq
        ahead = jnp.where(begin + bq < seq, 1, 0)
        dq = jnp.zeros((LANES, bq), jnp.float32)
        dq = lax.fori_loop(0, i, lambda t, c: tile(t * bq, bq, c, False, stuff), dq)
        dq = tile(begin, bq, dq, True, stuff)
        dq = lax.fori_loop(0, ahead, lambda t, c: tile(begin + bq, REACH, c, True, stuff), dq)
        return spin(dq.T * (HEAD_DIM**-0.5), cosines[rows, :], -sines[rows, :]).astype(low)

    def back_copy(k, i, device):
        half = lax.rem(i, per_row)
        rows = pl.ds(pl.multiple_of(half * bq, bq), bq)
        return remote(
            leaving.at[k, pl.ds(pl.multiple_of(i * bq, bq), bq)],
            d_qkv.at[rows, columns(k * n + me)],
            back_sent.at[k, i],
            back_got.at[k, me, half],
            "row",
            device,
        )

    def send(k, i, values):
        row = i // per_row
        half = lax.rem(i, per_row)

        @pl.when(row == me)
        def _():
            d_qkv[pl.ds(pl.multiple_of(half * bq, bq), bq), columns(k * n + me)] = values

        @pl.when(row != me)
        def _():
            leaving[k, pl.ds(pl.multiple_of(i * bq, bq), bq), :] = values
            back_copy(k, i, row).start()

    def keys_done(i):
        rows = pl.ds(pl.multiple_of(i * bq, bq), bq)
        send(1, i, spin(dk_acc[rows, :], cosines[rows, :], -sines[rows, :]).astype(low))
        send(2, i, dv_acc[rows, :].astype(low))

    for row in range(n - 1, -1, -1):
        @pl.when(row != me)
        def _(row=row):
            there = pl.ds(row * tokens, tokens)
            remote(d_mix.at[:, columns(0)], grads.at[there], g_sent.at[0], g_got.at[row], "row", me).wait_recv()

        def run(step, carry, row=row):
            i = row * per_row + per_row - 1 - step
            send(0, i, block(i))

            @pl.when(i + 1 < blocks)
            def _():
                keys_done(i + 1)

            return carry

        lax.fori_loop(0, per_row, run, 0)
    keys_done(0)

    for d in range(1, n):
        give(d).wait_send()

    def settle(i, carry):
        @pl.when(i // per_row != me)
        def _():
            half = lax.rem(i, per_row)
            rows = pl.ds(pl.multiple_of(half * bq, bq), bq)
            for k in range(3):
                back_copy(k, i, me).wait_send()
                remote(
                    leaving.at[k, pl.ds(0, bq)],
                    d_qkv.at[rows, columns(k * n + i // per_row)],
                    back_sent.at[k, 0],
                    back_got.at[k, i // per_row, half],
                    "row",
                    me,
                ).wait_recv()

        return carry

    lax.fori_loop(0, blocks, settle, 0)

    @pl.when(section != layer)
    def _():
        carry_copy.wait_send()

    @pl.when(section == layer)
    def _():
        carry_copy.wait_recv()


def attend_back(number, d_mix, spread, mixed, lse, block_all, cosines, sines, heads, n, layer, carry, bq=512):
    tokens = d_mix.shape[0]
    bq = min(bq, tokens)
    seq = n * tokens
    vmem = pl.BlockSpec(memory_space=pltpu.VMEM)
    low = jnp.bfloat16
    return pl.pallas_call(
        functools.partial(attend_back_kernel, heads, n, bq, layer),
        in_specs=[vmem] * 8 + [pl.BlockSpec(memory_space=pl.ANY)],
        out_specs=[vmem, pl.BlockSpec(memory_space=pl.ANY)],
        out_shape=[jax.ShapeDtypeStruct((tokens, 3 * n * LANES), low), jax.ShapeDtypeStruct(carry.shape, carry.dtype)],
        scratch_shapes=[
            pltpu.VMEM((seq, LANES), low),
            pltpu.VMEM((heads, LANES, seq), low),
            pltpu.VMEM((seq, LANES), jnp.float32),
            pltpu.VMEM((seq, LANES), jnp.float32),
            pltpu.VMEM((3, seq, LANES), low),
            pltpu.SemaphoreType.DMA((n - 1,)),
            pltpu.SemaphoreType.DMA((n,)),
            pltpu.SemaphoreType.DMA((3, seq // bq)),
            pltpu.SemaphoreType.DMA((3, n, tokens // bq)),
            pltpu.SemaphoreType.DMA,
            pltpu.SemaphoreType.DMA,
        ],
        compiler_params=pltpu.CompilerParams(
            collective_id=number, has_side_effects=True, vmem_limit_bytes=58 * 2**20
        ),
        cost_estimate=pl.CostEstimate(flops=10**10, bytes_accessed=3 * 10**8, transcendentals=0),
    )(block_all.reshape(1, seq), block_all.reshape(seq, 1), d_mix, spread, mixed, lse, cosines, sines, carry)


def norm_parts(values):
    mean = jnp.mean(values, axis=-1, keepdims=True)
    spread = jnp.mean(values * values, axis=-1, keepdims=True) - mean * mean
    return mean, lax.rsqrt(spread + epsilon)


def after_attention(total, c, ins, outs):
    stream, gain, shift = ins
    (after_ref,) = outs
    after = stream[c].astype(jnp.float32) + total
    after_ref[c] = after
    values = after.astype(jnp.bfloat16).astype(jnp.float32)
    mean, inverse = norm_parts(values)
    return ((values - mean) * inverse * gain[...] + shift[...]).astype(jnp.bfloat16)


def after_hidden(total, c, ins, outs):
    (after,) = ins
    return (after[c] + total).astype(jnp.bfloat16)


def behind_norm(total, c, ins, outs):
    grad, values_ref, gain = ins
    grad_ref, sums = outs
    values = values_ref[c].astype(jnp.bfloat16).astype(jnp.float32)
    mean, inverse = norm_parts(values)
    centred = (values - mean) * inverse
    scaled = total * gain[...]
    back = inverse * (
        scaled
        - jnp.mean(scaled, axis=-1, keepdims=True)
        - centred * jnp.mean(scaled * centred, axis=-1, keepdims=True)
    )
    given = grad[c] + back
    grad_ref[c] = given
    here = [jnp.sum(total * centred, axis=0, keepdims=True), jnp.sum(total, axis=0, keepdims=True)]

    @pl.when(c == 0)
    def _():
        sums[...] = jnp.zeros_like(sums)

    sums[...] += jnp.concatenate(here, axis=0)
    return given.astype(jnp.bfloat16)


def relay_kernel(
    middle, n_ins, n_outs, layers, n_after, polish, parts, n_row, n, chunks, lag, spread, partial, *refs
):
    ins, carry, refs = refs[:n_ins], refs[n_ins : n_ins + len(layers)], refs[n_ins + len(layers) + n_after :]
    whole, outs, refs = refs[0], refs[1 : 1 + n_outs], refs[1 + n_outs :]
    carried, refs = refs[: len(layers)], refs[len(layers) :]
    if parts:
        ins, (weights, bias, cosines, sines) = ins[:-4], ins[-4:]
        outs, landed = outs[:-1], outs[-1]
        *refs, leaving, part_sent, part_got, weight, weight_got = refs
        weight_copy = pltpu.make_async_copy(weights.at[pl.ds(weight.shape[0], weight.shape[0])], weight, weight_got)
        weight_copy.start()
    if polish:
        ins, (gain, shift) = ins[:-2], ins[-2:]
        outs, polished = outs[:-1], outs[-1]
    if spread:
        ins, more = ins[:-1], ins[-1]
        outs, all_sums, all_more = outs[:-2], outs[-2], outs[-1]
        *refs, more_sent, more_got = refs
    arrived, outgoing, total, sum_sent, sum_got, block_sent, block_got, carry_sent, carry_got, last_sent, last_got = refs
    section, i = lax.axis_index("section"), lax.axis_index("col")
    width = whole.shape[-1]
    first, last = i == 0, i == n - 1

    barrier = pltpu.get_barrier_semaphore()

    def greet(**place):
        pl.semaphore_signal(barrier, 1, device_id=place, device_id_type=pl.DeviceIdType.MESH)

    if spread:
        for d in range(1, 2 * n):
            greet(section=lax.rem(section + d // n, 2), col=lax.rem(i + d, n))
        pl.semaphore_wait(barrier, 2 * n - 1)
    else:
        greet(section=1 - section)
        me = lax.axis_index("row")
        row_peers = n_row - 1 if parts else 0
        for d in range(1, row_peers + 1):
            greet(row=lax.rem(me + d, n_row))

        @pl.when(i > 0)
        def _():
            greet(col=i - 1)

        @pl.when(i < n - 1)
        def _():
            greet(col=i + 1)

        @pl.when(first | last)
        def _():
            pl.semaphore_wait(barrier, 2 + row_peers)

        @pl.when((i > 0) & (i < n - 1))
        def _():
            pl.semaphore_wait(barrier, 3 + row_peers)

    def carry_copy(k):
        return remote(carry[k], carried[k], carry_sent.at[k], carry_got.at[k], "section", layers[k])

    others = [(s, d) for s in range(2) for d in range(n) if (s, d) != (0, 0)] if spread else []

    def more_copy(s, d):
        to = lax.rem(i + d, n)
        return pltpu.make_async_remote_copy(
            src_ref=more.at[:, pl.ds(pl.multiple_of(to * width, 128), width)],
            dst_ref=all_more.at[section, i],
            send_sem=more_sent.at[s, d],
            recv_sem=more_got.at[section, i],
            device_id={"section": lax.rem(section + s, 2), "col": to},
            device_id_type=pl.DeviceIdType.MESH,
        )

    def more_arrives(s, d):
        from_s, from_d = lax.rem(section + s, 2), lax.rem(i + d, n)
        return pltpu.make_async_remote_copy(
            src_ref=more.at[:, pl.ds(0, width)],
            dst_ref=all_more.at[from_s, from_d],
            send_sem=more_sent.at[s, d],
            recv_sem=more_got.at[from_s, from_d],
            device_id={"section": from_s, "col": from_d},
            device_id_type=pl.DeviceIdType.MESH,
        )

    for s, d in others:
        more_copy(s, d).start()
    if spread:
        all_more[section, i] = more[:, pl.ds(pl.multiple_of(i * width, 128), width)]

    for k, layer in enumerate(layers):
        @pl.when(section != layer)
        def _(k=k):
            carry_copy(k).start()

    def remote_col(source, target, sent, got, device):
        return remote(source, target, sent, got, "col", device)

    def sum_copy(c, j, right):
        slot = j + 1 if right else j
        return remote_col(
            outgoing.at[c, j], arrived.at[c, slot], sum_sent.at[c, j], sum_got.at[c, slot], i + 1 if right else i - 1
        )

    def block_copy(c, o, right, own=False):
        sent = n if own and not right else o
        return remote_col(whole.at[c, o], whole.at[c, o], block_sent.at[c, sent], block_got.at[0, c, o], i + 1 if right else i - 1)

    def slice_copy(c, d):
        to = lax.rem(i + d, n)
        return pltpu.make_async_remote_copy(
            src_ref=outgoing.at[c, i, :, pl.ds(pl.multiple_of(to * width, 128), width)],
            dst_ref=whole.at[section, c, i],
            send_sem=block_sent.at[c, d],
            recv_sem=block_got.at[section, c, i],
            device_id={"section": 0, "col": to},
            device_id_type=pl.DeviceIdType.MESH,
        )

    def arrive(c, slot):
        remote_col(outgoing.at[c, 0], arrived.at[c, slot], sum_sent.at[c, 0], sum_got.at[c, slot], i).wait_recv()

    def work(c, o):
        if polish:
            values = whole[c, o].astype(jnp.float32)
            mean, inverse = norm_parts(values)
            polished[c, o] = ((values - mean) * inverse * gain[...] + shift[...]).astype(jnp.bfloat16)

    rows = whole.shape[-2]
    per = max(1, min(chunks, LANES // (n * rows)))
    many = per * n * rows
    unit = max(1, n * per // n_row)
    tokens = chunks * n * rows

    def part_rows(source, b):
        return pl.ds(pl.multiple_of(source * tokens + b * many, many), many)

    def part_copy(b, d):
        to = lax.rem(me + d, n_row)
        return remote(
            leaving.at[d - 1, :, part_rows(0, b)],
            landed.at[:, part_rows(me, b)],
            part_sent.at[d - 1, b],
            part_got.at[me, b],
            "row",
            to,
        )

    def project(b, d):
        values = (polished if polish else whole)[pl.ds(b * per, per)].reshape(many, whole.shape[-1])
        here, there = part_rows(me, b), part_rows(0, b)
        t = lax.rem(me + d, n_row)
        for k in range(parts):
            column = columns(k * n_row + t)
            found = jnp.dot(values, weight[:, column], preferred_element_type=jnp.float32) + bias[:, column]
            if parts == 3 and k < 2:
                found = spin(found, cosines[here, :], sines[here, :])
            found = found.astype(jnp.bfloat16)
            if parts == 3 and k == 0:
                found = (found * jnp.asarray(HEAD_DIM**-0.5, jnp.bfloat16)).astype(jnp.bfloat16)

            @pl.when(d > 0)
            def _(k=k, found=found):
                leaving[d - 1, k, there, :] = found

            @pl.when(d == 0)
            def _(k=k, found=found):
                landed[k, here, :] = found

        @pl.when(d > 0)
        def _():
            part_copy(b, d).start()

    def sums_copy(d):
        to = lax.rem(i + d, n)
        return pltpu.make_async_remote_copy(
            src_ref=outs[-1].at[:, pl.ds(pl.multiple_of(to * width, 128), width)],
            dst_ref=all_sums.at[section, i],
            send_sem=last_sent.at[d],
            recv_sem=last_got.at[section, i],
            device_id={"section": 0, "col": to},
            device_id_type=pl.DeviceIdType.MESH,
        )

    def sums_arrive(s, o):
        return pltpu.make_async_remote_copy(
            src_ref=outs[-1].at[:, pl.ds(0, width)],
            dst_ref=all_sums.at[s, o],
            send_sem=last_sent.at[0],
            recv_sem=last_got.at[s, o],
            device_id={"section": 0, "col": o},
            device_id_type=pl.DeviceIdType.MESH,
        )

    def middle_slot(k):
        return jnp.maximum(lag * k + n - 1 - k, lag * (n - 1 - k) + k)

    def at(now, slot, allowed):
        since = now - slot
        c = jnp.maximum(since, 0) // n
        return c, allowed & (since >= 0) & (lax.rem(jnp.maximum(since, 0), n) == 0) & (since < n * chunks)

    def step(now, carry):
        for j in range(n - 1, 0, -1):
            c, due = at(now, lag * i + n - 1 - j, i < j)

            @pl.when(due & first)
            def _(c=c, j=j):
                outgoing[c, j] = partial[c, j]

            @pl.when(due & (i > 0))
            def _(c=c, j=j):
                arrive(c, j + 1)
                both = arrived[c, j + 1].astype(jnp.float32) + partial[c, j].astype(jnp.float32)
                outgoing[c, j] = both.astype(jnp.bfloat16)

            @pl.when(due)
            def _(c=c, j=j):
                sum_copy(c, j, True).start()

        for j in range(n - 1):
            c, due = at(now, lag * (n - 1 - i) + j, i > j)

            @pl.when(due & last)
            def _(c=c, j=j):
                outgoing[c, j] = partial[c, j]

            @pl.when(due & (i < n - 1))
            def _(c=c, j=j):
                arrive(c, j)
                both = arrived[c, j].astype(jnp.float32) + partial[c, j].astype(jnp.float32)
                outgoing[c, j] = both.astype(jnp.bfloat16)

            @pl.when(due)
            def _(c=c, j=j):
                sum_copy(c, j, False).start()

        c, due = at(now, middle_slot(i), i >= 0)

        @pl.when(due)
        def _():
            total[...] = partial[c, i].astype(jnp.float32)

        @pl.when(due & (i > 0))
        def _():
            arrive(c, i + 1)
            total[...] += arrived[c, i + 1].astype(jnp.float32)

        @pl.when(due & (i < n - 1))
        def _():
            arrive(c, i)
            total[...] += arrived[c, i].astype(jnp.float32)

        @pl.when(due)
        def _():
            block = middle(total[...], c, ins, outs)
            if spread:
                outgoing[c, i] = block
                for d in range(1, n):
                    slice_copy(c, d).start()

                @pl.when(section == 0)
                def _():
                    whole[0, c, i] = outgoing[c, i, :, pl.ds(pl.multiple_of(i * width, 128), width)]

                @pl.when(section != 0)
                def _():
                    slice_copy(c, 0).start()

            else:
                whole[c, i] = block
                work(c, i)

        if spread:
            return carry

        @pl.when(due & (i < n - 1))
        def _():
            block_copy(c, i, True, own=True).start()

        @pl.when(due & (i > 0))
        def _():
            block_copy(c, i, False, own=True).start()

        for o in range(n - 1):
            c, due = at(now, middle_slot(o) + lag * (i - o), i > o)

            @pl.when(due)
            def _(c=c, o=o):
                block_copy(c, o, True).wait_recv()

            @pl.when(due & (i < n - 1))
            def _(c=c, o=o):
                block_copy(c, o, True).start()

            @pl.when(due)
            def _(c=c, o=o):
                work(c, o)

        for o in range(1, n):
            c, due = at(now, middle_slot(o) + lag * (o - i), i < o)

            @pl.when(due)
            def _(c=c, o=o):
                block_copy(c, o, False).wait_recv()

            @pl.when(due & (i > 0))
            def _(c=c, o=o):
                block_copy(c, o, False).start()

            @pl.when(due)
            def _(c=c, o=o):
                work(c, o)

        if parts:
            since = now - (n * (per - 1) + 2 * lag * (n - 1))
            given = jnp.maximum(since, 0)
            turn = lax.rem(given, n * per) // unit

            @pl.when(since == 0)
            def _():
                weight_copy.wait()

            @pl.when((since >= 0) & (lax.rem(given, unit) == 0) & (turn < n_row) & (given < n * chunks))
            def _():
                project(given // (n * per), lax.rem(turn + 1, n_row))

        return carry

    steps = n * (chunks - 1) + 2 * lag * (n - 1) + 1
    lax.fori_loop(0, steps + (unit * (n_row - 1) if parts else 0), step, 0)

    if spread:
        for d in range(1, n):
            sums_copy(d).start()

        @pl.when(section == 0)
        def _():
            all_sums[0, i] = outs[-1][:, pl.ds(pl.multiple_of(i * width, 128), width)]

        @pl.when(section != 0)
        def _():
            sums_copy(0).start()

    def slice_arrives(c, s, o):
        return pltpu.make_async_remote_copy(
            src_ref=outgoing.at[c, 0, :, pl.ds(0, width)],
            dst_ref=whole.at[s, c, o],
            send_sem=block_sent.at[c, 0],
            recv_sem=block_got.at[s, c, o],
            device_id={"section": 0, "col": o},
            device_id_type=pl.DeviceIdType.MESH,
        )

    def settle(c, carry):
        for j in range(n):
            @pl.when(j != i)
            def _(j=j):
                sum_copy(c, j, True).wait_send()

        if spread:
            for d in range(1, n):
                slice_copy(c, d).wait_send()

            @pl.when(section != 0)
            def _():
                slice_copy(c, 0).wait_send()

            for s in range(2):
                for o in range(n):
                    @pl.when((section == 0) & ((s == 1) | (o != i)))
                    def _(s=s, o=o):
                        slice_arrives(c, s, o).wait_recv()

            return carry
        for o in range(n):
            @pl.when((o <= i) & (i < n - 1))
            def _(o=o):
                block_copy(c, o, True).wait_send()

            @pl.when((o > i) & (i > 0))
            def _(o=o):
                block_copy(c, o, True).wait_send()

        @pl.when(i > 0)
        def _():
            block_copy(c, i, False, own=True).wait_send()

        return carry

    lax.fori_loop(0, chunks, settle, 0)
    if spread:
        for d in range(1, n):
            sums_copy(d).wait_send()

        @pl.when(section != 0)
        def _():
            sums_copy(0).wait_send()

        for s in range(2):
            for o in range(n):
                @pl.when((section == 0) & ((s == 1) | (o != i)))
                def _(s=s, o=o):
                    sums_arrive(s, o).wait_recv()

    for s, d in others:
        more_copy(s, d).wait_send()
        more_arrives(s, d).wait_recv()

    if parts:
        def settle_parts(b, carry):
            for d in range(1, n_row):
                part_copy(b, d).wait_send()
                source = lax.rem(me + d, n_row)
                remote(
                    leaving.at[0, :, part_rows(0, b)],
                    landed.at[:, part_rows(source, b)],
                    part_sent.at[0, b],
                    part_got.at[source, b],
                    "row",
                    source,
                ).wait_recv()
            return carry

        lax.fori_loop(0, chunks // per, settle_parts, 0)

    for k, layer in enumerate(layers):
        @pl.when(section != layer)
        def _(k=k):
            carry_copy(k).wait_send()

        @pl.when(section == layer)
        def _(k=k):
            carry_copy(k).wait_recv()


def relay(middle, number, partial, ins, outs, n, spread=False, carry=(), behind=(), polish=(), project=(), n_row=1, lag=3, rows=RELAY_ROWS):
    tokens, features = partial.shape
    owned = tokens // n
    chunks = owned // rows
    blocks = lambda values: values.reshape(chunks, rows, features) if values.shape[0] == owned else values
    ins = [blocks(values) for values in ins] + list(polish) + list(project)
    parts = project[0].shape[1] // (n_row * LANES) if project else 0
    batches = chunks // max(1, min(chunks, LANES // (n * rows)))
    outs = list(outs) + ([(tokens, features)] if polish else []) + ([(parts, n_row * tokens, LANES)] if parts else []) + ([(2, n, 2, features // n), (2, n, 8, features // n)] if spread else [])
    out_shapes = [
        jax.ShapeDtypeStruct(
            (2, chunks, n, rows, features // n) if spread else (chunks, n, rows, features), jnp.bfloat16
        )
    ] + [
        jax.ShapeDtypeStruct((chunks, n, rows, features), jnp.bfloat16)
        if shape[0] == tokens
        else jax.ShapeDtypeStruct(shape, jnp.bfloat16)
        if shape[-1] == LANES
        else jax.ShapeDtypeStruct((chunks, rows, features) if shape[0] == owned else shape, jnp.float32)
        for shape in outs
    ]
    vmem, anywhere = pl.BlockSpec(memory_space=pltpu.VMEM), pl.BlockSpec(memory_space=pl.ANY)
    specs = [vmem] * (1 + len(ins))
    if project:
        specs[-4] = anywhere
    layers = tuple(layer for layer, _ in carry)
    carry = [values for _, values in carry]
    whole, *rest = pl.pallas_call(
        functools.partial(relay_kernel, middle, len(ins), len(outs), layers, len(behind), bool(polish), parts, n_row, n, chunks, lag, spread),
        in_specs=specs + [anywhere] * (len(carry) + len(behind)),
        out_specs=[vmem] * len(out_shapes) + [anywhere] * len(carry),
        out_shape=out_shapes + [jax.ShapeDtypeStruct(values.shape, values.dtype) for values in carry],
        scratch_shapes=[
            pltpu.VMEM((chunks, n + 1, rows, features), jnp.bfloat16),
            pltpu.VMEM((chunks, n, rows, features), jnp.bfloat16),
            pltpu.VMEM((rows, features), jnp.float32),
            pltpu.SemaphoreType.DMA((chunks, n)),
            pltpu.SemaphoreType.DMA((chunks, n + 1)),
            pltpu.SemaphoreType.DMA((chunks, n + 1)),
            pltpu.SemaphoreType.DMA((2 if spread else 1, chunks, n)),
            pltpu.SemaphoreType.DMA((max(1, len(carry)),)),
            pltpu.SemaphoreType.DMA((max(1, len(carry)),)),
            pltpu.SemaphoreType.DMA((n,)),
            pltpu.SemaphoreType.DMA((2, n)),
        ]
        + (
            [
                pltpu.VMEM((n_row - 1, parts, tokens, LANES), jnp.bfloat16),
                pltpu.SemaphoreType.DMA((n_row - 1, batches)),
                pltpu.SemaphoreType.DMA((n_row, batches)),
                pltpu.VMEM((features, project[0].shape[1]), jnp.bfloat16),
                pltpu.SemaphoreType.DMA,
            ]
            if parts
            else []
        )
        + ([pltpu.SemaphoreType.DMA((2, n)), pltpu.SemaphoreType.DMA((2, n))] if spread else []),
        compiler_params=pltpu.CompilerParams(
            collective_id=number, has_side_effects=True, vmem_limit_bytes=56 * 2**20
        ),
        cost_estimate=pl.CostEstimate(flops=0, bytes_accessed=35 * 10**7, transcendentals=0),
    )(partial.reshape(chunks, n, rows, features), *ins, *carry, *behind)
    shapes = {(chunks, rows, features): (owned, features), (chunks, n, rows, features): (tokens, features)}
    rest = [values.reshape(shapes.get(values.shape, values.shape)) for values in rest]
    return [whole.reshape((2, tokens, -1) if spread else (tokens, -1))] + rest


def gather_kernel(n, chunks, lag, own, small, angles, whole, smalls, normed, cosines, sines, sent, got, small_sent, small_got):
    section, i = lax.axis_index("section"), lax.axis_index("col")
    rows, width = own.shape[0] // chunks, own.shape[1]
    others = [(s, d) for s in range(2) for d in range(n) if (s, d) != (0, 0)]
    place = lambda s, d: {"section": lax.rem(section + s, 2), "col": lax.rem(i + d, n)}
    barrier = pltpu.get_barrier_semaphore()
    for s, d in others:
        pl.semaphore_signal(barrier, 1, device_id=place(s, d), device_id_type=pl.DeviceIdType.MESH)
    pl.semaphore_wait(barrier, len(others))

    def small_copy(s, d):
        return pltpu.make_async_remote_copy(
            src_ref=small,
            dst_ref=smalls.at[section, i],
            send_sem=small_sent.at[s, d],
            recv_sem=small_got.at[section, i],
            device_id=place(s, d),
            device_id_type=pl.DeviceIdType.MESH,
        )

    for s, d in others:
        small_copy(s, d).start()
    smalls[section, i] = small[...]

    def small_arrives(s, d):
        from_s, from_d = lax.rem(section + s, 2), lax.rem(i + d, n)
        return pltpu.make_async_remote_copy(
            src_ref=small,
            dst_ref=smalls.at[from_s, from_d],
            send_sem=small_sent.at[s, d],
            recv_sem=small_got.at[from_s, from_d],
            device_id=place(s, d),
            device_id_type=pl.DeviceIdType.MESH,
        )

    def norm(c):
        here = pl.ds(pl.multiple_of(c * rows, rows), rows)
        values = whole[here, :].astype(jnp.float32)
        mean, inverse = norm_parts(values)
        for o in range(n):
            part = slice(o * width, (o + 1) * width)
            gain, shift = smalls[0, o, 0:1, :], smalls[0, o, 2:3, :]
            normed[here, part] = ((values[:, part] - mean) * inverse * gain + shift).astype(jnp.bfloat16)

    def block(c, o, right, mine=False):
        part = whole.at[pl.ds(pl.multiple_of(c * rows, rows), rows), columns(o, width)]
        return remote(
            part, part, sent.at[c, n if mine and not right else o], got.at[c, o], "col", i + 1 if right else i - 1
        )

    def at(now, slot, allowed):
        since = jnp.maximum(now - slot, 0)
        return since // (n - 1), allowed & (now >= slot) & (lax.rem(since, n - 1) == 0) & (since < (n - 1) * chunks)

    def step(now, carry):
        c, due = at(now, 0, i >= 0)

        @pl.when(due)
        def _():
            here = pl.ds(pl.multiple_of(c * rows, rows), rows)
            whole[here, columns(i, width)] = own[here, :]

        @pl.when(due & (i < n - 1))
        def _():
            block(c, i, True, True).start()

        @pl.when(due & (i > 0))
        def _():
            block(c, i, False, True).start()

        for o in range(n):
            c, due = at(now, lag * jnp.abs(i - o), i != o)

            @pl.when(due)
            def _(c=c, o=o):
                block(c, o, True).wait_recv()

            @pl.when(due & (i > o) & (i < n - 1))
            def _(c=c, o=o):
                block(c, o, True).start()

            @pl.when(due & (i < o) & (i > 0))
            def _(c=c, o=o):
                block(c, o, False).start()

        c, due = at(now, lag * (n - 1), i >= 0)

        @pl.when(due)
        def _():
            norm(c)

        return carry

    turns = angles.shape[0] // 2
    lane = lax.broadcasted_iota(jnp.int32, (turns, LANES), 1)
    place_of = lax.broadcasted_iota(jnp.int32, (turns, LANES), 0)
    turned = lane % HEAD_DIM < 2 * turns
    picked = jnp.where(turned & (lane % turns == place_of), 1.0, 0.0)
    sign = jnp.where(lane % HEAD_DIM < turns, -1.0, 1.0)

    def spread_out(table, pick):
        return lax.dot_general(
            table, pick, (((0,), (0,)), ((), ())), precision=lax.Precision.HIGHEST, preferred_element_type=jnp.float32
        )

    still = jnp.where(turned[:1], 0.0, 1.0)
    cosines[...] = spread_out(angles[:turns, :], picked) + still
    sines[...] = spread_out(angles[turns:, :], picked * sign)
    for s, d in others:
        small_arrives(s, d).wait_recv()

    lax.fori_loop(0, (n - 1) * (chunks - 1) + lag * (n - 1) + 1, step, 0)

    def settle(c, carry):
        for o in range(n):
            @pl.when(((o <= i) & (i < n - 1)) | ((o > i) & (i > 0)))
            def _(o=o):
                block(c, o, True).wait_send()

        @pl.when(i > 0)
        def _():
            block(c, i, False, True).wait_send()

        return carry

    lax.fori_loop(0, chunks, settle, 0)
    for s, d in others:
        small_copy(s, d).wait_send()


def gathered(number, own, small, angles, n, lag=3, rows=64):
    tokens, width = own.shape
    chunks = tokens // rows
    vmem = pl.BlockSpec(memory_space=pltpu.VMEM)
    return pl.pallas_call(
        functools.partial(gather_kernel, n, chunks, lag),
        in_specs=[vmem] * 3,
        out_specs=[vmem] * 5,
        out_shape=[
            jax.ShapeDtypeStruct((tokens, n * width), own.dtype),
            jax.ShapeDtypeStruct((2, n) + small.shape, small.dtype),
            jax.ShapeDtypeStruct((tokens, n * width), own.dtype),
            jax.ShapeDtypeStruct((angles.shape[1], LANES), jnp.float32),
            jax.ShapeDtypeStruct((angles.shape[1], LANES), jnp.float32),
        ],
        scratch_shapes=[
            pltpu.SemaphoreType.DMA((chunks, n + 1)),
            pltpu.SemaphoreType.DMA((chunks, n)),
            pltpu.SemaphoreType.DMA((2, n)),
            pltpu.SemaphoreType.DMA((2, n)),
        ],
        compiler_params=pltpu.CompilerParams(
            collective_id=number, has_side_effects=True, vmem_limit_bytes=40 * 2**20
        ),
        cost_estimate=pl.CostEstimate(flops=0, bytes_accessed=25 * 10**7, transcendentals=0),
    )(own, small, angles)


def ffn_kernel(units, values, weight, down, gate_up, hidden, partial):
    both = jnp.dot(values[...], weight[...], preferred_element_type=jnp.float32)
    gate_up[...] = both
    gate, up = both[:, :units], both[:, units:]
    found = (gate * (1.0 / (1.0 + jnp.exp(-gate))) * up).astype(jnp.bfloat16)
    hidden[...] = found
    partial[...] = dot_last(found, down[...]).astype(partial.dtype)


def ffn_back_kernel(units, branch, gate_up, weight, down, d_gate_up, partial):
    d_hidden = jnp.dot(branch[...], down[...], preferred_element_type=jnp.float32)
    gate, up = gate_up[:, :units], gate_up[:, units:]
    sig = 1.0 / (1.0 + jnp.exp(-gate))
    d_gate_up[:, :units] = (d_hidden * up * sig * (1.0 + gate * (1.0 - sig))).astype(jnp.bfloat16)
    d_gate_up[:, units:] = (d_hidden * gate * sig).astype(jnp.bfloat16)
    partial[...] = dot_last(d_gate_up[...], weight[...]).astype(partial.dtype)


def ffn_call(kernel, layer, inputs, weight, down, outs, rows=256):
    tokens = inputs[0].shape[0]
    units = down.shape[1]
    by_rows = lambda width: pl.BlockSpec((rows, width), lambda i: (i, 0))
    once = lambda width: pl.BlockSpec((D, width), lambda i: (layer, 0), pipeline_mode=pl.Buffered(1))
    return pl.pallas_call(
        functools.partial(kernel, units),
        grid=(tokens // rows,),
        in_specs=[by_rows(values.shape[1]) for values in inputs] + [once(2 * units), once(units)],
        out_specs=[by_rows(width) for width, _ in outs],
        out_shape=[jax.ShapeDtypeStruct((tokens, width), kind) for width, kind in outs],
        compiler_params=pltpu.CompilerParams(vmem_limit_bytes=58 * 2**20),
        cost_estimate=pl.CostEstimate(flops=6 * tokens * D * units, bytes_accessed=4 * 10**7, transcendentals=0),
    )(*inputs, weight, down)


def rotary_angles(positions):
    half_dims = ROT // 2
    inverse_freq = 1.0 / 10000.0 ** (jnp.arange(half_dims, dtype=jnp.float32) * 2.0 / ROT)
    angles = positions.astype(jnp.float32)[None, :] * inverse_freq[:, None]
    return jnp.concatenate([jnp.cos(angles), jnp.sin(angles)])


def product(left, right):
    return jnp.dot(left, right, preferred_element_type=jnp.float32)


def per_device(
    inputs,
    cotangent,
    block_ids,
    norm_gains,
    norm_shifts,
    qkv_weight,
    qkv_bias,
    out_weight,
    gate_up_weight,
    down_weight,
):
    section = lax.axis_index("section")
    row = lax.axis_index("row")
    col = lax.axis_index("col")
    rows_axis = lax.axis_size("row")
    cols_axis = lax.axis_size("col")
    tokens, width = inputs.shape[1:]
    owned = tokens // cols_axis
    units = down_weight.shape[2]
    seq = tokens * rows_axis
    both = ("section", "row")
    whole_lanes = width == rows_axis * LANES
    heads = LANES // HEAD_DIM if whole_lanes else 1
    copies = 1 if whole_lanes else rows_axis * HEAD_DIM // width

    def expand(values):
        if whole_lanes:
            return values
        rows = values.shape[0]
        values = values.reshape(rows, -1, width // HEAD_DIM, HEAD_DIM)
        values = jnp.pad(jnp.repeat(values, copies, axis=2), ((0, 0), (0, 0), (0, 0), (0, LANES - HEAD_DIM)))
        return values.reshape(rows, -1)

    def contract(values):
        if whole_lanes:
            return values
        values = values.reshape(tokens, -1, rows_axis, LANES)[:, :, ::copies, :HEAD_DIM]
        return values.reshape(tokens, -1)

    def weights_of(block):
        block = block[0].reshape(block.shape[1], -1)
        return lax.all_gather(block, both, axis=0, tiled=True).reshape(2, D, -1)

    def mine(values):
        blocks = values.reshape(owned // RELAY_ROWS, cols_axis, RELAY_ROWS, -1)
        return lax.dynamic_index_in_dim(blocks, col, 1, keepdims=False).reshape(owned, -1)

    def my_features(values):
        return lax.dynamic_slice_in_dim(values, col * width, width, 1)

    own_small = jnp.concatenate([norm_gains[0], norm_shifts[0], qkv_bias[0], jnp.zeros((1, width), jnp.float32)])
    angles = rotary_angles(jnp.arange(seq, dtype=jnp.int32))
    stream, small, normed, cosines, sines = gathered(
        7, lax.dynamic_index_in_dim(inputs, section, 0, keepdims=False), own_small, angles, cols_axis
    )
    whole_small = small.transpose(0, 2, 1, 3).reshape(2, own_small.shape[0], D)
    gains, shifts = whole_small[:, :2], whole_small[:, 2:4]
    bias = lax.dynamic_index_in_dim(small, col, 1, keepdims=False)[:, 4:7].reshape(2, -1)

    qkv_w = weights_of(qkv_weight)
    out_w = weights_of(out_weight)
    gate_up_w = weights_of(gate_up_weight)
    down_w = weights_of(down_weight)

    ids = lax.dynamic_index_in_dim(block_ids, section, 0, keepdims=False)
    def feed_forward(layer, values):
        kind = jnp.bfloat16 if layer == 0 else jnp.float32
        if layer == 1 and units % LANES == 0:
            outs = [(2 * units, jnp.float32), (units, jnp.bfloat16), (D, kind)]
            return ffn_call(ffn_kernel, layer, [values], all_gate_up, all_down, outs)
        gate_up = product(values, gate_up_w[layer])
        hidden = (jax.nn.silu(gate_up[:, :units]) * gate_up[:, units:]).astype(jnp.bfloat16)
        return gate_up, hidden, dot_last(hidden, down_w[layer]).astype(kind)

    def feed_back(layer, branch, gate_up):
        if units % LANES == 0:
            outs = [(2 * units, jnp.bfloat16), (D, jnp.bfloat16)]
            return ffn_call(ffn_back_kernel, layer, [branch, gate_up], all_gate_up, all_down, outs)
        gate, up = gate_up[:, :units], gate_up[:, units:]
        d_hidden = product(branch, down_w[layer])
        sig = jax.nn.sigmoid(gate)
        d_gate = d_hidden * up * sig * (1.0 + gate * (1.0 - sig))
        d_up = d_hidden * gate * sig
        d_gate_up = jnp.concatenate([d_gate, d_up], axis=1).astype(jnp.bfloat16)
        return d_gate_up, dot_last(d_gate_up, gate_up_w[layer]).astype(jnp.bfloat16)

    all_gate_up, all_down = gate_up_w.reshape(2 * D, -1), down_w.reshape(2 * D, -1)
    kept = []
    hidden_out = []

    def gathered_part(which, half):
        values = lax.dynamic_index_in_dim(cotangent, which, 0, keepdims=False)
        cut = tokens * 3 // 8
        values = values[cut:] if half else values[:cut]
        return lax.all_gather(values, "col", axis=1, tiled=True)

    first_part = gathered_part(section, 0)
    waited = [first_part]
    for layer in range(2):
        if layer == 0:
            qkv = expand(product(normed, qkv_w[0]) + bias[0])
            spread, mixed, log_sums, attn_mix = attend(
                8, ids, heads, rows_axis, tokens, qkv=qkv, cosines=cosines, sines=sines
            )
        else:
            here = section + jnp.where(hidden_out[0][0, 0] == hidden_out[0][0, 0], 0, 1)
            second_part = gathered_part(here, 1)
            waited = [second_part]
            spread, mixed, log_sums, attn_mix = attend(9, ids, heads, rows_axis, tokens, spread=spread)
        attn_mix = contract(attn_mix)
        normed_two, after = relay(
            after_attention,
            layer,
            product(attn_mix, out_w[layer].T).astype(jnp.bfloat16),
            [mine(stream), gains[layer, 1:], shifts[layer, 1:]],
            [(owned, D)],
            cols_axis,
            behind=waited,
        )
        gate_up, hidden, partial = feed_forward(layer, normed_two)
        kept.append((stream, normed, spread, mixed, log_sums, attn_mix, after, normed_two, gate_up, hidden))
        if layer == 0:
            stream, normed, spread = relay(
                after_hidden,
                2,
                partial.astype(jnp.bfloat16),
                [after],
                [],
                cols_axis,
                polish=(gains[1, :1], shifts[1, :1]),
                project=(expand(qkv_w.reshape(2 * D, -1)), expand(bias[1:]), cosines, sines),
                n_row=rows_axis,
            )
            hidden_out.append(my_features(stream))
        else:
            blocks = partial.reshape(owned // RELAY_ROWS, cols_axis, RELAY_ROWS, D)
            owner = lax.broadcasted_iota(jnp.int32, blocks.shape, 1) == col
            blocks = blocks + jnp.where(owner, after.reshape(-1, 1, RELAY_ROWS, D), 0.0)
            result = blocks.reshape(tokens, D).astype(jnp.bfloat16)

    branch = jnp.concatenate([first_part, second_part])
    grad = mine(branch).astype(jnp.float32)
    weight_sums = [[], []]
    small_sums = []
    bias_grads = [None, None]
    input_out = [None, None]
    input_got = [None, None]
    hidden_got = [None, None]

    def collect(layer, term):
        weight_sums[layer].append(lax.psum_scatter(term, "row", scatter_dimension=0, tiled=True))
        return weight_sums[layer][-1]

    arrived = [[None] * 3, [None] * 3]
    def together(*values):
        return lax.optimization_barrier(values)

    for layer in (1, 0):
        stream, normed, spread, mixed, log_sums, attn_mix, after, normed_two, gate_up, hidden = kept[layer]
        d_gate_up, partial = feed_back(layer, branch, gate_up)
        partial, down_term, gate_up_term = together(
            partial,
            dot_first(branch, hidden).astype(jnp.bfloat16),
            dot_first(normed_two, d_gate_up).astype(jnp.bfloat16),
        )
        down_sum, gate_up_sum = collect(layer, down_term), collect(layer, gate_up_term)
        grad_attn, d_after, sums_two, *got = relay(
            behind_norm,
            3 + layer,
            partial,
            [grad, after, gains[layer, 1:]],
            [(owned, D), (2, D)],
            cols_axis,
            carry=[]
            if layer == 1
            else [(0, hidden_out[0]), (1, hidden_out[1]), (1, input_out[1]), (1, weight_sums[1][2])],
            behind=[] if layer == 1 else [weight_sums[1][0]],
        )
        if layer == 1:
            result = jnp.where(d_after[0, 0] == d_after[0, 0], result, 0)
            hidden_out.append(lax.psum_scatter(result, "col", scatter_dimension=1, tiled=True))
        else:
            hidden_got[0], hidden_got[1], input_got[1], arrived[1][2] = got
        small_sums += [sums_two]
        d_mix, out_term = together(
            product(grad_attn, out_w[layer]).astype(jnp.bfloat16), dot_first(grad_attn, attn_mix).astype(jnp.bfloat16)
        )
        out_sum = collect(layer, out_term)
        d_qkv, arrived[layer][1] = attend_back(
            10 + layer,
            expand(d_mix),
            spread,
            mixed,
            log_sums,
            ids,
            cosines,
            sines,
            heads,
            rows_axis,
            layer,
            gate_up_sum,
        )
        d_qkv = contract(d_qkv)
        partial, qkv_term, bias_grads[layer] = together(
            dot_last(d_qkv, qkv_w[layer]).astype(jnp.bfloat16),
            dot_first(normed, d_qkv).astype(jnp.bfloat16),
            jnp.sum(d_qkv.astype(jnp.float32), axis=0),
        )
        if layer == 1:
            qkv_terms = jnp.pad(qkv_term, ((D, 0), (0, 0)))
        else:
            qkv_terms = lax.dynamic_update_slice(qkv_terms, qkv_term, (0, 0))
            qkv_grad = lax.psum_scatter(qkv_terms, both, scatter_dimension=0, tiled=True).astype(jnp.float32)
        branch, grad, sums_one, *got = relay(
            behind_norm,
            5 + layer,
            partial,
            [d_after, mine(stream), gains[layer, :1]]
            + ([] if layer == 1 else [jnp.concatenate(small_sums + [jnp.zeros((2, D), jnp.float32)])]),
            [(owned, D), (2, D)],
            cols_axis,
            spread=layer == 0,
            carry=[] if layer == 1 else [(0, down_sum), (0, out_sum), (1, weight_sums[1][0])],
            behind=[hidden_out[1]] if layer == 1 else [],
        )
        if layer == 0:
            late_sums, early_sums, arrived[0][0], arrived[0][2], arrived[1][0] = got
        small_sums += [sums_one]
        input_out[layer] = my_features(branch) if layer == 1 else branch

    hidden_states = jnp.where(
        section == 0, jnp.stack([hidden_out[0], hidden_got[0]]), jnp.stack([hidden_got[1], hidden_out[1]])
    )
    input_grads = jnp.where(section == 0, input_out[0], jnp.stack([input_got[1], input_out[1]])).astype(jnp.float32)
    down_grad, gate_up_grad, out_grad = (
        jnp.where(section == 0, first, second).astype(jnp.float32)
        + jnp.where(section == 0, first_got, second_got).astype(jnp.float32)
        for first, second, first_got, second_got in zip(*weight_sums, *arrived)
    )
    early = 0.5 * jnp.sum(early_sums, axis=(0, 1))[:6]
    last = jnp.where(section == 0, jnp.sum(late_sums, axis=(0, 1)), 0.0)
    sums = lax.psum(jnp.concatenate([early, bias_grads[1].reshape(3, -1), bias_grads[0].reshape(3, -1), last]), both)
    early, last = sums[:12], sums[12:]
    norm_sums = jnp.where(section == 0, jnp.stack([last, early[4:6]]), jnp.stack([early[2:4], early[0:2]]))
    bias_sum = jnp.where(section == 0, early[9:12], early[6:9])
    return (
        hidden_states[None],
        input_grads[None],
        norm_sums[:, 0][None],
        norm_sums[:, 1][None],
        qkv_grad.reshape(qkv_weight.shape),
        bias_sum.reshape(qkv_bias.shape),
        out_grad[None],
        gate_up_grad.reshape(gate_up_weight.shape),
        down_grad[None],
    )


def solution(mesh):
    in_specs = (
        P(None, "row", "col"),
        P(None, "row", "col"),
        P(),
        P("section", None, "col"),
        P("section", None, "col"),
        P("section", "row", None, "col"),
        P("section", None, "col"),
        P("section", "row", "col"),
        P("section", "row", None, "col"),
        P("section", "row", "col"),
    )
    out_specs = (
        P("section", None, "row", "col"),
        P("section", None, "row", "col"),
        P("section", None, "col"),
        P("section", None, "col"),
        P("section", "row", None, "col"),
        P("section", None, "col"),
        P("section", "row", "col"),
        P("section", "row", None, "col"),
        P("section", "row", "col"),
    )
    return jax.shard_map(
        per_device, mesh=mesh, in_specs=in_specs, out_specs=out_specs, check_vma=False
    )
```

```python
import functools

import jax
import jax.numpy as jnp
from jax import lax
from jax.experimental import pallas as pl
from jax.experimental.pallas import tpu as pltpu
from jax.sharding import PartitionSpec as P

D = 2048
HEADS = 32
HEAD_DIM = 64
ROT = 16
LANES = 128
REACH = 256
RELAY_ROWS = 16


epsilon = 1e-05


def dot_last(a, b):
    return lax.dot_general(a, b, (((1,), (1,)), ((), ())), preferred_element_type=jnp.float32)


def dot_first(a, b):
    return lax.dot_general(a, b, (((0,), (0,)), ((), ())), preferred_element_type=jnp.float32)


def lanes_of(rows, head):
    lane = lax.broadcasted_iota(jnp.int32, (rows, LANES), 1)
    return lane // HEAD_DIM == head


def spin(x, cosines, sines):
    lane = lax.broadcasted_iota(jnp.int32, x.shape, 1)
    ahead, behind = pltpu.roll(x, LANES - ROT // 2, 1), pltpu.roll(x, ROT // 2, 1)
    return x * cosines + jnp.where(lane % ROT < ROT // 2, ahead, behind) * sines


def meet(axis, n):
    me = lax.axis_index(axis)
    barrier = pltpu.get_barrier_semaphore()
    for d in range(1, n):
        pl.semaphore_signal(
            barrier, 1, device_id={axis: lax.rem(me + d, n)}, device_id_type=pl.DeviceIdType.MESH
        )
    pl.semaphore_wait(barrier, n - 1)


def remote(source, target, sent, got, axis, device):
    return pltpu.make_async_remote_copy(
        src_ref=source,
        dst_ref=target,
        send_sem=sent,
        recv_sem=got,
        device_id={axis: device},
        device_id_type=pl.DeviceIdType.MESH,
    )


def columns(which, size=LANES):
    return pl.ds(pl.multiple_of(which * size, size), size)


def attend_kernel(heads, n, bq, given, bid_q, bid_k, *refs):
    me = lax.axis_index("row")
    if given:
        spread, mixed, lse_ref, mix, vone, scores, mix_sent, mix_got = refs
    else:
        qkv, cosines, sines, spread, mixed, lse_ref, mix, vone, scores, mix_sent, mix_got = refs[:11]
        leaving, qkv_sent, qkv_got = refs[11:]
    tokens = mix.shape[0]
    seq = n * tokens
    here = pl.ds(pl.multiple_of(me * tokens, tokens), tokens)
    low = jnp.bfloat16
    meet("row", n)

    def parts(t):
        cos, sin = cosines[here, :], sines[here, :]
        query = spin(qkv[:, columns(t)], cos, sin).astype(low) * jnp.asarray(HEAD_DIM**-0.5, low)
        key = spin(qkv[:, columns(n + t)], cos, sin).astype(low)
        return query.astype(low), key, qkv[:, columns(2 * n + t)].astype(low)

    def leave(d):
        to = lax.rem(me + d, n)
        return remote(leaving.at[d - 1], spread.at[:, here], qkv_sent.at[d - 1], qkv_got.at[me], "row", to)

    if not given:
        for d in range(1, n):
            for k, part in enumerate(parts(lax.rem(me + d, n))):
                leaving[d - 1, k] = part
            leave(d).start()
        for k, part in enumerate(parts(me)):
            spread[k, here, :] = part

    def come(row):
        if not given:
            @pl.when(row != me)
            def _():
                there = pl.ds(row * tokens, tokens)
                remote(leaving.at[0], spread.at[:, there], qkv_sent.at[0], qkv_got.at[row], "row", me).wait_recv()

        there = pl.ds(row * tokens, tokens)
        for h in range(heads):
            vone[h, there, :] = jnp.where(lanes_of(tokens, h), spread[2, there, :], jnp.ones((), low))

    def mix_copy(i, device):
        rows = pl.ds(lax.rem(i, tokens // bq) * bq, bq)
        return remote(
            mixed.at[pl.ds(i * bq, bq)], mix.at[rows, columns(me)], mix_sent.at[i], mix_got.at[me, lax.rem(i, tokens // bq)], "row", device
        )

    def block(i, carry):
        rows = pl.ds(pl.multiple_of(i * bq, bq), bq)
        q = spread[0, rows, :]
        bid = bid_q[rows, :]
        begin = i * bq
        ahead = jnp.where(begin + bq < seq, 1, 0)
        qs = [jnp.where(lanes_of(bq, h), q, jnp.zeros((), low)) for h in range(heads)]

        def score(start, size, tops, hide):
            span = pl.ds(pl.multiple_of(start, REACH), size)
            keys = spread[1, span, :]
            if hide:
                visible = bid_k[:, span] <= bid
            found = []
            for h in range(heads):
                s = dot_last(qs[h], keys)
                if hide:
                    s = jnp.where(visible, s, -1e30)
                scores[h, :, span] = s
                top = tops[h]
                for c in range(size // LANES):
                    top = jnp.maximum(top, s[:, c * LANES : (c + 1) * LANES])
                found.append(top)
            return tuple(found)

        tops = tuple(jnp.full((bq, LANES), -1e30, jnp.float32) for _ in range(heads))
        tops = lax.fori_loop(0, i // 2, lambda t, c: score(2 * t * bq, 2 * bq, c, False), tops)
        tops = lax.fori_loop(i // 2 * 2, i, lambda t, c: score(t * bq, bq, c, False), tops)
        tops = score(begin, bq, tops, True)
        tops = lax.fori_loop(0, ahead, lambda t, c: score(begin + bq, REACH, c, True), tops)
        tops = [jnp.max(top, axis=1, keepdims=True) for top in tops]

        def gather(start, size, sums):
            span = pl.ds(pl.multiple_of(start, REACH), size)
            found = []
            for h in range(heads):
                p = jnp.exp(scores[h, :, span] - tops[h]).astype(low)
                found.append(sums[h] + jnp.dot(p, vone[h, span, :], preferred_element_type=jnp.float32))
            return tuple(found)

        sums = tuple(jnp.zeros((bq, LANES), jnp.float32) for _ in range(heads))
        sums = lax.fori_loop(0, (i + 1) // 2, lambda t, c: gather(2 * t * bq, 2 * bq, c), sums)
        sums = lax.fori_loop((i + 1) // 2 * 2, i + 1, lambda t, c: gather(t * bq, bq, c), sums)
        sums = lax.fori_loop(0, ahead, lambda t, c: gather(begin + bq, REACH, c), sums)
        outcome = jnp.zeros((bq, LANES), jnp.float32)
        lse = jnp.zeros((bq, LANES), jnp.float32)
        for h in range(heads):
            totals = pltpu.roll(sums[h], HEAD_DIM, 1)
            outcome = jnp.where(lanes_of(bq, h), sums[h] / totals, outcome)
            lse = jnp.where(lanes_of(bq, h), tops[h] + jnp.log(totals), lse)
        mixed[rows, :] = outcome.astype(low)
        lse_ref[:, rows] = lse.T
        return carry

    per_row = tokens // bq
    for row in range(n):
        if row == 0:
            come(0)
        if row + 1 < n:
            come(row + 1)

        def run(half, carry, row=row):
            i = row * per_row + half
            block(i, 0)

            @pl.when(row == me)
            def _():
                mix[pl.ds(pl.multiple_of(half * bq, bq), bq), columns(me)] = mixed[pl.ds(pl.multiple_of(i * bq, bq), bq), :]

            @pl.when(row != me)
            def _():
                mix_copy(i, row).start()

            return carry

        lax.fori_loop(0, per_row, run, 0)

    if not given:
        for d in range(1, n):
            leave(d).wait_send()
    for i in range(n * per_row):
        @pl.when(i // per_row != me)
        def _(i=i):
            mix_copy(i, me).wait_send()

    for row in range(n):
        @pl.when(row != me)
        def _(row=row):
            for half in range(per_row):
                rows = pl.ds(half * bq, bq)
                remote(
                    mixed.at[pl.ds(0, bq)], mix.at[rows, columns(row)], mix_sent.at[0], mix_got.at[row, half], "row", me
                ).wait_recv()


def attend(number, block_all, heads, n, tokens, qkv=None, cosines=None, sines=None, spread=None, bq=512):
    bq = min(bq, tokens)
    seq = n * tokens
    vmem = pl.BlockSpec(memory_space=pltpu.VMEM)
    low = jnp.bfloat16
    given = spread is not None
    operands = [spread] if given else [qkv, cosines, sines]
    out_shape = [
        jax.ShapeDtypeStruct((3, seq, LANES), low),
        jax.ShapeDtypeStruct((seq, LANES), low),
        jax.ShapeDtypeStruct((LANES, seq), jnp.float32),
        jax.ShapeDtypeStruct((tokens, n * LANES), low),
    ][given:]
    exchange = [
        pltpu.VMEM((n - 1, 3, tokens, LANES), low),
        pltpu.SemaphoreType.DMA((n - 1,)),
        pltpu.SemaphoreType.DMA((n,)),
    ]
    found = pl.pallas_call(
        functools.partial(attend_kernel, heads, n, bq, given),
        in_specs=[vmem] * (2 + len(operands)),
        out_specs=[vmem] * len(out_shape),
        out_shape=out_shape,
        scratch_shapes=[
            pltpu.VMEM((heads, seq, LANES), low),
            pltpu.VMEM((heads, bq, seq), jnp.float32),
            pltpu.SemaphoreType.DMA((seq // bq,)),
            pltpu.SemaphoreType.DMA((n, tokens // bq)),
        ]
        + ([] if given else exchange),
        compiler_params=pltpu.CompilerParams(
            collective_id=number, has_side_effects=True, vmem_limit_bytes=58 * 2**20
        ),
        cost_estimate=pl.CostEstimate(flops=10**10, bytes_accessed=2 * 10**8, transcendentals=0),
    )(block_all.reshape(seq, 1), block_all.reshape(1, seq), *operands)
    return [spread] + list(found) if given else found


def attend_back_kernel(
    heads, n, bq, layer, bid_q, bid_k, d_mix, spread, mixed, lse_ref, cosines, sines, carry, *refs
):
    d_qkv, carried, grads, kone, dk_acc, dv_acc, leaving, g_sent, g_got, back_sent, back_got, carry_sent, carry_got = refs
    section = lax.axis_index("section")
    me = lax.axis_index("row")
    tokens = d_mix.shape[0]
    seq = n * tokens
    per_row = tokens // bq
    blocks = n * per_row
    low = jnp.bfloat16
    zero = jnp.zeros((), low)
    here = pl.ds(pl.multiple_of(me * tokens, tokens), tokens)
    barrier = pltpu.get_barrier_semaphore()
    pl.semaphore_signal(barrier, 1, device_id={"section": 1 - section}, device_id_type=pl.DeviceIdType.MESH)
    for d in range(1, n):
        pl.semaphore_signal(barrier, 1, device_id={"row": lax.rem(me + d, n)}, device_id_type=pl.DeviceIdType.MESH)
    pl.semaphore_wait(barrier, n)
    carry_copy = remote(carry, carried, carry_sent, carry_got, "section", layer)

    def give(d):
        to = lax.rem(me + d, n)
        return remote(d_mix.at[:, columns(to)], grads.at[here], g_sent.at[d - 1], g_got.at[me], "row", to)

    for d in range(1, n):
        give(d).start()

    @pl.when(section != layer)
    def _():
        carry_copy.start()

    grads[here, :] = d_mix[:, columns(me)]
    for h in range(heads):
        kone[h] = jnp.where(lanes_of(seq, h), spread[1], zero).T
    dk_acc[...] = jnp.zeros_like(dk_acc)
    dv_acc[...] = jnp.zeros_like(dv_acc)

    def tile(start, size, dq, hide, stuff):
        qs, gs, lses, deltas, bid = stuff
        span = pl.ds(pl.multiple_of(start, REACH), size)
        keys, values = spread[1, span, :], spread[2, span, :]
        dv, dk = dv_acc[span, :], dk_acc[span, :]
        if hide:
            visible = bid_k[span, :] <= bid
        for h in range(heads):
            s = dot_last(keys, qs[h])
            if hide:
                s = jnp.where(visible, s, -1e30)
            p = jnp.exp(s - lses[h])
            dp = dot_last(values, gs[h])
            ds = (p * (dp - deltas[h])).astype(low)
            dv = dv + jnp.dot(p.astype(low), gs[h], preferred_element_type=jnp.float32)
            dk = dk + jnp.dot(ds, qs[h], preferred_element_type=jnp.float32)
            dq = dq + jnp.dot(kone[h, :, span], ds, preferred_element_type=jnp.float32)
        dv_acc[span, :] = dv
        dk_acc[span, :] = dk
        return dq

    def block(i):
        rows = pl.ds(pl.multiple_of(i * bq, bq), bq)
        q, g = spread[0, rows, :], grads[rows, :]
        product = (g.astype(jnp.float32) * mixed[rows, :].astype(jnp.float32)).T
        span = lambda h: slice(h * HEAD_DIM, (h + 1) * HEAD_DIM)
        deltas = [jnp.sum(product[span(h)], axis=0, keepdims=True) for h in range(heads)]
        lses = [lse_ref[h * HEAD_DIM : h * HEAD_DIM + 1, rows] for h in range(heads)]
        qs = [jnp.where(lanes_of(bq, h), q, zero) for h in range(heads)]
        gs = [jnp.where(lanes_of(bq, h), g, zero) for h in range(heads)]
        stuff = (qs, gs, lses, deltas, bid_q[:, rows])
        begin = i * bq
        ahead = jnp.where(begin + bq < seq, 1, 0)
        dq = jnp.zeros((LANES, bq), jnp.float32)
        dq = lax.fori_loop(0, i, lambda t, c: tile(t * bq, bq, c, False, stuff), dq)
        dq = tile(begin, bq, dq, True, stuff)
        dq = lax.fori_loop(0, ahead, lambda t, c: tile(begin + bq, REACH, c, True, stuff), dq)
        return spin(dq.T * (HEAD_DIM**-0.5), cosines[rows, :], -sines[rows, :]).astype(low)

    def back_copy(k, i, device):
        half = lax.rem(i, per_row)
        rows = pl.ds(pl.multiple_of(half * bq, bq), bq)
        return remote(
            leaving.at[k, pl.ds(pl.multiple_of(i * bq, bq), bq)],
            d_qkv.at[rows, columns(k * n + me)],
            back_sent.at[k, i],
            back_got.at[k, me, half],
            "row",
            device,
        )

    def send(k, i, values):
        row = i // per_row
        half = lax.rem(i, per_row)

        @pl.when(row == me)
        def _():
            d_qkv[pl.ds(pl.multiple_of(half * bq, bq), bq), columns(k * n + me)] = values

        @pl.when(row != me)
        def _():
            leaving[k, pl.ds(pl.multiple_of(i * bq, bq), bq), :] = values
            back_copy(k, i, row).start()

    def keys_done(i):
        rows = pl.ds(pl.multiple_of(i * bq, bq), bq)
        send(1, i, spin(dk_acc[rows, :], cosines[rows, :], -sines[rows, :]).astype(low))
        send(2, i, dv_acc[rows, :].astype(low))

    for row in range(n - 1, -1, -1):
        @pl.when(row != me)
        def _(row=row):
            there = pl.ds(row * tokens, tokens)
            remote(d_mix.at[:, columns(0)], grads.at[there], g_sent.at[0], g_got.at[row], "row", me).wait_recv()

        def run(step, carry, row=row):
            i = row * per_row + per_row - 1 - step
            send(0, i, block(i))

            @pl.when(i + 1 < blocks)
            def _():
                keys_done(i + 1)

            return carry

        lax.fori_loop(0, per_row, run, 0)
    keys_done(0)

    for d in range(1, n):
        give(d).wait_send()

    def settle(i, carry):
        @pl.when(i // per_row != me)
        def _():
            half = lax.rem(i, per_row)
            rows = pl.ds(pl.multiple_of(half * bq, bq), bq)
            for k in range(3):
                back_copy(k, i, me).wait_send()
                remote(
                    leaving.at[k, pl.ds(0, bq)],
                    d_qkv.at[rows, columns(k * n + i // per_row)],
                    back_sent.at[k, 0],
                    back_got.at[k, i // per_row, half],
                    "row",
                    me,
                ).wait_recv()

        return carry

    lax.fori_loop(0, blocks, settle, 0)

    @pl.when(section != layer)
    def _():
        carry_copy.wait_send()

    @pl.when(section == layer)
    def _():
        carry_copy.wait_recv()


def attend_back(number, d_mix, spread, mixed, lse, block_all, cosines, sines, heads, n, layer, carry, bq=512):
    tokens = d_mix.shape[0]
    bq = min(bq, tokens)
    seq = n * tokens
    vmem = pl.BlockSpec(memory_space=pltpu.VMEM)
    low = jnp.bfloat16
    return pl.pallas_call(
        functools.partial(attend_back_kernel, heads, n, bq, layer),
        in_specs=[vmem] * 8 + [pl.BlockSpec(memory_space=pl.ANY)],
        out_specs=[vmem, pl.BlockSpec(memory_space=pl.ANY)],
        out_shape=[jax.ShapeDtypeStruct((tokens, 3 * n * LANES), low), jax.ShapeDtypeStruct(carry.shape, carry.dtype)],
        scratch_shapes=[
            pltpu.VMEM((seq, LANES), low),
            pltpu.VMEM((heads, LANES, seq), low),
            pltpu.VMEM((seq, LANES), jnp.float32),
            pltpu.VMEM((seq, LANES), jnp.float32),
            pltpu.VMEM((3, seq, LANES), low),
            pltpu.SemaphoreType.DMA((n - 1,)),
            pltpu.SemaphoreType.DMA((n,)),
            pltpu.SemaphoreType.DMA((3, seq // bq)),
            pltpu.SemaphoreType.DMA((3, n, tokens // bq)),
            pltpu.SemaphoreType.DMA,
            pltpu.SemaphoreType.DMA,
        ],
        compiler_params=pltpu.CompilerParams(
            collective_id=number, has_side_effects=True, vmem_limit_bytes=58 * 2**20
        ),
        cost_estimate=pl.CostEstimate(flops=10**10, bytes_accessed=3 * 10**8, transcendentals=0),
    )(block_all.reshape(1, seq), block_all.reshape(seq, 1), d_mix, spread, mixed, lse, cosines, sines, carry)


def norm_parts(values):
    mean = jnp.mean(values, axis=-1, keepdims=True)
    spread = jnp.mean(values * values, axis=-1, keepdims=True) - mean * mean
    return mean, lax.rsqrt(spread + epsilon)


def after_attention(total, c, ins, outs):
    stream, gain, shift = ins
    (after_ref,) = outs
    after = stream[c].astype(jnp.float32) + total
    after_ref[c] = after
    values = after.astype(jnp.bfloat16).astype(jnp.float32)
    mean, inverse = norm_parts(values)
    return ((values - mean) * inverse * gain[...] + shift[...]).astype(jnp.bfloat16)


def after_hidden(total, c, ins, outs):
    (after,) = ins
    return (after[c] + total).astype(jnp.bfloat16)


def behind_norm(total, c, ins, outs):
    grad, values_ref, gain = ins
    grad_ref, sums = outs
    values = values_ref[c].astype(jnp.bfloat16).astype(jnp.float32)
    mean, inverse = norm_parts(values)
    centred = (values - mean) * inverse
    scaled = total * gain[...]
    back = inverse * (
        scaled
        - jnp.mean(scaled, axis=-1, keepdims=True)
        - centred * jnp.mean(scaled * centred, axis=-1, keepdims=True)
    )
    given = grad[c] + back
    grad_ref[c] = given
    here = [jnp.sum(total * centred, axis=0, keepdims=True), jnp.sum(total, axis=0, keepdims=True)]

    @pl.when(c == 0)
    def _():
        sums[...] = jnp.zeros_like(sums)

    sums[...] += jnp.concatenate(here, axis=0)
    return given.astype(jnp.bfloat16)


def relay_kernel(
    middle, n_ins, n_outs, layers, n_after, polish, parts, n_row, n, chunks, lag, spread, partial, *refs
):
    ins, carry, refs = refs[:n_ins], refs[n_ins : n_ins + len(layers)], refs[n_ins + len(layers) + n_after :]
    whole, outs, refs = refs[0], refs[1 : 1 + n_outs], refs[1 + n_outs :]
    carried, refs = refs[: len(layers)], refs[len(layers) :]
    if parts:
        ins, (weights, bias, cosines, sines) = ins[:-4], ins[-4:]
        outs, landed = outs[:-1], outs[-1]
        *refs, leaving, part_sent, part_got, weight, weight_got = refs
        weight_copy = pltpu.make_async_copy(weights.at[pl.ds(weight.shape[0], weight.shape[0])], weight, weight_got)
        weight_copy.start()
    if polish:
        ins, (gain, shift) = ins[:-2], ins[-2:]
        outs, polished = outs[:-1], outs[-1]
    if spread:
        ins, more = ins[:-1], ins[-1]
        outs, all_sums, all_more = outs[:-2], outs[-2], outs[-1]
        *refs, more_sent, more_got = refs
    arrived, outgoing, total, sum_sent, sum_got, block_sent, block_got, carry_sent, carry_got, last_sent, last_got = refs
    section, i = lax.axis_index("section"), lax.axis_index("col")
    width = whole.shape[-1]
    first, last = i == 0, i == n - 1

    barrier = pltpu.get_barrier_semaphore()

    def greet(**place):
        pl.semaphore_signal(barrier, 1, device_id=place, device_id_type=pl.DeviceIdType.MESH)

    if spread:
        for d in range(1, 2 * n):
            greet(section=lax.rem(section + d // n, 2), col=lax.rem(i + d, n))
        pl.semaphore_wait(barrier, 2 * n - 1)
    else:
        greet(section=1 - section)
        me = lax.axis_index("row")
        row_peers = n_row - 1 if parts else 0
        for d in range(1, row_peers + 1):
            greet(row=lax.rem(me + d, n_row))

        @pl.when(i > 0)
        def _():
            greet(col=i - 1)

        @pl.when(i < n - 1)
        def _():
            greet(col=i + 1)

        @pl.when(first | last)
        def _():
            pl.semaphore_wait(barrier, 2 + row_peers)

        @pl.when((i > 0) & (i < n - 1))
        def _():
            pl.semaphore_wait(barrier, 3 + row_peers)

    def carry_copy(k):
        return remote(carry[k], carried[k], carry_sent.at[k], carry_got.at[k], "section", layers[k])

    others = [(s, d) for s in range(2) for d in range(n) if (s, d) != (0, 0)] if spread else []

    def more_copy(s, d):
        to = lax.rem(i + d, n)
        return pltpu.make_async_remote_copy(
            src_ref=more.at[:, pl.ds(pl.multiple_of(to * width, 128), width)],
            dst_ref=all_more.at[section, i],
            send_sem=more_sent.at[s, d],
            recv_sem=more_got.at[section, i],
            device_id={"section": lax.rem(section + s, 2), "col": to},
            device_id_type=pl.DeviceIdType.MESH,
        )

    def more_arrives(s, d):
        from_s, from_d = lax.rem(section + s, 2), lax.rem(i + d, n)
        return pltpu.make_async_remote_copy(
            src_ref=more.at[:, pl.ds(0, width)],
            dst_ref=all_more.at[from_s, from_d],
            send_sem=more_sent.at[s, d],
            recv_sem=more_got.at[from_s, from_d],
            device_id={"section": from_s, "col": from_d},
            device_id_type=pl.DeviceIdType.MESH,
        )

    for s, d in others:
        more_copy(s, d).start()
    if spread:
        all_more[section, i] = more[:, pl.ds(pl.multiple_of(i * width, 128), width)]

    for k, layer in enumerate(layers):
        @pl.when(section != layer)
        def _(k=k):
            carry_copy(k).start()

    def remote_col(source, target, sent, got, device):
        return remote(source, target, sent, got, "col", device)

    def sum_copy(c, j, right):
        slot = j + 1 if right else j
        return remote_col(
            outgoing.at[c, j], arrived.at[c, slot], sum_sent.at[c, j], sum_got.at[c, slot], i + 1 if right else i - 1
        )

    def block_copy(c, o, right, own=False):
        sent = n if own and not right else o
        return remote_col(whole.at[c, o], whole.at[c, o], block_sent.at[c, sent], block_got.at[0, c, o], i + 1 if right else i - 1)

    def slice_copy(c, d):
        to = lax.rem(i + d, n)
        return pltpu.make_async_remote_copy(
            src_ref=outgoing.at[c, i, :, pl.ds(pl.multiple_of(to * width, 128), width)],
            dst_ref=whole.at[section, c, i],
            send_sem=block_sent.at[c, d],
            recv_sem=block_got.at[section, c, i],
            device_id={"section": 0, "col": to},
            device_id_type=pl.DeviceIdType.MESH,
        )

    def arrive(c, slot):
        remote_col(outgoing.at[c, 0], arrived.at[c, slot], sum_sent.at[c, 0], sum_got.at[c, slot], i).wait_recv()

    def work(c, o):
        if polish:
            values = whole[c, o].astype(jnp.float32)
            mean, inverse = norm_parts(values)
            polished[c, o] = ((values - mean) * inverse * gain[...] + shift[...]).astype(jnp.bfloat16)

    rows = whole.shape[-2]
    per = max(1, min(chunks, LANES // (n * rows)))
    many = per * n * rows
    unit = max(1, n * per // n_row)
    tokens = chunks * n * rows

    def part_rows(source, b):
        return pl.ds(pl.multiple_of(source * tokens + b * many, many), many)

    def part_copy(b, d):
        to = lax.rem(me + d, n_row)
        return remote(
            leaving.at[d - 1, :, part_rows(0, b)],
            landed.at[:, part_rows(me, b)],
            part_sent.at[d - 1, b],
            part_got.at[me, b],
            "row",
            to,
        )

    def project(b, d):
        values = (polished if polish else whole)[pl.ds(b * per, per)].reshape(many, whole.shape[-1])
        here, there = part_rows(me, b), part_rows(0, b)
        t = lax.rem(me + d, n_row)
        for k in range(parts):
            column = columns(k * n_row + t)
            found = jnp.dot(values, weight[:, column], preferred_element_type=jnp.float32) + bias[:, column]
            if parts == 3 and k < 2:
                found = spin(found, cosines[here, :], sines[here, :])
            found = found.astype(jnp.bfloat16)
            if parts == 3 and k == 0:
                found = (found * jnp.asarray(HEAD_DIM**-0.5, jnp.bfloat16)).astype(jnp.bfloat16)

            @pl.when(d > 0)
            def _(k=k, found=found):
                leaving[d - 1, k, there, :] = found

            @pl.when(d == 0)
            def _(k=k, found=found):
                landed[k, here, :] = found

        @pl.when(d > 0)
        def _():
            part_copy(b, d).start()

    def sums_copy(d):
        to = lax.rem(i + d, n)
        return pltpu.make_async_remote_copy(
            src_ref=outs[-1].at[:, pl.ds(pl.multiple_of(to * width, 128), width)],
            dst_ref=all_sums.at[section, i],
            send_sem=last_sent.at[d],
            recv_sem=last_got.at[section, i],
            device_id={"section": 0, "col": to},
            device_id_type=pl.DeviceIdType.MESH,
        )

    def sums_arrive(s, o):
        return pltpu.make_async_remote_copy(
            src_ref=outs[-1].at[:, pl.ds(0, width)],
            dst_ref=all_sums.at[s, o],
            send_sem=last_sent.at[0],
            recv_sem=last_got.at[s, o],
            device_id={"section": 0, "col": o},
            device_id_type=pl.DeviceIdType.MESH,
        )

    def middle_slot(k):
        return jnp.maximum(lag * k + n - 1 - k, lag * (n - 1 - k) + k)

    def at(now, slot, allowed):
        since = now - slot
        c = jnp.maximum(since, 0) // n
        return c, allowed & (since >= 0) & (lax.rem(jnp.maximum(since, 0), n) == 0) & (since < n * chunks)

    def step(now, carry):
        for j in range(n - 1, 0, -1):
            c, due = at(now, lag * i + n - 1 - j, i < j)

            @pl.when(due & first)
            def _(c=c, j=j):
                outgoing[c, j] = partial[c, j]

            @pl.when(due & (i > 0))
            def _(c=c, j=j):
                arrive(c, j + 1)
                both = arrived[c, j + 1].astype(jnp.float32) + partial[c, j].astype(jnp.float32)
                outgoing[c, j] = both.astype(jnp.bfloat16)

            @pl.when(due)
            def _(c=c, j=j):
                sum_copy(c, j, True).start()

        for j in range(n - 1):
            c, due = at(now, lag * (n - 1 - i) + j, i > j)

            @pl.when(due & last)
            def _(c=c, j=j):
                outgoing[c, j] = partial[c, j]

            @pl.when(due & (i < n - 1))
            def _(c=c, j=j):
                arrive(c, j)
                both = arrived[c, j].astype(jnp.float32) + partial[c, j].astype(jnp.float32)
                outgoing[c, j] = both.astype(jnp.bfloat16)

            @pl.when(due)
            def _(c=c, j=j):
                sum_copy(c, j, False).start()

        c, due = at(now, middle_slot(i), i >= 0)

        @pl.when(due)
        def _():
            total[...] = partial[c, i].astype(jnp.float32)

        @pl.when(due & (i > 0))
        def _():
            arrive(c, i + 1)
            total[...] += arrived[c, i + 1].astype(jnp.float32)

        @pl.when(due & (i < n - 1))
        def _():
            arrive(c, i)
            total[...] += arrived[c, i].astype(jnp.float32)

        @pl.when(due)
        def _():
            block = middle(total[...], c, ins, outs)
            if spread:
                outgoing[c, i] = block
                for d in range(1, n):
                    slice_copy(c, d).start()

                @pl.when(section == 0)
                def _():
                    whole[0, c, i] = outgoing[c, i, :, pl.ds(pl.multiple_of(i * width, 128), width)]

                @pl.when(section != 0)
                def _():
                    slice_copy(c, 0).start()

            else:
                whole[c, i] = block
                work(c, i)

        if spread:
            return carry

        @pl.when(due & (i < n - 1))
        def _():
            block_copy(c, i, True, own=True).start()

        @pl.when(due & (i > 0))
        def _():
            block_copy(c, i, False, own=True).start()

        for o in range(n - 1):
            c, due = at(now, middle_slot(o) + lag * (i - o), i > o)

            @pl.when(due)
            def _(c=c, o=o):
                block_copy(c, o, True).wait_recv()

            @pl.when(due & (i < n - 1))
            def _(c=c, o=o):
                block_copy(c, o, True).start()

            @pl.when(due)
            def _(c=c, o=o):
                work(c, o)

        for o in range(1, n):
            c, due = at(now, middle_slot(o) + lag * (o - i), i < o)

            @pl.when(due)
            def _(c=c, o=o):
                block_copy(c, o, False).wait_recv()

            @pl.when(due & (i > 0))
            def _(c=c, o=o):
                block_copy(c, o, False).start()

            @pl.when(due)
            def _(c=c, o=o):
                work(c, o)

        if parts:
            since = now - (n * (per - 1) + 2 * lag * (n - 1))
            given = jnp.maximum(since, 0)
            turn = lax.rem(given, n * per) // unit

            @pl.when(since == 0)
            def _():
                weight_copy.wait()

            @pl.when((since >= 0) & (lax.rem(given, unit) == 0) & (turn < n_row) & (given < n * chunks))
            def _():
                project(given // (n * per), lax.rem(turn + 1, n_row))

        return carry

    steps = n * (chunks - 1) + 2 * lag * (n - 1) + 1
    lax.fori_loop(0, steps + (unit * (n_row - 1) if parts else 0), step, 0)

    if spread:
        for d in range(1, n):
            sums_copy(d).start()

        @pl.when(section == 0)
        def _():
            all_sums[0, i] = outs[-1][:, pl.ds(pl.multiple_of(i * width, 128), width)]

        @pl.when(section != 0)
        def _():
            sums_copy(0).start()

    def slice_arrives(c, s, o):
        return pltpu.make_async_remote_copy(
            src_ref=outgoing.at[c, 0, :, pl.ds(0, width)],
            dst_ref=whole.at[s, c, o],
            send_sem=block_sent.at[c, 0],
            recv_sem=block_got.at[s, c, o],
            device_id={"section": 0, "col": o},
            device_id_type=pl.DeviceIdType.MESH,
        )

    def settle(c, carry):
        for j in range(n):
            @pl.when(j != i)
            def _(j=j):
                sum_copy(c, j, True).wait_send()

        if spread:
            for d in range(1, n):
                slice_copy(c, d).wait_send()

            @pl.when(section != 0)
            def _():
                slice_copy(c, 0).wait_send()

            for s in range(2):
                for o in range(n):
                    @pl.when((section == 0) & ((s == 1) | (o != i)))
                    def _(s=s, o=o):
                        slice_arrives(c, s, o).wait_recv()

            return carry
        for o in range(n):
            @pl.when((o <= i) & (i < n - 1))
            def _(o=o):
                block_copy(c, o, True).wait_send()

            @pl.when((o > i) & (i > 0))
            def _(o=o):
                block_copy(c, o, True).wait_send()

        @pl.when(i > 0)
        def _():
            block_copy(c, i, False, own=True).wait_send()

        return carry

    lax.fori_loop(0, chunks, settle, 0)
    if spread:
        for d in range(1, n):
            sums_copy(d).wait_send()

        @pl.when(section != 0)
        def _():
            sums_copy(0).wait_send()

        for s in range(2):
            for o in range(n):
                @pl.when((section == 0) & ((s == 1) | (o != i)))
                def _(s=s, o=o):
                    sums_arrive(s, o).wait_recv()

    for s, d in others:
        more_copy(s, d).wait_send()
        more_arrives(s, d).wait_recv()

    if parts:
        def settle_parts(b, carry):
            for d in range(1, n_row):
                part_copy(b, d).wait_send()
                source = lax.rem(me + d, n_row)
                remote(
                    leaving.at[0, :, part_rows(0, b)],
                    landed.at[:, part_rows(source, b)],
                    part_sent.at[0, b],
                    part_got.at[source, b],
                    "row",
                    source,
                ).wait_recv()
            return carry

        lax.fori_loop(0, chunks // per, settle_parts, 0)

    for k, layer in enumerate(layers):
        @pl.when(section != layer)
        def _(k=k):
            carry_copy(k).wait_send()

        @pl.when(section == layer)
        def _(k=k):
            carry_copy(k).wait_recv()


def relay(middle, number, partial, ins, outs, n, spread=False, carry=(), behind=(), polish=(), project=(), n_row=1, lag=3, rows=RELAY_ROWS):
    tokens, features = partial.shape
    owned = tokens // n
    chunks = owned // rows
    blocks = lambda values: values.reshape(chunks, rows, features) if values.shape[0] == owned else values
    ins = [blocks(values) for values in ins] + list(polish) + list(project)
    parts = project[0].shape[1] // (n_row * LANES) if project else 0
    batches = chunks // max(1, min(chunks, LANES // (n * rows)))
    outs = list(outs) + ([(tokens, features)] if polish else []) + ([(parts, n_row * tokens, LANES)] if parts else []) + ([(2, n, 2, features // n), (2, n, 16, features // n)] if spread else [])
    out_shapes = [
        jax.ShapeDtypeStruct(
            (2, chunks, n, rows, features // n) if spread else (chunks, n, rows, features), jnp.bfloat16
        )
    ] + [
        jax.ShapeDtypeStruct((chunks, n, rows, features), jnp.bfloat16)
        if shape[0] == tokens
        else jax.ShapeDtypeStruct(shape, jnp.bfloat16)
        if shape[-1] == LANES
        else jax.ShapeDtypeStruct((chunks, rows, features) if shape[0] == owned else shape, jnp.float32)
        for shape in outs
    ]
    vmem, anywhere = pl.BlockSpec(memory_space=pltpu.VMEM), pl.BlockSpec(memory_space=pl.ANY)
    specs = [vmem] * (1 + len(ins))
    if project:
        specs[-4] = anywhere
    layers = tuple(layer for layer, _ in carry)
    carry = [values for _, values in carry]
    whole, *rest = pl.pallas_call(
        functools.partial(relay_kernel, middle, len(ins), len(outs), layers, len(behind), bool(polish), parts, n_row, n, chunks, lag, spread),
        in_specs=specs + [anywhere] * (len(carry) + len(behind)),
        out_specs=[vmem] * len(out_shapes) + [anywhere] * len(carry),
        out_shape=out_shapes + [jax.ShapeDtypeStruct(values.shape, values.dtype) for values in carry],
        scratch_shapes=[
            pltpu.VMEM((chunks, n + 1, rows, features), jnp.bfloat16),
            pltpu.VMEM((chunks, n, rows, features), jnp.bfloat16),
            pltpu.VMEM((rows, features), jnp.float32),
            pltpu.SemaphoreType.DMA((chunks, n)),
            pltpu.SemaphoreType.DMA((chunks, n + 1)),
            pltpu.SemaphoreType.DMA((chunks, n + 1)),
            pltpu.SemaphoreType.DMA((2 if spread else 1, chunks, n)),
            pltpu.SemaphoreType.DMA((max(1, len(carry)),)),
            pltpu.SemaphoreType.DMA((max(1, len(carry)),)),
            pltpu.SemaphoreType.DMA((n,)),
            pltpu.SemaphoreType.DMA((2, n)),
        ]
        + (
            [
                pltpu.VMEM((n_row - 1, parts, tokens, LANES), jnp.bfloat16),
                pltpu.SemaphoreType.DMA((n_row - 1, batches)),
                pltpu.SemaphoreType.DMA((n_row, batches)),
                pltpu.VMEM((features, project[0].shape[1]), jnp.bfloat16),
                pltpu.SemaphoreType.DMA,
            ]
            if parts
            else []
        )
        + ([pltpu.SemaphoreType.DMA((2, n)), pltpu.SemaphoreType.DMA((2, n))] if spread else []),
        compiler_params=pltpu.CompilerParams(
            collective_id=number, has_side_effects=True, vmem_limit_bytes=56 * 2**20
        ),
        cost_estimate=pl.CostEstimate(flops=0, bytes_accessed=35 * 10**7, transcendentals=0),
    )(partial.reshape(chunks, n, rows, features), *ins, *carry, *behind)
    shapes = {(chunks, rows, features): (owned, features), (chunks, n, rows, features): (tokens, features)}
    rest = [values.reshape(shapes.get(values.shape, values.shape)) for values in rest]
    return [whole.reshape((2, tokens, -1) if spread else (tokens, -1))] + rest


def gather_kernel(n, chunks, lag, own, small, angles, whole, smalls, normed, cosines, sines, sent, got, small_sent, small_got):
    section, i = lax.axis_index("section"), lax.axis_index("col")
    rows, width = own.shape[0] // chunks, own.shape[1]
    others = [(s, d) for s in range(2) for d in range(n) if (s, d) != (0, 0)]
    place = lambda s, d: {"section": lax.rem(section + s, 2), "col": lax.rem(i + d, n)}
    barrier = pltpu.get_barrier_semaphore()
    for s, d in others:
        pl.semaphore_signal(barrier, 1, device_id=place(s, d), device_id_type=pl.DeviceIdType.MESH)
    pl.semaphore_wait(barrier, len(others))

    def small_copy(s, d):
        return pltpu.make_async_remote_copy(
            src_ref=small,
            dst_ref=smalls.at[section, i],
            send_sem=small_sent.at[s, d],
            recv_sem=small_got.at[section, i],
            device_id=place(s, d),
            device_id_type=pl.DeviceIdType.MESH,
        )

    for s, d in others:
        small_copy(s, d).start()
    smalls[section, i] = small[...]

    def small_arrives(s, d):
        from_s, from_d = lax.rem(section + s, 2), lax.rem(i + d, n)
        return pltpu.make_async_remote_copy(
            src_ref=small,
            dst_ref=smalls.at[from_s, from_d],
            send_sem=small_sent.at[s, d],
            recv_sem=small_got.at[from_s, from_d],
            device_id=place(s, d),
            device_id_type=pl.DeviceIdType.MESH,
        )

    def norm(c):
        here = pl.ds(pl.multiple_of(c * rows, rows), rows)
        values = whole[here, :].astype(jnp.float32)
        mean, inverse = norm_parts(values)
        for o in range(n):
            part = slice(o * width, (o + 1) * width)
            gain, shift = smalls[0, o, 0:1, :], smalls[0, o, 2:3, :]
            normed[here, part] = ((values[:, part] - mean) * inverse * gain + shift).astype(jnp.bfloat16)

    def block(c, o, right, mine=False):
        part = whole.at[pl.ds(pl.multiple_of(c * rows, rows), rows), columns(o, width)]
        return remote(
            part, part, sent.at[c, n if mine and not right else o], got.at[c, o], "col", i + 1 if right else i - 1
        )

    def at(now, slot, allowed):
        since = jnp.maximum(now - slot, 0)
        return since // (n - 1), allowed & (now >= slot) & (lax.rem(since, n - 1) == 0) & (since < (n - 1) * chunks)

    def step(now, carry):
        c, due = at(now, 0, i >= 0)

        @pl.when(due)
        def _():
            here = pl.ds(pl.multiple_of(c * rows, rows), rows)
            whole[here, columns(i, width)] = own[here, :]

        @pl.when(due & (i < n - 1))
        def _():
            block(c, i, True, True).start()

        @pl.when(due & (i > 0))
        def _():
            block(c, i, False, True).start()

        for o in range(n):
            c, due = at(now, lag * jnp.abs(i - o), i != o)

            @pl.when(due)
            def _(c=c, o=o):
                block(c, o, True).wait_recv()

            @pl.when(due & (i > o) & (i < n - 1))
            def _(c=c, o=o):
                block(c, o, True).start()

            @pl.when(due & (i < o) & (i > 0))
            def _(c=c, o=o):
                block(c, o, False).start()

        c, due = at(now, lag * (n - 1), i >= 0)

        @pl.when(due)
        def _():
            norm(c)

        return carry

    turns = angles.shape[0] // 2
    lane = lax.broadcasted_iota(jnp.int32, (turns, LANES), 1)
    place_of = lax.broadcasted_iota(jnp.int32, (turns, LANES), 0)
    turned = lane % HEAD_DIM < 2 * turns
    picked = jnp.where(turned & (lane % turns == place_of), 1.0, 0.0)
    sign = jnp.where(lane % HEAD_DIM < turns, -1.0, 1.0)

    def spread_out(table, pick):
        return lax.dot_general(
            table, pick, (((0,), (0,)), ((), ())), precision=lax.Precision.HIGHEST, preferred_element_type=jnp.float32
        )

    still = jnp.where(turned[:1], 0.0, 1.0)
    cosines[...] = spread_out(angles[:turns, :], picked) + still
    sines[...] = spread_out(angles[turns:, :], picked * sign)
    for s, d in others:
        small_arrives(s, d).wait_recv()

    lax.fori_loop(0, (n - 1) * (chunks - 1) + lag * (n - 1) + 1, step, 0)

    def settle(c, carry):
        for o in range(n):
            @pl.when(((o <= i) & (i < n - 1)) | ((o > i) & (i > 0)))
            def _(o=o):
                block(c, o, True).wait_send()

        @pl.when(i > 0)
        def _():
            block(c, i, False, True).wait_send()

        return carry

    lax.fori_loop(0, chunks, settle, 0)
    for s, d in others:
        small_copy(s, d).wait_send()


def gathered(number, own, small, angles, n, lag=3, rows=64):
    tokens, width = own.shape
    chunks = tokens // rows
    vmem = pl.BlockSpec(memory_space=pltpu.VMEM)
    return pl.pallas_call(
        functools.partial(gather_kernel, n, chunks, lag),
        in_specs=[vmem] * 3,
        out_specs=[vmem] * 5,
        out_shape=[
            jax.ShapeDtypeStruct((tokens, n * width), own.dtype),
            jax.ShapeDtypeStruct((2, n) + small.shape, small.dtype),
            jax.ShapeDtypeStruct((tokens, n * width), own.dtype),
            jax.ShapeDtypeStruct((angles.shape[1], LANES), jnp.float32),
            jax.ShapeDtypeStruct((angles.shape[1], LANES), jnp.float32),
        ],
        scratch_shapes=[
            pltpu.SemaphoreType.DMA((chunks, n + 1)),
            pltpu.SemaphoreType.DMA((chunks, n)),
            pltpu.SemaphoreType.DMA((2, n)),
            pltpu.SemaphoreType.DMA((2, n)),
        ],
        compiler_params=pltpu.CompilerParams(
            collective_id=number, has_side_effects=True, vmem_limit_bytes=40 * 2**20
        ),
        cost_estimate=pl.CostEstimate(flops=0, bytes_accessed=25 * 10**7, transcendentals=0),
    )(own, small, angles)


def ffn_kernel(units, values, weight, down, gate_up, hidden, partial):
    both = jnp.dot(values[...], weight[...], preferred_element_type=jnp.float32)
    gate_up[...] = both
    gate, up = both[:, :units], both[:, units:]
    found = (gate * (1.0 / (1.0 + jnp.exp(-gate))) * up).astype(jnp.bfloat16)
    hidden[...] = found
    partial[...] = dot_last(found, down[...]).astype(partial.dtype)


def ffn_back_kernel(units, branch, gate_up, weight, down, d_gate_up, partial):
    d_hidden = jnp.dot(branch[...], down[...], preferred_element_type=jnp.float32)
    gate, up = gate_up[:, :units], gate_up[:, units:]
    sig = 1.0 / (1.0 + jnp.exp(-gate))
    d_gate_up[:, :units] = (d_hidden * up * sig * (1.0 + gate * (1.0 - sig))).astype(jnp.bfloat16)
    d_gate_up[:, units:] = (d_hidden * gate * sig).astype(jnp.bfloat16)
    partial[...] = dot_last(d_gate_up[...], weight[...]).astype(partial.dtype)


def ffn_call(kernel, layer, inputs, weight, down, outs, rows=256):
    tokens = inputs[0].shape[0]
    units = down.shape[1]
    by_rows = lambda width: pl.BlockSpec((rows, width), lambda i: (i, 0))
    once = lambda width: pl.BlockSpec((D, width), lambda i: (layer, 0), pipeline_mode=pl.Buffered(1))
    return pl.pallas_call(
        functools.partial(kernel, units),
        grid=(tokens // rows,),
        in_specs=[by_rows(values.shape[1]) for values in inputs] + [once(2 * units), once(units)],
        out_specs=[by_rows(width) for width, _ in outs],
        out_shape=[jax.ShapeDtypeStruct((tokens, width), kind) for width, kind in outs],
        compiler_params=pltpu.CompilerParams(vmem_limit_bytes=58 * 2**20),
        cost_estimate=pl.CostEstimate(flops=6 * tokens * D * units, bytes_accessed=4 * 10**7, transcendentals=0),
    )(*inputs, weight, down)


def rotary_angles(positions):
    half_dims = ROT // 2
    inverse_freq = 1.0 / 10000.0 ** (jnp.arange(half_dims, dtype=jnp.float32) * 2.0 / ROT)
    angles = positions.astype(jnp.float32)[None, :] * inverse_freq[:, None]
    return jnp.concatenate([jnp.cos(angles), jnp.sin(angles)])


def product(left, right):
    return jnp.dot(left, right, preferred_element_type=jnp.float32)


def per_device(
    inputs,
    cotangent,
    block_ids,
    norm_gains,
    norm_shifts,
    qkv_weight,
    qkv_bias,
    out_weight,
    gate_up_weight,
    down_weight,
):
    section = lax.axis_index("section")
    row = lax.axis_index("row")
    col = lax.axis_index("col")
    rows_axis = lax.axis_size("row")
    cols_axis = lax.axis_size("col")
    tokens, width = inputs.shape[1:]
    owned = tokens // cols_axis
    units = down_weight.shape[2]
    seq = tokens * rows_axis
    both = ("section", "row")
    whole_lanes = width == rows_axis * LANES
    heads = LANES // HEAD_DIM if whole_lanes else 1
    copies = 1 if whole_lanes else rows_axis * HEAD_DIM // width

    def expand(values):
        if whole_lanes:
            return values
        rows = values.shape[0]
        values = values.reshape(rows, -1, width // HEAD_DIM, HEAD_DIM)
        values = jnp.pad(jnp.repeat(values, copies, axis=2), ((0, 0), (0, 0), (0, 0), (0, LANES - HEAD_DIM)))
        return values.reshape(rows, -1)

    def contract(values):
        if whole_lanes:
            return values
        values = values.reshape(tokens, -1, rows_axis, LANES)[:, :, ::copies, :HEAD_DIM]
        return values.reshape(tokens, -1)

    def weights_of(block):
        block = block[0].reshape(block.shape[1], -1)
        return lax.all_gather(block, both, axis=0, tiled=True).reshape(2, D, -1)

    def mine(values):
        blocks = values.reshape(owned // RELAY_ROWS, cols_axis, RELAY_ROWS, -1)
        return lax.dynamic_index_in_dim(blocks, col, 1, keepdims=False).reshape(owned, -1)

    def my_features(values):
        return lax.dynamic_slice_in_dim(values, col * width, width, 1)

    own_small = jnp.concatenate([norm_gains[0], norm_shifts[0], qkv_bias[0], jnp.zeros((1, width), jnp.float32)])
    angles = rotary_angles(jnp.arange(seq, dtype=jnp.int32))
    stream, small, normed, cosines, sines = gathered(
        7, lax.dynamic_index_in_dim(inputs, section, 0, keepdims=False), own_small, angles, cols_axis
    )
    whole_small = small.transpose(0, 2, 1, 3).reshape(2, own_small.shape[0], D)
    gains, shifts = whole_small[:, :2], whole_small[:, 2:4]
    bias = lax.dynamic_index_in_dim(small, col, 1, keepdims=False)[:, 4:7].reshape(2, -1)

    qkv_w = weights_of(qkv_weight)
    out_w = weights_of(out_weight)
    gate_up_w = weights_of(gate_up_weight)
    down_w = weights_of(down_weight)

    ids = lax.dynamic_index_in_dim(block_ids, section, 0, keepdims=False)
    def feed_forward(layer, values):
        kind = jnp.bfloat16 if layer == 0 else jnp.float32
        if layer == 1 and units % LANES == 0:
            outs = [(2 * units, jnp.float32), (units, jnp.bfloat16), (D, kind)]
            return ffn_call(ffn_kernel, layer, [values], all_gate_up, all_down, outs)
        gate_up = product(values, gate_up_w[layer])
        hidden = (jax.nn.silu(gate_up[:, :units]) * gate_up[:, units:]).astype(jnp.bfloat16)
        return gate_up, hidden, dot_last(hidden, down_w[layer]).astype(kind)

    def feed_back(layer, branch, gate_up):
        if units % LANES == 0:
            outs = [(2 * units, jnp.bfloat16), (D, jnp.bfloat16)]
            return ffn_call(ffn_back_kernel, layer, [branch, gate_up], all_gate_up, all_down, outs)
        gate, up = gate_up[:, :units], gate_up[:, units:]
        d_hidden = product(branch, down_w[layer])
        sig = jax.nn.sigmoid(gate)
        d_gate = d_hidden * up * sig * (1.0 + gate * (1.0 - sig))
        d_up = d_hidden * gate * sig
        d_gate_up = jnp.concatenate([d_gate, d_up], axis=1).astype(jnp.bfloat16)
        return d_gate_up, dot_last(d_gate_up, gate_up_w[layer]).astype(jnp.bfloat16)

    all_gate_up, all_down = gate_up_w.reshape(2 * D, -1), down_w.reshape(2 * D, -1)
    kept = []
    hidden_out = []

    def gathered_part(which, half):
        values = lax.dynamic_index_in_dim(cotangent, which, 0, keepdims=False)
        cut = tokens // 4
        values = values[cut:] if half else values[:cut]
        return lax.all_gather(values, "col", axis=1, tiled=True)

    first_part = gathered_part(section, 0)
    waited = [first_part]
    for layer in range(2):
        if layer == 0:
            qkv = expand(product(normed, qkv_w[0]) + bias[0])
            spread, mixed, log_sums, attn_mix = attend(
                8, ids, heads, rows_axis, tokens, qkv=qkv, cosines=cosines, sines=sines
            )
        else:
            here = section + jnp.where(hidden_out[0][0, 0] == hidden_out[0][0, 0], 0, 1)
            second_part = gathered_part(here, 1)
            waited = [second_part]
            spread, mixed, log_sums, attn_mix = attend(9, ids, heads, rows_axis, tokens, spread=spread)
        attn_mix = contract(attn_mix)
        normed_two, after = relay(
            after_attention,
            layer,
            product(attn_mix, out_w[layer].T).astype(jnp.bfloat16),
            [mine(stream), gains[layer, 1:], shifts[layer, 1:]],
            [(owned, D)],
            cols_axis,
            behind=waited,
        )
        gate_up, hidden, partial = feed_forward(layer, normed_two)
        kept.append((stream, normed, spread, mixed, log_sums, attn_mix, after, normed_two, gate_up, hidden))
        if layer == 0:
            stream, normed, spread = relay(
                after_hidden,
                2,
                partial.astype(jnp.bfloat16),
                [after],
                [],
                cols_axis,
                polish=(gains[1, :1], shifts[1, :1]),
                project=(expand(qkv_w.reshape(2 * D, -1)), expand(bias[1:]), cosines, sines),
                n_row=rows_axis,
            )
            hidden_out.append(my_features(stream))
        else:
            blocks = partial.reshape(owned // RELAY_ROWS, cols_axis, RELAY_ROWS, D)
            owner = lax.broadcasted_iota(jnp.int32, blocks.shape, 1) == col
            blocks = blocks + jnp.where(owner, after.reshape(-1, 1, RELAY_ROWS, D), 0.0)
            result = blocks.reshape(tokens, D).astype(jnp.bfloat16)

    branch = jnp.concatenate([first_part, second_part])
    grad = mine(branch).astype(jnp.float32)
    weight_sums = [[], []]
    small_sums = []
    bias_grads = [None, None]
    input_out = [None, None]
    input_got = [None, None]
    hidden_got = [None, None]

    def collect(layer, term):
        weight_sums[layer].append(lax.psum_scatter(term, "row", scatter_dimension=0, tiled=True))
        return weight_sums[layer][-1]

    arrived = [[None] * 3, [None] * 3]
    def together(*values):
        return lax.optimization_barrier(values)

    def more_sums():
        rows = jnp.concatenate([bias_grads[1].reshape(3, -1), bias_grads[0].reshape(3, -1)])
        rows = lax.dynamic_update_slice(jnp.zeros((10, D), jnp.float32), rows, (0, col * width))
        return jnp.concatenate(small_sums + [rows])

    for layer in (1, 0):
        stream, normed, spread, mixed, log_sums, attn_mix, after, normed_two, gate_up, hidden = kept[layer]
        d_gate_up, partial = feed_back(layer, branch, gate_up)
        partial, down_term, gate_up_term = together(
            partial,
            dot_first(branch, hidden).astype(jnp.bfloat16),
            dot_first(normed_two, d_gate_up).astype(jnp.bfloat16),
        )
        down_sum, gate_up_sum = collect(layer, down_term), collect(layer, gate_up_term)
        grad_attn, d_after, sums_two, *got = relay(
            behind_norm,
            3 + layer,
            partial,
            [grad, after, gains[layer, 1:]],
            [(owned, D), (2, D)],
            cols_axis,
            carry=[]
            if layer == 1
            else [(0, hidden_out[0]), (1, hidden_out[1]), (1, input_out[1]), (1, weight_sums[1][2])],
            behind=[] if layer == 1 else [weight_sums[1][0]],
        )
        if layer == 1:
            result = jnp.where(d_after[0, 0] == d_after[0, 0], result, 0)
            hidden_out.append(lax.psum_scatter(result, "col", scatter_dimension=1, tiled=True))
        else:
            hidden_got[0], hidden_got[1], input_got[1], arrived[1][2] = got
        small_sums += [sums_two]
        d_mix, out_term = together(
            product(grad_attn, out_w[layer]).astype(jnp.bfloat16), dot_first(grad_attn, attn_mix).astype(jnp.bfloat16)
        )
        out_sum = collect(layer, out_term)
        d_qkv, arrived[layer][1] = attend_back(
            10 + layer,
            expand(d_mix),
            spread,
            mixed,
            log_sums,
            ids,
            cosines,
            sines,
            heads,
            rows_axis,
            layer,
            gate_up_sum,
        )
        d_qkv = contract(d_qkv)
        partial, qkv_term, bias_grads[layer] = together(
            dot_last(d_qkv, qkv_w[layer]).astype(jnp.bfloat16),
            dot_first(normed, d_qkv).astype(jnp.bfloat16),
            jnp.sum(d_qkv.astype(jnp.float32), axis=0),
        )
        if layer == 1:
            qkv_terms = jnp.pad(qkv_term, ((D, 0), (0, 0)))
        else:
            qkv_terms = lax.dynamic_update_slice(qkv_terms, qkv_term, (0, 0))
            qkv_grad = lax.psum_scatter(qkv_terms, both, scatter_dimension=0, tiled=True).astype(jnp.float32)
        branch, grad, sums_one, *got = relay(
            behind_norm,
            5 + layer,
            partial,
            [d_after, mine(stream), gains[layer, :1]]
            + ([] if layer == 1 else [more_sums()]),
            [(owned, D), (2, D)],
            cols_axis,
            spread=layer == 0,
            carry=[] if layer == 1 else [(0, down_sum), (0, out_sum), (1, weight_sums[1][0])],
            behind=[hidden_out[1]] if layer == 1 else [],
        )
        if layer == 0:
            late_sums, early_sums, arrived[0][0], arrived[0][2], arrived[1][0] = got
        small_sums += [sums_one]
        input_out[layer] = my_features(branch) if layer == 1 else branch

    hidden_states = jnp.where(
        section == 0, jnp.stack([hidden_out[0], hidden_got[0]]), jnp.stack([hidden_got[1], hidden_out[1]])
    )
    input_grads = jnp.where(section == 0, input_out[0], jnp.stack([input_got[1], input_out[1]])).astype(jnp.float32)
    down_grad, gate_up_grad, out_grad = (
        jnp.where(section == 0, first, second).astype(jnp.float32)
        + jnp.where(section == 0, first_got, second_got).astype(jnp.float32)
        for first, second, first_got, second_got in zip(*weight_sums, *arrived)
    )
    sums = lax.psum(jnp.concatenate([jnp.sum(early_sums, axis=(0, 1))[:12], jnp.sum(late_sums, axis=(0, 1))]), "row")
    early, last = sums[:12], sums[12:]
    norm_sums = jnp.where(section == 0, jnp.stack([last, early[4:6]]), jnp.stack([early[2:4], early[0:2]]))
    bias_sum = jnp.where(section == 0, early[9:12], early[6:9])
    return (
        hidden_states[None],
        input_grads[None],
        norm_sums[:, 0][None],
        norm_sums[:, 1][None],
        qkv_grad.reshape(qkv_weight.shape),
        bias_sum.reshape(qkv_bias.shape),
        out_grad[None],
        gate_up_grad.reshape(gate_up_weight.shape),
        down_grad[None],
    )


def solution(mesh):
    in_specs = (
        P(None, "row", "col"),
        P(None, "row", "col"),
        P(),
        P("section", None, "col"),
        P("section", None, "col"),
        P("section", "row", None, "col"),
        P("section", None, "col"),
        P("section", "row", "col"),
        P("section", "row", None, "col"),
        P("section", "row", "col"),
    )
    out_specs = (
        P("section", None, "row", "col"),
        P("section", None, "row", "col"),
        P("section", None, "col"),
        P("section", None, "col"),
        P("section", "row", None, "col"),
        P("section", None, "col"),
        P("section", "row", "col"),
        P("section", "row", None, "col"),
        P("section", "row", "col"),
    )
    return jax.shard_map(
        per_device, mesh=mesh, in_specs=in_specs, out_specs=out_specs, check_vma=False
    )
```
